32 devices in a mesh: seq: 8 (over z, x), tp: 4 (over y, core).
Axes of the slice: x: 2, y: 2, z: 4, core: 2. Of those that a mesh axis runs over, the one named last changes fastest.
Arguments:
- tokens: bfloat16 [6144, 1024], P('seq'), may hold values from -6 to 6
- grad_out: bfloat16 [6144, 1024], P('seq'), may hold values from -6 to 6
- noise_level: int32 [16], replicated, may hold values from 0 to 999
- context_mask: int32 [16], replicated, may hold values 0 or 1
- frame_clip: int32 [16], replicated, may hold values from 0 to 2, as said below
- level_table: bfloat16 [1000, 1024], replicated, may hold values from -6 to 6
- master: float32 [4, 4718592], P('tp', 'seq')
- moment_one: float32 [4, 4718592], P('tp', 'seq')
- moment_two: float32 [4, 4718592], P('tp', 'seq'), as said below
- average: float32 [4, 4718592], P('tp', 'seq')
Outputs:
- result: bfloat16 [6144, 1024], P('seq')
- input_grad: float32 [6144, 1024], P('seq')
- new_master: float32 [4, 4718592], P('tp', 'seq')
- new_one: float32 [4, 4718592], P('tp', 'seq')
- new_two: float32 [4, 4718592], P('tp', 'seq')
- new_average: float32 [4, 4718592], P('tp', 'seq')
The draws below stay inside these ranges and needn't reach their ends.
Inputs may be any that keep to these rules, and one draw needn't show every extreme that they name: `frame_clip`: clip 0 has exactly one frame among the 2 frames of each token group; every other clip has 4 to 7 frames. `moment_two`: positive.
All inputs are finite; a program needn't handle non-finite values.
Results may differ from the reference program's by a relative error of at most 0.02.
The reference program's roundings to bfloat16 on the way count: a program that leaves them out, or rounds other values in their place, can miss the bound.
Values may be sent and summed in bfloat16 or wider, within the bound.
A program may use at most 256 MiB of HBM per device.

```python
import math
import jax
import jax.numpy as jnp
from jax import lax

D = 1024
HEADS = 16
HEAD = 64
FF = 4096
LEVELS = 1000
TOK_FRAME = 384
F_DEV = 2
STEP = 7
FRAMES = 16
TOK_DEV = 768
TOKENS = 6144
CLIPS = 3
HD_TP = 256
FF_TP = 1024
MOD_TP = 1536
PER_TP = 4718592
N_SEQ = 8
N_TP = 4


def segment_values(first, second, third, fourth, fifth):
    index_row = jnp.arange(PER_TP, dtype=jnp.int32)
    edge_one = 3 * D * HD_TP
    edge_two = edge_one + HD_TP * D
    edge_three = edge_two + D * FF_TP
    edge_four = edge_three + FF_TP * D
    picked = jnp.where(index_row < edge_one, first, jnp.where(index_row < edge_two, second, jnp.where(index_row < edge_three, third, jnp.where(index_row < edge_four, fourth, fifth))))
    return jnp.broadcast_to(picked.astype(jnp.float32)[None, :], (N_TP, PER_TP))


def weight_scales():
    return segment_values(D ** (-0.5), 4.0 * D ** (-0.5), D ** (-0.5), FF ** (-0.5), D ** (-0.5))


def gradient_scales():
    root = TOKENS ** 0.5
    return segment_values(0.1 * root, 0.15 * root, 0.4 * root, 0.3 * root, 0.2 * root)


def base_noise(own_key):
    return jax.random.truncated_normal(own_key, -6.0, 6.0, (N_TP, PER_TP), jnp.float32)


def draw_master(key, part):
    return base_noise(jax.random.fold_in(key, 11)) * weight_scales()


def draw_average(key, part):
    return base_noise(jax.random.fold_in(key, 12)) * weight_scales()


def draw_moment_one(key, part):
    return base_noise(jax.random.fold_in(key, 13)) * gradient_scales()


def draw_moment_two(key, part):
    own_key = jax.random.fold_in(key, 14)
    factor = jnp.exp(jax.random.uniform(own_key, (N_TP, PER_TP), jnp.float32, math.log(0.5), math.log(8.0)))
    scales = gradient_scales()
    return scales * scales * factor


def draw_frame_clip(key, part):
    own_key = jax.random.fold_in(key, 5)
    first_key, second_key = jax.random.split(own_key)
    chosen = jax.random.randint(first_key, (N_SEQ, 1), 0, F_DEV)
    places = jnp.arange(F_DEV, dtype=jnp.int32)[None, :]
    in_long = (places == chosen).reshape(FRAMES)
    if CLIPS == 1:
        return jnp.zeros((FRAMES,), jnp.int32)
    short_count = N_SEQ * (F_DEV - 1)
    short_slot = jnp.where(in_long, 0, 1).astype(jnp.int32)
    ranks = jnp.clip(jnp.cumsum(short_slot) - 1, 0, short_count - 1)
    shuffled = jax.random.permutation(second_key, short_count).astype(jnp.int32)
    short_ids = 1 + jnp.minimum(shuffled[ranks] // 4, CLIPS - 2)
    return jnp.where(in_long, 0, short_ids).astype(jnp.int32)


def touch_ends(array, stream_key, smallest, high):
    spot = [jax.random.randint(jax.random.fold_in(stream_key, axis), (), 0, length) for axis, length in enumerate(array.shape)]
    widest = array.shape.index(max(array.shape))
    beside = spot[:widest] + [(spot[widest] + 1) % array.shape[widest]] + spot[widest + 1:]
    return array.at[tuple(spot)].set(smallest).at[tuple(beside)].set(high)


def block_scale(rng, extent, cuts, least, largest):
    def one(axis_at, blocks):
        steps = jax.random.uniform(jax.random.fold_in(jax.random.fold_in(rng, 6), axis_at), (blocks,), jnp.float32, least / len(cuts), largest / len(cuts))
        return jnp.repeat(jnp.exp(steps), extent[axis_at] // blocks).reshape((-1,) + (1,) * (len(extent) - axis_at - 1))

    factor_of = one(*cuts[0])
    for cut in cuts[1:]:
        factor_of = factor_of * one(*cut)
    return factor_of


def normal_values(key, shape, scale, limit, cuts=(), held_as=jnp.bfloat16):
    loudness = block_scale(key, shape, cuts, -0.22, 0.18) if cuts else 1.0
    values = jax.random.normal(key, shape, jnp.float32) * scale * loudness
    return jnp.minimum(jnp.maximum(values, -limit), limit).astype(held_as)


def setup_inputs(seed: int = 0) -> dict:
    splits = jax.random.split(jax.random.key(seed), 11)
    return {
        "tokens": normal_values(splits[0], (TOKENS, D), 1.0, 6.0, ((0, 8),)),
        "grad_out": normal_values(splits[1], (TOKENS, D), 1.0, 6.0, ((0, 8),)),
        "noise_level": touch_ends(jax.random.randint(splits[2], (FRAMES,), 0, LEVELS), jax.random.fold_in(splits[2], 1), 0, LEVELS - 1).astype(jnp.int32),
        "context_mask": touch_ends((jax.random.randint(splits[3], (FRAMES,), 0, 4) < 1).astype(jnp.int32), jax.random.fold_in(splits[3], 1), 0, 1),
        "frame_clip": draw_frame_clip(jax.random.fold_in(splits[10], 71), 0),
        "level_table": normal_values(splits[5], (LEVELS, D), 1.0, 6.0),
        "master": draw_master(jax.random.fold_in(splits[10], 71), 0),
        "moment_one": draw_moment_one(jax.random.fold_in(splits[10], 71), 0),
        "moment_two": draw_moment_two(jax.random.fold_in(splits[10], 71), 0),
        "average": draw_average(jax.random.fold_in(splits[10], 71), 0),
    }


NORM_EPSILON = 1e-06
RATE_FACTOR = 2.5
BETA_FIRST = 0.5
BETA_SECOND = 0.5
ADAM_EPSILON = 1e-08
WEIGHT_DECAY = 0.01
AVERAGE_RATE = 0.9
MASKED_SCORE = -1e+30
HIGHEST = lax.Precision.HIGHEST

@jax.custom_vjp
def low(v):
    return lax.optimization_barrier(v.astype(jnp.bfloat16)).astype(jnp.float32)

@jax.custom_vjp
def low_back(v):
    return v

def low_keep(v):
    return (low(v), None)

def low_pass(kept, grad):
    return (grad,)

def back_keep(v):
    return (v, None)

def back_low(kept, grad):
    return (low(grad),)
low.defvjp(low_keep, low_pass)
low_back.defvjp(back_keep, back_low)

def norm_rows(rows):
    centred = rows - lax.optimization_barrier(jnp.mean(rows, axis=1, keepdims=True))
    return centred * lax.rsqrt(lax.optimization_barrier(jnp.mean(centred * centred, axis=1, keepdims=True)) + NORM_EPSILON)

def unpack(weight_row):
    edge_one = 3 * D * HD_TP
    edge_two = edge_one + HD_TP * D
    edge_three = edge_two + D * FF_TP
    edge_four = edge_three + FF_TP * D
    return (weight_row[:edge_one].reshape(D, 3 * HD_TP), weight_row[edge_one:edge_two].reshape(HD_TP, D), weight_row[edge_two:edge_three].reshape(D, FF_TP), weight_row[edge_three:edge_four].reshape(FF_TP, D), weight_row[edge_four:].reshape(D, MOD_TP))

def assemble(weights):
    shards = [unpack(weights[shard]) for shard in range(N_TP)]
    w_query = jnp.concatenate([pieces[0][:, :HD_TP] for pieces in shards], axis=1)
    w_key = jnp.concatenate([pieces[0][:, HD_TP:2 * HD_TP] for pieces in shards], axis=1)
    w_value = jnp.concatenate([pieces[0][:, 2 * HD_TP:] for pieces in shards], axis=1)
    w_qkv = jnp.concatenate([w_query, w_key, w_value], axis=1)
    w_out = jnp.concatenate([pieces[1] for pieces in shards], axis=0)
    w_up = jnp.concatenate([pieces[2] for pieces in shards], axis=1)
    w_down = jnp.concatenate([pieces[3] for pieces in shards], axis=0)
    w_mod = jnp.concatenate([pieces[4] for pieces in shards], axis=1)
    return (w_qkv, w_out, w_up, w_down, w_mod)

def attention(queries, key_rows, value_rows, frame_clip):
    key_heads = key_rows.reshape(TOKENS, HEADS, HEAD)
    value_heads = value_rows.reshape(TOKENS, HEADS, HEAD)
    key_frames = jnp.arange(TOKENS, dtype=jnp.int32) // TOK_FRAME
    key_clips = jnp.repeat(frame_clip, TOK_FRAME)
    query_blocks = queries.reshape(N_SEQ, TOK_DEV, HEADS, HEAD)

    def one_block(arguments):
        block, position = arguments
        query_frames = lax.dynamic_slice_in_dim(key_frames, position * TOK_DEV, TOK_DEV)
        query_clips = lax.dynamic_slice_in_dim(key_clips, position * TOK_DEV, TOK_DEV)
        visible = (query_clips[:, None] == key_clips[None, :]) & (key_frames[None, :] <= query_frames[:, None])
        scores = low_back(jnp.einsum('qhe,khe->hqk', block, key_heads, precision=HIGHEST) * HEAD ** (-0.5))
        weights = jax.nn.softmax(jnp.where(visible[None], scores, MASKED_SCORE), axis=2)
        return jnp.einsum('hqk,khe->qhe', weights, value_heads, precision=HIGHEST)
    outputs = lax.map(jax.checkpoint(one_block), (query_blocks, jnp.arange(N_SEQ, dtype=jnp.int32)))
    return outputs.reshape(TOKENS, HEADS * HEAD)

def layer(rows, weights, condition, frame_clip):
    w_qkv, w_out, w_up, w_down, w_mod = assemble(low(weights))
    modulation = low_back(jnp.dot(condition, w_mod, precision=HIGHEST))
    shift_one, scale_one, gate_one, shift_two, scale_two, gate_two = [jnp.repeat(modulation[:, column_part * D:(column_part + 1) * D], TOK_FRAME, axis=0) for column_part in range(6)]
    first_in = low(norm_rows(rows) * (1.0 + scale_one) + shift_one)
    projected = low_back(low(jnp.dot(first_in, w_qkv, precision=HIGHEST)))
    width = HEADS * HEAD
    attended = low_back(low(attention(projected[:, :width], projected[:, width:2 * width], projected[:, 2 * width:], frame_clip)))
    attn = low_back(jnp.dot(attended, w_out, precision=HIGHEST))
    middle = rows + gate_one * attn
    second_in = low(norm_rows(middle) * (1.0 + scale_two) + shift_two)
    up_rows = low_back(jnp.dot(second_in, w_up, precision=HIGHEST))
    hidden = low(jax.nn.gelu(up_rows, approximate=True))
    mlp = low_back(jnp.dot(hidden, w_down, precision=HIGHEST))
    return middle + gate_two * mlp

def reference(tokens, grad_out, noise_level, context_mask, frame_clip, level_table, master, moment_one, moment_two, average):
    effective = noise_level * (1 - context_mask)
    one_hot = (effective[:, None] == jnp.arange(LEVELS, dtype=jnp.int32)[None, :]).astype(jnp.float32)
    embed = jnp.dot(one_hot, level_table.astype(jnp.float32), precision=HIGHEST)
    condition = low(jax.nn.silu(embed))

    def apply(rows, weights):
        return layer(rows, weights, condition, frame_clip)
    result, backward = jax.vjp(apply, tokens.astype(jnp.float32), master)
    input_grad, grads = backward(grad_out.astype(jnp.float32))
    learn_rate = RATE_FACTOR * D ** (-0.5)
    new_one = BETA_FIRST * moment_one + (1.0 - BETA_FIRST) * grads
    new_two = BETA_SECOND * moment_two + (1.0 - BETA_SECOND) * grads * grads
    first_hat = new_one / (1.0 - BETA_FIRST ** STEP)
    second_hat = new_two / (1.0 - BETA_SECOND ** STEP)
    new_master = master - learn_rate * (first_hat / (jnp.sqrt(second_hat) + ADAM_EPSILON) + WEIGHT_DECAY * master)
    new_average = AVERAGE_RATE * average + (1.0 - AVERAGE_RATE) * new_master
    return (result.astype(jnp.bfloat16), input_grad, new_master, new_one, new_two, new_average)
```

```python
import functools

import jax
import jax.numpy as jnp
from jax import lax
from jax.experimental import pallas as pl
from jax.experimental.pallas import tpu as pltpu
from jax.sharding import PartitionSpec as P

D = 1024
HEADS = 16
HEAD = 64
FF = 4096
TOK_FRAME = 384
STEP = 7
TP = 4
ZN = 4
HD = HEADS * HEAD // TP
QKV = 3 * HD
FT = FF // TP
MT = 6 * D // TP
F_DEV = 2
BROWS = HD + 2 * FT
LANES = 128
MCOLS = MT // LANES

NORM_EPSILON = 1e-06
RATE_FACTOR = 2.5
BETA_FIRST = 0.5
BETA_SECOND = 0.5
ADAM_EPSILON = 1e-08
WEIGHT_DECAY = 0.01
AVERAGE_RATE = 0.9
MESH = pl.DeviceIdType.MESH
VM = pl.BlockSpec(memory_space=pltpu.VMEM)
SM = pl.BlockSpec(memory_space=pltpu.SMEM)
DMA = pltpu.SemaphoreType.DMA
F32 = jnp.float32
BF16 = jnp.bfloat16
VMEM_LIMIT = 56 * 2**20


def mm(left, right):
    return jnp.dot(left, right, preferred_element_type=F32)


def mm_tn(left, right):
    return lax.dot_general(left, right, (((0,), (0,)), ((), ())), preferred_element_type=F32)


def mm_nt(left, right):
    return lax.dot_general(left, right, (((1,), (1,)), ((), ())), preferred_element_type=F32)


class Plan:
    def __init__(self, seq_count):
        self.n = seq_count
        self.r = seq_count // ZN
        self.shard = (D * QKV + BROWS * D + D * MT) // seq_count
        self.unit = self.shard // 3
        self.uq = self.unit // QKV
        self.ub = self.unit // D
        self.um = self.unit // MT
        self.nq = D // self.uq
        self.nb = self.nq + BROWS // self.ub
        self.nm = D // self.um
        self.first_mod = self.nb // 3
        self.flat_rows = self.unit // LANES
        self.frames = seq_count * F_DEV


def place(plan):
    s = lax.axis_index("seq")
    t = lax.axis_index("tp")
    return s, t, lax.div(s, plan.r), lax.rem(s, plan.r)


def remote(src, dst, send_sem, recv_sem, s, t):
    return pltpu.make_async_remote_copy(
        src_ref=src,
        dst_ref=dst,
        send_sem=send_sem,
        recv_sem=recv_sem,
        device_id=(s, t),
        device_id_type=MESH,
    )


def greet(peers):
    barrier = pltpu.get_barrier_semaphore()
    for s, t in peers:
        pl.semaphore_signal(barrier, inc=1, device_id=(s, t), device_id_type=MESH)
    pl.semaphore_wait(barrier, len(peers))


def by_kind(plan, k, act):
    @pl.when(k < plan.nq)
    def _():
        act("q")

    @pl.when((k >= plan.nq) & (k < plan.nb))
    def _():
        act("b")


def call(kernel, outs, scratch, ins, cid=None, cost=None, name=None):
    params = dict(vmem_limit_bytes=VMEM_LIMIT)
    if cid is not None:
        params.update(collective_id=cid, has_side_effects=True)
    return pl.pallas_call(
        kernel,
        out_shape=outs,
        in_specs=ins,
        out_specs=jax.tree.map(lambda _: VM, outs),
        scratch_shapes=scratch,
        compiler_params=pltpu.CompilerParams(**params),
        name=name,
    )


def gather_kernel(
    plan, master, cond, wq, wb, mod, tile, macc, mpart, mrecv,
    send_sem, recv_sem, msend, mrecv_sem, tsend, trecv,
):
    s, t, z, r = place(plan)
    n, rn = plan.n, plan.r
    greet(
        [(lax.rem(s + d, n), t) for d in range(1, n)]
        + [(s, lax.rem(t + d, TP)) for d in range(1, TP)]
    )

    def unit(k, kind):
        if kind == "q":
            return wq.at[pl.ds(pl.multiple_of(k * plan.uq, plan.uq), plan.uq)]
        return wb.at[pl.ds(pl.multiple_of((k - plan.nq) * plan.ub, plan.ub), plan.ub)]

    def move(k, lu, kind, sem, owner_r, to_s):
        ref = unit(k, kind)
        return remote(ref, ref, send_sem.at[lu, sem], recv_sem.at[lu, owner_r], to_s, t)

    def spread(k, lu, up, down, act):
        def for_kind(kind):
            if up is not None:
                @pl.when(up)
                def _():
                    act(move(k, lu, kind, 0, r, s + rn))
            if down is not None:
                @pl.when(down)
                def _():
                    act(move(k, lu, kind, 1, r, s - rn))
            for d in range(1, rn):
                act(move(k, lu, kind, 1 + d, r, z * rn + lax.rem(r + d, rn)))

        by_kind(plan, k, for_kind)

    start = lambda copy: copy.start()
    finish = lambda copy: copy.wait_send()

    for i in range(3):
        k = 3 * s + i
        base = i * plan.flat_rows

        def fill(kind):
            if kind == "q":
                rows, ref, at, cols = plan.uq, wq, k * plan.uq, QKV // LANES
            else:
                rows, ref, at, cols = plan.ub, wb, (k - plan.nq) * plan.ub, D // LANES
            at = pl.multiple_of(at, rows)
            for j in range(cols):
                ref[pl.ds(at, rows), j * LANES : (j + 1) * LANES] = master[
                    pl.ds(base + j, rows, stride=cols), :
                ].astype(BF16)

        by_kind(plan, k, fill)
        spread(k, 3 * z + i, z < ZN - 1, z > 0, start)

    macc[...] = jnp.zeros_like(macc)
    for i in range(3):
        k = 3 * s + i
        base = i * plan.flat_rows

        @pl.when(k >= plan.nb)
        def _():
            for j in range(MCOLS):
                tile[:, j * LANES : (j + 1) * LANES] = master[
                    pl.ds(base + j, plan.um, stride=MCOLS), :
                ].astype(BF16)
            macc[...] += mm(cond[k - plan.nb], tile[...])

    fm = plan.first_mod

    @pl.when(s >= fm)
    def _():
        for f in range(plan.frames):
            for j in range(MCOLS):
                mpart[f // F_DEV, pl.ds((f % F_DEV) * MCOLS + j, 1), :] = macc[
                    pl.ds(f, 1), j * LANES : (j + 1) * LANES
                ]
        mrecv[s - fm] = mpart[s]
        for d in range(1, n):
            to = lax.rem(s + d, n)
            remote(mpart.at[to], mrecv.at[s - fm], msend.at[d - 1], mrecv_sem.at[s - fm], to, t).start()

    for src in range(fm, n):
        @pl.when(s != src)
        def _():
            remote(
                mpart.at[0], mrecv.at[src - fm], msend.at[0], mrecv_sem.at[src - fm], s, t
            ).wait_recv()

    total = mrecv[0]
    for src in range(1, n - fm):
        total = total + mrecv[src]
    mod[t] = total
    for d in range(1, TP):
        remote(mod.at[t], mod.at[t], tsend.at[d - 1], trecv.at[t], s, lax.rem(t + d, TP)).start()

    for d in range(1, ZN):
        for i in range(3):
            for side in (0, 1):
                zs = z - d if side == 0 else z + d
                k = 3 * (zs * rn + r) + i
                lu = 3 * zs + i

                @pl.when((zs >= 0) & (zs < ZN))
                def _():
                    by_kind(plan, k, lambda kind: move(k, lu, kind, 0, r, s).wait_recv())
                    if side == 0:
                        spread(k, lu, z < ZN - 1, None, start)
                    else:
                        spread(k, lu, None, z > 0, start)

    for d in range(1, rn):
        other = lax.rem(r + d, rn)
        for zs in range(ZN):
            for i in range(3):
                k = 3 * (zs * rn + other) + i
                by_kind(plan, k, lambda kind: move(k, 3 * zs + i, kind, 0, other, s).wait_recv())

    for d in range(1, TP):
        other = lax.rem(t + d, TP)
        remote(mod.at[t], mod.at[other], tsend.at[0], trecv.at[other], s, t).wait_recv()
        remote(mod.at[t], mod.at[t], tsend.at[d - 1], trecv.at[t], s, other).wait_send()

    @pl.when(s >= fm)
    def _():
        for d in range(1, n):
            to = lax.rem(s + d, n)
            remote(mpart.at[to], mrecv.at[s - fm], msend.at[d - 1], mrecv_sem.at[s - fm], to, t).wait_send()

    for i in range(3):
        spread(3 * s + i, 3 * z + i, z < ZN - 1, z > 0, finish)
    for d in range(1, ZN):
        for i in range(3):
            for side in (0, 1):
                zs = z - d if side == 0 else z + d
                k = 3 * (zs * rn + r) + i
                lu = 3 * zs + i

                @pl.when((zs >= 0) & (zs < ZN))
                def _():
                    if side == 0:
                        spread(k, lu, z < ZN - 1, None, finish)
                    else:
                        spread(k, lu, None, z > 0, finish)


def gather_weights(plan, master, cond_units, cid):
    n = plan.n
    mrows = F_DEV * MCOLS
    return call(
        functools.partial(gather_kernel, plan),
        (
            jax.ShapeDtypeStruct((D, QKV), BF16),
            jax.ShapeDtypeStruct((BROWS, D), BF16),
            jax.ShapeDtypeStruct((TP, mrows, LANES), F32),
        ),
        [
            pltpu.VMEM((plan.um, MT), BF16),
            pltpu.VMEM((plan.frames, MT), F32),
            pltpu.VMEM((n, mrows, LANES), F32),
            pltpu.VMEM((n - plan.first_mod, mrows, LANES), F32),
            DMA((3 * ZN, plan.r + 1)),
            DMA((3 * ZN, plan.r)),
            DMA((n - 1,)),
            DMA((n - plan.first_mod,)),
            DMA((TP - 1,)),
            DMA((TP,)),
        ],
        [VM, VM],
        cid,
        name="gather_weights",
    )(master, cond_units)


def qkv_kernel(plan, q, kv, q_out, kv_out, qs, ks, rs, qr, kr, rr):
    s, t, z, r = place(plan)
    rn = plan.r
    greet(
        [(lax.rem(z + d, ZN) * rn + r, t) for d in range(1, ZN)]
        + [(z * rn + lax.rem(r + d, rn), t) for d in range(1, rn)]
    )

    def kv_copy(d):
        h = lax.rem(z + d, ZN)
        return remote(kv.at[h], kv_out.at[s], ks.at[d - 1], kr.at[z], h * rn + r, t)

    def q_copy(d):
        h = lax.rem(z + d, ZN)
        return remote(q.at[h], q_out.at[z], qs.at[d - 1], qr.at[z], h * rn + r, t)

    def side_copy(zs, e):
        at = zs * rn + r
        src = kv_out.at[at]
        return remote(src, src, rs.at[zs, e - 1], rr.at[at], z * rn + lax.rem(r + e, rn), t)

    for d in range(1, ZN):
        kv_copy(d).start()
    for d in range(1, ZN):
        q_copy(d).start()
    kv_out[s] = kv[z]
    q_out[z] = q[z]
    for e in range(1, rn):
        side_copy(z, e).start()
    for d in range(1, ZN):
        zs = lax.rem(z + d, ZN)
        remote(kv.at[0], kv_out.at[zs * rn + r], ks.at[0], kr.at[zs], s, t).wait_recv()
        for e in range(1, rn):
            side_copy(zs, e).start()
    for d in range(1, ZN):
        zs = lax.rem(z + d, ZN)
        remote(q.at[0], q_out.at[zs], qs.at[0], qr.at[zs], s, t).wait_recv()
    for e in range(1, rn):
        for zs in range(ZN):
            at = zs * rn + lax.rem(r + e, rn)
            remote(kv_out.at[at], kv_out.at[at], rs.at[0, 0], rr.at[at], s, t).wait_recv()
    for d in range(1, ZN):
        kv_copy(d).wait_send()
        q_copy(d).wait_send()
    for zs in range(ZN):
        for e in range(1, rn):
            side_copy(zs, e).wait_send()


def exchange_qkv(plan, q, kv, cid):
    rn = plan.r
    return call(
        functools.partial(qkv_kernel, plan),
        (
            jax.ShapeDtypeStruct((ZN, TOK_FRAME, LANES), BF16),
            jax.ShapeDtypeStruct((plan.n, F_DEV * TOK_FRAME, LANES), BF16),
        ),
        [DMA((ZN - 1,)), DMA((ZN - 1,)), DMA((ZN, rn - 1)), DMA((ZN,)), DMA((ZN,)), DMA((plan.n,))],
        [VM, VM],
        cid,
        name="exchange_qkv",
    )(q, kv)


def heads_kernel(plan, x, out, send_sem, recv_sem):
    s, t, z, r = place(plan)
    rn = plan.r
    greet([(lax.rem(z + d, ZN) * rn + r, t) for d in range(1, ZN)])

    def copy(d):
        to = lax.rem(z + d, ZN)
        return remote(x.at[to], out.at[z], send_sem.at[d - 1], recv_sem.at[z], to * rn + r, t)

    for d in range(1, ZN):
        copy(d).start()
    out[z] = x[z]
    for d in range(1, ZN):
        zs = lax.rem(z + d, ZN)
        remote(x.at[0], out.at[zs], send_sem.at[0], recv_sem.at[zs], s, t).wait_recv()
    for d in range(1, ZN):
        copy(d).wait_send()


def exchange_heads(plan, x, cid, name):
    return call(
        functools.partial(heads_kernel, plan),
        jax.ShapeDtypeStruct(x.shape, x.dtype),
        [DMA((ZN - 1,)), DMA((ZN,))],
        [VM],
        cid,
        name=name,
    )(x)


def dkv_kernel(plan, dq, dkv, q_out, kv_out, stage, side, qs, ks, rs, qr, kr, rr):
    s, t, z, r = place(plan)
    rn = plan.r
    greet(
        [(lax.rem(z + d, ZN) * rn + r, t) for d in range(1, ZN)]
        + [(z * rn + lax.rem(r + d, rn), t) for d in range(1, rn)]
    )

    def side_copy(d, e):
        zs = lax.rem(z + d, ZN)
        other = lax.rem(r + e, rn)
        return remote(
            dkv.at[zs * rn + other], side.at[e - 1, d], rs.at[d, e - 1], rr.at[d, e - 1],
            z * rn + other, t,
        )

    def q_copy(d):
        to = lax.rem(z + d, ZN)
        return remote(dq.at[to], q_out.at[z], qs.at[d - 1], qr.at[z], to * rn + r, t)

    def kv_copy(d):
        to = lax.rem(z + d, ZN)
        return remote(stage.at[d], kv_out.at[z], ks.at[d - 1], kr.at[z], to * rn + r, t)

    order = list(range(1, ZN)) + [0]
    for d in order:
        for e in range(1, rn):
            side_copy(d, e).start()
    for d in range(1, ZN):
        q_copy(d).start()
    q_out[z] = dq[z]
    for d in order:
        zs = lax.rem(z + d, ZN)
        total = dkv[zs * rn + r].astype(F32)
        for e in range(1, rn):
            side_copy(d, e).wait_recv()
            total = total + side[e - 1, d].astype(F32)
        if d == 0:
            kv_out[z] = total.astype(BF16)
        else:
            stage[d] = total.astype(BF16)
            kv_copy(d).start()
    for d in range(1, ZN):
        zs = lax.rem(z + d, ZN)
        remote(dq.at[0], q_out.at[zs], qs.at[0], qr.at[zs], s, t).wait_recv()
        remote(stage.at[d], kv_out.at[zs], ks.at[0], kr.at[zs], s, t).wait_recv()
    for d in range(1, ZN):
        q_copy(d).wait_send()
        kv_copy(d).wait_send()
    for d in order:
        for e in range(1, rn):
            side_copy(d, e).wait_send()


def exchange_dkv(plan, dq, dkv, cid):
    rn = plan.r
    rows = F_DEV * TOK_FRAME
    return call(
        functools.partial(dkv_kernel, plan),
        (
            jax.ShapeDtypeStruct((ZN, TOK_FRAME, LANES), BF16),
            jax.ShapeDtypeStruct((ZN, rows, LANES), BF16),
        ),
        [
            pltpu.VMEM((ZN, rows, LANES), BF16),
            pltpu.VMEM((rn - 1, ZN, rows, LANES), BF16),
            DMA((ZN - 1,)), DMA((ZN - 1,)), DMA((ZN, rn - 1)),
            DMA((ZN,)), DMA((ZN,)), DMA((ZN, rn - 1)),
        ],
        [VM, VM],
        cid,
        name="exchange_dkv",
    )(dq, dkv)


def padded(rows, low):
    zero = jnp.zeros_like(rows)
    return jnp.concatenate([rows, zero] if low else [zero, rows], axis=1)


def attend_kernel(plan, meta, q, kv, o, ot, lse, m_ref, l_ref, acc):
    r = meta[plan.frames]
    scale = HEAD ** (-0.5)

    def group(zq, carry):
        parts = []
        for f in range(F_DEV):
            frame = (zq * plan.r + r) * F_DEV + f
            clip = meta[frame]
            pack = q[zq]
            qz = padded(pack[:, f * HEAD : (f + 1) * HEAD], True) * jnp.asarray(scale, BF16)
            m_ref[...] = jnp.full_like(m_ref, -1e30)
            l_ref[...] = jnp.zeros_like(l_ref)
            acc[...] = jnp.zeros_like(acc)

            def block(j, inner):
                @pl.when(meta[j] == clip)
                def _():
                    rows = pl.multiple_of(lax.rem(j, F_DEV) * TOK_FRAME, TOK_FRAME)
                    keys = kv[lax.div(j, F_DEV), pl.ds(rows, TOK_FRAME), :]
                    st = mm_nt(keys, qz)
                    m_old = m_ref[...]
                    m_new = jnp.maximum(m_old, jnp.max(st, axis=0, keepdims=True))
                    p = jnp.exp(st - m_new)
                    alpha = jnp.exp(m_old - m_new)
                    m_ref[...] = m_new
                    l_ref[...] = l_ref[...] * alpha + jnp.sum(p, axis=0, keepdims=True)
                    acc[...] = acc[...] * alpha + mm_tn(keys, p.astype(BF16))

                return inner

            lax.fori_loop(0, frame + 1, block, 0)
            total = l_ref[...]
            out = acc[HEAD:, :] / total
            ot[zq * F_DEV + f] = out
            lse[zq * F_DEV + f] = m_ref[...] + jnp.log(total)
            parts.append(out.T)
        o[zq] = jnp.concatenate(parts, axis=1).astype(BF16)
        return carry

    lax.fori_loop(0, ZN, group, 0)


def attend(plan, meta, q, kv):
    frames = ZN * F_DEV
    return call(
        functools.partial(attend_kernel, plan),
        (
            jax.ShapeDtypeStruct((ZN, TOK_FRAME, LANES), BF16),
            jax.ShapeDtypeStruct((frames, HEAD, TOK_FRAME), F32),
            jax.ShapeDtypeStruct((frames, 1, TOK_FRAME), F32),
        ),
        [
            pltpu.VMEM((1, TOK_FRAME), F32),
            pltpu.VMEM((1, TOK_FRAME), F32),
            pltpu.VMEM((LANES, TOK_FRAME), F32),
        ],
        [SM, VM, VM],
        name="attend",
    )(meta, q, kv)


def attend_back_kernel(plan, meta, q, kv, do, ot, lse, dq, dkv, dkv_acc, dq_acc):
    r = meta[plan.frames]
    scale = HEAD ** (-0.5)
    dkv_acc[...] = jnp.zeros_like(dkv_acc)

    def group(zq, carry):
        parts = []
        for f in range(F_DEV):
            frame = (zq * plan.r + r) * F_DEV + f
            clip = meta[frame]
            columns = slice(f * HEAD, (f + 1) * HEAD)
            qz = padded(q[zq][:, columns], True) * jnp.asarray(scale, BF16)
            grads = do[zq][:, columns]
            doz = padded(grads, False)
            delta = jnp.sum(grads.astype(F32).T * ot[zq * F_DEV + f], axis=0, keepdims=True)
            logs = lse[zq * F_DEV + f]
            dq_acc[...] = jnp.zeros_like(dq_acc)

            def block(j, inner):
                @pl.when(meta[j] == clip)
                def _():
                    g = lax.div(j, F_DEV)
                    rows = pl.multiple_of(lax.rem(j, F_DEV) * TOK_FRAME, TOK_FRAME)
                    keys = kv[g, pl.ds(rows, TOK_FRAME), :]
                    pt = jnp.exp(mm_nt(keys, qz) - logs)
                    dst = (pt * (mm_nt(keys, doz) - delta)).astype(BF16)
                    dkv_acc[g, pl.ds(rows, TOK_FRAME), :] += mm(dst, qz) + mm(pt.astype(BF16), doz)
                    dq_acc[...] += mm_tn(keys, dst)

                return inner

            lax.fori_loop(0, frame + 1, block, 0)
            parts.append((dq_acc[:HEAD, :] * scale).T)
        dq[zq] = jnp.concatenate(parts, axis=1).astype(BF16)
        return carry

    lax.fori_loop(0, ZN, group, 0)
    dkv[...] = dkv_acc[...].astype(BF16)


def attend_back(plan, meta, q, kv, do, ot, lse):
    return call(
        functools.partial(attend_back_kernel, plan),
        (
            jax.ShapeDtypeStruct((ZN, TOK_FRAME, LANES), BF16),
            jax.ShapeDtypeStruct((plan.n, F_DEV * TOK_FRAME, LANES), BF16),
        ),
        [
            pltpu.VMEM((plan.n, F_DEV * TOK_FRAME, LANES), F32),
            pltpu.VMEM((LANES, TOK_FRAME), F32),
        ],
        [SM, VM, VM, VM, VM, VM],
        name="attend_back",
    )(meta, q, kv, do, ot, lse)


def total_kernel(chunks, part, out, sbuf, cbuf, ybuf, yrecv, ss, cs, ys, yr, osem, orsem):
    s = lax.axis_index("seq")
    t = lax.axis_index("tp")
    core = lax.rem(t, 2)
    sibling = t + 1 - 2 * core
    across = lax.rem(t + 2, TP)
    greet([(s, sibling), (s, across)])
    half = TOK_FRAME
    rows = half // chunks
    mine = core * half
    theirs = half - mine

    def c_copy(ch):
        return remote(sbuf.at[ch], cbuf.at[ch], ss.at[ch], cs.at[ch], s, sibling)

    def y_copy(ch):
        return remote(ybuf.at[ch], yrecv.at[ch], ys.at[ch], yr.at[ch], s, across)

    def o_copy(ch, base):
        ref = out.at[pl.ds(pl.multiple_of(base + ch * rows, rows), rows)]
        return remote(ref, ref, osem.at[ch], orsem.at[ch], s, sibling)

    for ch in range(chunks):
        sbuf[ch] = part[pl.ds(pl.multiple_of(theirs + ch * rows, rows), rows), :].astype(BF16)
        c_copy(ch).start()
    for ch in range(chunks):
        c_copy(ch).wait_recv()
        ybuf[ch] = (
            part[pl.ds(pl.multiple_of(mine + ch * rows, rows), rows), :] + cbuf[ch].astype(F32)
        ).astype(BF16)
        y_copy(ch).start()
    for ch in range(chunks):
        y_copy(ch).wait_recv()
        out[pl.ds(pl.multiple_of(mine + ch * rows, rows), rows), :] = ybuf[ch].astype(F32) + yrecv[
            ch
        ].astype(F32)
        o_copy(ch, mine).start()
    for ch in range(chunks):
        o_copy(ch, theirs).wait_recv()
    for ch in range(chunks):
        c_copy(ch).wait_send()
        y_copy(ch).wait_send()
        o_copy(ch, mine).wait_send()


def total_tp(part, cid, name):
    chunks = 4
    rows = TOK_FRAME // chunks
    buf = pltpu.VMEM((chunks, rows, D), BF16)
    return call(
        functools.partial(total_kernel, chunks),
        jax.ShapeDtypeStruct(part.shape, F32),
        [buf] * 4 + [DMA((chunks,))] * 6,
        [VM],
        cid,
        name=name,
    )(part)


def scatter_kernel(plan, gq, gb, oq, ob, rq, rb, cq, cb, rs, rr, cs, cr):
    s, t, z, r = place(plan)
    rn = plan.r
    greet(
        [(z * rn + lax.rem(r + d, rn), t) for d in range(1, rn)]
        + [(lax.rem(z + d, ZN) * rn + r, t) for d in (1, ZN - 1)]
    )

    def own(k, kind):
        if kind == "q":
            return gq.at[pl.ds(pl.multiple_of(k * plan.uq, plan.uq), plan.uq)]
        return gb.at[pl.ds(pl.multiple_of((k - plan.nq) * plan.ub, plan.ub), plan.ub)]

    a = 2 - lax.div(z, 2)
    b = 2 * lax.div(ZN - 1 - z, ZN - 1)

    def owner(j):
        return lax.rem(a * j + b, 3)

    def side_copy(zo, i, d, kind):
        other = lax.rem(r + d, rn)
        k = 3 * (zo * rn + other) + i
        lu = 3 * zo + i
        buf = rq if kind == "q" else rb
        return k, remote(
            own(k, kind), buf.at[d - 1, lu], rs.at[lu, d - 1], rr.at[lu, d - 1], z * rn + other, t
        )

    def chain_copy(lu, kind, side, to):
        src = (rq if kind == "q" else rb).at[0, lu]
        dst = (cq if kind == "q" else cb).at[side, lu]
        return remote(src, dst, cs.at[lu], cr.at[lu, side], to, t)

    for j in range(3):
        for i in range(3):
            for d in range(1, rn):
                k = 3 * (owner(j) * rn + lax.rem(r + d, rn)) + i
                by_kind(plan, k, lambda kind: side_copy(owner(j), i, d, kind)[1].start())

    for j in range(3):
        zo = owner(j)
        for i in range(3):
            k = 3 * (zo * rn + r) + i
            lu = 3 * zo + i

            def step(kind):
                side = rq if kind == "q" else rb
                chain = cq if kind == "q" else cb
                out = oq if kind == "q" else ob
                for d in range(1, rn):
                    remote(
                        own(k, kind), side.at[d - 1, lu], rs.at[lu, d - 1], rr.at[lu, d - 1], s, t
                    ).wait_recv()
                total = own(k, kind)[...].astype(F32)
                for d in range(1, rn):
                    total = total + side[d - 1, lu].astype(F32)
                out[i] = total

                @pl.when((zo <= z) & (z < ZN - 1))
                def _():
                    chain_copy(lu, kind, 0, s).wait_recv()
                    out[i] += chain[0, lu].astype(F32)

                @pl.when((zo >= z) & (z > 0))
                def _():
                    chain_copy(lu, kind, 1, s).wait_recv()
                    out[i] += chain[1, lu].astype(F32)

                @pl.when(zo != z)
                def _():
                    side[0, lu] = out[i].astype(BF16)

                @pl.when(zo < z)
                def _():
                    chain_copy(lu, kind, 0, s - rn).start()

                @pl.when(zo > z)
                def _():
                    chain_copy(lu, kind, 1, s + rn).start()

            by_kind(plan, k, step)

    for j in range(3):
        zo = owner(j)
        for i in range(3):
            for d in range(1, rn):
                k = 3 * (zo * rn + lax.rem(r + d, rn)) + i
                by_kind(plan, k, lambda kind: side_copy(zo, i, d, kind)[1].wait_send())
            k = 3 * (zo * rn + r) + i

            def close(kind):
                @pl.when(zo != z)
                def _():
                    chain_copy(3 * zo + i, kind, 0, s).wait_send()

            by_kind(plan, k, close)


def scatter_grads(plan, gq, gb, cid):
    rn = plan.r
    return call(
        functools.partial(scatter_kernel, plan),
        (
            jax.ShapeDtypeStruct((3, plan.uq, QKV), F32),
            jax.ShapeDtypeStruct((3, plan.ub, D), F32),
        ),
        [
            pltpu.VMEM((rn - 1, 9, plan.uq, QKV), BF16),
            pltpu.VMEM((rn - 1, 9, plan.ub, D), BF16),
            pltpu.VMEM((2, 9, plan.uq, QKV), BF16),
            pltpu.VMEM((2, 9, plan.ub, D), BF16),
            DMA((9, rn - 1)), DMA((9, rn - 1)), DMA((9,)), DMA((9, 2)),
        ],
        [VM, VM],
        cid,
        name="scatter_grads",
    )(gq, gb)


def adam_kernel(plan, meta, oq, ob, cond, dmod, master, one, two, average, n_master, n_one, n_two, n_average):
    s = meta[0]
    rate = RATE_FACTOR * D ** (-0.5)
    scale_one = 1.0 / (1.0 - BETA_FIRST**STEP)
    scale_two = 1.0 / (1.0 - BETA_SECOND**STEP)

    def update(rows, grad):
        first = BETA_FIRST * one[rows, :] + (1.0 - BETA_FIRST) * grad
        second = BETA_SECOND * two[rows, :] + (1.0 - BETA_SECOND) * grad * grad
        weight = master[rows, :]
        weight = weight - rate * (
            (first * scale_one) / (jnp.sqrt(second * scale_two) + ADAM_EPSILON)
            + WEIGHT_DECAY * weight
        )
        n_one[rows, :] = first
        n_two[rows, :] = second
        n_master[rows, :] = weight
        n_average[rows, :] = AVERAGE_RATE * average[rows, :] + (1.0 - AVERAGE_RATE) * weight

    for i in range(3):
        k = 3 * s + i
        base = i * plan.flat_rows

        def from_matrix(kind):
            src = oq if kind == "q" else ob
            rows = plan.uq if kind == "q" else plan.ub
            cols = (QKV if kind == "q" else D) // LANES
            for j in range(cols):
                update(
                    pl.ds(base + j, rows, stride=cols), src[i, :, j * LANES : (j + 1) * LANES]
                )

        by_kind(plan, k, from_matrix)

        @pl.when(k >= plan.nb)
        def _():
            at = cond[k - plan.nb]
            for j in range(MCOLS):
                update(
                    pl.ds(base + j, plan.um, stride=MCOLS),
                    mm(at, dmod[:, j * LANES : (j + 1) * LANES]),
                )


def adam(plan, meta, oq, ob, cond_rows, dmod, master, one, two, average):
    shape = jax.ShapeDtypeStruct(master.shape, F32)
    return call(
        functools.partial(adam_kernel, plan),
        (shape,) * 4,
        [],
        [SM] + [VM] * 8,
        name="adam",
    )(meta, oq, ob, cond_rows, dmod, master, one, two, average)


def normalize(rows):
    centred = rows - jnp.mean(rows, axis=1, keepdims=True)
    inverse = lax.rsqrt(jnp.mean(centred * centred, axis=1, keepdims=True) + NORM_EPSILON)
    return (centred * inverse, inverse)


def norm_back(grads, normed, inverse):
    return inverse * (
        grads
        - jnp.mean(grads, axis=1, keepdims=True)
        - normed * jnp.mean(grads * normed, axis=1, keepdims=True)
    )


def by_frame(rows):
    return rows.reshape(F_DEV, TOK_FRAME, rows.shape[1])


def frame_scale(rows, factor):
    return (by_frame(rows) * factor[:, None, :]).reshape(rows.shape)


def frame_affine(rows, factor, offset_rows):
    return (by_frame(rows) * (1.0 + factor)[:, None, :] + offset_rows[:, None, :]).reshape(
        rows.shape
    )


def frame_total(rows):
    return jnp.sum(by_frame(rows), axis=1)


def pack_heads(rows):
    return rows.reshape(F_DEV, TOK_FRAME, ZN, HEAD).transpose(2, 1, 0, 3).reshape(
        ZN, TOK_FRAME, F_DEV * HEAD
    )


def unpack_heads(packs):
    return packs.reshape(ZN, TOK_FRAME, F_DEV, HEAD).transpose(2, 1, 0, 3).reshape(
        F_DEV * TOK_FRAME, ZN * HEAD
    )


def local(
    tokens,
    grad_out,
    noise_level,
    context_mask,
    frame_clip,
    level_table,
    master,
    moment_one,
    moment_two,
    average,
):
    plan = Plan(lax.axis_size("seq"))
    s = lax.axis_index("seq")
    t = lax.axis_index("tp")
    rows = F_DEV * TOK_FRAME
    flat = lambda x: x.reshape(-1, LANES)

    effective = noise_level * (1 - context_mask)
    one_hot = (
        effective[:, None] == jnp.arange(level_table.shape[0], dtype=jnp.int32)[None, :]
    ).astype(BF16)
    condition = jax.nn.silu(mm(one_hot, level_table)).astype(BF16)
    cond_units = condition.reshape(plan.frames, plan.nm, plan.um).transpose(1, 0, 2)

    wq, wb, mod_blocks = gather_weights(plan, flat(master), cond_units, 0)
    w_out, w_up, w_down = wb[:HD], wb[HD : HD + FT], wb[HD + FT :]
    modulation = (
        mod_blocks.reshape(TP, F_DEV, MT).transpose(1, 0, 2).reshape(F_DEV, TP * MT)
    )
    shift_one, scale_one, gate_one, shift_two, scale_two, gate_two = [
        modulation[:, part * D : (part + 1) * D] for part in range(6)
    ]

    inputs = tokens.astype(F32)
    normed_one, inverse_one = normalize(inputs)
    first_in = frame_affine(normed_one, scale_one, shift_one).astype(BF16)
    projected = mm(first_in, wq).astype(BF16)
    kv = jnp.stack(
        [
            jnp.concatenate(
                [
                    projected[:, HD + h * HEAD : HD + (h + 1) * HEAD],
                    projected[:, 2 * HD + h * HEAD : 2 * HD + (h + 1) * HEAD],
                ],
                axis=1,
            )
            for h in range(ZN)
        ]
    )
    q_mine, kv_all = exchange_qkv(plan, pack_heads(projected[:, :HD]), kv, 1)
    meta = jnp.concatenate([frame_clip, lax.rem(s, plan.r)[None]]).astype(jnp.int32)
    o_mine, o_rows, lse = attend(plan, meta, q_mine, kv_all)
    attended = unpack_heads(exchange_heads(plan, o_mine, 2, "exchange_o"))
    attn = total_tp(mm(attended, w_out), 3, "total_attn")

    middle = inputs + frame_scale(attn, gate_one)
    normed_two, inverse_two = normalize(middle)
    second_in = frame_affine(normed_two, scale_two, shift_two).astype(BF16)
    up_rows = mm(second_in, w_up)
    activated, gelu_back = jax.vjp(functools.partial(jax.nn.gelu, approximate=True), up_rows)
    hidden = activated.astype(BF16)
    mlp = total_tp(mm(hidden, w_down), 4, "total_mlp")
    result = (middle + frame_scale(mlp, gate_two)).astype(BF16)
    upstream = grad_out.astype(F32)
    gate_two_grad = frame_total(mlp * upstream)
    mlp_grad = frame_scale(upstream, gate_two).astype(BF16)
    down_grad = mm_tn(hidden, mlp_grad)
    up_grad = gelu_back(mm_nt(mlp_grad, w_down))[0].astype(BF16)
    up_weight_grad = mm_tn(second_in, up_grad)
    second_grad = total_tp(mm_nt(up_grad, w_up), 5, "total_second")
    scale_two_grad = frame_total(second_grad * normed_two)
    shift_two_grad = frame_total(second_grad)
    middle_grad = upstream + norm_back(
        frame_scale(second_grad, 1.0 + scale_two), normed_two, inverse_two
    )
    gate_one_grad = frame_total(attn * middle_grad)
    attn_grad = frame_scale(middle_grad, gate_one).astype(BF16)
    out_weight_grad = mm_tn(attended, attn_grad)
    attended_grad = mm_nt(attn_grad, w_out).astype(BF16)
    do_mine = exchange_heads(plan, pack_heads(attended_grad), 6, "exchange_do")
    dq_mine, dkv_all = attend_back(plan, meta, q_mine, kv_all, do_mine, o_rows, lse)
    dq_heads, dkv_heads = exchange_dkv(plan, dq_mine, dkv_all, 7)
    qkv_grad = jnp.concatenate(
        [unpack_heads(dq_heads)]
        + [dkv_heads[h][:, :HEAD] for h in range(ZN)]
        + [dkv_heads[h][:, HEAD:] for h in range(ZN)],
        axis=1,
    )
    qkv_weight_grad = mm_tn(first_in, qkv_grad)
    first_grad = total_tp(mm_nt(qkv_grad, wq), 8, "total_first")
    scale_one_grad = frame_total(first_grad * normed_one)
    shift_one_grad = frame_total(first_grad)
    input_grad = middle_grad + norm_back(
        frame_scale(first_grad, 1.0 + scale_one), normed_one, inverse_one
    )
    mod_terms = jnp.concatenate(
        [
            shift_one_grad,
            scale_one_grad,
            gate_one_grad,
            shift_two_grad,
            scale_two_grad,
            gate_two_grad,
        ],
        axis=1,
    )
    mod_grad = lax.all_gather(
        lax.dynamic_slice_in_dim(mod_terms, t * MT, MT, axis=1), "seq", axis=0, tiled=True
    ).astype(BF16)
    grads_b = jnp.concatenate([out_weight_grad, up_weight_grad, down_grad], axis=0).astype(BF16)
    own_q, own_b = scatter_grads(plan, qkv_weight_grad.astype(BF16), grads_b, 9)
    updated = adam(
        plan,
        s[None].astype(jnp.int32),
        own_q,
        own_b,
        cond_units.transpose(0, 2, 1),
        mod_grad,
        flat(master),
        flat(moment_one),
        flat(moment_two),
        flat(average),
    )
    new_master, new_one, new_two, new_average = [x.reshape(master.shape) for x in updated]
    return (result, input_grad, new_master, new_one, new_two, new_average)


def solution(mesh):
    token_spec = P("seq", None)
    weight_spec = P("tp", "seq")
    in_specs = (token_spec, token_spec, P(), P(), P(), P()) + (weight_spec,) * 4
    out_specs = (token_spec, token_spec) + (weight_spec,) * 4
    return jax.shard_map(local, mesh=mesh, in_specs=in_specs, out_specs=out_specs, check_vma=False)
```

```python
import functools

import jax
import jax.numpy as jnp
from jax import lax
from jax.experimental import pallas as pl
from jax.experimental.pallas import tpu as pltpu
from jax.sharding import PartitionSpec as P

D = 1024
HEADS = 16
HEAD = 64
FF = 4096
TOK_FRAME = 384
STEP = 7
TP = 4
ZN = 4
HD = HEADS * HEAD // TP
QKV = 3 * HD
FT = FF // TP
MT = 6 * D // TP
F_DEV = 2
BROWS = HD + 2 * FT
LANES = 128
MCOLS = MT // LANES
PACK = TOK_FRAME // 2
TILE = 256
TILES = D // TILE

NORM_EPSILON = 1e-06
RATE_FACTOR = 2.5
BETA_FIRST = 0.5
BETA_SECOND = 0.5
ADAM_EPSILON = 1e-08
WEIGHT_DECAY = 0.01
AVERAGE_RATE = 0.9
GELU_A = 0.7978845608028654
GELU_B = 0.044715
MESH = pl.DeviceIdType.MESH
VM = pl.BlockSpec(memory_space=pltpu.VMEM)
SM = pl.BlockSpec(memory_space=pltpu.SMEM)
DMA = pltpu.SemaphoreType.DMA
F32 = jnp.float32
BF16 = jnp.bfloat16
VMEM_LIMIT = 56 * 2**20


def mm(left, right):
    return jnp.dot(left, right, preferred_element_type=F32)


def mm_tn(left, right):
    return lax.dot_general(left, right, (((0,), (0,)), ((), ())), preferred_element_type=F32)


def mm_nt(left, right):
    return lax.dot_general(left, right, (((1,), (1,)), ((), ())), preferred_element_type=F32)


def normalize(rows):
    centred = rows - jnp.mean(rows, axis=1, keepdims=True)
    inverse = lax.rsqrt(jnp.mean(centred * centred, axis=1, keepdims=True) + NORM_EPSILON)
    return (centred * inverse, inverse)


def norm_back(grads, normed, inverse):
    return inverse * (
        grads
        - jnp.mean(grads, axis=1, keepdims=True)
        - normed * jnp.mean(grads * normed, axis=1, keepdims=True)
    )


class Plan:
    def __init__(self, seq_count):
        self.n = seq_count
        self.r = seq_count // ZN
        self.shard = (D * QKV + BROWS * D + D * MT) // seq_count
        self.unit = self.shard // 3
        self.uq = self.unit // QKV
        self.ub = self.unit // D
        self.um = self.unit // MT
        self.nq = D // self.uq
        self.nb = self.nq + BROWS // self.ub
        self.nm = D // self.um
        self.first_mod = self.nb // 3
        self.flat_rows = self.unit // LANES
        self.frames = seq_count * F_DEV


def place(plan):
    s = lax.axis_index("seq")
    t = lax.axis_index("tp")
    return s, t, lax.div(s, plan.r), lax.rem(s, plan.r)


def remote(src, dst, send_sem, recv_sem, s, t):
    return pltpu.make_async_remote_copy(
        src_ref=src,
        dst_ref=dst,
        send_sem=send_sem,
        recv_sem=recv_sem,
        device_id=(s, t),
        device_id_type=MESH,
    )


def greet(peers):
    barrier = pltpu.get_barrier_semaphore()
    for s, t in peers:
        pl.semaphore_signal(barrier, inc=1, device_id=(s, t), device_id_type=MESH)
    pl.semaphore_wait(barrier, len(peers))


def by_kind(plan, k, act):
    @pl.when(k < plan.nq)
    def _():
        act("q")

    @pl.when((k >= plan.nq) & (k < plan.nb))
    def _():
        act("b")


def call(kernel, outs, scratch, ins, cid=None, cost=None, name=None):
    params = dict(vmem_limit_bytes=VMEM_LIMIT)
    if cid is not None:
        params.update(collective_id=cid, has_side_effects=True)
    return pl.pallas_call(
        kernel,
        out_shape=outs,
        in_specs=ins,
        out_specs=jax.tree.map(lambda _: VM, outs),
        scratch_shapes=scratch,
        compiler_params=pltpu.CompilerParams(**params),
        name=name,
    )


def gather_kernel(
    plan, master, cond, wq, wb, mod, wo, tile, macc, mpart, mrecv,
    send_sem, recv_sem, msend, mrecv_sem, tsend, trecv, osend, orecv,
):
    s, t, z, r = place(plan)
    n, rn = plan.n, plan.r
    greet(
        [(lax.rem(s + d, n), t) for d in range(1, n)]
        + [(s, lax.rem(t + d, TP)) for d in range(1, TP)]
    )

    def unit(k, kind):
        if kind == "q":
            return wq.at[pl.ds(pl.multiple_of(k * plan.uq, plan.uq), plan.uq)]
        return wb.at[pl.ds(pl.multiple_of((k - plan.nq) * plan.ub, plan.ub), plan.ub)]

    def move(k, lu, kind, sem, owner_r, to_s):
        ref = unit(k, kind)
        return remote(ref, ref, send_sem.at[lu, sem], recv_sem.at[lu, owner_r], to_s, t)

    def spread(k, lu, up, down, act):
        def for_kind(kind):
            if up is not None:
                @pl.when(up)
                def _():
                    act(move(k, lu, kind, 0, r, s + rn))
            if down is not None:
                @pl.when(down)
                def _():
                    act(move(k, lu, kind, 1, r, s - rn))
            for d in range(1, rn):
                act(move(k, lu, kind, 1 + d, r, z * rn + lax.rem(r + d, rn)))

        by_kind(plan, k, for_kind)

    start = lambda copy: copy.start()
    finish = lambda copy: copy.wait_send()

    for i in range(3):
        k = 3 * s + i
        base = i * plan.flat_rows

        def fill(kind):
            if kind == "q":
                rows, ref, at, cols = plan.uq, wq, k * plan.uq, QKV // LANES
            else:
                rows, ref, at, cols = plan.ub, wb, (k - plan.nq) * plan.ub, D // LANES
            at = pl.multiple_of(at, rows)
            for j in range(cols):
                ref[pl.ds(at, rows), j * LANES : (j + 1) * LANES] = master[
                    pl.ds(base + j, rows, stride=cols), :
                ].astype(BF16)

        by_kind(plan, k, fill)
        spread(k, 3 * z + i, z < ZN - 1, z > 0, start)

    macc[...] = jnp.zeros_like(macc)
    for i in range(3):
        k = 3 * s + i
        base = i * plan.flat_rows

        @pl.when(k >= plan.nb)
        def _():
            for j in range(MCOLS):
                tile[:, j * LANES : (j + 1) * LANES] = master[
                    pl.ds(base + j, plan.um, stride=MCOLS), :
                ].astype(BF16)
            macc[...] += mm(cond[k - plan.nb], tile[...])

    fm = plan.first_mod

    @pl.when(s >= fm)
    def _():
        for f in range(plan.frames):
            for j in range(MCOLS):
                mpart[f // F_DEV, pl.ds((f % F_DEV) * MCOLS + j, 1), :] = macc[
                    pl.ds(f, 1), j * LANES : (j + 1) * LANES
                ]
        mrecv[s - fm] = mpart[s]
        for d in range(1, n):
            to = lax.rem(s + d, n)
            remote(mpart.at[to], mrecv.at[s - fm], msend.at[d - 1], mrecv_sem.at[s - fm], to, t).start()

    for src in range(fm, n):
        @pl.when(s != src)
        def _():
            remote(
                mpart.at[0], mrecv.at[src - fm], msend.at[0], mrecv_sem.at[src - fm], s, t
            ).wait_recv()

    total = mrecv[0]
    for src in range(1, n - fm):
        total = total + mrecv[src]
    mod[t] = total
    for d in range(1, TP):
        remote(mod.at[t], mod.at[t], tsend.at[d - 1], trecv.at[t], s, lax.rem(t + d, TP)).start()

    for d in range(1, ZN):
        for i in range(3):
            for side in (0, 1):
                zs = z - d if side == 0 else z + d
                k = 3 * (zs * rn + r) + i
                lu = 3 * zs + i

                @pl.when((zs >= 0) & (zs < ZN))
                def _():
                    by_kind(plan, k, lambda kind: move(k, lu, kind, 0, r, s).wait_recv())
                    if side == 0:
                        spread(k, lu, z < ZN - 1, None, start)
                    else:
                        spread(k, lu, None, z > 0, start)

    for d in range(1, rn):
        other = lax.rem(r + d, rn)
        for zs in range(ZN):
            for i in range(3):
                k = 3 * (zs * rn + other) + i
                by_kind(plan, k, lambda kind: move(k, 3 * zs + i, kind, 0, other, s).wait_recv())

    wo[t] = wb[:HD]
    for d in range(1, TP):
        remote(wo.at[t], wo.at[t], osend.at[d - 1], orecv.at[t], s, lax.rem(t + d, TP)).start()
    for d in range(1, TP):
        other = lax.rem(t + d, TP)
        remote(wo.at[t], wo.at[other], osend.at[0], orecv.at[other], s, t).wait_recv()
        remote(wo.at[t], wo.at[t], osend.at[d - 1], orecv.at[t], s, other).wait_send()
        remote(mod.at[t], mod.at[other], tsend.at[0], trecv.at[other], s, t).wait_recv()
        remote(mod.at[t], mod.at[t], tsend.at[d - 1], trecv.at[t], s, other).wait_send()

    @pl.when(s >= fm)
    def _():
        for d in range(1, n):
            to = lax.rem(s + d, n)
            remote(mpart.at[to], mrecv.at[s - fm], msend.at[d - 1], mrecv_sem.at[s - fm], to, t).wait_send()

    for i in range(3):
        spread(3 * s + i, 3 * z + i, z < ZN - 1, z > 0, finish)
    for d in range(1, ZN):
        for i in range(3):
            for side in (0, 1):
                zs = z - d if side == 0 else z + d
                k = 3 * (zs * rn + r) + i
                lu = 3 * zs + i

                @pl.when((zs >= 0) & (zs < ZN))
                def _():
                    if side == 0:
                        spread(k, lu, z < ZN - 1, None, finish)
                    else:
                        spread(k, lu, None, z > 0, finish)


def gather_weights(plan, master, cond_units, cid):
    n = plan.n
    mrows = F_DEV * MCOLS
    return call(
        functools.partial(gather_kernel, plan),
        (
            jax.ShapeDtypeStruct((D, QKV), BF16),
            jax.ShapeDtypeStruct((BROWS, D), BF16),
            jax.ShapeDtypeStruct((TP, mrows, LANES), F32),
            jax.ShapeDtypeStruct((TP, HD, D), BF16),
        ),
        [
            pltpu.VMEM((plan.um, MT), BF16),
            pltpu.VMEM((plan.frames, MT), F32),
            pltpu.VMEM((n, mrows, LANES), F32),
            pltpu.VMEM((n - plan.first_mod, mrows, LANES), F32),
            DMA((3 * ZN, plan.r + 1)),
            DMA((3 * ZN, plan.r)),
            DMA((n - 1,)),
            DMA((n - plan.first_mod,)),
            DMA((TP - 1,)),
            DMA((TP,)),
            DMA((TP - 1,)),
            DMA((TP,)),
        ],
        [VM, VM],
        cid,
        name="gather_weights",
    )(master, cond_units)


def qkv_kernel(plan, q, kv, q_out, kv_out, qs, ks, rs, qr, kr, rr):
    s, t, z, r = place(plan)
    rn = plan.r
    greet(
        [(lax.rem(z + d, ZN) * rn + r, t) for d in range(1, ZN)]
        + [(z * rn + lax.rem(r + d, rn), t) for d in range(1, rn)]
    )

    def kv_copy(d):
        h = lax.rem(z + d, ZN)
        return remote(kv.at[h], kv_out.at[s], ks.at[d - 1], kr.at[z], h * rn + r, t)

    def q_copy(d):
        h = lax.rem(z + d, ZN)
        return remote(q.at[h], q_out.at[z], qs.at[d - 1], qr.at[z], h * rn + r, t)

    def side_copy(zs, e):
        at = zs * rn + r
        src = kv_out.at[at]
        return remote(src, src, rs.at[zs, e - 1], rr.at[at], z * rn + lax.rem(r + e, rn), t)

    for d in range(1, ZN):
        kv_copy(d).start()
    for d in range(1, ZN):
        q_copy(d).start()
    kv_out[s] = kv[z]
    q_out[z] = q[z]
    for e in range(1, rn):
        side_copy(z, e).start()
    for d in range(1, ZN):
        zs = lax.rem(z + d, ZN)
        remote(kv.at[0], kv_out.at[zs * rn + r], ks.at[0], kr.at[zs], s, t).wait_recv()
        for e in range(1, rn):
            side_copy(zs, e).start()
    for d in range(1, ZN):
        zs = lax.rem(z + d, ZN)
        remote(q.at[0], q_out.at[zs], qs.at[0], qr.at[zs], s, t).wait_recv()
    for e in range(1, rn):
        for zs in range(ZN):
            at = zs * rn + lax.rem(r + e, rn)
            remote(kv_out.at[at], kv_out.at[at], rs.at[0, 0], rr.at[at], s, t).wait_recv()
    for d in range(1, ZN):
        kv_copy(d).wait_send()
        q_copy(d).wait_send()
    for zs in range(ZN):
        for e in range(1, rn):
            side_copy(zs, e).wait_send()


def exchange_qkv(plan, q, kv, cid):
    rn = plan.r
    return call(
        functools.partial(qkv_kernel, plan),
        (
            jax.ShapeDtypeStruct((ZN, TOK_FRAME, LANES), BF16),
            jax.ShapeDtypeStruct((plan.n, F_DEV * TOK_FRAME, LANES), BF16),
        ),
        [DMA((ZN - 1,)), DMA((ZN - 1,)), DMA((ZN, rn - 1)), DMA((ZN,)), DMA((ZN,)), DMA((plan.n,))],
        [VM, VM],
        cid,
        name="exchange_qkv",
    )(q, kv)


def dkv_kernel(plan, dq, dkv, q_out, kv_out, stage, side, qs, ks, rs, qr, kr, rr):
    s, t, z, r = place(plan)
    rn = plan.r
    greet(
        [(lax.rem(z + d, ZN) * rn + r, t) for d in range(1, ZN)]
        + [(z * rn + lax.rem(r + d, rn), t) for d in range(1, rn)]
    )

    def side_copy(d, e):
        zs = lax.rem(z + d, ZN)
        other = lax.rem(r + e, rn)
        return remote(
            dkv.at[zs * rn + other], side.at[e - 1, d], rs.at[d, e - 1], rr.at[d, e - 1],
            z * rn + other, t,
        )

    def q_copy(d):
        to = lax.rem(z + d, ZN)
        return remote(dq.at[to], q_out.at[z], qs.at[d - 1], qr.at[z], to * rn + r, t)

    def kv_copy(d):
        to = lax.rem(z + d, ZN)
        return remote(stage.at[d], kv_out.at[z], ks.at[d - 1], kr.at[z], to * rn + r, t)

    order = list(range(1, ZN)) + [0]
    for d in order:
        for e in range(1, rn):
            side_copy(d, e).start()
    for d in range(1, ZN):
        q_copy(d).start()
    q_out[z] = dq[z]
    for d in order:
        zs = lax.rem(z + d, ZN)
        total = dkv[zs * rn + r].astype(F32)
        for e in range(1, rn):
            side_copy(d, e).wait_recv()
            total = total + side[e - 1, d].astype(F32)
        if d == 0:
            kv_out[z] = total.astype(BF16)
        else:
            stage[d] = total.astype(BF16)
            kv_copy(d).start()
    for d in range(1, ZN):
        zs = lax.rem(z + d, ZN)
        remote(dq.at[0], q_out.at[zs], qs.at[0], qr.at[zs], s, t).wait_recv()
        remote(stage.at[d], kv_out.at[zs], ks.at[0], kr.at[zs], s, t).wait_recv()
    for d in range(1, ZN):
        q_copy(d).wait_send()
        kv_copy(d).wait_send()
    for d in order:
        for e in range(1, rn):
            side_copy(d, e).wait_send()


def exchange_dkv(plan, dq, dkv, cid):
    rn = plan.r
    rows = F_DEV * TOK_FRAME
    return call(
        functools.partial(dkv_kernel, plan),
        (
            jax.ShapeDtypeStruct((ZN, TOK_FRAME, LANES), BF16),
            jax.ShapeDtypeStruct((ZN, rows, LANES), BF16),
        ),
        [
            pltpu.VMEM((ZN, rows, LANES), BF16),
            pltpu.VMEM((rn - 1, ZN, rows, LANES), BF16),
            DMA((ZN - 1,)), DMA((ZN - 1,)), DMA((ZN, rn - 1)),
            DMA((ZN,)), DMA((ZN,)), DMA((ZN, rn - 1)),
        ],
        [VM, VM],
        cid,
        name="exchange_dkv",
    )(dq, dkv)


def padded(rows, low):
    zero = jnp.zeros_like(rows)
    return jnp.concatenate([rows, zero] if low else [zero, rows], axis=1)


def attend_kernel(plan, meta, q, kv, o, ot, lse, m_ref, l_ref, acc):
    r = meta[plan.frames]
    scale = HEAD ** (-0.5)

    def group(zq, carry):
        for f in range(F_DEV):
            frame = (zq * plan.r + r) * F_DEV + f
            clip = meta[frame]
            pack = q[zq]
            qz = padded(pack[:, f * HEAD : (f + 1) * HEAD], True) * jnp.asarray(scale, BF16)
            m_ref[...] = jnp.full_like(m_ref, -1e30)
            l_ref[...] = jnp.zeros_like(l_ref)
            acc[...] = jnp.zeros_like(acc)

            def block(j, inner):
                @pl.when(meta[j] == clip)
                def _():
                    rows = pl.multiple_of(lax.rem(j, F_DEV) * TOK_FRAME, TOK_FRAME)
                    keys = kv[lax.div(j, F_DEV), pl.ds(rows, TOK_FRAME), :]
                    st = mm_nt(keys, qz)
                    m_old = m_ref[...]
                    m_new = jnp.maximum(m_old, jnp.max(st, axis=0, keepdims=True))
                    p = jnp.exp(st - m_new)
                    alpha = jnp.exp(m_old - m_new)
                    m_ref[...] = m_new
                    l_ref[...] = l_ref[...] * alpha + jnp.sum(p, axis=0, keepdims=True)
                    acc[...] = acc[...] * alpha + mm_tn(keys, p.astype(BF16))

                return inner

            lax.fori_loop(0, frame + 1, block, 0)
            total = l_ref[...]
            out = acc[HEAD:, :] / total
            ot[zq * F_DEV + f] = out
            lse[zq * F_DEV + f] = m_ref[...] + jnp.log(total)
            rows = out.T
            o[zq, f] = jnp.concatenate([rows[:PACK], rows[PACK:]], axis=1).astype(BF16)
        return carry

    lax.fori_loop(0, ZN, group, 0)


def attend(plan, meta, q, kv):
    frames = ZN * F_DEV
    return call(
        functools.partial(attend_kernel, plan),
        (
            jax.ShapeDtypeStruct((ZN, F_DEV, PACK, LANES), BF16),
            jax.ShapeDtypeStruct((frames, HEAD, TOK_FRAME), F32),
            jax.ShapeDtypeStruct((frames, 1, TOK_FRAME), F32),
        ),
        [
            pltpu.VMEM((1, TOK_FRAME), F32),
            pltpu.VMEM((1, TOK_FRAME), F32),
            pltpu.VMEM((LANES, TOK_FRAME), F32),
        ],
        [SM, VM, VM],
        name="attend",
    )(meta, q, kv)


def attend_back_kernel(plan, meta, q, kv, do, ot, lse, dq, dkv, dkv_acc, dq_acc):
    r = meta[plan.frames]
    scale = HEAD ** (-0.5)
    dkv_acc[...] = jnp.zeros_like(dkv_acc)

    def group(zq, carry):
        parts = []
        for f in range(F_DEV):
            frame = (zq * plan.r + r) * F_DEV + f
            clip = meta[frame]
            columns = slice(f * HEAD, (f + 1) * HEAD)
            qz = padded(q[zq][:, columns], True) * jnp.asarray(scale, BF16)
            grads = jnp.concatenate([do[zq, f][:, :HEAD], do[zq, f][:, HEAD:]], axis=0)
            doz = padded(grads, False)
            delta = jnp.sum(grads.astype(F32).T * ot[zq * F_DEV + f], axis=0, keepdims=True)
            logs = lse[zq * F_DEV + f]
            dq_acc[...] = jnp.zeros_like(dq_acc)

            def block(j, inner):
                @pl.when(meta[j] == clip)
                def _():
                    g = lax.div(j, F_DEV)
                    rows = pl.multiple_of(lax.rem(j, F_DEV) * TOK_FRAME, TOK_FRAME)
                    keys = kv[g, pl.ds(rows, TOK_FRAME), :]
                    pt = jnp.exp(mm_nt(keys, qz) - logs)
                    dst = (pt * (mm_nt(keys, doz) - delta)).astype(BF16)
                    dkv_acc[g, pl.ds(rows, TOK_FRAME), :] += mm(dst, qz) + mm(pt.astype(BF16), doz)
                    dq_acc[...] += mm_tn(keys, dst)

                return inner

            lax.fori_loop(0, frame + 1, block, 0)
            parts.append((dq_acc[:HEAD, :] * scale).T)
        dq[zq] = jnp.concatenate(parts, axis=1).astype(BF16)
        return carry

    lax.fori_loop(0, ZN, group, 0)
    dkv[...] = dkv_acc[...].astype(BF16)


def attend_back(plan, meta, q, kv, do, ot, lse):
    return call(
        functools.partial(attend_back_kernel, plan),
        (
            jax.ShapeDtypeStruct((ZN, TOK_FRAME, LANES), BF16),
            jax.ShapeDtypeStruct((plan.n, F_DEV * TOK_FRAME, LANES), BF16),
        ),
        [
            pltpu.VMEM((plan.n, F_DEV * TOK_FRAME, LANES), F32),
            pltpu.VMEM((LANES, TOK_FRAME), F32),
        ],
        [SM, VM, VM, VM, VM, VM],
        name="attend_back",
    )(meta, q, kv, do, ot, lse)


def total_kernel(chunks, part, out, sbuf, cbuf, ybuf, yrecv, ss, cs, ys, yr, osem, orsem):
    s = lax.axis_index("seq")
    t = lax.axis_index("tp")
    core = lax.rem(t, 2)
    sibling = t + 1 - 2 * core
    across = lax.rem(t + 2, TP)
    greet([(s, sibling), (s, across)])
    half = TOK_FRAME
    rows = half // chunks
    mine = core * half
    theirs = half - mine

    def c_copy(ch):
        return remote(sbuf.at[ch], cbuf.at[ch], ss.at[ch], cs.at[ch], s, sibling)

    def y_copy(ch):
        return remote(ybuf.at[ch], yrecv.at[ch], ys.at[ch], yr.at[ch], s, across)

    def o_copy(ch, base):
        ref = out.at[pl.ds(pl.multiple_of(base + ch * rows, rows), rows)]
        return remote(ref, ref, osem.at[ch], orsem.at[ch], s, sibling)

    for ch in range(chunks):
        sbuf[ch] = part[pl.ds(pl.multiple_of(theirs + ch * rows, rows), rows), :].astype(BF16)
        c_copy(ch).start()
    for ch in range(chunks):
        c_copy(ch).wait_recv()
        ybuf[ch] = (
            part[pl.ds(pl.multiple_of(mine + ch * rows, rows), rows), :] + cbuf[ch].astype(F32)
        ).astype(BF16)
        y_copy(ch).start()
    for ch in range(chunks):
        y_copy(ch).wait_recv()
        out[pl.ds(pl.multiple_of(mine + ch * rows, rows), rows), :] = ybuf[ch].astype(F32) + yrecv[
            ch
        ].astype(F32)
        o_copy(ch, mine).start()
    for ch in range(chunks):
        o_copy(ch, theirs).wait_recv()
    for ch in range(chunks):
        c_copy(ch).wait_send()
        y_copy(ch).wait_send()
        o_copy(ch, mine).wait_send()


def total_tp(part, cid, name):
    chunks = 4
    rows = TOK_FRAME // chunks
    buf = pltpu.VMEM((chunks, rows, D), BF16)
    return call(
        functools.partial(total_kernel, chunks),
        jax.ShapeDtypeStruct(part.shape, F32),
        [buf] * 4 + [DMA((chunks,))] * 6,
        [VM],
        cid,
        name=name,
    )(part)


def loop(count, step, body):
    def turn(i, carry):
        body(pl.multiple_of(i * step, step))
        return carry

    lax.fori_loop(0, count // step, turn, 0)


def add_to(ref, row, values):
    ref[pl.ds(row, 1), :] += jnp.sum(values, axis=0, keepdims=True)


def middle_kernel(
    plan, o_mine, wo, wb, tokens, grad_out, mod,
    result, gb, do_out, dmid, dmod,
    oall, attended, attn, mid, norm, inv, sin, hidden, dmlp, dhid, dup,
    own, csend, crecv, ysend, yrecv, dattn, dsend, dwo, wsend, wrecv,
    o_s, o_r, f_s, f_r, n_s, n_r, c_s, c_r, y_s, y_r, d_s, d_r, w_s, w_r, e_s, e_r,
):
    s, t, z, r = place(plan)
    rn = plan.r
    y = lax.div(t, 2)
    c = lax.rem(t, 2)
    sib = 2 * y + 1 - c
    across = lax.rem(t + 2, TP)
    mine = pl.multiple_of(c * TOK_FRAME, TOK_FRAME)
    theirs = pl.multiple_of((1 - c) * TOK_FRAME, TOK_FRAME)
    pairs = [(d, e) for d in range(ZN) for e in range(2)][1:]

    def partner(d, e):
        return lax.rem(z + d, ZN), (c if e == 0 else 1 - c)

    greet(
        [(partner(d, e)[0] * rn + r, 2 * y + partner(d, e)[1]) for d, e in pairs]
        + [(s, across)]
    )

    def o_copy(d, e):
        zd, cd = partner(d, e)
        return remote(
            o_mine.at[zd, cd], oall.at[y * 8 + c * ZN + z], o_s.at[2 * d + e],
            o_r.at[c * ZN + z], zd * rn + r, 2 * y + cd,
        )

    def f_copy(slot):
        ref = oall.at[y * 8 + slot]
        return remote(ref, ref, f_s.at[slot], f_r.at[slot], s, across)

    for d, e in pairs:
        o_copy(d, e).start()
    oall[y * 8 + c * ZN + z] = o_mine[z, c]
    f_copy(c * ZN + z).start()

    def d_mlp(f):
        def body(at):
            rows = pl.ds(f * TOK_FRAME + at, 64)
            dmlp[rows, :] = (grad_out[rows, :].astype(F32) * mod[f * 6 + 5 : f * 6 + 6, :]).astype(
                BF16
            )

        loop(TOK_FRAME, 64, body)

    for f in range(F_DEV):
        d_mlp(f)

    def d_hidden(at):
        dhid[:, pl.ds(at, TILE)] = mm_nt(dmlp[...], wb[pl.ds(HD + FT + at, TILE), :])

    loop(FT, TILE, d_hidden)

    for d, e in pairs:
        zd, cd = partner(d, e)
        slot = cd * ZN + zd
        remote(o_mine.at[0, 0], oall.at[y * 8 + slot], o_s.at[0], o_r.at[slot], s, t).wait_recv()
        f_copy(slot).start()
    for slot in range(8):
        remote(
            oall.at[0], oall.at[(1 - y) * 8 + slot], f_s.at[slot], f_r.at[slot], s, t
        ).wait_recv()
    for m in range(HEADS // 2):
        a, b = oall[2 * m], oall[2 * m + 1]
        cols = slice(m * LANES, (m + 1) * LANES)
        attended[:PACK, cols] = jnp.concatenate([a[:, :HEAD], b[:, :HEAD]], axis=1)
        attended[PACK:, cols] = jnp.concatenate([a[:, HEAD:], b[:, HEAD:]], axis=1)

    def attn_tile(at):
        attn[:, pl.ds(at, TILE)] = mm(attended[...], wo[:, pl.ds(at, TILE)])

    loop(D, TILE, attn_tile)

    row = lambda part: mod[pl.ds(c * 6 + part, 1), :]

    def norm_rows(at):
        rows = pl.ds(at, 64)
        values = tokens[pl.ds(mine + at, 64), :].astype(F32) + row(2) * attn[rows, :]
        mid[rows, :] = values
        normed, inverse = normalize(values)
        norm[rows, :] = normed
        inv[rows, :] = inverse
        sin[pl.ds(mine + at, 64), :] = (normed * (1.0 + row(4)) + row(3)).astype(BF16)

    loop(TOK_FRAME, 64, norm_rows)

    def n_copy(base):
        ref = sin.at[pl.ds(base, TOK_FRAME)]
        return remote(ref, ref, n_s.at[0], n_r.at[0], s, sib)

    n_copy(mine).start()

    def feed(base):
        rows = pl.ds(base, TOK_FRAME)

        def tile(at):
            cols = pl.ds(at, TILE)
            u = mm(sin[rows, :], wb[HD : HD + FT, cols])
            square = u * u
            inner = GELU_A * u * (1.0 + GELU_B * square)
            th = jnp.tanh(inner)
            half = 0.5 * (1.0 + th)
            hidden[rows, cols] = (u * half).astype(BF16)
            slope = half + 0.5 * u * (1.0 - th * th) * (GELU_A * (1.0 + 3.0 * GELU_B * square))
            dup[rows, cols] = (dhid[rows, cols] * slope).astype(BF16)

        loop(FT, TILE, tile)

    feed(mine)
    n_copy(theirs).wait_recv()
    feed(theirs)

    def c_copy(w, n):
        return remote(csend.at[w, n], crecv.at[w, n], c_s.at[w, n], c_r.at[w, n], s, sib)

    def y_copy(w, n):
        return remote(ysend.at[w, n], yrecv.at[w, n], y_s.at[w, n], y_r.at[w, n], s, across)

    def pass_on(w, n):
        c_copy(w, n).wait_recv()
        ysend[w, n] = (own[n] + crecv[w, n].astype(F32)).astype(BF16)
        y_copy(w, n).start()

    def product(w, base, n):
        rows = pl.ds(base, TOK_FRAME)
        if w == 0:
            return mm_nt(dup[rows, :], wb[HD + n * TILE : HD + (n + 1) * TILE, :])
        return mm(hidden[rows, :], wb[HD + FT :, n * TILE : (n + 1) * TILE])

    for w in range(2):
        for n in range(TILES):
            csend[w, n] = product(w, theirs, n).astype(BF16)
            c_copy(w, n).start()
            own[n] = product(w, mine, n)
            if n:
                pass_on(w, n - 1)
        pass_on(w, TILES - 1)

    def down_grad(at):
        gb[pl.ds(HD + FT + at, TILE), :] = mm_tn(hidden[:, pl.ds(at, TILE)], dmlp[...]).astype(BF16)

    def up_grad(at):
        gb[pl.ds(HD + at, TILE), :] = mm_tn(sin[:, pl.ds(at, TILE)], dup[...]).astype(BF16)

    loop(FT, TILE, down_grad)
    loop(D, TILE, up_grad)

    dm = dmod.at[c]
    dm[...] = jnp.zeros_like(dm)
    for n in range(TILES):
        y_copy(0, n).wait_recv()

    def total(w, rows):
        return jnp.concatenate(
            [ysend[w, n, rows].astype(F32) + yrecv[w, n, rows].astype(F32) for n in range(TILES)],
            axis=1,
        )

    def back_rows(at):
        rows = pl.ds(at, 64)
        tok_rows = pl.ds(mine + at, 64)
        grads = total(0, rows)
        normed = norm[rows, :]
        add_to(dm, 1, grads)
        add_to(dm, 2, grads * normed)
        values = grad_out[tok_rows, :].astype(F32) + norm_back(
            grads * (1.0 + row(4)), normed, inv[rows, :]
        )
        dmid[tok_rows, :] = values
        add_to(dm, 0, attn[rows, :] * values)
        dattn[rows, :] = (row(2) * values).astype(BF16)

    loop(TOK_FRAME, 64, back_rows)
    for ch in range(2):
        part = mm_nt(dattn[...], wo[pl.ds(pl.multiple_of((2 * y + ch) * HD, HD), HD), :]).astype(BF16)
        for zh in range(ZN):
            cols = slice(zh * HEAD, (zh + 1) * HEAD)
            dsend[ch * ZN + zh] = jnp.concatenate([part[:PACK, cols], part[PACK:, cols]], axis=1)

    def d_copy(d, e):
        zd, cd = partner(d, e)
        return remote(
            dsend.at[cd * ZN + zd], do_out.at[z, c], d_s.at[2 * d + e], d_r.at[2 * z + c],
            zd * rn + r, 2 * y + cd,
        )

    for d, e in pairs:
        d_copy(d, e).start()
    do_out[z, c] = dsend[c * ZN + z]

    def o_grad(head_core):
        cols = pl.ds(pl.multiple_of((2 * y + head_core) * HD, HD), HD)
        return mm_tn(attended[:, cols], dattn[...])

    w_copy = remote(wsend, wrecv, w_s, w_r, s, sib)
    wsend[...] = o_grad(1 - c).astype(BF16)
    w_copy.start()
    dwo[...] = o_grad(c)

    for n in range(TILES):
        y_copy(1, n).wait_recv()

    def result_rows(at):
        rows = pl.ds(at, 64)
        tok_rows = pl.ds(mine + at, 64)
        mlp = total(1, rows)
        add_to(dm, 3, mlp * grad_out[tok_rows, :].astype(F32))
        result[tok_rows, :] = (mid[rows, :] + row(5) * mlp).astype(BF16)

    loop(TOK_FRAME, 64, result_rows)

    def e_copies(core, base):
        rows = pl.ds(base, TOK_FRAME)
        return [
            remote(ref, ref, e_s.at[i], e_r.at[i], s, sib)
            for i, ref in enumerate((result.at[rows], dmid.at[rows], dmod.at[core]))
        ]

    for copy in e_copies(c, mine):
        copy.start()
    w_copy.wait_recv()
    gb[:HD, :] = (dwo[...] + wrecv[...].astype(F32)).astype(BF16)

    for d, e in pairs:
        zd, cd = partner(d, e)
        remote(
            dsend.at[0], do_out.at[zd, cd], d_s.at[0], d_r.at[2 * zd + cd], s, t
        ).wait_recv()
    for copy in e_copies(1 - c, theirs):
        copy.wait_recv()
    for d, e in pairs:
        o_copy(d, e).wait_send()
        d_copy(d, e).wait_send()
    for slot in range(8):
        f_copy(slot).wait_send()
    n_copy(mine).wait_send()
    for w in range(2):
        for n in range(TILES):
            c_copy(w, n).wait_send()
            y_copy(w, n).wait_send()
    w_copy.wait_send()
    for copy in e_copies(c, mine):
        copy.wait_send()


def middle_part(plan, o_mine, wo, wb, tokens, grad_out, mod_rows, cid):
    rows = F_DEV * TOK_FRAME
    half = lambda dtype: pltpu.VMEM((TOK_FRAME, D), dtype)
    full = lambda dtype: pltpu.VMEM((rows, D), dtype)
    tiles = pltpu.VMEM((2, TILES, TOK_FRAME, TILE), BF16)
    return call(
        functools.partial(middle_kernel, plan),
        (
            jax.ShapeDtypeStruct((rows, D), BF16),
            jax.ShapeDtypeStruct((BROWS, D), BF16),
            jax.ShapeDtypeStruct((ZN, F_DEV, PACK, LANES), BF16),
            jax.ShapeDtypeStruct((rows, D), F32),
            jax.ShapeDtypeStruct((F_DEV, 8, D), F32),
        ),
        [
            pltpu.VMEM((HEADS, PACK, LANES), BF16),
            half(BF16), half(F32), half(F32), half(F32), pltpu.VMEM((TOK_FRAME, 1), F32),
            full(BF16), full(BF16), full(BF16), full(F32), full(BF16),
            pltpu.VMEM((TILES, TOK_FRAME, TILE), F32), tiles, tiles, tiles, tiles,
            half(BF16), pltpu.VMEM((8, PACK, LANES), BF16),
            pltpu.VMEM((HD, D), F32), pltpu.VMEM((HD, D), BF16), pltpu.VMEM((HD, D), BF16),
            DMA((8,)), DMA((8,)), DMA((8,)), DMA((8,)), DMA((1,)), DMA((1,)),
            DMA((2, TILES)), DMA((2, TILES)), DMA((2, TILES)), DMA((2, TILES)),
            DMA((8,)), DMA((8,)), DMA, DMA, DMA((3,)), DMA((3,)),
        ],
        [VM] * 6,
        cid,
        name="middle_part",
    )(o_mine, wo, wb, tokens, grad_out, mod_rows)


def scatter_kernel(plan, gq, gb, oq, ob, rq, rb, cq, cb, rs, rr, cs, cr):
    s, t, z, r = place(plan)
    rn = plan.r
    greet(
        [(z * rn + lax.rem(r + d, rn), t) for d in range(1, rn)]
        + [(lax.rem(z + d, ZN) * rn + r, t) for d in (1, ZN - 1)]
    )

    def own(k, kind):
        if kind == "q":
            return gq.at[pl.ds(pl.multiple_of(k * plan.uq, plan.uq), plan.uq)]
        return gb.at[pl.ds(pl.multiple_of((k - plan.nq) * plan.ub, plan.ub), plan.ub)]

    a = 2 - lax.div(z, 2)
    b = 2 * lax.div(ZN - 1 - z, ZN - 1)

    def owner(j):
        return lax.rem(a * j + b, 3)

    def side_copy(zo, i, d, kind):
        other = lax.rem(r + d, rn)
        k = 3 * (zo * rn + other) + i
        lu = 3 * zo + i
        buf = rq if kind == "q" else rb
        return k, remote(
            own(k, kind), buf.at[d - 1, lu], rs.at[lu, d - 1], rr.at[lu, d - 1], z * rn + other, t
        )

    def chain_copy(lu, kind, side, to):
        src = (rq if kind == "q" else rb).at[0, lu]
        dst = (cq if kind == "q" else cb).at[side, lu]
        return remote(src, dst, cs.at[lu], cr.at[lu, side], to, t)

    for j in range(3):
        for i in range(3):
            for d in range(1, rn):
                k = 3 * (owner(j) * rn + lax.rem(r + d, rn)) + i
                by_kind(plan, k, lambda kind: side_copy(owner(j), i, d, kind)[1].start())

    for j in range(3):
        zo = owner(j)
        for i in range(3):
            k = 3 * (zo * rn + r) + i
            lu = 3 * zo + i

            def step(kind):
                side = rq if kind == "q" else rb
                chain = cq if kind == "q" else cb
                out = oq if kind == "q" else ob
                for d in range(1, rn):
                    remote(
                        own(k, kind), side.at[d - 1, lu], rs.at[lu, d - 1], rr.at[lu, d - 1], s, t
                    ).wait_recv()
                total = own(k, kind)[...].astype(F32)
                for d in range(1, rn):
                    total = total + side[d - 1, lu].astype(F32)
                out[i] = total

                @pl.when((zo <= z) & (z < ZN - 1))
                def _():
                    chain_copy(lu, kind, 0, s).wait_recv()
                    out[i] += chain[0, lu].astype(F32)

                @pl.when((zo >= z) & (z > 0))
                def _():
                    chain_copy(lu, kind, 1, s).wait_recv()
                    out[i] += chain[1, lu].astype(F32)

                @pl.when(zo != z)
                def _():
                    side[0, lu] = out[i].astype(BF16)

                @pl.when(zo < z)
                def _():
                    chain_copy(lu, kind, 0, s - rn).start()

                @pl.when(zo > z)
                def _():
                    chain_copy(lu, kind, 1, s + rn).start()

            by_kind(plan, k, step)

    for j in range(3):
        zo = owner(j)
        for i in range(3):
            for d in range(1, rn):
                k = 3 * (zo * rn + lax.rem(r + d, rn)) + i
                by_kind(plan, k, lambda kind: side_copy(zo, i, d, kind)[1].wait_send())
            k = 3 * (zo * rn + r) + i

            def close(kind):
                @pl.when(zo != z)
                def _():
                    chain_copy(3 * zo + i, kind, 0, s).wait_send()

            by_kind(plan, k, close)


def scatter_grads(plan, gq, gb, cid):
    rn = plan.r
    return call(
        functools.partial(scatter_kernel, plan),
        (
            jax.ShapeDtypeStruct((3, plan.uq, QKV), F32),
            jax.ShapeDtypeStruct((3, plan.ub, D), F32),
        ),
        [
            pltpu.VMEM((rn - 1, 9, plan.uq, QKV), BF16),
            pltpu.VMEM((rn - 1, 9, plan.ub, D), BF16),
            pltpu.VMEM((2, 9, plan.uq, QKV), BF16),
            pltpu.VMEM((2, 9, plan.ub, D), BF16),
            DMA((9, rn - 1)), DMA((9, rn - 1)), DMA((9,)), DMA((9, 2)),
        ],
        [VM, VM],
        cid,
        name="scatter_grads",
    )(gq, gb)


def adam_kernel(plan, meta, oq, ob, cond, dmod, master, one, two, average, n_master, n_one, n_two, n_average):
    s = meta[0]
    rate = RATE_FACTOR * D ** (-0.5)
    scale_one = 1.0 / (1.0 - BETA_FIRST**STEP)
    scale_two = 1.0 / (1.0 - BETA_SECOND**STEP)

    def update(rows, grad):
        first = BETA_FIRST * one[rows, :] + (1.0 - BETA_FIRST) * grad
        second = BETA_SECOND * two[rows, :] + (1.0 - BETA_SECOND) * grad * grad
        weight = master[rows, :]
        weight = weight - rate * (
            (first * scale_one) / (jnp.sqrt(second * scale_two) + ADAM_EPSILON)
            + WEIGHT_DECAY * weight
        )
        n_one[rows, :] = first
        n_two[rows, :] = second
        n_master[rows, :] = weight
        n_average[rows, :] = AVERAGE_RATE * average[rows, :] + (1.0 - AVERAGE_RATE) * weight

    for i in range(3):
        k = 3 * s + i
        base = i * plan.flat_rows

        def from_matrix(kind):
            src = oq if kind == "q" else ob
            rows = plan.uq if kind == "q" else plan.ub
            cols = (QKV if kind == "q" else D) // LANES
            for j in range(cols):
                update(
                    pl.ds(base + j, rows, stride=cols), src[i, :, j * LANES : (j + 1) * LANES]
                )

        by_kind(plan, k, from_matrix)

        @pl.when(k >= plan.nb)
        def _():
            at = cond[k - plan.nb]
            for j in range(MCOLS):
                update(
                    pl.ds(base + j, plan.um, stride=MCOLS),
                    mm(at, dmod[:, j * LANES : (j + 1) * LANES]),
                )


def adam(plan, meta, oq, ob, cond_rows, dmod, master, one, two, average):
    shape = jax.ShapeDtypeStruct(master.shape, F32)
    return call(
        functools.partial(adam_kernel, plan),
        (shape,) * 4,
        [],
        [SM] + [VM] * 8,
        name="adam",
    )(meta, oq, ob, cond_rows, dmod, master, one, two, average)


def by_frame(rows):
    return rows.reshape(F_DEV, TOK_FRAME, rows.shape[1])


def frame_scale(rows, factor):
    return (by_frame(rows) * factor[:, None, :]).reshape(rows.shape)


def frame_affine(rows, factor, offset_rows):
    return (by_frame(rows) * (1.0 + factor)[:, None, :] + offset_rows[:, None, :]).reshape(
        rows.shape
    )


def frame_total(rows):
    return jnp.sum(by_frame(rows), axis=1)


def pack_heads(rows):
    return rows.reshape(F_DEV, TOK_FRAME, ZN, HEAD).transpose(2, 1, 0, 3).reshape(
        ZN, TOK_FRAME, F_DEV * HEAD
    )


def unpack_heads(packs):
    return packs.reshape(ZN, TOK_FRAME, F_DEV, HEAD).transpose(2, 1, 0, 3).reshape(
        F_DEV * TOK_FRAME, ZN * HEAD
    )


def local(
    tokens,
    grad_out,
    noise_level,
    context_mask,
    frame_clip,
    level_table,
    master,
    moment_one,
    moment_two,
    average,
):
    plan = Plan(lax.axis_size("seq"))
    s = lax.axis_index("seq")
    t = lax.axis_index("tp")
    rows = F_DEV * TOK_FRAME
    flat = lambda x: x.reshape(-1, LANES)

    effective = noise_level * (1 - context_mask)
    one_hot = (
        effective[:, None] == jnp.arange(level_table.shape[0], dtype=jnp.int32)[None, :]
    ).astype(BF16)
    condition = jax.nn.silu(mm(one_hot, level_table)).astype(BF16)
    cond_units = condition.reshape(plan.frames, plan.nm, plan.um).transpose(1, 0, 2)

    wq, wb, mod_blocks, wo = gather_weights(plan, flat(master), cond_units, 0)
    modulation = (
        mod_blocks.reshape(TP, F_DEV, MT).transpose(1, 0, 2).reshape(F_DEV, TP * MT)
    )
    mod_rows = modulation.reshape(F_DEV * 6, D)
    shift_one, scale_one = modulation[:, :D], modulation[:, D : 2 * D]

    inputs = tokens.astype(F32)
    normed_one, inverse_one = normalize(inputs)
    first_in = frame_affine(normed_one, scale_one, shift_one).astype(BF16)
    projected = mm(first_in, wq).astype(BF16)
    kv = jnp.stack(
        [
            jnp.concatenate(
                [
                    projected[:, HD + h * HEAD : HD + (h + 1) * HEAD],
                    projected[:, 2 * HD + h * HEAD : 2 * HD + (h + 1) * HEAD],
                ],
                axis=1,
            )
            for h in range(ZN)
        ]
    )
    q_mine, kv_all = exchange_qkv(plan, pack_heads(projected[:, :HD]), kv, 1)
    meta = jnp.concatenate([frame_clip, lax.rem(s, plan.r)[None]]).astype(jnp.int32)
    o_mine, o_rows, lse = attend(plan, meta, q_mine, kv_all)
    result, grads_b, do_mine, middle_grad, mod_four = middle_part(
        plan, o_mine, wo.reshape(HEADS * HEAD, D), wb, tokens, grad_out, mod_rows, 2
    )
    dq_mine, dkv_all = attend_back(plan, meta, q_mine, kv_all, do_mine, o_rows, lse)
    dq_heads, dkv_heads = exchange_dkv(plan, dq_mine, dkv_all, 7)
    qkv_grad = jnp.concatenate(
        [unpack_heads(dq_heads)]
        + [dkv_heads[h][:, :HEAD] for h in range(ZN)]
        + [dkv_heads[h][:, HEAD:] for h in range(ZN)],
        axis=1,
    )
    qkv_weight_grad = mm_tn(first_in, qkv_grad)
    first_grad = total_tp(mm_nt(qkv_grad, wq), 8, "total_first")
    scale_one_grad = frame_total(first_grad * normed_one)
    shift_one_grad = frame_total(first_grad)
    input_grad = middle_grad + norm_back(
        frame_scale(first_grad, 1.0 + scale_one), normed_one, inverse_one
    )
    mod_terms = jnp.concatenate(
        [
            shift_one_grad,
            scale_one_grad,
            mod_four[:, :4].reshape(F_DEV, 4 * D),
        ],
        axis=1,
    )
    mod_grad = lax.all_gather(
        lax.dynamic_slice_in_dim(mod_terms, t * MT, MT, axis=1), "seq", axis=0, tiled=True
    ).astype(BF16)
    own_q, own_b = scatter_grads(plan, qkv_weight_grad.astype(BF16), grads_b, 9)
    updated = adam(
        plan,
        s[None].astype(jnp.int32),
        own_q,
        own_b,
        cond_units.transpose(0, 2, 1),
        mod_grad,
        flat(master),
        flat(moment_one),
        flat(moment_two),
        flat(average),
    )
    new_master, new_one, new_two, new_average = [x.reshape(master.shape) for x in updated]
    return (result, input_grad, new_master, new_one, new_two, new_average)


def solution(mesh):
    token_spec = P("seq", None)
    weight_spec = P("tp", "seq")
    in_specs = (token_spec, token_spec, P(), P(), P(), P()) + (weight_spec,) * 4
    out_specs = (token_spec, token_spec) + (weight_spec,) * 4
    return jax.shard_map(local, mesh=mesh, in_specs=in_specs, out_specs=out_specs, check_vma=False)
```

```python
import functools

import jax
import jax.numpy as jnp
from jax import lax
from jax.experimental import pallas as pl
from jax.experimental.pallas import tpu as pltpu
from jax.sharding import PartitionSpec as P

D = 1024
HEADS = 16
HEAD = 64
FF = 4096
TOK_FRAME = 384
STEP = 7
TP = 4
ZN = 4
HD = HEADS * HEAD // TP
QKV = 3 * HD
FT = FF // TP
MT = 6 * D // TP
F_DEV = 2
BROWS = HD + 2 * FT
LANES = 128
MCOLS = MT // LANES
PACK = TOK_FRAME // 2
TILE = 256
TILES = D // TILE

NORM_EPSILON = 1e-06
RATE_FACTOR = 2.5
BETA_FIRST = 0.5
BETA_SECOND = 0.5
ADAM_EPSILON = 1e-08
WEIGHT_DECAY = 0.01
AVERAGE_RATE = 0.9
GELU_A = 0.7978845608028654
GELU_B = 0.044715
MESH = pl.DeviceIdType.MESH
VM = pl.BlockSpec(memory_space=pltpu.VMEM)
SM = pl.BlockSpec(memory_space=pltpu.SMEM)
DMA = pltpu.SemaphoreType.DMA
F32 = jnp.float32
BF16 = jnp.bfloat16
VMEM_LIMIT = 56 * 2**20


def mm(left, right):
    return jnp.dot(left, right, preferred_element_type=F32)


def mm_tn(left, right):
    return lax.dot_general(left, right, (((0,), (0,)), ((), ())), preferred_element_type=F32)


def mm_nt(left, right):
    return lax.dot_general(left, right, (((1,), (1,)), ((), ())), preferred_element_type=F32)


def normalize(rows):
    centred = rows - jnp.mean(rows, axis=1, keepdims=True)
    inverse = lax.rsqrt(jnp.mean(centred * centred, axis=1, keepdims=True) + NORM_EPSILON)
    return (centred * inverse, inverse)


def norm_back(grads, normed, inverse):
    return inverse * (
        grads
        - jnp.mean(grads, axis=1, keepdims=True)
        - normed * jnp.mean(grads * normed, axis=1, keepdims=True)
    )


class Plan:
    def __init__(self, seq_count):
        self.n = seq_count
        self.r = seq_count // ZN
        self.shard = (D * QKV + BROWS * D + D * MT) // seq_count
        self.unit = self.shard // 3
        self.uq = self.unit // QKV
        self.ub = self.unit // D
        self.um = self.unit // MT
        self.nq = D // self.uq
        self.nb = self.nq + BROWS // self.ub
        self.nm = D // self.um
        self.first_mod = self.nb // 3
        self.flat_rows = self.unit // LANES
        self.frames = seq_count * F_DEV


def place(plan):
    s = lax.axis_index("seq")
    t = lax.axis_index("tp")
    return s, t, lax.div(s, plan.r), lax.rem(s, plan.r)


def remote(src, dst, send_sem, recv_sem, s, t):
    return pltpu.make_async_remote_copy(
        src_ref=src,
        dst_ref=dst,
        send_sem=send_sem,
        recv_sem=recv_sem,
        device_id=(s, t),
        device_id_type=MESH,
    )


def greet(peers):
    barrier = pltpu.get_barrier_semaphore()
    for s, t in peers:
        pl.semaphore_signal(barrier, inc=1, device_id=(s, t), device_id_type=MESH)
    pl.semaphore_wait(barrier, len(peers))


def by_kind(plan, k, act, low=0, high=None):
    high = plan.nb if high is None else high
    q_high, b_low = min(plan.nq, high), max(plan.nq, low)
    if low < q_high:
        @pl.when((k >= low) & (k < q_high))
        def _():
            act("q")

    if b_low < high:
        @pl.when((k >= b_low) & (k < high))
        def _():
            act("b")


def unit_of(plan, k, kind, wq, wb):
    if kind == "q":
        return wq.at[pl.ds(pl.multiple_of(k * plan.uq, plan.uq), plan.uq)]
    return wb.at[pl.ds(pl.multiple_of((k - plan.nq) * plan.ub, plan.ub), plan.ub)]


def call(kernel, outs, scratch, ins, cid=None, cost=None, name=None):
    params = dict(vmem_limit_bytes=VMEM_LIMIT)
    if cid is not None:
        params.update(collective_id=cid, has_side_effects=True)
    return pl.pallas_call(
        kernel,
        out_shape=outs,
        in_specs=ins,
        out_specs=jax.tree.map(lambda _: VM, outs),
        scratch_shapes=scratch,
        compiler_params=pltpu.CompilerParams(**params),
        name=name,
    )


def gather_kernel(
    plan, master, cond, wq, wb, mod, wo, tile, macc, mpart, mrecv,
    send_sem, recv_sem, msend, mrecv_sem, tsend, trecv, osend, orecv,
):
    s, t, z, r = place(plan)
    n, rn = plan.n, plan.r
    greet(
        [(lax.rem(s + d, n), t) for d in range(1, n)]
        + [(s, lax.rem(t + d, TP)) for d in range(1, TP)]
    )

    def unit(k, kind):
        if kind == "q":
            return wq.at[pl.ds(pl.multiple_of(k * plan.uq, plan.uq), plan.uq)]
        return wb.at[pl.ds(pl.multiple_of((k - plan.nq) * plan.ub, plan.ub), plan.ub)]

    def move(k, lu, kind, sem, owner_r, to_s):
        ref = unit(k, kind)
        return remote(ref, ref, send_sem.at[lu, sem], recv_sem.at[lu, owner_r], to_s, t)

    def spread(k, lu, up, down, act):
        def for_kind(kind):
            if up is not None:
                @pl.when(up)
                def _():
                    act(move(k, lu, kind, 0, r, s + rn))
            if down is not None:
                @pl.when(down)
                def _():
                    act(move(k, lu, kind, 1, r, s - rn))
            for d in range(1, rn):
                act(move(k, lu, kind, 1 + d, r, z * rn + lax.rem(r + d, rn)))

        by_kind(plan, k, for_kind)

    start = lambda copy: copy.start()
    finish = lambda copy: copy.wait_send()

    for i in range(3):
        k = 3 * s + i
        base = i * plan.flat_rows

        def fill(kind):
            if kind == "q":
                rows, ref, at, cols = plan.uq, wq, k * plan.uq, QKV // LANES
            else:
                rows, ref, at, cols = plan.ub, wb, (k - plan.nq) * plan.ub, D // LANES
            at = pl.multiple_of(at, rows)
            for j in range(cols):
                ref[pl.ds(at, rows), j * LANES : (j + 1) * LANES] = master[
                    pl.ds(base + j, rows, stride=cols), :
                ].astype(BF16)

        by_kind(plan, k, fill)
        spread(k, 3 * z + i, z < ZN - 1, z > 0, start)

    macc[...] = jnp.zeros_like(macc)
    for i in range(3):
        k = 3 * s + i
        base = i * plan.flat_rows

        @pl.when(k >= plan.nb)
        def _():
            for j in range(MCOLS):
                tile[:, j * LANES : (j + 1) * LANES] = master[
                    pl.ds(base + j, plan.um, stride=MCOLS), :
                ].astype(BF16)
            macc[...] += mm(cond[k - plan.nb], tile[...])

    fm = plan.first_mod

    @pl.when(s >= fm)
    def _():
        for f in range(plan.frames):
            for j in range(MCOLS):
                mpart[f // F_DEV, pl.ds((f % F_DEV) * MCOLS + j, 1), :] = macc[
                    pl.ds(f, 1), j * LANES : (j + 1) * LANES
                ]
        mrecv[s - fm] = mpart[s]
        for d in range(1, n):
            to = lax.rem(s + d, n)
            remote(mpart.at[to], mrecv.at[s - fm], msend.at[d - 1], mrecv_sem.at[s - fm], to, t).start()

    for src in range(fm, n):
        @pl.when(s != src)
        def _():
            remote(
                mpart.at[0], mrecv.at[src - fm], msend.at[0], mrecv_sem.at[src - fm], s, t
            ).wait_recv()

    total = mrecv[0]
    for src in range(1, n - fm):
        total = total + mrecv[src]
    mod[t] = total
    for d in range(1, TP):
        remote(mod.at[t], mod.at[t], tsend.at[d - 1], trecv.at[t], s, lax.rem(t + d, TP)).start()

    for d in range(1, ZN):
        for i in range(3):
            for side in (0, 1):
                zs = z - d if side == 0 else z + d
                k = 3 * (zs * rn + r) + i
                lu = 3 * zs + i

                @pl.when((zs >= 0) & (zs < ZN))
                def _():
                    by_kind(plan, k, lambda kind: move(k, lu, kind, 0, r, s).wait_recv())
                    if side == 0:
                        spread(k, lu, z < ZN - 1, None, start)
                    else:
                        spread(k, lu, None, z > 0, start)

    for d in range(1, rn):
        other = lax.rem(r + d, rn)
        for zs in range(ZN):
            for i in range(3):
                k = 3 * (zs * rn + other) + i
                by_kind(plan, k, lambda kind: move(k, 3 * zs + i, kind, 0, other, s).wait_recv())

    wo[t] = wb[:HD]
    for d in range(1, TP):
        remote(wo.at[t], wo.at[t], osend.at[d - 1], orecv.at[t], s, lax.rem(t + d, TP)).start()
    for d in range(1, TP):
        other = lax.rem(t + d, TP)
        remote(wo.at[t], wo.at[other], osend.at[0], orecv.at[other], s, t).wait_recv()
        remote(wo.at[t], wo.at[t], osend.at[d - 1], orecv.at[t], s, other).wait_send()
        remote(mod.at[t], mod.at[other], tsend.at[0], trecv.at[other], s, t).wait_recv()
        remote(mod.at[t], mod.at[t], tsend.at[d - 1], trecv.at[t], s, other).wait_send()

    @pl.when(s >= fm)
    def _():
        for d in range(1, n):
            to = lax.rem(s + d, n)
            remote(mpart.at[to], mrecv.at[s - fm], msend.at[d - 1], mrecv_sem.at[s - fm], to, t).wait_send()

    for i in range(3):
        spread(3 * s + i, 3 * z + i, z < ZN - 1, z > 0, finish)
    for d in range(1, ZN):
        for i in range(3):
            for side in (0, 1):
                zs = z - d if side == 0 else z + d
                k = 3 * (zs * rn + r) + i
                lu = 3 * zs + i

                @pl.when((zs >= 0) & (zs < ZN))
                def _():
                    if side == 0:
                        spread(k, lu, z < ZN - 1, None, finish)
                    else:
                        spread(k, lu, None, z > 0, finish)


def gather_weights(plan, master, cond_units, cid):
    n = plan.n
    mrows = F_DEV * MCOLS
    return call(
        functools.partial(gather_kernel, plan),
        (
            jax.ShapeDtypeStruct((D, QKV), BF16),
            jax.ShapeDtypeStruct((BROWS, D), BF16),
            jax.ShapeDtypeStruct((TP, mrows, LANES), F32),
            jax.ShapeDtypeStruct((TP, HD, D), BF16),
        ),
        [
            pltpu.VMEM((plan.um, MT), BF16),
            pltpu.VMEM((plan.frames, MT), F32),
            pltpu.VMEM((n, mrows, LANES), F32),
            pltpu.VMEM((n - plan.first_mod, mrows, LANES), F32),
            DMA((3 * ZN, plan.r + 1)),
            DMA((3 * ZN, plan.r)),
            DMA((n - 1,)),
            DMA((n - plan.first_mod,)),
            DMA((TP - 1,)),
            DMA((TP,)),
            DMA((TP - 1,)),
            DMA((TP,)),
        ],
        [VM, VM],
        cid,
        name="gather_weights",
    )(master, cond_units)


def qkv_kernel(plan, q, kv, q_out, kv_out, qs, ks, rs, qr, kr, rr):
    s, t, z, r = place(plan)
    rn = plan.r
    greet(
        [(lax.rem(z + d, ZN) * rn + r, t) for d in range(1, ZN)]
        + [(z * rn + lax.rem(r + d, rn), t) for d in range(1, rn)]
    )

    def kv_copy(d):
        h = lax.rem(z + d, ZN)
        return remote(kv.at[h], kv_out.at[s], ks.at[d - 1], kr.at[z], h * rn + r, t)

    def q_copy(d):
        h = lax.rem(z + d, ZN)
        return remote(q.at[h], q_out.at[z], qs.at[d - 1], qr.at[z], h * rn + r, t)

    def side_copy(zs, e):
        at = zs * rn + r
        src = kv_out.at[at]
        return remote(src, src, rs.at[zs, e - 1], rr.at[at], z * rn + lax.rem(r + e, rn), t)

    for d in range(1, ZN):
        kv_copy(d).start()
    for d in range(1, ZN):
        q_copy(d).start()
    kv_out[s] = kv[z]
    q_out[z] = q[z]
    for e in range(1, rn):
        side_copy(z, e).start()
    for d in range(1, ZN):
        zs = lax.rem(z + d, ZN)
        remote(kv.at[0], kv_out.at[zs * rn + r], ks.at[0], kr.at[zs], s, t).wait_recv()
        for e in range(1, rn):
            side_copy(zs, e).start()
    for d in range(1, ZN):
        zs = lax.rem(z + d, ZN)
        remote(q.at[0], q_out.at[zs], qs.at[0], qr.at[zs], s, t).wait_recv()
    for e in range(1, rn):
        for zs in range(ZN):
            at = zs * rn + lax.rem(r + e, rn)
            remote(kv_out.at[at], kv_out.at[at], rs.at[0, 0], rr.at[at], s, t).wait_recv()
    for d in range(1, ZN):
        kv_copy(d).wait_send()
        q_copy(d).wait_send()
    for zs in range(ZN):
        for e in range(1, rn):
            side_copy(zs, e).wait_send()


def exchange_qkv(plan, q, kv, cid):
    rn = plan.r
    return call(
        functools.partial(qkv_kernel, plan),
        (
            jax.ShapeDtypeStruct((ZN, TOK_FRAME, LANES), BF16),
            jax.ShapeDtypeStruct((plan.n, F_DEV * TOK_FRAME, LANES), BF16),
        ),
        [DMA((ZN - 1,)), DMA((ZN - 1,)), DMA((ZN, rn - 1)), DMA((ZN,)), DMA((ZN,)), DMA((plan.n,))],
        [VM, VM],
        cid,
        name="exchange_qkv",
    )(q, kv)


def padded(rows, low):
    zero = jnp.zeros_like(rows)
    return jnp.concatenate([rows, zero] if low else [zero, rows], axis=1)


def attend_kernel(plan, meta, q, kv, o, ot, lse, m_ref, l_ref, acc):
    r = meta[plan.frames]
    scale = HEAD ** (-0.5)

    def group(zq, carry):
        for f in range(F_DEV):
            frame = (zq * plan.r + r) * F_DEV + f
            clip = meta[frame]
            pack = q[zq]
            qz = padded(pack[:, f * HEAD : (f + 1) * HEAD], True) * jnp.asarray(scale, BF16)
            m_ref[...] = jnp.full_like(m_ref, -1e30)
            l_ref[...] = jnp.zeros_like(l_ref)
            acc[...] = jnp.zeros_like(acc)

            def block(j, inner):
                @pl.when(meta[j] == clip)
                def _():
                    rows = pl.multiple_of(lax.rem(j, F_DEV) * TOK_FRAME, TOK_FRAME)
                    keys = kv[lax.div(j, F_DEV), pl.ds(rows, TOK_FRAME), :]
                    st = mm_nt(keys, qz)
                    m_old = m_ref[...]
                    m_new = jnp.maximum(m_old, jnp.max(st, axis=0, keepdims=True))
                    p = jnp.exp(st - m_new)
                    alpha = jnp.exp(m_old - m_new)
                    m_ref[...] = m_new
                    l_ref[...] = l_ref[...] * alpha + jnp.sum(p, axis=0, keepdims=True)
                    acc[...] = acc[...] * alpha + mm_tn(keys, p.astype(BF16))

                return inner

            lax.fori_loop(0, frame + 1, block, 0)
            total = l_ref[...]
            out = acc[HEAD:, :] / total
            ot[zq * F_DEV + f] = out
            lse[zq * F_DEV + f] = m_ref[...] + jnp.log(total)
            rows = out.T
            o[zq, f] = jnp.concatenate([rows[:PACK], rows[PACK:]], axis=1).astype(BF16)
        return carry

    lax.fori_loop(0, ZN, group, 0)


def attend(plan, meta, q, kv):
    frames = ZN * F_DEV
    return call(
        functools.partial(attend_kernel, plan),
        (
            jax.ShapeDtypeStruct((ZN, F_DEV, PACK, LANES), BF16),
            jax.ShapeDtypeStruct((frames, HEAD, TOK_FRAME), F32),
            jax.ShapeDtypeStruct((frames, 1, TOK_FRAME), F32),
        ),
        [
            pltpu.VMEM((1, TOK_FRAME), F32),
            pltpu.VMEM((1, TOK_FRAME), F32),
            pltpu.VMEM((LANES, TOK_FRAME), F32),
        ],
        [SM, VM, VM],
        name="attend",
    )(meta, q, kv)


def attend_back_kernel(plan, meta, q, kv, do, ot, lse, dq, dkv, dkv_acc, dq_acc):
    r = meta[plan.frames]
    scale = HEAD ** (-0.5)
    dkv_acc[...] = jnp.zeros_like(dkv_acc)

    def group(zq, carry):
        parts = []
        for f in range(F_DEV):
            frame = (zq * plan.r + r) * F_DEV + f
            clip = meta[frame]
            columns = slice(f * HEAD, (f + 1) * HEAD)
            qz = padded(q[zq][:, columns], True) * jnp.asarray(scale, BF16)
            grads = jnp.concatenate([do[zq, f][:, :HEAD], do[zq, f][:, HEAD:]], axis=0)
            doz = padded(grads, False)
            delta = jnp.sum(grads.astype(F32).T * ot[zq * F_DEV + f], axis=0, keepdims=True)
            logs = lse[zq * F_DEV + f]
            dq_acc[...] = jnp.zeros_like(dq_acc)

            def block(j, inner):
                @pl.when(meta[j] == clip)
                def _():
                    g = lax.div(j, F_DEV)
                    rows = pl.multiple_of(lax.rem(j, F_DEV) * TOK_FRAME, TOK_FRAME)
                    keys = kv[g, pl.ds(rows, TOK_FRAME), :]
                    pt = jnp.exp(mm_nt(keys, qz) - logs)
                    dst = (pt * (mm_nt(keys, doz) - delta)).astype(BF16)
                    dkv_acc[g, pl.ds(rows, TOK_FRAME), :] += mm(dst, qz) + mm(pt.astype(BF16), doz)
                    dq_acc[...] += mm_tn(keys, dst)

                return inner

            lax.fori_loop(0, frame + 1, block, 0)
            parts.append((dq_acc[:HEAD, :] * scale).T)
        dq[zq] = jnp.concatenate(parts, axis=1).astype(BF16)
        return carry

    lax.fori_loop(0, ZN, group, 0)
    dkv[...] = dkv_acc[...].astype(BF16)


def attend_back(plan, meta, q, kv, do, ot, lse):
    return call(
        functools.partial(attend_back_kernel, plan),
        (
            jax.ShapeDtypeStruct((ZN, TOK_FRAME, LANES), BF16),
            jax.ShapeDtypeStruct((plan.n, F_DEV * TOK_FRAME, LANES), BF16),
        ),
        [
            pltpu.VMEM((plan.n, F_DEV * TOK_FRAME, LANES), F32),
            pltpu.VMEM((LANES, TOK_FRAME), F32),
        ],
        [SM, VM, VM, VM, VM, VM],
        name="attend_back",
    )(meta, q, kv, do, ot, lse)


def loop(count, step, body):
    def turn(i, carry):
        body(pl.multiple_of(i * step, step))
        return carry

    lax.fori_loop(0, count // step, turn, 0)


def add_to(ref, row, values):
    ref[pl.ds(row, 1), :] += jnp.sum(values, axis=0, keepdims=True)


def middle_kernel(
    plan, o_mine, wo, wb, tokens, grad_out, mod,
    result, gb, do_out, dmid, dmod,
    oall, attended, attn, mid, norm, inv, sin, hidden, dmlp, dhid, dup,
    own, csend, crecv, ysend, yrecv, dattn, dsend, dwo, wsend, wrecv,
    o_s, o_r, f_s, f_r, n_s, n_r, c_s, c_r, y_s, y_r, d_s, d_r, w_s, w_r, e_s, e_r,
):
    s, t, z, r = place(plan)
    rn = plan.r
    y = lax.div(t, 2)
    c = lax.rem(t, 2)
    sib = 2 * y + 1 - c
    across = lax.rem(t + 2, TP)
    mine = pl.multiple_of(c * TOK_FRAME, TOK_FRAME)
    theirs = pl.multiple_of((1 - c) * TOK_FRAME, TOK_FRAME)
    pairs = [(d, e) for d in range(ZN) for e in range(2)][1:]

    def partner(d, e):
        return lax.rem(z + d, ZN), (c if e == 0 else 1 - c)

    greet(
        [(partner(d, e)[0] * rn + r, 2 * y + partner(d, e)[1]) for d, e in pairs]
        + [(s, across)]
    )

    def o_copy(d, e):
        zd, cd = partner(d, e)
        return remote(
            o_mine.at[zd, cd], oall.at[y * 8 + c * ZN + z], o_s.at[2 * d + e],
            o_r.at[c * ZN + z], zd * rn + r, 2 * y + cd,
        )

    def f_copy(slot):
        ref = oall.at[y * 8 + slot]
        return remote(ref, ref, f_s.at[slot], f_r.at[slot], s, across)

    for d, e in pairs:
        o_copy(d, e).start()
    oall[y * 8 + c * ZN + z] = o_mine[z, c]
    f_copy(c * ZN + z).start()

    def d_mlp(f):
        def body(at):
            rows = pl.ds(f * TOK_FRAME + at, 64)
            dmlp[rows, :] = (grad_out[rows, :].astype(F32) * mod[f * 6 + 5 : f * 6 + 6, :]).astype(
                BF16
            )

        loop(TOK_FRAME, 64, body)

    for f in range(F_DEV):
        d_mlp(f)

    def d_hidden(at):
        dhid[:, pl.ds(at, TILE)] = mm_nt(dmlp[...], wb[pl.ds(HD + FT + at, TILE), :])

    loop(FT, TILE, d_hidden)

    for d, e in pairs:
        zd, cd = partner(d, e)
        slot = cd * ZN + zd
        remote(o_mine.at[0, 0], oall.at[y * 8 + slot], o_s.at[0], o_r.at[slot], s, t).wait_recv()
        f_copy(slot).start()
    for slot in range(8):
        remote(
            oall.at[0], oall.at[(1 - y) * 8 + slot], f_s.at[slot], f_r.at[slot], s, t
        ).wait_recv()
    for m in range(HEADS // 2):
        a, b = oall[2 * m], oall[2 * m + 1]
        cols = slice(m * LANES, (m + 1) * LANES)
        attended[:PACK, cols] = jnp.concatenate([a[:, :HEAD], b[:, :HEAD]], axis=1)
        attended[PACK:, cols] = jnp.concatenate([a[:, HEAD:], b[:, HEAD:]], axis=1)

    def attn_tile(at):
        attn[:, pl.ds(at, TILE)] = mm(attended[...], wo[:, pl.ds(at, TILE)])

    loop(D, TILE, attn_tile)

    row = lambda part: mod[pl.ds(c * 6 + part, 1), :]

    def norm_rows(at):
        rows = pl.ds(at, 64)
        values = tokens[pl.ds(mine + at, 64), :].astype(F32) + row(2) * attn[rows, :]
        mid[rows, :] = values
        normed, inverse = normalize(values)
        norm[rows, :] = normed
        inv[rows, :] = inverse
        sin[pl.ds(mine + at, 64), :] = (normed * (1.0 + row(4)) + row(3)).astype(BF16)

    loop(TOK_FRAME, 64, norm_rows)

    def n_copy(base):
        ref = sin.at[pl.ds(base, TOK_FRAME)]
        return remote(ref, ref, n_s.at[0], n_r.at[0], s, sib)

    n_copy(mine).start()

    def feed(base):
        rows = pl.ds(base, TOK_FRAME)

        def tile(at):
            cols = pl.ds(at, TILE)
            u = mm(sin[rows, :], wb[HD : HD + FT, cols])
            square = u * u
            inner = GELU_A * u * (1.0 + GELU_B * square)
            th = jnp.tanh(inner)
            half = 0.5 * (1.0 + th)
            hidden[rows, cols] = (u * half).astype(BF16)
            slope = half + 0.5 * u * (1.0 - th * th) * (GELU_A * (1.0 + 3.0 * GELU_B * square))
            dup[rows, cols] = (dhid[rows, cols] * slope).astype(BF16)

        loop(FT, TILE, tile)

    feed(mine)
    n_copy(theirs).wait_recv()
    feed(theirs)

    def c_copy(w, n):
        return remote(csend.at[w, n], crecv.at[w, n], c_s.at[w, n], c_r.at[w, n], s, sib)

    def y_copy(w, n):
        return remote(ysend.at[w, n], yrecv.at[w, n], y_s.at[w, n], y_r.at[w, n], s, across)

    def pass_on(w, n):
        c_copy(w, n).wait_recv()
        ysend[w, n] = (own[n] + crecv[w, n].astype(F32)).astype(BF16)
        y_copy(w, n).start()

    def product(w, base, n):
        rows = pl.ds(base, TOK_FRAME)
        if w == 0:
            return mm_nt(dup[rows, :], wb[HD + n * TILE : HD + (n + 1) * TILE, :])
        return mm(hidden[rows, :], wb[HD + FT :, n * TILE : (n + 1) * TILE])

    for w in range(2):
        for n in range(TILES):
            csend[w, n] = product(w, theirs, n).astype(BF16)
            c_copy(w, n).start()
            own[n] = product(w, mine, n)
            if n:
                pass_on(w, n - 1)
        pass_on(w, TILES - 1)

    def down_grad(at):
        gb[pl.ds(HD + FT + at, TILE), :] = mm_tn(hidden[:, pl.ds(at, TILE)], dmlp[...]).astype(BF16)

    def up_grad(at):
        gb[pl.ds(HD + at, TILE), :] = mm_tn(sin[:, pl.ds(at, TILE)], dup[...]).astype(BF16)

    loop(FT, TILE, down_grad)
    loop(D, TILE, up_grad)

    dm = dmod
    dm[...] = jnp.zeros_like(dm)
    for n in range(TILES):
        y_copy(0, n).wait_recv()

    def total(w, rows):
        return jnp.concatenate(
            [ysend[w, n, rows].astype(F32) + yrecv[w, n, rows].astype(F32) for n in range(TILES)],
            axis=1,
        )

    def back_rows(at):
        rows = pl.ds(at, 64)
        tok_rows = pl.ds(mine + at, 64)
        grads = total(0, rows)
        normed = norm[rows, :]
        add_to(dm, 1, grads)
        add_to(dm, 2, grads * normed)
        values = grad_out[tok_rows, :].astype(F32) + norm_back(
            grads * (1.0 + row(4)), normed, inv[rows, :]
        )
        dmid[rows, :] = values
        add_to(dm, 0, attn[rows, :] * values)
        dattn[rows, :] = (row(2) * values).astype(BF16)

    loop(TOK_FRAME, 64, back_rows)
    for ch in range(2):
        part = mm_nt(dattn[...], wo[pl.ds(pl.multiple_of((2 * y + ch) * HD, HD), HD), :]).astype(BF16)
        for zh in range(ZN):
            cols = slice(zh * HEAD, (zh + 1) * HEAD)
            dsend[ch * ZN + zh] = jnp.concatenate([part[:PACK, cols], part[PACK:, cols]], axis=1)

    def d_copy(d, e):
        zd, cd = partner(d, e)
        return remote(
            dsend.at[cd * ZN + zd], do_out.at[z, c], d_s.at[2 * d + e], d_r.at[2 * z + c],
            zd * rn + r, 2 * y + cd,
        )

    for d, e in pairs:
        d_copy(d, e).start()
    do_out[z, c] = dsend[c * ZN + z]

    def o_grad(head_core):
        cols = pl.ds(pl.multiple_of((2 * y + head_core) * HD, HD), HD)
        return mm_tn(attended[:, cols], dattn[...])

    w_copy = remote(wsend, wrecv, w_s, w_r, s, sib)
    wsend[...] = o_grad(1 - c).astype(BF16)
    w_copy.start()
    dwo[...] = o_grad(c)

    for n in range(TILES):
        y_copy(1, n).wait_recv()

    def result_rows(at):
        rows = pl.ds(at, 64)
        tok_rows = pl.ds(mine + at, 64)
        mlp = total(1, rows)
        add_to(dm, 3, mlp * grad_out[tok_rows, :].astype(F32))
        result[tok_rows, :] = (mid[rows, :] + row(5) * mlp).astype(BF16)

    loop(TOK_FRAME, 64, result_rows)

    def e_copy(base):
        ref = result.at[pl.ds(base, TOK_FRAME)]
        return remote(ref, ref, e_s, e_r, s, sib)

    e_copy(mine).start()
    w_copy.wait_recv()
    gb[:HD, :] = (dwo[...] + wrecv[...].astype(F32)).astype(BF16)

    for d, e in pairs:
        zd, cd = partner(d, e)
        remote(
            dsend.at[0], do_out.at[zd, cd], d_s.at[0], d_r.at[2 * zd + cd], s, t
        ).wait_recv()
    e_copy(theirs).wait_recv()
    for d, e in pairs:
        o_copy(d, e).wait_send()
        d_copy(d, e).wait_send()
    for slot in range(8):
        f_copy(slot).wait_send()
    n_copy(mine).wait_send()
    for w in range(2):
        for n in range(TILES):
            c_copy(w, n).wait_send()
            y_copy(w, n).wait_send()
    w_copy.wait_send()
    e_copy(mine).wait_send()


def middle_part(plan, o_mine, wo, wb, tokens, grad_out, mod_rows, cid):
    rows = F_DEV * TOK_FRAME
    half = lambda dtype: pltpu.VMEM((TOK_FRAME, D), dtype)
    full = lambda dtype: pltpu.VMEM((rows, D), dtype)
    tiles = pltpu.VMEM((2, TILES, TOK_FRAME, TILE), BF16)
    return call(
        functools.partial(middle_kernel, plan),
        (
            jax.ShapeDtypeStruct((rows, D), BF16),
            jax.ShapeDtypeStruct((BROWS, D), BF16),
            jax.ShapeDtypeStruct((ZN, F_DEV, PACK, LANES), BF16),
            jax.ShapeDtypeStruct((TOK_FRAME, D), F32),
            jax.ShapeDtypeStruct((8, D), F32),
        ),
        [
            pltpu.VMEM((HEADS, PACK, LANES), BF16),
            half(BF16), half(F32), half(F32), half(F32), pltpu.VMEM((TOK_FRAME, 1), F32),
            full(BF16), full(BF16), full(BF16), full(F32), full(BF16),
            pltpu.VMEM((TILES, TOK_FRAME, TILE), F32), tiles, tiles, tiles, tiles,
            half(BF16), pltpu.VMEM((8, PACK, LANES), BF16),
            pltpu.VMEM((HD, D), F32), pltpu.VMEM((HD, D), BF16), pltpu.VMEM((HD, D), BF16),
            DMA((8,)), DMA((8,)), DMA((8,)), DMA((8,)), DMA((1,)), DMA((1,)),
            DMA((2, TILES)), DMA((2, TILES)), DMA((2, TILES)), DMA((2, TILES)),
            DMA((8,)), DMA((8,)), DMA, DMA, DMA, DMA,
        ],
        [VM] * 6,
        cid,
        name="middle_part",
    )(o_mine, wo, wb, tokens, grad_out, mod_rows)


def tail_kernel(
    plan, dq, dkv, first_in, wq, tokens, dmid, mod, dm4, gb,
    igrad, oq, ob, dall,
    stage, side, q_in, kv_in, dqkv, gq, own, csend, crecv, ysend, yrecv, dm, dm3, dboth,
    rq, rb, cq, cb,
    q_s, q_r, k_s, k_r, x_s, x_r, c_s, c_r, y_s, y_r, e_s, e_r, h_s, h_r, m_s, m_r, r_s, r_r, t_s, t_r,
):
    s, t, z, r = place(plan)
    n, rn = plan.n, plan.r
    y = lax.div(t, 2)
    c = lax.rem(t, 2)
    sib = 2 * y + 1 - c
    across = lax.rem(t + 2, TP)
    mine = pl.multiple_of(c * TOK_FRAME, TOK_FRAME)
    theirs = pl.multiple_of((1 - c) * TOK_FRAME, TOK_FRAME)
    greet([(lax.rem(s + d, n), t) for d in range(1, n)] + [(s, sib), (s, across)])

    def side_copy(d, e):
        zs = lax.rem(z + d, ZN)
        other = lax.rem(r + e, rn)
        return remote(
            dkv.at[zs * rn + other], side.at[e - 1, d], x_s.at[d, e - 1], x_r.at[d, e - 1],
            z * rn + other, t,
        )

    def q_copy(d):
        to = lax.rem(z + d, ZN)
        return remote(dq.at[to], q_in.at[z], q_s.at[d - 1], q_r.at[z], to * rn + r, t)

    def kv_copy(d):
        to = lax.rem(z + d, ZN)
        return remote(stage.at[d], kv_in.at[z], k_s.at[d - 1], k_r.at[z], to * rn + r, t)

    order = list(range(1, ZN)) + [0]
    for d in order:
        for e in range(1, rn):
            side_copy(d, e).start()
    for d in range(1, ZN):
        q_copy(d).start()
    q_in[z] = dq[z]
    for d in order:
        zs = lax.rem(z + d, ZN)
        total = dkv[zs * rn + r].astype(F32)
        for e in range(1, rn):
            side_copy(d, e).wait_recv()
            total = total + side[e - 1, d].astype(F32)
        if d == 0:
            kv_in[z] = total.astype(BF16)
        else:
            stage[d] = total.astype(BF16)
            kv_copy(d).start()

    def owner(j):
        a = 2 - lax.div(z, 2)
        b = 2 * lax.div(ZN - 1 - z, ZN - 1)
        return lax.rem(a * j + b, 3)

    def grad_copy(zo, i, d, kind):
        other = lax.rem(r + d, rn)
        k = 3 * (zo * rn + other) + i
        lu = 3 * zo + i
        buf = rq if kind == "q" else rb
        return remote(
            unit_of(plan, k, kind, gq, gb), buf.at[d - 1, lu], r_s.at[lu, d - 1],
            r_r.at[lu, d - 1], z * rn + other, t,
        )

    def grad_sides(owners, low, high, act):
        for zo in owners:
            for i in range(3):
                for d in range(1, rn):
                    k = 3 * (zo * rn + lax.rem(r + d, rn)) + i
                    by_kind(plan, k, lambda kind: act(grad_copy(zo, i, d, kind)), low, high)

    def chain_copy(lu, kind, below, to):
        src = (rq if kind == "q" else rb).at[0, lu]
        dst = cq.at[lu] if kind == "q" else cb.at[below, lu]
        return remote(src, dst, t_s.at[lu], t_r.at[lu, below], to, t)

    def grad_chain(owners, low, high):
        for zo in owners:
            for i in range(3):
                k = 3 * (zo * rn + r) + i
                lu = 3 * zo + i

                def step(kind):
                    part = rq if kind == "q" else rb
                    out = oq if kind == "q" else ob
                    unit = unit_of(plan, k, kind, gq, gb)
                    rows = plan.uq if kind == "q" else plan.ub
                    for d in range(1, rn):
                        remote(
                            unit, part.at[d - 1, lu], r_s.at[lu, d - 1], r_r.at[lu, d - 1], s, t
                        ).wait_recv()
                    above = (zo <= z) & (z < ZN - 1)
                    below = (zo >= z) & (z > 0)

                    @pl.when(above)
                    def _():
                        chain_copy(lu, kind, 0, s).wait_recv()

                    if kind == "b":
                        @pl.when(below)
                        def _():
                            chain_copy(lu, kind, 1, s).wait_recv()

                    def here(at):
                        total = unit[pl.ds(at, 16), :].astype(F32)
                        for d in range(1, rn):
                            total = total + part[d - 1, lu, pl.ds(at, 16), :].astype(F32)
                        return total

                    def from_chain(at, below):
                        ref = cq.at[lu] if kind == "q" else cb.at[below, lu]
                        return ref[pl.ds(at, 16), :].astype(F32)

                    @pl.when(zo != z)
                    def _():
                        @pl.when((zo < z) & (z == ZN - 1) | (zo > z) & (z == 0))
                        def _():
                            def body(at):
                                part[0, lu, pl.ds(at, 16), :] = here(at).astype(BF16)

                            loop(rows, 16, body)

                        @pl.when((zo < z) & (z < ZN - 1))
                        def _():
                            def body(at):
                                part[0, lu, pl.ds(at, 16), :] = (here(at) + from_chain(at, 0)).astype(BF16)

                            loop(rows, 16, body)

                        if kind == "b":
                            @pl.when((zo > z) & (z > 0))
                            def _():
                                def body(at):
                                    part[0, lu, pl.ds(at, 16), :] = (here(at) + from_chain(at, 1)).astype(BF16)

                                loop(rows, 16, body)

                    @pl.when(zo < z)
                    def _():
                        chain_copy(lu, kind, 0, s - rn).start()

                    if kind == "b":
                        @pl.when(zo > z)
                        def _():
                            chain_copy(lu, kind, 1, s + rn).start()

                    @pl.when((zo == z) & (z == 0))
                    def _():
                        def body(at):
                            out[i, pl.ds(at, 16), :] = here(at) + from_chain(at, 0)

                        loop(rows, 16, body)

                    if kind == "b":
                        @pl.when((zo == z) & (z > 0))
                        def _():
                            def body(at):
                                out[i, pl.ds(at, 16), :] = here(at) + from_chain(at, 0) + from_chain(at, 1)

                            loop(rows, 16, body)

                by_kind(plan, k, step, low, high)

    def grad_close(owners, low, high):
        grad_sides(owners, low, high, lambda copy: copy.wait_send())
        for zo in owners:
            for i in range(3):
                def close(kind):
                    @pl.when(zo != z)
                    def _():
                        chain_copy(3 * zo + i, kind, 0, s).wait_send()

                by_kind(plan, 3 * (zo * rn + r) + i, close, low, high)

    every = [owner(j) for j in range(3)]
    start = lambda copy: copy.start()
    grad_sides(every, plan.nq, plan.nb, start)

    for d in range(1, ZN):
        zs = lax.rem(z + d, ZN)
        remote(dq.at[0], q_in.at[zs], q_s.at[0], q_r.at[zs], s, t).wait_recv()
        remote(stage.at[d], kv_in.at[zs], k_s.at[0], k_r.at[zs], s, t).wait_recv()
    for p in range(2):
        cols = slice(p * LANES, (p + 1) * LANES)
        a, b = q_in[2 * p], q_in[2 * p + 1]
        dqkv[:TOK_FRAME, cols] = jnp.concatenate([a[:, :HEAD], b[:, :HEAD]], axis=1)
        dqkv[TOK_FRAME:, cols] = jnp.concatenate([a[:, HEAD:], b[:, HEAD:]], axis=1)
        a, b = kv_in[2 * p], kv_in[2 * p + 1]
        dqkv[:, HD + p * LANES : HD + (p + 1) * LANES] = jnp.concatenate(
            [a[:, :HEAD], b[:, :HEAD]], axis=1
        )
        dqkv[:, 2 * HD + p * LANES : 2 * HD + (p + 1) * LANES] = jnp.concatenate(
            [a[:, HEAD:], b[:, HEAD:]], axis=1
        )

    def q_grad(at):
        gq[pl.ds(at, TILE), :] = mm_tn(first_in[:, pl.ds(at, TILE)], dqkv[...]).astype(BF16)

    loop(D, TILE, q_grad)
    grad_sides([0], 0, plan.nq, start)

    def c_copy(w):
        return remote(csend.at[w], crecv.at[w], c_s.at[w], c_r.at[w], s, sib)

    def y_copy(w):
        return remote(ysend.at[w], yrecv.at[w], y_s.at[w], y_r.at[w], s, across)

    def pass_on(w):
        c_copy(w).wait_recv()
        ysend[w] = (own[w] + crecv[w].astype(F32)).astype(BF16)
        y_copy(w).start()

    for w in range(TILES):
        weights = wq[w * TILE : (w + 1) * TILE, :]
        csend[w] = mm_nt(dqkv[pl.ds(theirs, TOK_FRAME), :], weights).astype(BF16)
        c_copy(w).start()
        own[w] = mm_nt(dqkv[pl.ds(mine, TOK_FRAME), :], weights)
        if w:
            pass_on(w - 1)
    pass_on(TILES - 1)

    grad_chain(every, plan.nq, plan.nb)

    for w in range(TILES):
        y_copy(w).wait_recv()
    row = lambda part: mod[pl.ds(c * 6 + part, 1), :]
    dm[...] = jnp.zeros_like(dm)

    def input_rows(at):
        rows = pl.ds(at, 64)
        tok_rows = pl.ds(mine + at, 64)
        grads = jnp.concatenate(
            [ysend[w, rows].astype(F32) + yrecv[w, rows].astype(F32) for w in range(TILES)], axis=1
        )
        normed, inverse = normalize(tokens[tok_rows, :].astype(F32))
        add_to(dm, 0, grads)
        add_to(dm, 1, grads * normed)
        igrad[tok_rows, :] = dmid[rows, :] + norm_back(grads * (1.0 + row(1)), normed, inverse)

    loop(TOK_FRAME, 64, input_rows)

    def e_copy(base):
        ref = igrad.at[pl.ds(base, TOK_FRAME)]
        return remote(ref, ref, e_s, e_r, s, sib)

    e_copy(mine).start()

    for block in range(6 * D // LANES):
        part, at = block // (D // LANES), block % (D // LANES)
        src = dm if part < 2 else dm4
        lane = slice(at * LANES, (at + 1) * LANES)
        from_row = part if part < 2 else part - 2
        dm3[block // MCOLS, block % MCOLS : block % MCOLS + 1, :] = src[from_row : from_row + 1, lane]
    h_copy = lambda frame: remote(dm3.at[sib], dboth.at[frame], h_s, h_r, s, sib)
    h_copy(c).start()
    dboth[c] = dm3[t]
    h_copy(1 - c).wait_recv()

    def m_copy(src):
        return remote(dboth, dall.at[s], m_s.at[src - plan.first_mod], m_r.at[s], src, t)

    for src in range(plan.first_mod, n):
        @pl.when(s == src)
        def _():
            dall[s] = dboth[...]

        @pl.when(s != src)
        def _():
            m_copy(src).start()

    grad_chain([0], 0, plan.nq)

    @pl.when(s >= plan.first_mod)
    def _():
        for d in range(1, n):
            other = lax.rem(s + d, n)
            remote(dboth, dall.at[other], m_s.at[0], m_r.at[other], s, t).wait_recv()

    e_copy(theirs).wait_recv()
    for d in range(1, ZN):
        q_copy(d).wait_send()
        kv_copy(d).wait_send()
    for d in order:
        for e in range(1, rn):
            side_copy(d, e).wait_send()
    grad_close(every, plan.nq, plan.nb)
    grad_close([0], 0, plan.nq)
    for w in range(TILES):
        c_copy(w).wait_send()
        y_copy(w).wait_send()
    e_copy(mine).wait_send()
    h_copy(c).wait_send()
    for src in range(plan.first_mod, n):
        @pl.when(s != src)
        def _():
            m_copy(src).wait_send()


def tail_part(plan, dq, dkv, first_in, wq, tokens, dmid, mod_rows, dm4, gb, cid):
    n, rn = plan.n, plan.r
    rows = F_DEV * TOK_FRAME
    tiles = pltpu.VMEM((TILES, TOK_FRAME, TILE), BF16)
    mods = n - plan.first_mod
    return call(
        functools.partial(tail_kernel, plan),
        (
            jax.ShapeDtypeStruct((rows, D), F32),
            jax.ShapeDtypeStruct((3, plan.uq, QKV), F32),
            jax.ShapeDtypeStruct((3, plan.ub, D), F32),
            jax.ShapeDtypeStruct((n, F_DEV, 16, LANES), F32),
        ),
        [
            pltpu.VMEM((ZN, rows, LANES), BF16),
            pltpu.VMEM((rn - 1, ZN, rows, LANES), BF16),
            pltpu.VMEM((ZN, TOK_FRAME, LANES), BF16),
            pltpu.VMEM((ZN, rows, LANES), BF16),
            pltpu.VMEM((rows, QKV), BF16),
            pltpu.VMEM((D, QKV), BF16),
            pltpu.VMEM((TILES, TOK_FRAME, TILE), F32), tiles, tiles, tiles, tiles,
            pltpu.VMEM((8, D), F32),
            pltpu.VMEM((TP, 16, LANES), F32),
            pltpu.VMEM((F_DEV, 16, LANES), F32),
            pltpu.VMEM((rn - 1, 3, plan.uq, QKV), BF16),
            pltpu.VMEM((rn - 1, 9, plan.ub, D), BF16),
            pltpu.VMEM((3, plan.uq, QKV), BF16),
            pltpu.VMEM((2, 9, plan.ub, D), BF16),
            DMA((ZN - 1,)), DMA((ZN,)), DMA((ZN - 1,)), DMA((ZN,)), DMA((ZN, rn - 1)), DMA((ZN, rn - 1)),
            DMA((TILES,)), DMA((TILES,)), DMA((TILES,)), DMA((TILES,)),
            DMA, DMA, DMA, DMA, DMA((mods,)), DMA((n,)),
            DMA((9, rn - 1)), DMA((9, rn - 1)), DMA((9,)), DMA((9, 2)),
        ],
        [VM] * 9,
        cid,
        name="tail_part",
    )(dq, dkv, first_in, wq, tokens, dmid, mod_rows, dm4, gb)


def adam_kernel(plan, meta, oq, ob, cond, dmod, master, one, two, average, n_master, n_one, n_two, n_average):
    s = meta[0]
    rate = RATE_FACTOR * D ** (-0.5)
    scale_one = 1.0 / (1.0 - BETA_FIRST**STEP)
    scale_two = 1.0 / (1.0 - BETA_SECOND**STEP)

    def update(rows, grad):
        first = BETA_FIRST * one[rows, :] + (1.0 - BETA_FIRST) * grad
        second = BETA_SECOND * two[rows, :] + (1.0 - BETA_SECOND) * grad * grad
        weight = master[rows, :]
        weight = weight - rate * (
            (first * scale_one) / (jnp.sqrt(second * scale_two) + ADAM_EPSILON)
            + WEIGHT_DECAY * weight
        )
        n_one[rows, :] = first
        n_two[rows, :] = second
        n_master[rows, :] = weight
        n_average[rows, :] = AVERAGE_RATE * average[rows, :] + (1.0 - AVERAGE_RATE) * weight

    for i in range(3):
        k = 3 * s + i
        base = i * plan.flat_rows

        def from_matrix(kind):
            src = oq if kind == "q" else ob
            rows = plan.uq if kind == "q" else plan.ub
            cols = (QKV if kind == "q" else D) // LANES
            for j in range(cols):
                update(
                    pl.ds(base + j, rows, stride=cols), src[i, :, j * LANES : (j + 1) * LANES]
                )

        by_kind(plan, k, from_matrix)

        @pl.when(k >= plan.nb)
        def _():
            at = cond[k - plan.nb]
            for j in range(MCOLS):
                update(
                    pl.ds(base + j, plan.um, stride=MCOLS),
                    mm(at, dmod[pl.ds(j, plan.frames, stride=16), :].astype(BF16)),
                )


def adam(plan, meta, oq, ob, cond_rows, dmod, master, one, two, average):
    shape = jax.ShapeDtypeStruct(master.shape, F32)
    return call(
        functools.partial(adam_kernel, plan),
        (shape,) * 4,
        [],
        [SM] + [VM] * 8,
        name="adam",
    )(meta, oq, ob, cond_rows, dmod, master, one, two, average)


def by_frame(rows):
    return rows.reshape(F_DEV, TOK_FRAME, rows.shape[1])


def frame_affine(rows, factor, offset_rows):
    return (by_frame(rows) * (1.0 + factor)[:, None, :] + offset_rows[:, None, :]).reshape(
        rows.shape
    )


def pack_heads(rows):
    return rows.reshape(F_DEV, TOK_FRAME, ZN, HEAD).transpose(2, 1, 0, 3).reshape(
        ZN, TOK_FRAME, F_DEV * HEAD
    )


def local(
    tokens,
    grad_out,
    noise_level,
    context_mask,
    frame_clip,
    level_table,
    master,
    moment_one,
    moment_two,
    average,
):
    plan = Plan(lax.axis_size("seq"))
    s = lax.axis_index("seq")
    t = lax.axis_index("tp")
    rows = F_DEV * TOK_FRAME
    flat = lambda x: x.reshape(-1, LANES)

    effective = noise_level * (1 - context_mask)
    one_hot = (
        effective[:, None] == jnp.arange(level_table.shape[0], dtype=jnp.int32)[None, :]
    ).astype(BF16)
    condition = jax.nn.silu(mm(one_hot, level_table)).astype(BF16)
    cond_units = condition.reshape(plan.frames, plan.nm, plan.um).transpose(1, 0, 2)

    wq, wb, mod_blocks, wo = gather_weights(plan, flat(master), cond_units, 0)
    modulation = (
        mod_blocks.reshape(TP, F_DEV, MT).transpose(1, 0, 2).reshape(F_DEV, TP * MT)
    )
    mod_rows = modulation.reshape(F_DEV * 6, D)
    shift_one, scale_one = modulation[:, :D], modulation[:, D : 2 * D]

    inputs = tokens.astype(F32)
    normed_one, inverse_one = normalize(inputs)
    first_in = frame_affine(normed_one, scale_one, shift_one).astype(BF16)
    projected = mm(first_in, wq).astype(BF16)
    kv = jnp.stack(
        [
            jnp.concatenate(
                [
                    projected[:, HD + h * HEAD : HD + (h + 1) * HEAD],
                    projected[:, 2 * HD + h * HEAD : 2 * HD + (h + 1) * HEAD],
                ],
                axis=1,
            )
            for h in range(ZN)
        ]
    )
    q_mine, kv_all = exchange_qkv(plan, pack_heads(projected[:, :HD]), kv, 1)
    meta = jnp.concatenate([frame_clip, lax.rem(s, plan.r)[None]]).astype(jnp.int32)
    o_mine, o_rows, lse = attend(plan, meta, q_mine, kv_all)
    result, grads_b, do_mine, middle_grad, mod_four = middle_part(
        plan, o_mine, wo.reshape(HEADS * HEAD, D), wb, tokens, grad_out, mod_rows, 2
    )
    dq_mine, dkv_all = attend_back(plan, meta, q_mine, kv_all, do_mine, o_rows, lse)
    input_grad, own_q, own_b, mod_all = tail_part(
        plan, dq_mine, dkv_all, first_in, wq, tokens, middle_grad, mod_rows, mod_four, grads_b, 3
    )
    updated = adam(
        plan,
        s[None].astype(jnp.int32),
        own_q,
        own_b,
        cond_units.transpose(0, 2, 1),
        flat(mod_all),
        flat(master),
        flat(moment_one),
        flat(moment_two),
        flat(average),
    )
    new_master, new_one, new_two, new_average = [x.reshape(master.shape) for x in updated]
    return (result, input_grad, new_master, new_one, new_two, new_average)


def solution(mesh):
    token_spec = P("seq", None)
    weight_spec = P("tp", "seq")
    in_specs = (token_spec, token_spec, P(), P(), P(), P()) + (weight_spec,) * 4
    out_specs = (token_spec, token_spec) + (weight_spec,) * 4
    return jax.shard_map(local, mesh=mesh, in_specs=in_specs, out_specs=out_specs, check_vma=False)
```

```python
import functools

import jax
import jax.numpy as jnp
from jax import lax
from jax.experimental import pallas as pl
from jax.experimental.pallas import tpu as pltpu
from jax.sharding import PartitionSpec as P

D = 1024
HEADS = 16
HEAD = 64
FF = 4096
TOK_FRAME = 384
STEP = 7
TP = 4
ZN = 4
HD = HEADS * HEAD // TP
QKV = 3 * HD
FT = FF // TP
MT = 6 * D // TP
F_DEV = 2
BROWS = HD + 2 * FT
LANES = 128
MCOLS = MT // LANES
PACK = TOK_FRAME // 2
TILE = 256
TILES = D // TILE

NORM_EPSILON = 1e-06
RATE_FACTOR = 2.5
BETA_FIRST = 0.5
BETA_SECOND = 0.5
ADAM_EPSILON = 1e-08
WEIGHT_DECAY = 0.01
AVERAGE_RATE = 0.9
GELU_A = 0.7978845608028654
GELU_B = 0.044715
MESH = pl.DeviceIdType.MESH
VM = pl.BlockSpec(memory_space=pltpu.VMEM)
SM = pl.BlockSpec(memory_space=pltpu.SMEM)
DMA = pltpu.SemaphoreType.DMA
F32 = jnp.float32
BF16 = jnp.bfloat16
VMEM_LIMIT = 56 * 2**20


def mm(left, right):
    return jnp.dot(left, right, preferred_element_type=F32)


def mm_tn(left, right):
    return lax.dot_general(left, right, (((0,), (0,)), ((), ())), preferred_element_type=F32)


def mm_nt(left, right):
    return lax.dot_general(left, right, (((1,), (1,)), ((), ())), preferred_element_type=F32)


def normalize(rows):
    centred = rows - jnp.mean(rows, axis=1, keepdims=True)
    inverse = lax.rsqrt(jnp.mean(centred * centred, axis=1, keepdims=True) + NORM_EPSILON)
    return (centred * inverse, inverse)


def norm_back(grads, normed, inverse):
    return inverse * (
        grads
        - jnp.mean(grads, axis=1, keepdims=True)
        - normed * jnp.mean(grads * normed, axis=1, keepdims=True)
    )


def loop(count, step, body):
    def turn(i, carry):
        body(pl.multiple_of(i * step, step))
        return carry

    lax.fori_loop(0, count // step, turn, 0)


def add_to(ref, row, values):
    ref[pl.ds(row, 1), :] += jnp.sum(values, axis=0, keepdims=True)


class Plan:
    def __init__(self, seq_count):
        self.n = seq_count
        self.r = seq_count // ZN
        self.shard = (D * QKV + BROWS * D + D * MT) // seq_count
        self.unit = self.shard // 3
        self.uq = self.unit // QKV
        self.ub = self.unit // D
        self.um = self.unit // MT
        self.nq = D // self.uq
        self.nb = self.nq + BROWS // self.ub
        self.nm = D // self.um
        self.first_mod = self.nb // 3
        self.flat_rows = self.unit // LANES
        self.frames = seq_count * F_DEV


def place(plan):
    s = lax.axis_index("seq")
    t = lax.axis_index("tp")
    return s, t, lax.div(s, plan.r), lax.rem(s, plan.r)


def remote(src, dst, send_sem, recv_sem, s, t):
    return pltpu.make_async_remote_copy(
        src_ref=src,
        dst_ref=dst,
        send_sem=send_sem,
        recv_sem=recv_sem,
        device_id=(s, t),
        device_id_type=MESH,
    )


def greet(peers):
    barrier = pltpu.get_barrier_semaphore()
    for s, t in peers:
        pl.semaphore_signal(barrier, inc=1, device_id=(s, t), device_id_type=MESH)
    pl.semaphore_wait(barrier, len(peers))


def by_kind(plan, k, act, low=0, high=None):
    high = plan.nb if high is None else high
    q_high, b_low = min(plan.nq, high), max(plan.nq, low)
    if low < q_high:
        @pl.when((k >= low) & (k < q_high))
        def _():
            act("q")

    if b_low < high:
        @pl.when((k >= b_low) & (k < high))
        def _():
            act("b")


def unit_of(plan, k, kind, wq, wb):
    if kind == "q":
        return wq.at[pl.ds(pl.multiple_of(k * plan.uq, plan.uq), plan.uq)]
    return wb.at[pl.ds(pl.multiple_of((k - plan.nq) * plan.ub, plan.ub), plan.ub)]


def call(kernel, outs, scratch, ins, cid=None, cost=None, name=None):
    params = dict(vmem_limit_bytes=VMEM_LIMIT)
    if cid is not None:
        params.update(collective_id=cid, has_side_effects=True)
    return pl.pallas_call(
        kernel,
        out_shape=outs,
        in_specs=ins,
        out_specs=jax.tree.map(lambda _: VM, outs),
        scratch_shapes=scratch,
        compiler_params=pltpu.CompilerParams(**params),
        cost_estimate=cost,
        name=name,
    )


class Travel:
    def __init__(self, plan, wb, send_sem, recv_sem, low, high):
        self.plan, self.wb, self.low, self.high = plan, wb, low, high
        self.send_sem, self.recv_sem = send_sem, recv_sem
        self.s, self.t, self.z, self.r = place(plan)

    def move(self, k, lu, sem, owner_r, to_s):
        ref = unit_of(self.plan, k, "b", None, self.wb)
        return remote(ref, ref, self.send_sem.at[lu, sem], self.recv_sem.at[lu, owner_r], to_s, self.t)

    def spread(self, k, lu, act, up=None, down=None, sides=True):
        plan, rn = self.plan, self.plan.r

        def go(kind):
            if up is not None:
                @pl.when(up)
                def _():
                    act(self.move(k, lu, 0, self.r, self.s + rn))
            if down is not None:
                @pl.when(down)
                def _():
                    act(self.move(k, lu, 1, self.r, self.s - rn))
            if sides:
                for d in range(1, rn):
                    act(self.move(k, lu, 1 + d, self.r, self.z * rn + lax.rem(self.r + d, rn)))

        by_kind(plan, k, go, self.low, self.high)

    def own(self, act, up=True, down=True, sides=True):
        for i in range(3):
            self.spread(
                3 * self.s + i,
                3 * self.z + i,
                act,
                (self.z < ZN - 1) if up else None,
                (self.z > 0) if down else None,
                sides,
            )

    def line(self, d, act, wait=True):
        for i in range(3):
            for side in (0, 1):
                zs = self.z - d if side == 0 else self.z + d
                k = 3 * (zs * self.plan.r + self.r) + i
                lu = 3 * zs + i

                @pl.when((zs >= 0) & (zs < ZN))
                def _():
                    if wait:
                        by_kind(
                            self.plan, k,
                            lambda kind: self.move(k, lu, 0, self.r, self.s).wait_recv(),
                            self.low, self.high,
                        )
                    if side == 0:
                        self.spread(k, lu, act, self.z < ZN - 1, None)
                    else:
                        self.spread(k, lu, act, None, self.z > 0)

    def from_sides(self):
        rn = self.plan.r
        for d in range(1, rn):
            other = lax.rem(self.r + d, rn)
            for zs in range(ZN):
                for i in range(3):
                    k = 3 * (zs * rn + other) + i
                    by_kind(
                        self.plan, k,
                        lambda kind: self.move(k, 3 * zs + i, 0, other, self.s).wait_recv(),
                        self.low, self.high,
                    )

    def close(self):
        done = lambda copy: copy.wait_send()
        self.own(done)
        for d in range(1, ZN):
            self.line(d, done, wait=False)


def head_kernel(
    plan, master, cond, tokens,
    wq, wb, mods, first_in, q_out, kv_out,
    tile, macc, mpart, mrecv, mod, norm, q_send, kv_send,
    qp_s, qc_s, q_r, b_s, b_r, m_s, m_r, t_s, t_r, as_, ar, ks, kr, xs, xr,
):
    s, t, z, r = place(plan)
    n, rn = plan.n, plan.r
    greet(
        [(lax.rem(s + d, n), t) for d in range(1, n)]
        + [(s, lax.rem(t + d, TP)) for d in range(1, TP)]
    )
    start = lambda copy: copy.start()
    done = lambda copy: copy.wait_send()
    half = plan.uq // 2

    def q_rows(k, h):
        return wq.at[pl.ds(pl.multiple_of(k * plan.uq + h * half, half), half)]

    def q_copy(k, h, sem, to_s):
        ref = q_rows(k, h)
        return remote(ref, ref, sem, q_r.at[2 * k + h], to_s, t)

    def q_arrived(k, h):
        q_copy(k, h, qc_s.at[0, 0], s).wait_recv()

    def column(j):
        return r + rn * lax.rem(j + r, 2)

    def q_own(act):
        for i in range(3):
            k = 3 * s + i

            @pl.when(k < plan.nq)
            def _():
                for h in range(2):
                    for d in range(1, rn):
                        act(q_copy(k, h, qp_s.at[2 * i + h, d - 1], lax.rem(r + d, rn)))

    def q_line(act, wait):
        for j in range(2):
            k = column(j)
            for h in range(2):
                if wait:
                    @pl.when((z > 0) | (lax.div(k, 3) != r))
                    def _():
                        q_arrived(k, h)

                @pl.when(z < ZN - 1)
                def _():
                    act(q_copy(k, h, qc_s.at[2 * j + h, 0], s + rn))

                @pl.when(z > 0)
                def _():
                    for d in range(1, rn):
                        act(
                            q_copy(
                                k, h, qc_s.at[2 * j + h, d], z * rn + lax.rem(r + d, rn)
                            )
                        )

    travel = Travel(plan, wb, b_s, b_r, plan.nq, plan.nb)

    for i in range(3):
        k = 3 * s + i
        base = i * plan.flat_rows

        def fill(kind):
            if kind == "q":
                rows, ref, at, cols = plan.uq, wq, k * plan.uq, QKV // LANES
            else:
                rows, ref, at, cols = plan.ub, wb, (k - plan.nq) * plan.ub, D // LANES
            at = pl.multiple_of(at, rows)
            for j in range(cols):
                ref[pl.ds(at, rows), j * LANES : (j + 1) * LANES] = master[
                    pl.ds(base + j, rows, stride=cols), :
                ].astype(BF16)

        by_kind(plan, k, fill)

        @pl.when(k < plan.nq)
        def _():
            for h in range(2):
                for d in range(1, rn):
                    q_copy(k, h, qp_s.at[2 * i + h, d - 1], lax.rem(r + d, rn)).start()

    @pl.when(z == 0)
    def _():
        q_line(start, True)

    travel.own(start, up=False, sides=False)

    macc[...] = jnp.zeros_like(macc)
    for i in range(3):
        k = 3 * s + i
        base = i * plan.flat_rows

        @pl.when(k >= plan.nb)
        def _():
            for j in range(MCOLS):
                tile[:, j * LANES : (j + 1) * LANES] = master[
                    pl.ds(base + j, plan.um, stride=MCOLS), :
                ].astype(BF16)
            macc[...] += mm(cond[k - plan.nb], tile[...])

    fm = plan.first_mod

    def m_copy(d):
        to = lax.rem(s + d, n)
        return remote(mpart.at[to], mrecv.at[s - fm], m_s.at[d - 1], m_r.at[s - fm], to, t)

    @pl.when(s >= fm)
    def _():
        for f in range(plan.frames):
            for j in range(MCOLS):
                mpart[f // F_DEV, pl.ds((f % F_DEV) * MCOLS + j, 1), :] = macc[
                    pl.ds(f, 1), j * LANES : (j + 1) * LANES
                ]
        mrecv[s - fm] = mpart[s]
        for d in range(1, n):
            m_copy(d).start()

    def norm_rows(at):
        rows = pl.ds(at, 64)
        norm[rows, :] = normalize(tokens[rows, :].astype(F32))[0]

    loop(F_DEV * TOK_FRAME, 64, norm_rows)

    @pl.when(z > 0)
    def _():
        q_line(start, True)

    travel.own(start, down=False)

    for src in range(fm, n):
        @pl.when(s != src)
        def _():
            remote(mpart.at[0], mrecv.at[src - fm], m_s.at[0], m_r.at[src - fm], s, t).wait_recv()

    total = mrecv[0]
    for src in range(1, n - fm):
        total = total + mrecv[src]
    mod[t] = total

    def t_copy(d):
        return remote(mod.at[t], mod.at[t], t_s.at[d - 1], t_r.at[t], s, lax.rem(t + d, TP))

    for d in range(1, TP):
        t_copy(d).start()
    for d in range(1, TP):
        other = lax.rem(t + d, TP)
        remote(mod.at[t], mod.at[other], t_s.at[0], t_r.at[other], s, t).wait_recv()
    for f in range(F_DEV):
        for block in range(TP * MCOLS):
            part, at = block // (D // LANES), block % (D // LANES)
            mods[f * 6 + part : f * 6 + part + 1, at * LANES : (at + 1) * LANES] = mod[
                block // MCOLS, f * MCOLS + block % MCOLS : f * MCOLS + block % MCOLS + 1, :
            ]

    def affine(f):
        def body(at):
            rows = pl.ds(f * TOK_FRAME + at, 64)
            first_in[rows, :] = (
                norm[rows, :] * (1.0 + mods[f * 6 + 1 : f * 6 + 2, :]) + mods[f * 6 : f * 6 + 1, :]
            ).astype(BF16)

        loop(TOK_FRAME, 64, body)

    for f in range(F_DEV):
        affine(f)

    for k in range(plan.nq):
        for h in range(2):
            if rn > 1:
                at_zero = (z == 0) & (k // 3 != r) & (k % rn != r)

                @pl.when(at_zero | (z > 0) & (k % rn != r))
                def _():
                    q_arrived(k, h)

    keys = mm(first_in[...], wq[:, HD : 2 * HD]).astype(BF16)
    values = mm(first_in[...], wq[:, 2 * HD :]).astype(BF16)
    for h in range(ZN):
        cols = slice(h * HEAD, (h + 1) * HEAD)
        kv_send[h] = jnp.concatenate([keys[:, cols], values[:, cols]], axis=1)

    def kv_copy(d):
        h = lax.rem(z + d, ZN)
        return remote(kv_send.at[h], kv_out.at[s], ks.at[d - 1], kr.at[z], h * rn + r, t)

    def a_copy(d):
        h = lax.rem(z + d, ZN)
        return remote(q_send.at[h], q_out.at[z], as_.at[d - 1], ar.at[z], h * rn + r, t)

    def side_copy(zs, e):
        at = zs * rn + r
        ref = kv_out.at[at]
        return remote(ref, ref, xs.at[zs, e - 1], xr.at[at], z * rn + lax.rem(r + e, rn), t)

    for d in range(1, ZN):
        kv_copy(d).start()
    kv_out[s] = kv_send[z]
    for e in range(1, rn):
        side_copy(z, e).start()
    queries = mm(first_in[...], wq[:, :HD]).astype(BF16)
    for h in range(ZN):
        cols = slice(h * HEAD, (h + 1) * HEAD)
        q_send[h] = jnp.concatenate([queries[:TOK_FRAME, cols], queries[TOK_FRAME:, cols]], axis=1)
    for d in range(1, ZN):
        a_copy(d).start()
    q_out[z] = q_send[z]

    travel.line(1, start)
    for d in range(1, ZN):
        zs = lax.rem(z + d, ZN)
        remote(kv_send.at[0], kv_out.at[zs * rn + r], ks.at[0], kr.at[zs], s, t).wait_recv()
        for e in range(1, rn):
            side_copy(zs, e).start()
    for d in range(2, ZN):
        travel.line(d, start)
    for d in range(1, ZN):
        zs = lax.rem(z + d, ZN)
        remote(q_send.at[0], q_out.at[zs], as_.at[0], ar.at[zs], s, t).wait_recv()
    for e in range(1, rn):
        for zs in range(ZN):
            at = zs * rn + lax.rem(r + e, rn)
            remote(kv_out.at[at], kv_out.at[at], xs.at[0, 0], xr.at[at], s, t).wait_recv()
    travel.from_sides()

    q_own(done)
    q_line(done, False)
    travel.close()

    @pl.when(s >= fm)
    def _():
        for d in range(1, n):
            m_copy(d).wait_send()

    for d in range(1, TP):
        t_copy(d).wait_send()
    for d in range(1, ZN):
        kv_copy(d).wait_send()
        a_copy(d).wait_send()
    for zs in range(ZN):
        for e in range(1, rn):
            side_copy(zs, e).wait_send()


def head_part(plan, master, cond_units, tokens, cid):
    n, rn = plan.n, plan.r
    mrows = F_DEV * MCOLS
    rows = F_DEV * TOK_FRAME
    mods = n - plan.first_mod
    return call(
        functools.partial(head_kernel, plan),
        (
            jax.ShapeDtypeStruct((D, QKV), BF16),
            jax.ShapeDtypeStruct((BROWS, D), BF16),
            jax.ShapeDtypeStruct((F_DEV * 6, D), F32),
            jax.ShapeDtypeStruct((rows, D), BF16),
            jax.ShapeDtypeStruct((ZN, TOK_FRAME, LANES), BF16),
            jax.ShapeDtypeStruct((n, rows, LANES), BF16),
        ),
        [
            pltpu.VMEM((plan.um, MT), BF16),
            pltpu.VMEM((plan.frames, MT), F32),
            pltpu.VMEM((n, mrows, LANES), F32),
            pltpu.VMEM((mods, mrows, LANES), F32),
            pltpu.VMEM((TP, mrows, LANES), F32),
            pltpu.VMEM((rows, D), F32),
            pltpu.VMEM((ZN, TOK_FRAME, LANES), BF16),
            pltpu.VMEM((ZN, rows, LANES), BF16),
            DMA((6, rn - 1)), DMA((4, rn)), DMA((2 * plan.nq,)),
            DMA((3 * ZN, rn + 1)), DMA((3 * ZN, rn)),
            DMA((n - 1,)), DMA((mods,)), DMA((TP - 1,)), DMA((TP,)),
            DMA((ZN - 1,)), DMA((ZN,)), DMA((ZN - 1,)), DMA((ZN,)), DMA((ZN, rn - 1)), DMA((n,)),
        ],
        [VM] * 3,
        cid,
        name="head_part",
    )(master, cond_units, tokens)


def padded(rows, low):
    zero = jnp.zeros_like(rows)
    return jnp.concatenate([rows, zero] if low else [zero, rows], axis=1)


def attend_kernel(plan, meta, q, kv, o, ot, lse, m_ref, l_ref, acc):
    r = meta[plan.frames]
    scale = HEAD ** (-0.5)

    def group(zq, carry):
        for f in range(F_DEV):
            frame = (zq * plan.r + r) * F_DEV + f
            clip = meta[frame]
            pack = q[zq]
            qz = padded(pack[:, f * HEAD : (f + 1) * HEAD], True) * jnp.asarray(scale, BF16)
            m_ref[...] = jnp.full_like(m_ref, -1e30)
            l_ref[...] = jnp.zeros_like(l_ref)
            acc[...] = jnp.zeros_like(acc)

            def block(j, inner):
                @pl.when(meta[j] == clip)
                def _():
                    rows = pl.multiple_of(lax.rem(j, F_DEV) * TOK_FRAME, TOK_FRAME)
                    keys = kv[lax.div(j, F_DEV), pl.ds(rows, TOK_FRAME), :]
                    st = mm_nt(keys, qz)
                    m_old = m_ref[...]
                    m_new = jnp.maximum(m_old, jnp.max(st, axis=0, keepdims=True))
                    p = jnp.exp(st - m_new)
                    alpha = jnp.exp(m_old - m_new)
                    m_ref[...] = m_new
                    l_ref[...] = l_ref[...] * alpha + jnp.sum(p, axis=0, keepdims=True)
                    acc[...] = acc[...] * alpha + mm_tn(keys, p.astype(BF16))

                return inner

            lax.fori_loop(0, frame + 1, block, 0)
            total = l_ref[...]
            out = acc[HEAD:, :] / total
            ot[zq * F_DEV + f] = out
            lse[zq * F_DEV + f] = m_ref[...] + jnp.log(total)
            rows = out.T
            o[zq, f] = jnp.concatenate([rows[:PACK], rows[PACK:]], axis=1).astype(BF16)
        return carry

    lax.fori_loop(0, ZN, group, 0)


def attend(plan, meta, q, kv):
    frames = ZN * F_DEV
    return call(
        functools.partial(attend_kernel, plan),
        (
            jax.ShapeDtypeStruct((ZN, F_DEV, PACK, LANES), BF16),
            jax.ShapeDtypeStruct((frames, HEAD, TOK_FRAME), F32),
            jax.ShapeDtypeStruct((frames, 1, TOK_FRAME), F32),
        ),
        [
            pltpu.VMEM((1, TOK_FRAME), F32),
            pltpu.VMEM((1, TOK_FRAME), F32),
            pltpu.VMEM((LANES, TOK_FRAME), F32),
        ],
        [SM, VM, VM],
        cost=pl.CostEstimate(flops=2 * 10**10, bytes_accessed=6 * 10**7, transcendentals=10**7),
        name="attend",
    )(meta, q, kv)


def attend_back_kernel(plan, meta, q, kv, do, ot, lse, dq, dkv, dkv_acc, dq_acc):
    r = meta[plan.frames]
    scale = HEAD ** (-0.5)
    dkv_acc[...] = jnp.zeros_like(dkv_acc)

    def group(zq, carry):
        parts = []
        for f in range(F_DEV):
            frame = (zq * plan.r + r) * F_DEV + f
            clip = meta[frame]
            columns = slice(f * HEAD, (f + 1) * HEAD)
            qz = padded(q[zq][:, columns], True) * jnp.asarray(scale, BF16)
            grads = jnp.concatenate([do[zq, f][:, :HEAD], do[zq, f][:, HEAD:]], axis=0)
            doz = padded(grads, False)
            delta = jnp.sum(grads.astype(F32).T * ot[zq * F_DEV + f], axis=0, keepdims=True)
            logs = lse[zq * F_DEV + f]
            dq_acc[...] = jnp.zeros_like(dq_acc)

            def block(j, inner):
                @pl.when(meta[j] == clip)
                def _():
                    g = lax.div(j, F_DEV)
                    rows = pl.multiple_of(lax.rem(j, F_DEV) * TOK_FRAME, TOK_FRAME)
                    keys = kv[g, pl.ds(rows, TOK_FRAME), :]
                    pt = jnp.exp(mm_nt(keys, qz) - logs)
                    dst = (pt * (mm_nt(keys, doz) - delta)).astype(BF16)
                    dkv_acc[g, pl.ds(rows, TOK_FRAME), :] += mm(dst, qz) + mm(pt.astype(BF16), doz)
                    dq_acc[...] += mm_tn(keys, dst)

                return inner

            lax.fori_loop(0, frame + 1, block, 0)
            parts.append((dq_acc[:HEAD, :] * scale).T)
        dq[zq] = jnp.concatenate(parts, axis=1).astype(BF16)
        return carry

    lax.fori_loop(0, ZN, group, 0)
    dkv[...] = dkv_acc[...].astype(BF16)


def attend_back(plan, meta, q, kv, do, ot, lse):
    return call(
        functools.partial(attend_back_kernel, plan),
        (
            jax.ShapeDtypeStruct((ZN, TOK_FRAME, LANES), BF16),
            jax.ShapeDtypeStruct((plan.n, F_DEV * TOK_FRAME, LANES), BF16),
        ),
        [
            pltpu.VMEM((plan.n, F_DEV * TOK_FRAME, LANES), F32),
            pltpu.VMEM((LANES, TOK_FRAME), F32),
        ],
        [SM, VM, VM, VM, VM, VM],
        name="attend_back",
    )(meta, q, kv, do, ot, lse)


def middle_kernel(
    plan, o_mine, wo_across, wb, tokens, grad_out, mod,
    result, gb, do_out, dmid, dmod,
    wo, oall, attended, attn, mid, norm, inv, sin, hidden, dmlp, dhid, dup,
    own, csend, crecv, ysend, yrecv, dattn, dsend, dwo, wsend, wrecv,
    o_s, o_r, f_s, f_r, n_s, n_r, c_s, c_r, y_s, y_r, d_s, d_r, w_s, w_r, e_s, e_r, p_s, p_r,
):
    s, t, z, r = place(plan)
    rn = plan.r
    y = lax.div(t, 2)
    c = lax.rem(t, 2)
    sib = 2 * y + 1 - c
    across = lax.rem(t + 2, TP)
    mine = pl.multiple_of(c * TOK_FRAME, TOK_FRAME)
    theirs = pl.multiple_of((1 - c) * TOK_FRAME, TOK_FRAME)
    pairs = [(d, e) for d in range(ZN) for e in range(2)][1:]

    def partner(d, e):
        return lax.rem(z + d, ZN), (c if e == 0 else 1 - c)

    greet(
        [(partner(d, e)[0] * rn + r, 2 * y + partner(d, e)[1]) for d, e in pairs]
        + [(s, across)]
    )

    def o_copy(d, e):
        zd, cd = partner(d, e)
        return remote(
            o_mine.at[zd, cd], oall.at[y * 8 + c * ZN + z], o_s.at[2 * d + e],
            o_r.at[c * ZN + z], zd * rn + r, 2 * y + cd,
        )

    def f_copy(slot):
        ref = oall.at[y * 8 + slot]
        return remote(ref, ref, f_s.at[slot], f_r.at[slot], s, across)

    def p_copy(i, tp):
        ref = wo.at[pl.ds(pl.multiple_of(tp * HD, HD), HD)]
        return remote(ref, ref, p_s.at[i], p_r.at[i], s, sib)

    for d, e in pairs:
        o_copy(d, e).start()
    wo[pl.ds(pl.multiple_of(t * HD, HD), HD), :] = wb[:HD, :]
    p_copy(0, t).start()
    wo[pl.ds(pl.multiple_of(across * HD, HD), HD), :] = wo_across[...]
    p_copy(1, across).start()
    oall[y * 8 + c * ZN + z] = o_mine[z, c]
    f_copy(c * ZN + z).start()

    def d_mlp(f):
        def body(at):
            rows = pl.ds(f * TOK_FRAME + at, 64)
            dmlp[rows, :] = (grad_out[rows, :].astype(F32) * mod[f * 6 + 5 : f * 6 + 6, :]).astype(
                BF16
            )

        loop(TOK_FRAME, 64, body)

    for f in range(F_DEV):
        d_mlp(f)

    def d_hidden(at):
        dhid[:, pl.ds(at, TILE)] = mm_nt(dmlp[...], wb[pl.ds(HD + FT + at, TILE), :])

    loop(FT, TILE, d_hidden)

    for d, e in pairs:
        zd, cd = partner(d, e)
        slot = cd * ZN + zd
        remote(o_mine.at[0, 0], oall.at[y * 8 + slot], o_s.at[0], o_r.at[slot], s, t).wait_recv()
        f_copy(slot).start()
    for slot in range(8):
        remote(
            oall.at[0], oall.at[(1 - y) * 8 + slot], f_s.at[slot], f_r.at[slot], s, t
        ).wait_recv()
    for m in range(HEADS // 2):
        a, b = oall[2 * m], oall[2 * m + 1]
        cols = slice(m * LANES, (m + 1) * LANES)
        attended[:PACK, cols] = jnp.concatenate([a[:, :HEAD], b[:, :HEAD]], axis=1)
        attended[PACK:, cols] = jnp.concatenate([a[:, HEAD:], b[:, HEAD:]], axis=1)

    p_copy(0, sib).wait_recv()
    p_copy(1, lax.rem(sib + 2, TP)).wait_recv()

    def attn_tile(at):
        attn[:, pl.ds(at, TILE)] = mm(attended[...], wo[:, pl.ds(at, TILE)])

    loop(D, TILE, attn_tile)

    row = lambda part: mod[pl.ds(c * 6 + part, 1), :]

    def norm_rows(at):
        rows = pl.ds(at, 64)
        values = tokens[pl.ds(mine + at, 64), :].astype(F32) + row(2) * attn[rows, :]
        mid[rows, :] = values
        normed, inverse = normalize(values)
        norm[rows, :] = normed
        inv[rows, :] = inverse
        sin[pl.ds(mine + at, 64), :] = (normed * (1.0 + row(4)) + row(3)).astype(BF16)

    loop(TOK_FRAME, 64, norm_rows)

    def n_copy(base):
        ref = sin.at[pl.ds(base, TOK_FRAME)]
        return remote(ref, ref, n_s.at[0], n_r.at[0], s, sib)

    n_copy(mine).start()

    def feed(base):
        rows = pl.ds(base, TOK_FRAME)

        def tile(at):
            cols = pl.ds(at, TILE)
            u = mm(sin[rows, :], wb[HD : HD + FT, cols])
            square = u * u
            inner = GELU_A * u * (1.0 + GELU_B * square)
            th = jnp.tanh(inner)
            half = 0.5 * (1.0 + th)
            hidden[rows, cols] = (u * half).astype(BF16)
            slope = half + 0.5 * u * (1.0 - th * th) * (GELU_A * (1.0 + 3.0 * GELU_B * square))
            dup[rows, cols] = (dhid[rows, cols] * slope).astype(BF16)

        loop(FT, TILE, tile)

    feed(mine)
    n_copy(theirs).wait_recv()
    feed(theirs)

    def c_copy(w, n):
        return remote(csend.at[w, n], crecv.at[w, n], c_s.at[w, n], c_r.at[w, n], s, sib)

    def y_copy(w, n):
        return remote(ysend.at[w, n], yrecv.at[w, n], y_s.at[w, n], y_r.at[w, n], s, across)

    def pass_on(w, n):
        c_copy(w, n).wait_recv()
        ysend[w, n] = (own[n] + crecv[w, n].astype(F32)).astype(BF16)
        y_copy(w, n).start()

    def product(w, base, n):
        rows = pl.ds(base, TOK_FRAME)
        if w == 0:
            return mm_nt(dup[rows, :], wb[HD + n * TILE : HD + (n + 1) * TILE, :])
        return mm(hidden[rows, :], wb[HD + FT :, n * TILE : (n + 1) * TILE])

    for w in range(2):
        for n in range(TILES):
            csend[w, n] = product(w, theirs, n).astype(BF16)
            c_copy(w, n).start()
            own[n] = product(w, mine, n)
            if n:
                pass_on(w, n - 1)
        pass_on(w, TILES - 1)

    def down_grad(at):
        gb[pl.ds(HD + FT + at, TILE), :] = mm_tn(hidden[:, pl.ds(at, TILE)], dmlp[...]).astype(BF16)

    def up_grad(at):
        gb[pl.ds(HD + at, TILE), :] = mm_tn(sin[:, pl.ds(at, TILE)], dup[...]).astype(BF16)

    loop(FT, TILE, down_grad)
    loop(D, TILE, up_grad)

    dm = dmod
    dm[...] = jnp.zeros_like(dm)
    for n in range(TILES):
        y_copy(0, n).wait_recv()

    def total(w, rows):
        return jnp.concatenate(
            [ysend[w, n, rows].astype(F32) + yrecv[w, n, rows].astype(F32) for n in range(TILES)],
            axis=1,
        )

    def back_rows(at):
        rows = pl.ds(at, 64)
        tok_rows = pl.ds(mine + at, 64)
        grads = total(0, rows)
        normed = norm[rows, :]
        add_to(dm, 1, grads)
        add_to(dm, 2, grads * normed)
        values = grad_out[tok_rows, :].astype(F32) + norm_back(
            grads * (1.0 + row(4)), normed, inv[rows, :]
        )
        dmid[rows, :] = values
        add_to(dm, 0, attn[rows, :] * values)
        dattn[rows, :] = (row(2) * values).astype(BF16)

    loop(TOK_FRAME, 64, back_rows)
    for ch in range(2):
        part = mm_nt(dattn[...], wo[pl.ds(pl.multiple_of((2 * y + ch) * HD, HD), HD), :]).astype(BF16)
        for zh in range(ZN):
            cols = slice(zh * HEAD, (zh + 1) * HEAD)
            dsend[ch * ZN + zh] = jnp.concatenate([part[:PACK, cols], part[PACK:, cols]], axis=1)

    def d_copy(d, e):
        zd, cd = partner(d, e)
        return remote(
            dsend.at[cd * ZN + zd], do_out.at[z, c], d_s.at[2 * d + e], d_r.at[2 * z + c],
            zd * rn + r, 2 * y + cd,
        )

    for d, e in pairs:
        d_copy(d, e).start()
    do_out[z, c] = dsend[c * ZN + z]

    def o_grad(head_core):
        cols = pl.ds(pl.multiple_of((2 * y + head_core) * HD, HD), HD)
        return mm_tn(attended[:, cols], dattn[...])

    w_copy = remote(wsend, wrecv, w_s, w_r, s, sib)
    wsend[...] = o_grad(1 - c).astype(BF16)
    w_copy.start()
    dwo[...] = o_grad(c)

    for n in range(TILES):
        y_copy(1, n).wait_recv()

    def result_rows(at):
        rows = pl.ds(at, 64)
        tok_rows = pl.ds(mine + at, 64)
        mlp = total(1, rows)
        add_to(dm, 3, mlp * grad_out[tok_rows, :].astype(F32))
        result[tok_rows, :] = (mid[rows, :] + row(5) * mlp).astype(BF16)

    loop(TOK_FRAME, 64, result_rows)

    def e_copy(base):
        ref = result.at[pl.ds(base, TOK_FRAME)]
        return remote(ref, ref, e_s, e_r, s, sib)

    e_copy(mine).start()
    w_copy.wait_recv()
    gb[:HD, :] = (dwo[...] + wrecv[...].astype(F32)).astype(BF16)

    for d, e in pairs:
        zd, cd = partner(d, e)
        remote(
            dsend.at[0], do_out.at[zd, cd], d_s.at[0], d_r.at[2 * zd + cd], s, t
        ).wait_recv()
    e_copy(theirs).wait_recv()
    for d, e in pairs:
        o_copy(d, e).wait_send()
        d_copy(d, e).wait_send()
    for slot in range(8):
        f_copy(slot).wait_send()
    n_copy(mine).wait_send()
    p_copy(0, t).wait_send()
    p_copy(1, across).wait_send()
    for w in range(2):
        for n in range(TILES):
            c_copy(w, n).wait_send()
            y_copy(w, n).wait_send()
    w_copy.wait_send()
    e_copy(mine).wait_send()


def middle_part(plan, o_mine, wo_across, wb, tokens, grad_out, mod_rows, cid):
    rows = F_DEV * TOK_FRAME
    half = lambda dtype: pltpu.VMEM((TOK_FRAME, D), dtype)
    full = lambda dtype: pltpu.VMEM((rows, D), dtype)
    tiles = pltpu.VMEM((2, TILES, TOK_FRAME, TILE), BF16)
    return call(
        functools.partial(middle_kernel, plan),
        (
            jax.ShapeDtypeStruct((rows, D), BF16),
            jax.ShapeDtypeStruct((BROWS, D), BF16),
            jax.ShapeDtypeStruct((ZN, F_DEV, PACK, LANES), BF16),
            jax.ShapeDtypeStruct((TOK_FRAME, D), F32),
            jax.ShapeDtypeStruct((8, D), F32),
        ),
        [
            pltpu.VMEM((HEADS * HEAD, D), BF16),
            pltpu.VMEM((HEADS, PACK, LANES), BF16),
            half(BF16), half(F32), half(F32), half(F32), pltpu.VMEM((TOK_FRAME, 1), F32),
            full(BF16), full(BF16), full(BF16), full(F32), full(BF16),
            pltpu.VMEM((TILES, TOK_FRAME, TILE), F32), tiles, tiles, tiles, tiles,
            half(BF16), pltpu.VMEM((8, PACK, LANES), BF16),
            pltpu.VMEM((HD, D), F32), pltpu.VMEM((HD, D), BF16), pltpu.VMEM((HD, D), BF16),
            DMA((8,)), DMA((8,)), DMA((8,)), DMA((8,)), DMA((1,)), DMA((1,)),
            DMA((2, TILES)), DMA((2, TILES)), DMA((2, TILES)), DMA((2, TILES)),
            DMA((8,)), DMA((8,)), DMA, DMA, DMA, DMA, DMA((2,)), DMA((2,)),
        ],
        [VM] * 6,
        cid,
        name="middle_part",
    )(o_mine, wo_across, wb, tokens, grad_out, mod_rows)


def tail_kernel(
    plan, dq, dkv, first_in, wq, tokens, dmid, mod, dm4, gb,
    igrad, oq, ob, dall,
    stage, side, q_in, kv_in, dqkv, gq, own, csend, crecv, ysend, yrecv, dm, dm3, dboth,
    rq, rb, cq, cb,
    q_s, q_r, k_s, k_r, x_s, x_r, c_s, c_r, y_s, y_r, e_s, e_r, h_s, h_r, m_s, m_r, r_s, r_r, t_s, t_r,
):
    s, t, z, r = place(plan)
    n, rn = plan.n, plan.r
    y = lax.div(t, 2)
    c = lax.rem(t, 2)
    sib = 2 * y + 1 - c
    across = lax.rem(t + 2, TP)
    mine = pl.multiple_of(c * TOK_FRAME, TOK_FRAME)
    theirs = pl.multiple_of((1 - c) * TOK_FRAME, TOK_FRAME)
    greet([(lax.rem(s + d, n), t) for d in range(1, n)] + [(s, sib), (s, across)])

    def side_copy(d, e):
        zs = lax.rem(z + d, ZN)
        other = lax.rem(r + e, rn)
        return remote(
            dkv.at[zs * rn + other], side.at[e - 1, d], x_s.at[d, e - 1], x_r.at[d, e - 1],
            z * rn + other, t,
        )

    def q_copy(d):
        to = lax.rem(z + d, ZN)
        return remote(dq.at[to], q_in.at[z], q_s.at[d - 1], q_r.at[z], to * rn + r, t)

    def kv_copy(d):
        to = lax.rem(z + d, ZN)
        return remote(stage.at[d], kv_in.at[z], k_s.at[d - 1], k_r.at[z], to * rn + r, t)

    order = list(range(1, ZN)) + [0]
    for d in order:
        for e in range(1, rn):
            side_copy(d, e).start()
    for d in range(1, ZN):
        q_copy(d).start()
    q_in[z] = dq[z]
    for d in order:
        zs = lax.rem(z + d, ZN)
        total = dkv[zs * rn + r].astype(F32)
        for e in range(1, rn):
            side_copy(d, e).wait_recv()
            total = total + side[e - 1, d].astype(F32)
        if d == 0:
            kv_in[z] = total.astype(BF16)
        else:
            stage[d] = total.astype(BF16)
            kv_copy(d).start()

    def owner(j):
        a = 2 - lax.div(z, 2)
        b = 2 * lax.div(ZN - 1 - z, ZN - 1)
        return lax.rem(a * j + b, 3)

    def grad_copy(zo, i, d, kind):
        other = lax.rem(r + d, rn)
        k = 3 * (zo * rn + other) + i
        lu = 3 * zo + i
        buf = rq if kind == "q" else rb
        return remote(
            unit_of(plan, k, kind, gq, gb), buf.at[d - 1, lu], r_s.at[lu, d - 1],
            r_r.at[lu, d - 1], z * rn + other, t,
        )

    def grad_sides(owners, low, high, act):
        for zo in owners:
            for i in range(3):
                for d in range(1, rn):
                    k = 3 * (zo * rn + lax.rem(r + d, rn)) + i
                    by_kind(plan, k, lambda kind: act(grad_copy(zo, i, d, kind)), low, high)

    def chain_copy(lu, kind, below, to):
        src = (rq if kind == "q" else rb).at[0, lu]
        dst = cq.at[lu] if kind == "q" else cb.at[below, lu]
        return remote(src, dst, t_s.at[lu], t_r.at[lu, below], to, t)

    def grad_chain(owners, low, high):
        for zo in owners:
            for i in range(3):
                k = 3 * (zo * rn + r) + i
                lu = 3 * zo + i

                def step(kind):
                    part = rq if kind == "q" else rb
                    out = oq if kind == "q" else ob
                    unit = unit_of(plan, k, kind, gq, gb)
                    rows = plan.uq if kind == "q" else plan.ub
                    for d in range(1, rn):
                        remote(
                            unit, part.at[d - 1, lu], r_s.at[lu, d - 1], r_r.at[lu, d - 1], s, t
                        ).wait_recv()
                    above = (zo <= z) & (z < ZN - 1)
                    below = (zo >= z) & (z > 0)

                    @pl.when(above)
                    def _():
                        chain_copy(lu, kind, 0, s).wait_recv()

                    if kind == "b":
                        @pl.when(below)
                        def _():
                            chain_copy(lu, kind, 1, s).wait_recv()

                    def here(at):
                        total = unit[pl.ds(at, 16), :].astype(F32)
                        for d in range(1, rn):
                            total = total + part[d - 1, lu, pl.ds(at, 16), :].astype(F32)
                        return total

                    def from_chain(at, below):
                        ref = cq.at[lu] if kind == "q" else cb.at[below, lu]
                        return ref[pl.ds(at, 16), :].astype(F32)

                    @pl.when(zo != z)
                    def _():
                        @pl.when((zo < z) & (z == ZN - 1) | (zo > z) & (z == 0))
                        def _():
                            def body(at):
                                part[0, lu, pl.ds(at, 16), :] = here(at).astype(BF16)

                            loop(rows, 16, body)

                        @pl.when((zo < z) & (z < ZN - 1))
                        def _():
                            def body(at):
                                part[0, lu, pl.ds(at, 16), :] = (here(at) + from_chain(at, 0)).astype(BF16)

                            loop(rows, 16, body)

                        if kind == "b":
                            @pl.when((zo > z) & (z > 0))
                            def _():
                                def body(at):
                                    part[0, lu, pl.ds(at, 16), :] = (here(at) + from_chain(at, 1)).astype(BF16)

                                loop(rows, 16, body)

                    @pl.when(zo < z)
                    def _():
                        chain_copy(lu, kind, 0, s - rn).start()

                    if kind == "b":
                        @pl.when(zo > z)
                        def _():
                            chain_copy(lu, kind, 1, s + rn).start()

                    @pl.when((zo == z) & (z == 0))
                    def _():
                        def body(at):
                            out[i, pl.ds(at, 16), :] = here(at) + from_chain(at, 0)

                        loop(rows, 16, body)

                    if kind == "b":
                        @pl.when((zo == z) & (z > 0))
                        def _():
                            def body(at):
                                out[i, pl.ds(at, 16), :] = here(at) + from_chain(at, 0) + from_chain(at, 1)

                            loop(rows, 16, body)

                by_kind(plan, k, step, low, high)

    def grad_close(owners, low, high):
        grad_sides(owners, low, high, lambda copy: copy.wait_send())
        for zo in owners:
            for i in range(3):
                def close(kind):
                    @pl.when(zo != z)
                    def _():
                        chain_copy(3 * zo + i, kind, 0, s).wait_send()

                by_kind(plan, 3 * (zo * rn + r) + i, close, low, high)

    every = [owner(j) for j in range(3)]
    start = lambda copy: copy.start()
    grad_sides(every, plan.nq, plan.nb, start)

    for d in range(1, ZN):
        zs = lax.rem(z + d, ZN)
        remote(dq.at[0], q_in.at[zs], q_s.at[0], q_r.at[zs], s, t).wait_recv()
        remote(stage.at[d], kv_in.at[zs], k_s.at[0], k_r.at[zs], s, t).wait_recv()
    for p in range(2):
        cols = slice(p * LANES, (p + 1) * LANES)
        a, b = q_in[2 * p], q_in[2 * p + 1]
        dqkv[:TOK_FRAME, cols] = jnp.concatenate([a[:, :HEAD], b[:, :HEAD]], axis=1)
        dqkv[TOK_FRAME:, cols] = jnp.concatenate([a[:, HEAD:], b[:, HEAD:]], axis=1)
        a, b = kv_in[2 * p], kv_in[2 * p + 1]
        dqkv[:, HD + p * LANES : HD + (p + 1) * LANES] = jnp.concatenate(
            [a[:, :HEAD], b[:, :HEAD]], axis=1
        )
        dqkv[:, 2 * HD + p * LANES : 2 * HD + (p + 1) * LANES] = jnp.concatenate(
            [a[:, HEAD:], b[:, HEAD:]], axis=1
        )

    def q_grad(at):
        gq[pl.ds(at, TILE), :] = mm_tn(first_in[:, pl.ds(at, TILE)], dqkv[...]).astype(BF16)

    loop(D, TILE, q_grad)
    grad_sides([0], 0, plan.nq, start)

    def c_copy(w):
        return remote(csend.at[w], crecv.at[w], c_s.at[w], c_r.at[w], s, sib)

    def y_copy(w):
        return remote(ysend.at[w], yrecv.at[w], y_s.at[w], y_r.at[w], s, across)

    def pass_on(w):
        c_copy(w).wait_recv()
        ysend[w] = (own[w] + crecv[w].astype(F32)).astype(BF16)
        y_copy(w).start()

    for w in range(TILES):
        weights = wq[w * TILE : (w + 1) * TILE, :]
        csend[w] = mm_nt(dqkv[pl.ds(theirs, TOK_FRAME), :], weights).astype(BF16)
        c_copy(w).start()
        own[w] = mm_nt(dqkv[pl.ds(mine, TOK_FRAME), :], weights)
        if w:
            pass_on(w - 1)
    pass_on(TILES - 1)

    grad_chain(every, plan.nq, plan.nb)

    for w in range(TILES):
        y_copy(w).wait_recv()
    row = lambda part: mod[pl.ds(c * 6 + part, 1), :]
    dm[...] = jnp.zeros_like(dm)

    def input_rows(at):
        rows = pl.ds(at, 64)
        tok_rows = pl.ds(mine + at, 64)
        grads = jnp.concatenate(
            [ysend[w, rows].astype(F32) + yrecv[w, rows].astype(F32) for w in range(TILES)], axis=1
        )
        normed, inverse = normalize(tokens[tok_rows, :].astype(F32))
        add_to(dm, 0, grads)
        add_to(dm, 1, grads * normed)
        igrad[tok_rows, :] = dmid[rows, :] + norm_back(grads * (1.0 + row(1)), normed, inverse)

    loop(TOK_FRAME, 64, input_rows)

    def e_copy(base):
        ref = igrad.at[pl.ds(base, TOK_FRAME)]
        return remote(ref, ref, e_s, e_r, s, sib)

    e_copy(mine).start()

    for block in range(6 * D // LANES):
        part, at = block // (D // LANES), block % (D // LANES)
        src = dm if part < 2 else dm4
        lane = slice(at * LANES, (at + 1) * LANES)
        from_row = part if part < 2 else part - 2
        dm3[block // MCOLS, block % MCOLS : block % MCOLS + 1, :] = src[from_row : from_row + 1, lane]
    h_copy = lambda frame: remote(dm3.at[sib], dboth.at[frame], h_s, h_r, s, sib)
    h_copy(c).start()
    dboth[c] = dm3[t]
    h_copy(1 - c).wait_recv()

    def m_copy(src):
        return remote(dboth, dall.at[s], m_s.at[src - plan.first_mod], m_r.at[s], src, t)

    for src in range(plan.first_mod, n):
        @pl.when(s == src)
        def _():
            dall[s] = dboth[...]

        @pl.when(s != src)
        def _():
            m_copy(src).start()

    grad_chain([0], 0, plan.nq)

    @pl.when(s >= plan.first_mod)
    def _():
        for d in range(1, n):
            other = lax.rem(s + d, n)
            remote(dboth, dall.at[other], m_s.at[0], m_r.at[other], s, t).wait_recv()

    e_copy(theirs).wait_recv()
    for d in range(1, ZN):
        q_copy(d).wait_send()
        kv_copy(d).wait_send()
    for d in order:
        for e in range(1, rn):
            side_copy(d, e).wait_send()
    grad_close(every, plan.nq, plan.nb)
    grad_close([0], 0, plan.nq)
    for w in range(TILES):
        c_copy(w).wait_send()
        y_copy(w).wait_send()
    e_copy(mine).wait_send()
    h_copy(c).wait_send()
    for src in range(plan.first_mod, n):
        @pl.when(s != src)
        def _():
            m_copy(src).wait_send()


def tail_part(plan, dq, dkv, first_in, wq, tokens, dmid, mod_rows, dm4, gb, cid):
    n, rn = plan.n, plan.r
    rows = F_DEV * TOK_FRAME
    tiles = pltpu.VMEM((TILES, TOK_FRAME, TILE), BF16)
    mods = n - plan.first_mod
    return call(
        functools.partial(tail_kernel, plan),
        (
            jax.ShapeDtypeStruct((rows, D), F32),
            jax.ShapeDtypeStruct((3, plan.uq, QKV), F32),
            jax.ShapeDtypeStruct((3, plan.ub, D), F32),
            jax.ShapeDtypeStruct((n, F_DEV, 16, LANES), F32),
        ),
        [
            pltpu.VMEM((ZN, rows, LANES), BF16),
            pltpu.VMEM((rn - 1, ZN, rows, LANES), BF16),
            pltpu.VMEM((ZN, TOK_FRAME, LANES), BF16),
            pltpu.VMEM((ZN, rows, LANES), BF16),
            pltpu.VMEM((rows, QKV), BF16),
            pltpu.VMEM((D, QKV), BF16),
            pltpu.VMEM((TILES, TOK_FRAME, TILE), F32), tiles, tiles, tiles, tiles,
            pltpu.VMEM((8, D), F32),
            pltpu.VMEM((TP, 16, LANES), F32),
            pltpu.VMEM((F_DEV, 16, LANES), F32),
            pltpu.VMEM((rn - 1, 3, plan.uq, QKV), BF16),
            pltpu.VMEM((rn - 1, 9, plan.ub, D), BF16),
            pltpu.VMEM((3, plan.uq, QKV), BF16),
            pltpu.VMEM((2, 9, plan.ub, D), BF16),
            DMA((ZN - 1,)), DMA((ZN,)), DMA((ZN - 1,)), DMA((ZN,)), DMA((ZN, rn - 1)), DMA((ZN, rn - 1)),
            DMA((TILES,)), DMA((TILES,)), DMA((TILES,)), DMA((TILES,)),
            DMA, DMA, DMA, DMA, DMA((mods,)), DMA((n,)),
            DMA((9, rn - 1)), DMA((9, rn - 1)), DMA((9,)), DMA((9, 2)),
        ],
        [VM] * 9,
        cid,
        name="tail_part",
    )(dq, dkv, first_in, wq, tokens, dmid, mod_rows, dm4, gb)


def adam_kernel(plan, meta, oq, ob, cond, dmod, master, one, two, average, n_master, n_one, n_two, n_average):
    s = meta[0]
    rate = RATE_FACTOR * D ** (-0.5)
    scale_one = 1.0 / (1.0 - BETA_FIRST**STEP)
    scale_two = 1.0 / (1.0 - BETA_SECOND**STEP)

    def update(rows, grad):
        first = BETA_FIRST * one[rows, :] + (1.0 - BETA_FIRST) * grad
        second = BETA_SECOND * two[rows, :] + (1.0 - BETA_SECOND) * grad * grad
        weight = master[rows, :]
        weight = weight - rate * (
            (first * scale_one) / (jnp.sqrt(second * scale_two) + ADAM_EPSILON)
            + WEIGHT_DECAY * weight
        )
        n_one[rows, :] = first
        n_two[rows, :] = second
        n_master[rows, :] = weight
        n_average[rows, :] = AVERAGE_RATE * average[rows, :] + (1.0 - AVERAGE_RATE) * weight

    for i in range(3):
        k = 3 * s + i
        base = i * plan.flat_rows

        def from_matrix(kind):
            src = oq if kind == "q" else ob
            rows = plan.uq if kind == "q" else plan.ub
            cols = (QKV if kind == "q" else D) // LANES
            for j in range(cols):
                update(
                    pl.ds(base + j, rows, stride=cols), src[i, :, j * LANES : (j + 1) * LANES]
                )

        by_kind(plan, k, from_matrix)

        @pl.when(k >= plan.nb)
        def _():
            at = cond[k - plan.nb]
            for j in range(MCOLS):
                update(
                    pl.ds(base + j, plan.um, stride=MCOLS),
                    mm(at, dmod[pl.ds(j, plan.frames, stride=16), :].astype(BF16)),
                )


def adam(plan, meta, oq, ob, cond_rows, dmod, master, one, two, average):
    shape = jax.ShapeDtypeStruct(master.shape, F32)
    return call(
        functools.partial(adam_kernel, plan),
        (shape,) * 4,
        [],
        [SM] + [VM] * 8,
        name="adam",
    )(meta, oq, ob, cond_rows, dmod, master, one, two, average)


def local(
    tokens,
    grad_out,
    noise_level,
    context_mask,
    frame_clip,
    level_table,
    master,
    moment_one,
    moment_two,
    average,
):
    plan = Plan(lax.axis_size("seq"))
    s = lax.axis_index("seq")
    t = lax.axis_index("tp")
    flat = lambda x: x.reshape(-1, LANES)

    effective = noise_level * (1 - context_mask)
    one_hot = (
        effective[:, None] == jnp.arange(level_table.shape[0], dtype=jnp.int32)[None, :]
    ).astype(BF16)
    condition = jax.nn.silu(mm(one_hot, level_table)).astype(BF16)
    cond_units = condition.reshape(plan.frames, plan.nm, plan.um).transpose(1, 0, 2)

    wq, wb, mod_rows, first_in, q_mine, kv_all = head_part(
        plan, flat(master), cond_units, tokens, 0
    )
    wo_across = lax.ppermute(wb[:HD], "tp", [(i, (i + 2) % TP) for i in range(TP)])
    meta = jnp.concatenate([frame_clip, lax.rem(s, plan.r)[None]]).astype(jnp.int32)
    o_mine, o_rows, lse = attend(plan, meta, q_mine, kv_all)
    result, grads_b, do_mine, middle_grad, mod_four = middle_part(
        plan, o_mine, wo_across, wb, tokens, grad_out, mod_rows, 2
    )
    dq_mine, dkv_all = attend_back(plan, meta, q_mine, kv_all, do_mine, o_rows, lse)
    input_grad, own_q, own_b, mod_all = tail_part(
        plan, dq_mine, dkv_all, first_in, wq, tokens, middle_grad, mod_rows, mod_four, grads_b, 3
    )
    updated = adam(
        plan,
        s[None].astype(jnp.int32),
        own_q,
        own_b,
        cond_units.transpose(0, 2, 1),
        flat(mod_all),
        flat(master),
        flat(moment_one),
        flat(moment_two),
        flat(average),
    )
    new_master, new_one, new_two, new_average = [x.reshape(master.shape) for x in updated]
    return (result, input_grad, new_master, new_one, new_two, new_average)


def solution(mesh):
    token_spec = P("seq", None)
    weight_spec = P("tp", "seq")
    in_specs = (token_spec, token_spec, P(), P(), P(), P()) + (weight_spec,) * 4
    out_specs = (token_spec, token_spec) + (weight_spec,) * 4
    return jax.shard_map(local, mesh=mesh, in_specs=in_specs, out_specs=out_specs, check_vma=False)
```

```python
import functools

import jax
import jax.numpy as jnp
from jax import lax
from jax.experimental import pallas as pl
from jax.experimental.pallas import tpu as pltpu
from jax.sharding import PartitionSpec as P

D = 1024
HEADS = 16
HEAD = 64
FF = 4096
TOK_FRAME = 384
STEP = 7
TP = 4
ZN = 4
HD = HEADS * HEAD // TP
QKV = 3 * HD
FT = FF // TP
MT = 6 * D // TP
F_DEV = 2
BROWS = HD + 2 * FT
LANES = 128
MCOLS = MT // LANES
PACK = TOK_FRAME // 2
TILE = 256
TILES = D // TILE

NORM_EPSILON = 1e-06
RATE_FACTOR = 2.5
BETA_FIRST = 0.5
BETA_SECOND = 0.5
ADAM_EPSILON = 1e-08
WEIGHT_DECAY = 0.01
AVERAGE_RATE = 0.9
GELU_A = 0.7978845608028654
GELU_B = 0.044715
MESH = pl.DeviceIdType.MESH
VM = pl.BlockSpec(memory_space=pltpu.VMEM)
SM = pl.BlockSpec(memory_space=pltpu.SMEM)
ANY = pl.BlockSpec(memory_space=pl.ANY)
DMA = pltpu.SemaphoreType.DMA
F32 = jnp.float32
BF16 = jnp.bfloat16
VMEM_LIMIT = 56 * 2**20


def mm(left, right):
    return jnp.dot(left, right, preferred_element_type=F32)


def mm_tn(left, right):
    return lax.dot_general(left, right, (((0,), (0,)), ((), ())), preferred_element_type=F32)


def mm_nt(left, right):
    return lax.dot_general(left, right, (((1,), (1,)), ((), ())), preferred_element_type=F32)


def normalize(rows):
    centred = rows - jnp.mean(rows, axis=1, keepdims=True)
    inverse = lax.rsqrt(jnp.mean(centred * centred, axis=1, keepdims=True) + NORM_EPSILON)
    return (centred * inverse, inverse)


def norm_back(grads, normed, inverse):
    return inverse * (
        grads
        - jnp.mean(grads, axis=1, keepdims=True)
        - normed * jnp.mean(grads * normed, axis=1, keepdims=True)
    )


def loop(count, step, body):
    def turn(i, carry):
        body(pl.multiple_of(i * step, step))
        return carry

    lax.fori_loop(0, count // step, turn, 0)


def add_to(ref, row, values):
    ref[pl.ds(row, 1), :] += jnp.sum(values, axis=0, keepdims=True)


class Plan:
    def __init__(self, seq_count):
        self.n = seq_count
        self.r = seq_count // ZN
        self.shard = (D * QKV + BROWS * D + D * MT) // seq_count
        self.unit = self.shard // 3
        self.uq = self.unit // QKV
        self.ub = self.unit // D
        self.um = self.unit // MT
        self.nq = D // self.uq
        self.nb = self.nq + BROWS // self.ub
        self.nm = D // self.um
        self.first_mod = self.nb // 3
        self.half = (self.nq + self.nb) // 2
        self.flat_rows = self.unit // LANES
        self.frames = seq_count * F_DEV
        self.late = list(range(self.nq, self.half))
        self.early = list(range(self.half, self.nb))
        self.outs = self.late[: -(-HD // self.ub)]
        self.sided = self.late[len(self.outs) :]
        self.rank, self.ranks = self.ranked(self.early)
        self.late_rank, self.late_ranks = self.ranked(self.sided)

    def ranked(self, units):
        seen, rank = {}, {}
        for k in units:
            column = self.home(k)[1]
            rank[k] = seen.get(column, 0)
            seen[column] = rank[k] + 1
        return rank, max(seen.values())

    def home(self, k):
        return (k // 3) // self.r, (k // 3) % self.r


def place(plan):
    s = lax.axis_index("seq")
    t = lax.axis_index("tp")
    return s, t, lax.div(s, plan.r), lax.rem(s, plan.r)


def remote(src, dst, send_sem, recv_sem, s, t):
    return pltpu.make_async_remote_copy(
        src_ref=src,
        dst_ref=dst,
        send_sem=send_sem,
        recv_sem=recv_sem,
        device_id=(s, t),
        device_id_type=MESH,
    )


def greet(peers):
    barrier = pltpu.get_barrier_semaphore()
    for s, t in peers:
        pl.semaphore_signal(barrier, inc=1, device_id=(s, t), device_id_type=MESH)
    pl.semaphore_wait(barrier, len(peers))


def by_kind(plan, k, act, low=0, high=None):
    high = plan.nb if high is None else high
    q_high, b_low = min(plan.nq, high), max(plan.nq, low)
    if low < q_high:
        @pl.when((k >= low) & (k < q_high))
        def _():
            act("q")

    if b_low < high:
        @pl.when((k >= b_low) & (k < high))
        def _():
            act("b")


def unit_of(plan, k, kind, wq, wb):
    if kind == "q":
        return wq.at[pl.ds(pl.multiple_of(k * plan.uq, plan.uq), plan.uq)]
    return wb.at[pl.ds(pl.multiple_of((k - plan.nq) * plan.ub, plan.ub), plan.ub)]


def call(kernel, outs, scratch, ins, cid=None, cost=None, name=None, out_specs=None):
    params = dict(vmem_limit_bytes=VMEM_LIMIT)
    if cid is not None:
        params.update(collective_id=cid, has_side_effects=True)
    return pl.pallas_call(
        kernel,
        out_shape=outs,
        in_specs=ins,
        out_specs=out_specs or jax.tree.map(lambda _: VM, outs),
        scratch_shapes=scratch,
        compiler_params=pltpu.CompilerParams(**params),
        cost_estimate=cost,
        name=name,
    )


def head_kernel(
    plan, master, cond, tokens,
    wq, w_out, w_side, w_early, own_b, mods, first_in, q_out, kv_out,
    tile, macc, mpart, mrecv, mod, norm, q_send, kv_send,
    qp_s, qc_s, q_r, wo_s, wo_r, ws_s, ws_r, we_s, we_r, loc_s, m_s, m_r, t_s, t_r, as_, ar, ks, kr, xs, xr,
):
    s, t, z, r = place(plan)
    n, rn = plan.n, plan.r
    greet(
        [(lax.rem(s + d, n), t) for d in range(1, n)]
        + [(s, lax.rem(t + d, TP)) for d in range(1, TP)]
    )
    start = lambda copy: copy.start()
    done = lambda copy: copy.wait_send()
    half = plan.uq // 2

    def q_rows(k, h):
        return wq.at[pl.ds(pl.multiple_of(k * plan.uq + h * half, half), half)]

    def q_copy(k, h, sem, to_s):
        ref = q_rows(k, h)
        return remote(ref, ref, sem, q_r.at[2 * k + h], to_s, t)

    def q_arrived(k, h):
        q_copy(k, h, qc_s.at[0, 0], s).wait_recv()

    def column(j):
        return r + rn * lax.rem(j + r, 2)

    def q_own(act):
        for away in (True, False):
            for i in range(3):
                k = 3 * s + i

                @pl.when((k < plan.nq) & ((lax.rem(k, rn) != r) == away))
                def _():
                    for h in range(2):
                        for d in range(1, rn):
                            act(q_copy(k, h, qp_s.at[2 * i + h, d - 1], lax.rem(r + d, rn)))

    def q_line(act, wait):
        for j in range(2):
            k = column(j)
            for h in range(2):
                if wait:
                    @pl.when((z > 0) | (lax.div(k, 3) != r))
                    def _():
                        q_arrived(k, h)

                @pl.when(z < ZN - 1)
                def _():
                    act(q_copy(k, h, qc_s.at[2 * j + h, 0], s + rn))

                @pl.when(z > 0)
                def _():
                    for d in range(1, rn):
                        act(
                            q_copy(
                                k, h, qc_s.at[2 * j + h, d], z * rn + lax.rem(r + d, rn)
                            )
                        )

    def slot(k):
        if k in plan.outs:
            at = k - plan.nq
            return w_out.at[at], wo_s.at[at], wo_r.at[at]
        if k in plan.sided:
            at = plan.late_rank[k]
            return w_side.at[at], ws_s.at[at], ws_r.at[at]
        return w_early.at[k - plan.half], we_s.at[plan.rank[k]], we_r.at[k - plan.half]

    def along(k, src, act, up):
        dst, send_sem, recv_sem = slot(k)
        if up and k < plan.half:
            @pl.when(z < ZN - 1)
            def _():
                act(remote(src, dst, send_sem.at[0], recv_sem, s + rn, t))

        if not up:
            @pl.when(z > 0)
            def _():
                act(remote(src, dst, send_sem.at[1], recv_sem, s - rn, t))

    def beside(k, src, act):
        if k in plan.sided:
            return
        dst, send_sem, recv_sem = slot(k)
        for d in range(1, rn):
            act(
                remote(
                    src, dst, send_sem.at[1 + d], recv_sem, z * rn + lax.rem(r + d, rn), t
                )
            )

    def arrived(k):
        dst, send_sem, recv_sem = slot(k)
        remote(own_b.at[0], dst, send_sem.at[0], recv_sem, s, t).wait_recv()

    def keep(k):
        return pltpu.make_async_copy(own_b.at[k % 3], slot(k)[0], loc_s.at[k % 3])

    def owned(units, act):
        for k in units:
            @pl.when(s == k // 3)
            def _():
                act(k, own_b.at[k % 3])

    def pass_along(units, d, act, wait):
        for k in units:
            zo, ro = plan.home(k)
            if k < plan.half and zo + d < ZN:
                @pl.when((r == ro) & (z == zo + d))
                def _():
                    if wait:
                        arrived(k)
                    along(k, slot(k)[0], act, True)
                    beside(k, slot(k)[0], act)

            if zo - d >= 0:
                @pl.when((r == ro) & (z == zo - d))
                def _():
                    if wait:
                        arrived(k)
                    along(k, slot(k)[0], act, False)
                    beside(k, slot(k)[0], act)

    units = plan.late + plan.early
    first_up = [k for k in plan.late if k % 3 == 0 and plan.home(k)[0] > 0]
    later_up = [k for k in plan.late if k not in first_up]

    for i in range(3):
        k = 3 * s + i
        base = i * plan.flat_rows

        def fill(kind):
            rows, cols = (plan.uq, QKV // LANES) if kind == "q" else (plan.ub, D // LANES)
            at = pl.multiple_of(k * plan.uq, plan.uq)
            for j in range(cols):
                values = master[pl.ds(base + j, rows, stride=cols), :].astype(BF16)
                if kind == "q":
                    wq[pl.ds(at, rows), j * LANES : (j + 1) * LANES] = values
                else:
                    own_b[i, :, j * LANES : (j + 1) * LANES] = values

        by_kind(plan, k, fill)

    q_own(start)

    @pl.when(z == 0)
    def _():
        q_line(start, True)

    owned(units, lambda k, src: along(k, src, start, False))
    owned(first_up, lambda k, src: along(k, src, start, True))
    owned(units, lambda k, src: keep(k).start())

    macc[...] = jnp.zeros_like(macc)
    for i in range(3):
        k = 3 * s + i
        base = i * plan.flat_rows

        @pl.when(k >= plan.nb)
        def _():
            for j in range(MCOLS):
                tile[:, j * LANES : (j + 1) * LANES] = master[
                    pl.ds(base + j, plan.um, stride=MCOLS), :
                ].astype(BF16)
            macc[...] += mm(cond[k - plan.nb], tile[...])

    fm = plan.first_mod

    def m_copy(d):
        to = lax.rem(s + d, n)
        return remote(mpart.at[to], mrecv.at[s - fm], m_s.at[d - 1], m_r.at[s - fm], to, t)

    @pl.when(s >= fm)
    def _():
        for f in range(plan.frames):
            for j in range(MCOLS):
                mpart[f // F_DEV, pl.ds((f % F_DEV) * MCOLS + j, 1), :] = macc[
                    pl.ds(f, 1), j * LANES : (j + 1) * LANES
                ]
        mrecv[s - fm] = mpart[s]
        for d in range(1, n):
            m_copy(d).start()

    def norm_rows(at):
        rows = pl.ds(at, 64)
        norm[rows, :] = normalize(tokens[rows, :].astype(F32))[0]

    loop(F_DEV * TOK_FRAME, 64, norm_rows)

    @pl.when(z > 0)
    def _():
        q_line(start, True)

    owned(plan.outs, lambda k, src: along(k, src, start, True))
    owned([k for k in later_up if k not in plan.outs], lambda k, src: along(k, src, start, True))
    owned(units, lambda k, src: beside(k, src, start))
    pass_along(first_up, 1, start, True)

    for src in range(fm, n):
        @pl.when(s != src)
        def _():
            remote(mpart.at[0], mrecv.at[src - fm], m_s.at[0], m_r.at[src - fm], s, t).wait_recv()

    total = mrecv[0]
    for src in range(1, n - fm):
        total = total + mrecv[src]
    mod[t] = total

    def t_copy(d):
        return remote(mod.at[t], mod.at[t], t_s.at[d - 1], t_r.at[t], s, lax.rem(t + d, TP))

    for d in range(1, TP):
        t_copy(d).start()
    for d in range(1, TP):
        other = lax.rem(t + d, TP)
        remote(mod.at[t], mod.at[other], t_s.at[0], t_r.at[other], s, t).wait_recv()
    for f in range(F_DEV):
        for block in range(TP * MCOLS):
            part, at = block // (D // LANES), block % (D // LANES)
            mods[f * 6 + part : f * 6 + part + 1, at * LANES : (at + 1) * LANES] = mod[
                block // MCOLS, f * MCOLS + block % MCOLS : f * MCOLS + block % MCOLS + 1, :
            ]

    def affine(f):
        def body(at):
            rows = pl.ds(f * TOK_FRAME + at, 64)
            first_in[rows, :] = (
                norm[rows, :] * (1.0 + mods[f * 6 + 1 : f * 6 + 2, :]) + mods[f * 6 : f * 6 + 1, :]
            ).astype(BF16)

        loop(TOK_FRAME, 64, body)

    for f in range(F_DEV):
        affine(f)

    for k in range(plan.nq):
        for h in range(2):
            if rn > 1:
                at_zero = (z == 0) & (k // 3 != r) & (k % rn != r)

                @pl.when(at_zero | (z > 0) & (k % rn != r))
                def _():
                    q_arrived(k, h)

    keys = mm(first_in[...], wq[:, HD : 2 * HD]).astype(BF16)
    values = mm(first_in[...], wq[:, 2 * HD :]).astype(BF16)
    for h in range(ZN):
        cols = slice(h * HEAD, (h + 1) * HEAD)
        kv_send[h] = jnp.concatenate([keys[:, cols], values[:, cols]], axis=1)

    def kv_copy(d):
        h = lax.rem(z + d, ZN)
        return remote(kv_send.at[h], kv_out.at[s], ks.at[d - 1], kr.at[z], h * rn + r, t)

    def a_copy(d):
        h = lax.rem(z + d, ZN)
        return remote(q_send.at[h], q_out.at[z], as_.at[d - 1], ar.at[z], h * rn + r, t)

    def side_copy(zs, e):
        at = zs * rn + r
        ref = kv_out.at[at]
        return remote(ref, ref, xs.at[zs, e - 1], xr.at[at], z * rn + lax.rem(r + e, rn), t)

    for d in range(1, ZN):
        kv_copy(d).start()
    kv_out[s] = kv_send[z]
    for e in range(1, rn):
        side_copy(z, e).start()
    queries = mm(first_in[...], wq[:, :HD]).astype(BF16)
    for h in range(ZN):
        cols = slice(h * HEAD, (h + 1) * HEAD)
        q_send[h] = jnp.concatenate([queries[:TOK_FRAME, cols], queries[TOK_FRAME:, cols]], axis=1)
    for d in range(1, ZN):
        a_copy(d).start()
    q_out[z] = q_send[z]

    rest = [k for k in units if k not in first_up]
    pass_along(rest, 1, start, True)
    for d in range(1, ZN):
        zs = lax.rem(z + d, ZN)
        remote(kv_send.at[0], kv_out.at[zs * rn + r], ks.at[0], kr.at[zs], s, t).wait_recv()
        for e in range(1, rn):
            side_copy(zs, e).start()
    for d in range(2, ZN):
        pass_along(units, d, start, True)
    for d in range(1, ZN):
        zs = lax.rem(z + d, ZN)
        remote(q_send.at[0], q_out.at[zs], as_.at[0], ar.at[zs], s, t).wait_recv()
    for e in range(1, rn):
        for zs in range(ZN):
            at = zs * rn + lax.rem(r + e, rn)
            remote(kv_out.at[at], kv_out.at[at], xs.at[0, 0], xr.at[at], s, t).wait_recv()
    for k in plan.outs + plan.early:
        zo, ro = plan.home(k)

        @pl.when((r != ro) & ((z <= zo) | (k in plan.outs)))
        def _():
            arrived(k)


    q_own(done)
    q_line(done, False)
    owned(units, lambda k, src: along(k, src, done, False))
    owned(plan.late, lambda k, src: along(k, src, done, True))
    owned(units, lambda k, src: beside(k, src, done))
    owned(units, lambda k, src: keep(k).wait())
    for d in range(1, ZN):
        pass_along(units, d, done, False)

    @pl.when(s >= fm)
    def _():
        for d in range(1, n):
            m_copy(d).wait_send()

    for d in range(1, TP):
        t_copy(d).wait_send()
    for d in range(1, ZN):
        kv_copy(d).wait_send()
        a_copy(d).wait_send()
    for zs in range(ZN):
        for e in range(1, rn):
            side_copy(zs, e).wait_send()


def head_part(plan, master, cond_units, tokens, cid):
    n, rn = plan.n, plan.r
    mrows = F_DEV * MCOLS
    rows = F_DEV * TOK_FRAME
    mods = n - plan.first_mod
    return call(
        functools.partial(head_kernel, plan),
        (
            jax.ShapeDtypeStruct((D, QKV), BF16),
            jax.ShapeDtypeStruct((len(plan.outs), plan.ub, D), BF16),
            jax.ShapeDtypeStruct((plan.late_ranks, plan.ub, D), BF16),
            jax.ShapeDtypeStruct((len(plan.early), plan.ub, D), BF16),
            jax.ShapeDtypeStruct((3, plan.ub, D), BF16),
            jax.ShapeDtypeStruct((F_DEV * 6, D), F32),
            jax.ShapeDtypeStruct((rows, D), BF16),
            jax.ShapeDtypeStruct((ZN, TOK_FRAME, LANES), BF16),
            jax.ShapeDtypeStruct((n, rows, LANES), BF16),
        ),
        [
            pltpu.VMEM((plan.um, MT), BF16),
            pltpu.VMEM((plan.frames, MT), F32),
            pltpu.VMEM((n, mrows, LANES), F32),
            pltpu.VMEM((mods, mrows, LANES), F32),
            pltpu.VMEM((TP, mrows, LANES), F32),
            pltpu.VMEM((rows, D), F32),
            pltpu.VMEM((ZN, TOK_FRAME, LANES), BF16),
            pltpu.VMEM((ZN, rows, LANES), BF16),
            DMA((6, rn - 1)), DMA((4, rn)), DMA((2 * plan.nq,)),
            DMA((len(plan.outs), rn + 1)), DMA((len(plan.outs),)),
            DMA((plan.late_ranks, 2)), DMA((plan.late_ranks,)),
            DMA((plan.ranks, rn + 1)), DMA((len(plan.early),)), DMA((3,)),
            DMA((n - 1,)), DMA((mods,)), DMA((TP - 1,)), DMA((TP,)),
            DMA((ZN - 1,)), DMA((ZN,)), DMA((ZN - 1,)), DMA((ZN,)), DMA((ZN, rn - 1)), DMA((n,)),
        ],
        [VM] * 3,
        cid,
        out_specs=(VM, ANY, ANY, ANY, VM, VM, VM, VM, VM),
        name="head_part",
    )(master, cond_units, tokens)


def padded(rows, low):
    zero = jnp.zeros_like(rows)
    return jnp.concatenate([rows, zero] if low else [zero, rows], axis=1)


def attend_kernel(plan, meta, q, kv, o, ot, lse, m_ref, l_ref, acc):
    r = meta[plan.frames]
    scale = HEAD ** (-0.5)

    def group(zq, carry):
        for f in range(F_DEV):
            frame = (zq * plan.r + r) * F_DEV + f
            clip = meta[frame]
            pack = q[zq]
            qz = padded(pack[:, f * HEAD : (f + 1) * HEAD], True) * jnp.asarray(scale, BF16)
            m_ref[...] = jnp.full_like(m_ref, -1e30)
            l_ref[...] = jnp.zeros_like(l_ref)
            acc[...] = jnp.zeros_like(acc)

            def block(j, inner):
                @pl.when(meta[j] == clip)
                def _():
                    rows = pl.multiple_of(lax.rem(j, F_DEV) * TOK_FRAME, TOK_FRAME)
                    keys = kv[lax.div(j, F_DEV), pl.ds(rows, TOK_FRAME), :]
                    st = mm_nt(keys, qz)
                    m_old = m_ref[...]
                    m_new = jnp.maximum(m_old, jnp.max(st, axis=0, keepdims=True))
                    p = jnp.exp(st - m_new)
                    alpha = jnp.exp(m_old - m_new)
                    m_ref[...] = m_new
                    l_ref[...] = l_ref[...] * alpha + jnp.sum(p, axis=0, keepdims=True)
                    acc[...] = acc[...] * alpha + mm_tn(keys, p.astype(BF16))

                return inner

            lax.fori_loop(0, frame + 1, block, 0)
            total = l_ref[...]
            out = acc[HEAD:, :] / total
            ot[zq * F_DEV + f] = out
            lse[zq * F_DEV + f] = m_ref[...] + jnp.log(total)
            rows = out.T
            o[zq, f] = jnp.concatenate([rows[:PACK], rows[PACK:]], axis=1).astype(BF16)
        return carry

    lax.fori_loop(0, ZN, group, 0)


def attend(plan, meta, q, kv):
    frames = ZN * F_DEV
    return call(
        functools.partial(attend_kernel, plan),
        (
            jax.ShapeDtypeStruct((ZN, F_DEV, PACK, LANES), BF16),
            jax.ShapeDtypeStruct((frames, HEAD, TOK_FRAME), F32),
            jax.ShapeDtypeStruct((frames, 1, TOK_FRAME), F32),
        ),
        [
            pltpu.VMEM((1, TOK_FRAME), F32),
            pltpu.VMEM((1, TOK_FRAME), F32),
            pltpu.VMEM((LANES, TOK_FRAME), F32),
        ],
        [SM, VM, VM],
        cost=pl.CostEstimate(flops=2 * 10**10, bytes_accessed=6 * 10**7, transcendentals=10**7),
        name="attend",
    )(meta, q, kv)


def attend_back_kernel(plan, meta, q, kv, do, ot, lse, dq, dkv, dkv_acc, dq_acc):
    r = meta[plan.frames]
    scale = HEAD ** (-0.5)
    dkv_acc[...] = jnp.zeros_like(dkv_acc)

    def group(zq, carry):
        parts = []
        for f in range(F_DEV):
            frame = (zq * plan.r + r) * F_DEV + f
            clip = meta[frame]
            columns = slice(f * HEAD, (f + 1) * HEAD)
            qz = padded(q[zq][:, columns], True) * jnp.asarray(scale, BF16)
            grads = jnp.concatenate([do[zq, f][:, :HEAD], do[zq, f][:, HEAD:]], axis=0)
            doz = padded(grads, False)
            delta = jnp.sum(grads.astype(F32).T * ot[zq * F_DEV + f], axis=0, keepdims=True)
            logs = lse[zq * F_DEV + f]
            dq_acc[...] = jnp.zeros_like(dq_acc)

            def block(j, inner):
                @pl.when(meta[j] == clip)
                def _():
                    g = lax.div(j, F_DEV)
                    rows = pl.multiple_of(lax.rem(j, F_DEV) * TOK_FRAME, TOK_FRAME)
                    keys = kv[g, pl.ds(rows, TOK_FRAME), :]
                    pt = jnp.exp(mm_nt(keys, qz) - logs)
                    dst = (pt * (mm_nt(keys, doz) - delta)).astype(BF16)
                    dkv_acc[g, pl.ds(rows, TOK_FRAME), :] += mm(dst, qz) + mm(pt.astype(BF16), doz)
                    dq_acc[...] += mm_tn(keys, dst)

                return inner

            lax.fori_loop(0, frame + 1, block, 0)
            parts.append((dq_acc[:HEAD, :] * scale).T)
        dq[zq] = jnp.concatenate(parts, axis=1).astype(BF16)
        return carry

    lax.fori_loop(0, ZN, group, 0)
    dkv[...] = dkv_acc[...].astype(BF16)


def attend_back(plan, meta, q, kv, do, ot, lse):
    return call(
        functools.partial(attend_back_kernel, plan),
        (
            jax.ShapeDtypeStruct((ZN, TOK_FRAME, LANES), BF16),
            jax.ShapeDtypeStruct((plan.n, F_DEV * TOK_FRAME, LANES), BF16),
        ),
        [
            pltpu.VMEM((plan.n, F_DEV * TOK_FRAME, LANES), F32),
            pltpu.VMEM((LANES, TOK_FRAME), F32),
        ],
        [SM, VM, VM, VM, VM, VM],
        cost=pl.CostEstimate(flops=3 * 10**10, bytes_accessed=9 * 10**7, transcendentals=10**7),
        name="attend_back",
    )(meta, q, kv, do, ot, lse)


def middle_kernel(
    plan, o_mine, wo_across, w_out, w_side, w_beside, w_early, w_below, tokens, grad_out, mod,
    result, gb, esum, do_out, dmid, dmod,
    wb, eside, wo, oall, attended, attn, mid, norm, inv, sin, hidden, dmlp, slopes, dup,
    own, csend, crecv, ysend, yrecv, dattn, dsend, dwo, wsend, wrecv,
    o_s, o_r, f_s, f_r, n_s, n_r, c_s, c_r, y_s, y_r, d_s, d_r, w_s, w_r, e_s, e_r, p_s, p_r, l_s, u_s, u_r, g_s, g_r,
):
    s, t, z, r = place(plan)
    rn = plan.r
    y = lax.div(t, 2)
    c = lax.rem(t, 2)
    sib = 2 * y + 1 - c
    across = lax.rem(t + 2, TP)
    mine = pl.multiple_of(c * TOK_FRAME, TOK_FRAME)
    theirs = pl.multiple_of((1 - c) * TOK_FRAME, TOK_FRAME)
    pairs = [(d, e) for d in range(ZN) for e in range(2)][1:]

    def partner(d, e):
        return lax.rem(z + d, ZN), (c if e == 0 else 1 - c)

    greet(
        [(partner(d, e)[0] * rn + r, 2 * y + partner(d, e)[1]) for d, e in pairs]
        + [(s, across)]
        + [(z * rn + lax.rem(r + d, rn), t) for d in range(1, rn)]
    )

    def home(k):
        return (k // 3) // rn, (k // 3) % rn, k - plan.half

    def w_rows(ref, k):
        return ref.at[pl.ds((k - plan.nq) * plan.ub, plan.ub)]

    def late_loads(act):
        for k in plan.late:
            sem = l_s.at[k - plan.nq]
            if k in plan.outs:
                act(pltpu.make_async_copy(w_out.at[k - plan.nq], w_rows(wb, k), sem))
            else:
                zo, ro = plan.home(k)
                rank = plan.late_rank[k]

                @pl.when(r == ro)
                def _():
                    act(pltpu.make_async_copy(w_side.at[rank], w_rows(wb, k), sem))

                @pl.when(r != ro)
                def _():
                    d = lax.rem(r - ro + rn, rn)
                    act(pltpu.make_async_copy(w_beside.at[d - 1, rank], w_rows(wb, k), sem))

    def loads(act):
        for k in plan.early:
            zo, ro, at = home(k)

            @pl.when(z <= zo)
            def _():
                act(pltpu.make_async_copy(w_early.at[at], w_rows(wb, k), l_s.at[len(plan.late) + at]))

            @pl.when((z == zo + 1) & (r == ro))
            def _():
                act(
                    pltpu.make_async_copy(
                        w_below.at[k % 3], w_rows(wb, k), l_s.at[len(plan.late) + at]
                    )
                )

    def rise(k, src, act):
        zo, ro, at = home(k)

        @pl.when(z < ZN - 1)
        def _():
            act(remote(src, w_rows(wb, k), u_s.at[at, 0], u_r.at[at], s + rn, t))

        for d in range(1, rn):
            act(
                remote(
                    src, w_rows(wb, k), u_s.at[at, d], u_r.at[at],
                    z * rn + lax.rem(r + d, rn), t,
                )
            )

    def risen(k):
        remote(w_below.at[0], w_rows(wb, k), u_s.at[0, 0], u_r.at[k - plan.half], s, t).wait_recv()

    def rises(act, first, wait):
        for k in plan.early:
            zo, ro, at = home(k)
            if first:
                @pl.when((z == zo + 1) & (r == ro))
                def _():
                    rise(k, w_below.at[k % 3], act)
            else:
                @pl.when((z > zo + 1) & (r == ro))
                def _():
                    if wait:
                        risen(k)
                    rise(k, w_rows(wb, k), act)

    def o_copy(d, e):
        zd, cd = partner(d, e)
        return remote(
            o_mine.at[zd, cd], oall.at[y * 8 + c * ZN + z], o_s.at[2 * d + e],
            o_r.at[c * ZN + z], zd * rn + r, 2 * y + cd,
        )

    def f_copy(slot):
        ref = oall.at[y * 8 + slot]
        return remote(ref, ref, f_s.at[slot], f_r.at[slot], s, across)

    def p_copy(i, tp):
        ref = wo.at[pl.ds(pl.multiple_of(tp * HD, HD), HD)]
        return remote(ref, ref, p_s.at[i], p_r.at[i], s, sib)

    for d, e in pairs:
        o_copy(d, e).start()
    start = lambda copy: copy.start()
    rises(start, True, False)
    late_loads(start)
    loads(start)
    late_loads(lambda copy: copy.wait())
    wo[pl.ds(pl.multiple_of(t * HD, HD), HD), :] = wb[:HD, :]
    p_copy(0, t).start()
    wo[pl.ds(pl.multiple_of(across * HD, HD), HD), :] = wo_across[...]
    p_copy(1, across).start()
    oall[y * 8 + c * ZN + z] = o_mine[z, c]
    f_copy(c * ZN + z).start()

    def d_mlp(f):
        def body(at):
            rows = pl.ds(f * TOK_FRAME + at, 64)
            dmlp[rows, :] = (grad_out[rows, :].astype(F32) * mod[f * 6 + 5 : f * 6 + 6, :]).astype(
                BF16
            )

        loop(TOK_FRAME, 64, body)

    for f in range(F_DEV):
        d_mlp(f)

    for d, e in pairs:
        zd, cd = partner(d, e)
        slot = cd * ZN + zd
        remote(o_mine.at[0, 0], oall.at[y * 8 + slot], o_s.at[0], o_r.at[slot], s, t).wait_recv()
        f_copy(slot).start()
    for slot in range(8):
        remote(
            oall.at[0], oall.at[(1 - y) * 8 + slot], f_s.at[slot], f_r.at[slot], s, t
        ).wait_recv()
    for m in range(HEADS // 2):
        a, b = oall[2 * m], oall[2 * m + 1]
        cols = slice(m * LANES, (m + 1) * LANES)
        attended[:PACK, cols] = jnp.concatenate([a[:, :HEAD], b[:, :HEAD]], axis=1)
        attended[PACK:, cols] = jnp.concatenate([a[:, HEAD:], b[:, HEAD:]], axis=1)

    p_copy(0, sib).wait_recv()
    p_copy(1, lax.rem(sib + 2, TP)).wait_recv()

    def attn_tile(at):
        attn[:, pl.ds(at, TILE)] = mm(attended[...], wo[:, pl.ds(at, TILE)])

    loop(D, TILE, attn_tile)
    rises(start, False, True)

    row = lambda part: mod[pl.ds(c * 6 + part, 1), :]

    def norm_rows(at):
        rows = pl.ds(at, 64)
        values = tokens[pl.ds(mine + at, 64), :].astype(F32) + row(2) * attn[rows, :]
        mid[rows, :] = values
        normed, inverse = normalize(values)
        norm[rows, :] = normed
        inv[rows, :] = inverse
        sin[pl.ds(mine + at, 64), :] = (normed * (1.0 + row(4)) + row(3)).astype(BF16)

    loop(TOK_FRAME, 64, norm_rows)

    def n_copy(base):
        ref = sin.at[pl.ds(base, TOK_FRAME)]
        return remote(ref, ref, n_s.at[0], n_r.at[0], s, sib)

    n_copy(mine).start()
    loads(lambda copy: copy.wait())
    for k in plan.early:
        zo, ro, at = home(k)

        @pl.when((z > zo) & (r != ro))
        def _():
            risen(k)

    def feed(base):
        rows = pl.ds(base, TOK_FRAME)

        def tile(at):
            cols = pl.ds(at, TILE)
            u = mm(sin[rows, :], wb[HD : HD + FT, cols])
            square = u * u
            inner = GELU_A * u * (1.0 + GELU_B * square)
            th = jnp.tanh(inner)
            half = 0.5 * (1.0 + th)
            hidden[rows, cols] = (u * half).astype(BF16)
            slopes[rows, cols] = half + 0.5 * u * (1.0 - th * th) * (
                GELU_A * (1.0 + 3.0 * GELU_B * square)
            )

        loop(FT, TILE, tile)

    feed(mine)
    n_copy(theirs).wait_recv()
    feed(theirs)

    def d_up(at):
        cols = pl.ds(at, TILE)
        dup[:, cols] = (mm_nt(dmlp[...], wb[pl.ds(HD + FT + at, TILE), :]) * slopes[:, cols]).astype(
            BF16
        )

    loop(FT, TILE, d_up)

    def c_copy(w, n):
        return remote(csend.at[w, n], crecv.at[w, n], c_s.at[w, n], c_r.at[w, n], s, sib)

    def y_copy(w, n):
        return remote(ysend.at[w, n], yrecv.at[w, n], y_s.at[w, n], y_r.at[w, n], s, across)

    def pass_on(w, n):
        c_copy(w, n).wait_recv()
        ysend[w, n] = (own[n] + crecv[w, n].astype(F32)).astype(BF16)
        y_copy(w, n).start()

    def product(w, base, n):
        rows = pl.ds(base, TOK_FRAME)
        if w == 0:
            return mm_nt(dup[rows, :], wb[HD + n * TILE : HD + (n + 1) * TILE, :])
        return mm(hidden[rows, :], wb[HD + FT :, n * TILE : (n + 1) * TILE])

    for w in range(2):
        for n in range(TILES):
            csend[w, n] = product(w, theirs, n).astype(BF16)
            c_copy(w, n).start()
            own[n] = product(w, mine, n)
            if n:
                pass_on(w, n - 1)
        pass_on(w, TILES - 1)

    def down_grad(at):
        gb[pl.ds(HD + FT + at, TILE), :] = mm_tn(hidden[:, pl.ds(at, TILE)], dmlp[...]).astype(BF16)

    def up_grad(at):
        gb[pl.ds(HD + at, TILE), :] = mm_tn(sin[:, pl.ds(at, TILE)], dup[...]).astype(BF16)

    loop(FT, TILE, down_grad)
    loop(D, TILE, up_grad)

    def early_grad(k, d):
        zo, ro, at = home(k)
        slot = lax.rem(ro - r + rn, rn) - 1 if d is None else d - 1
        return remote(
            w_rows(gb, k), eside.at[slot, plan.rank[k]], g_s.at[at], g_r.at[slot, plan.rank[k]],
            z * rn + ro, t,
        )

    def early_grads(act):
        for k in plan.early:
            zo, ro, at = home(k)

            @pl.when(r != ro)
            def _():
                act(early_grad(k, None))

    early_grads(start)

    dm = dmod
    dm[...] = jnp.zeros_like(dm)
    for n in range(TILES):
        y_copy(0, n).wait_recv()

    def total(w, rows):
        return jnp.concatenate(
            [ysend[w, n, rows].astype(F32) + yrecv[w, n, rows].astype(F32) for n in range(TILES)],
            axis=1,
        )

    def back_rows(at):
        rows = pl.ds(at, 64)
        tok_rows = pl.ds(mine + at, 64)
        grads = total(0, rows)
        normed = norm[rows, :]
        add_to(dm, 1, grads)
        add_to(dm, 2, grads * normed)
        values = grad_out[tok_rows, :].astype(F32) + norm_back(
            grads * (1.0 + row(4)), normed, inv[rows, :]
        )
        dmid[rows, :] = values
        add_to(dm, 0, attn[rows, :] * values)
        dattn[rows, :] = (row(2) * values).astype(BF16)

    loop(TOK_FRAME, 64, back_rows)
    for ch in range(2):
        part = mm_nt(dattn[...], wo[pl.ds(pl.multiple_of((2 * y + ch) * HD, HD), HD), :]).astype(BF16)
        for zh in range(ZN):
            cols = slice(zh * HEAD, (zh + 1) * HEAD)
            dsend[ch * ZN + zh] = jnp.concatenate([part[:PACK, cols], part[PACK:, cols]], axis=1)

    def d_copy(d, e):
        zd, cd = partner(d, e)
        return remote(
            dsend.at[cd * ZN + zd], do_out.at[z, c], d_s.at[2 * d + e], d_r.at[2 * z + c],
            zd * rn + r, 2 * y + cd,
        )

    for d, e in pairs:
        d_copy(d, e).start()
    do_out[z, c] = dsend[c * ZN + z]

    def o_grad(head_core):
        cols = pl.ds(pl.multiple_of((2 * y + head_core) * HD, HD), HD)
        return mm_tn(attended[:, cols], dattn[...])

    w_copy = remote(wsend, wrecv, w_s, w_r, s, sib)
    wsend[...] = o_grad(1 - c).astype(BF16)
    w_copy.start()
    dwo[...] = o_grad(c)

    for n in range(TILES):
        y_copy(1, n).wait_recv()

    def result_rows(at):
        rows = pl.ds(at, 64)
        tok_rows = pl.ds(mine + at, 64)
        mlp = total(1, rows)
        add_to(dm, 3, mlp * grad_out[tok_rows, :].astype(F32))
        result[tok_rows, :] = (mid[rows, :] + row(5) * mlp).astype(BF16)

    loop(TOK_FRAME, 64, result_rows)

    def e_copy(base):
        ref = result.at[pl.ds(base, TOK_FRAME)]
        return remote(ref, ref, e_s, e_r, s, sib)

    e_copy(mine).start()
    w_copy.wait_recv()
    gb[:HD, :] = (dwo[...] + wrecv[...].astype(F32)).astype(BF16)

    for d, e in pairs:
        zd, cd = partner(d, e)
        remote(
            dsend.at[0], do_out.at[zd, cd], d_s.at[0], d_r.at[2 * zd + cd], s, t
        ).wait_recv()
    for k in plan.early:
        zo, ro, at = home(k)

        @pl.when(r == ro)
        def _():
            rank = plan.rank[k]
            for d in range(1, rn):
                early_grad(k, d).wait_recv()

            def body(at):
                rows = pl.ds(at, 16)
                total = gb[pl.ds((k - plan.nq) * plan.ub + at, 16), :].astype(F32)
                for d in range(1, rn):
                    total = total + eside[d - 1, rank, rows, :].astype(F32)
                esum[rank, rows, :] = total.astype(BF16)

            loop(plan.ub, 16, body)

    e_copy(theirs).wait_recv()
    done = lambda copy: copy.wait_send()
    early_grads(done)
    rises(done, True, False)
    rises(done, False, False)
    for d, e in pairs:
        o_copy(d, e).wait_send()
        d_copy(d, e).wait_send()
    for slot in range(8):
        f_copy(slot).wait_send()
    n_copy(mine).wait_send()
    p_copy(0, t).wait_send()
    p_copy(1, across).wait_send()
    for w in range(2):
        for n in range(TILES):
            c_copy(w, n).wait_send()
            y_copy(w, n).wait_send()
    w_copy.wait_send()
    e_copy(mine).wait_send()


def middle_part(plan, o_mine, wo_across, weights, tokens, grad_out, mod_rows, cid):
    rn, count = plan.r, len(plan.early)
    rows = F_DEV * TOK_FRAME
    half = lambda dtype: pltpu.VMEM((TOK_FRAME, D), dtype)
    full = lambda dtype: pltpu.VMEM((rows, D), dtype)
    tiles = pltpu.VMEM((2, TILES, TOK_FRAME, TILE), BF16)
    return call(
        functools.partial(middle_kernel, plan),
        (
            jax.ShapeDtypeStruct((rows, D), BF16),
            jax.ShapeDtypeStruct((BROWS, D), BF16),
            jax.ShapeDtypeStruct((plan.ranks, plan.ub, D), BF16),
            jax.ShapeDtypeStruct((ZN, F_DEV, PACK, LANES), BF16),
            jax.ShapeDtypeStruct((TOK_FRAME, D), F32),
            jax.ShapeDtypeStruct((8, D), F32),
        ),
        [
            pltpu.VMEM((BROWS, D), BF16),
            pltpu.VMEM((rn - 1, plan.ranks, plan.ub, D), BF16),
            pltpu.VMEM((HEADS * HEAD, D), BF16),
            pltpu.VMEM((HEADS, PACK, LANES), BF16),
            half(BF16), half(F32), half(F32), half(F32), pltpu.VMEM((TOK_FRAME, 1), F32),
            full(BF16), full(BF16), full(BF16), full(F32), full(BF16),
            pltpu.VMEM((TILES, TOK_FRAME, TILE), F32), tiles, tiles, tiles, tiles,
            half(BF16), pltpu.VMEM((8, PACK, LANES), BF16),
            pltpu.VMEM((HD, D), F32), pltpu.VMEM((HD, D), BF16), pltpu.VMEM((HD, D), BF16),
            DMA((8,)), DMA((8,)), DMA((8,)), DMA((8,)), DMA((1,)), DMA((1,)),
            DMA((2, TILES)), DMA((2, TILES)), DMA((2, TILES)), DMA((2, TILES)),
            DMA((8,)), DMA((8,)), DMA, DMA, DMA, DMA, DMA((2,)), DMA((2,)),
            DMA((len(plan.late) + count,)), DMA((count, rn)), DMA((count,)), DMA((count,)), DMA((rn - 1, plan.ranks)),
        ],
        [VM, VM, ANY, ANY, ANY, ANY, ANY, VM, VM, VM],
        cid,
        name="middle_part",
    )(o_mine, wo_across, *weights, tokens, grad_out, mod_rows)


def tail_kernel(
    plan, dq, dkv, first_in, wq, tokens, dmid, mod, dm4, gb, esum, e_above, e_below,
    igrad, oq, ob, dall,
    stage, side, q_in, kv_in, dqkv, gq, own, csend, crecv, ysend, yrecv, dm, dm3, dboth,
    rb, cb, estage, ebuf, qside, qpeer, qchain, qstage,
    q_s, q_r, k_s, k_r, x_s, x_r, c_s, c_r, y_s, y_r, e_s, e_r, h_s, h_r, m_s, m_r, r_s, r_r, t_s, t_r,
    es_s, es_r, qo_s, qs_r, qp_r, qc_s, qc_r,
):
    s, t, z, r = place(plan)
    n, rn = plan.n, plan.r
    y = lax.div(t, 2)
    c = lax.rem(t, 2)
    sib = 2 * y + 1 - c
    across = lax.rem(t + 2, TP)
    mine = pl.multiple_of(c * TOK_FRAME, TOK_FRAME)
    theirs = pl.multiple_of((1 - c) * TOK_FRAME, TOK_FRAME)
    greet([(lax.rem(s + d, n), t) for d in range(1, n)] + [(s, sib), (s, across)])

    def side_copy(d, e):
        zs = lax.rem(z + d, ZN)
        other = lax.rem(r + e, rn)
        return remote(
            dkv.at[zs * rn + other], side.at[e - 1, d], x_s.at[d, e - 1], x_r.at[d, e - 1],
            z * rn + other, t,
        )

    def q_copy(d):
        to = lax.rem(z + d, ZN)
        return remote(dq.at[to], q_in.at[z], q_s.at[d - 1], q_r.at[z], to * rn + r, t)

    def kv_copy(d):
        to = lax.rem(z + d, ZN)
        return remote(stage.at[d], kv_in.at[z], k_s.at[d - 1], k_r.at[z], to * rn + r, t)

    order = list(range(1, ZN)) + [0]
    for d in order:
        for e in range(1, rn):
            side_copy(d, e).start()
    for d in range(1, ZN):
        q_copy(d).start()
    q_in[z] = dq[z]
    for d in order:
        zs = lax.rem(z + d, ZN)
        total = dkv[zs * rn + r].astype(F32)
        for e in range(1, rn):
            side_copy(d, e).wait_recv()
            total = total + side[e - 1, d].astype(F32)
        if d == 0:
            kv_in[z] = total.astype(BF16)
        else:
            stage[d] = total.astype(BF16)
            kv_copy(d).start()

    def b_rows(k):
        return gb.at[pl.ds(pl.multiple_of((k - plan.nq) * plan.ub, plan.ub), plan.ub)]

    def late(k, act):
        by_kind(plan, k, lambda kind: act(), plan.nq, plan.half)

    def late_sides(act):
        for zo in range(2):
            for i in range(3):
                for d in range(1, rn):
                    other = lax.rem(r + d, rn)
                    k = 3 * (zo * rn + other) + i
                    lu = 3 * zo + i
                    late(
                        k,
                        lambda: act(
                            remote(
                                b_rows(k), rb.at[d - 1, lu], r_s.at[lu, d - 1], r_r.at[lu, d - 1],
                                z * rn + other, t,
                            )
                        ),
                    )

    def late_copy(lu, below, to):
        return remote(rb.at[0, lu], cb.at[below, lu], t_s.at[lu], t_r.at[lu, below], to, t)

    def late_step(zo, i, here_z, above, below, final):
        k = 3 * (zo * rn + r) + i
        lu = 3 * zo + i

        def act():
            unit = b_rows(k)
            for d in range(1, rn):
                remote(
                    unit, rb.at[d - 1, lu], r_s.at[lu, d - 1], r_r.at[lu, d - 1], s, t
                ).wait_recv()
            if above:
                late_copy(lu, 0, s).wait_recv()
            if below:
                late_copy(lu, 1, s).wait_recv()

            def body(at):
                rows = pl.ds(at, 16)
                total = unit[rows, :].astype(F32)
                for d in range(1, rn):
                    total = total + rb[d - 1, lu, rows, :].astype(F32)
                if above:
                    total = total + cb[0, lu, rows, :].astype(F32)
                if below:
                    total = total + cb[1, lu, rows, :].astype(F32)
                if final:
                    ob[i, rows, :] = total
                else:
                    rb[0, lu, rows, :] = total.astype(BF16)

            loop(plan.ub, 16, body)
            if not final:
                late_copy(lu, 0 if here_z > zo else 1, s - rn if here_z > zo else s + rn).start()

        @pl.when(z == here_z)
        def _():
            late(k, act)

    def late_close():
        late_sides(lambda copy: copy.wait_send())
        for zo in range(2):
            for i in range(3):
                @pl.when(z != zo)
                def _():
                    late(
                        3 * (zo * rn + r) + i, lambda: late_copy(3 * zo + i, 0, s).wait_send()
                    )

    def early_units(act):
        for k in plan.early:
            zo, ro, rank = (k // 3) // rn, (k // 3) % rn, plan.rank[k]

            @pl.when(r == ro)
            def _():
                act(k, zo, rank)

    def early_copy(rank, to):
        return remote(estage.at[rank], ebuf.at[rank], es_s.at[rank], es_r.at[rank], to, t)

    def early_send(k, zo, rank):
        source, came, step = (1, e_below, rn) if zo == 2 else (2, e_above, -rn)

        @pl.when(z == source)
        def _():
            def body(at):
                rows = pl.ds(at, 16)
                estage[rank, rows, :] = (
                    esum[rank, rows, :].astype(F32) + came[rank, rows, :].astype(F32)
                ).astype(BF16)

            loop(plan.ub, 16, body)
            early_copy(rank, s + step).start()

    def early_final(k, zo, rank):
        came = e_above if zo == 2 else e_below

        @pl.when(z == zo)
        def _():
            early_copy(rank, s).wait_recv()

            def body(at):
                rows = pl.ds(at, 16)
                ob[k % 3, rows, :] = (
                    esum[rank, rows, :].astype(F32)
                    + came[rank, rows, :].astype(F32)
                    + ebuf[rank, rows, :].astype(F32)
                )

            loop(plan.ub, 16, body)

    def early_done(k, zo, rank):
        @pl.when(z == 3 - zo)
        def _():
            early_copy(rank, s).wait_send()

    hq = plan.uq // 2

    def q_rows(k, h):
        return gq.at[pl.ds(pl.multiple_of(k * plan.uq + h * hq, hq), hq)]

    def q_sides(k, act):
        tc, ro, j = k % rn, k // 3, k // rn
        for h in range(2):
            @pl.when((z > 0) & (r != tc))
            def _():
                slot = lax.rem(tc - r + rn, rn) - 1
                act(
                    remote(
                        q_rows(k, h), qside.at[slot, 2 * j + h], qo_s.at[2 * k + h],
                        qs_r.at[slot, 2 * j + h], z * rn + tc, t,
                    )
                )

            @pl.when((z == 0) & (r != ro) & (r != tc))
            def _():
                slot = lax.rem(ro - r + rn, rn) - 1
                act(
                    remote(
                        q_rows(k, h), qpeer.at[slot, 2 * (k % 3) + h], qo_s.at[2 * k + h],
                        qp_r.at[slot, 2 * (k % 3) + h], ro, t,
                    )
                )

    def q_down(at, to):
        return remote(qstage.at[at], qchain.at[at], qc_s.at[at], qc_r.at[at], to, t)

    def q_chain(top):
        for j in range(2):
            k = r + rn * j
            for h in range(2):
                at = 2 * j + h

                @pl.when(z == ZN - 1 if top else (z > 0) & (z < ZN - 1))
                def _():
                    for d in range(1, rn):
                        remote(
                            q_rows(k, h), qside.at[d - 1, at], qo_s.at[0], qs_r.at[d - 1, at], s, t
                        ).wait_recv()
                    if not top:
                        q_down(at, s).wait_recv()
                    unit = q_rows(k, h)

                    def body(row):
                        rows = pl.ds(row, 16)
                        total = unit[rows, :].astype(F32)
                        for d in range(1, rn):
                            total = total + qside[d - 1, at, rows, :].astype(F32)
                        if not top:
                            total = total + qchain[at, rows, :].astype(F32)
                        qstage[at, rows, :] = total.astype(BF16)

                    loop(hq, 16, body)
                    q_down(at, s - rn).start()

    def q_last_copy(k, h):
        tc, ro, j = k % rn, k // 3, k // rn
        slot = (ro - tc + rn) % rn - 1
        return remote(
            qstage.at[2 * j + h], qpeer.at[slot, 2 * (k % 3) + h], qc_s.at[2 * j + h],
            qp_r.at[slot, 2 * (k % 3) + h], ro, t,
        )

    def q_ground(act):
        for k in range(plan.nq):
            if k % rn != k // 3:
                @pl.when((z == 0) & (r == k % rn))
                def _():
                    for h in range(2):
                        act(k, h)

    def q_turn(k, h):
        at = 2 * (k // rn) + h
        q_down(at, s).wait_recv()
        unit = q_rows(k, h)

        def body(row):
            rows = pl.ds(row, 16)
            qstage[at, rows, :] = (
                unit[rows, :].astype(F32) + qchain[at, rows, :].astype(F32)
            ).astype(BF16)

        loop(hq, 16, body)
        q_last_copy(k, h).start()

    def q_final():
        for k in range(plan.nq):
            @pl.when((z == 0) & (r == k // 3))
            def _():
                straight = k % rn == k // 3
                for h in range(2):
                    at = 2 * (k // rn) + h
                    if straight:
                        q_down(at, s).wait_recv()
                    for d in range(1, rn):
                        remote(
                            q_rows(k, h), qpeer.at[d - 1, 2 * (k % 3) + h], qo_s.at[0],
                            qp_r.at[d - 1, 2 * (k % 3) + h], s, t,
                        ).wait_recv()
                    unit = q_rows(k, h)

                    def body(row):
                        rows = pl.ds(row, 16)
                        total = unit[rows, :].astype(F32)
                        for d in range(1, rn):
                            total = total + qpeer[d - 1, 2 * (k % 3) + h, rows, :].astype(F32)
                        if straight:
                            total = total + qchain[at, rows, :].astype(F32)
                        oq[k % 3, pl.ds(h * hq + row, 16), :] = total

                    loop(hq, 16, body)

    start = lambda copy: copy.start()
    done = lambda copy: copy.wait_send()
    late_sides(start)
    early_units(early_send)
    for zo in range(2):
        for i in range(3):
            late_step(zo, i, ZN - 1, False, False, False)
    for i in range(3):
        late_step(1, i, 0, False, False, False)

    for d in range(1, ZN):
        zs = lax.rem(z + d, ZN)
        remote(dq.at[0], q_in.at[zs], q_s.at[0], q_r.at[zs], s, t).wait_recv()
        remote(stage.at[d], kv_in.at[zs], k_s.at[0], k_r.at[zs], s, t).wait_recv()
    for p in range(2):
        cols = slice(p * LANES, (p + 1) * LANES)
        a, b = q_in[2 * p], q_in[2 * p + 1]
        dqkv[:TOK_FRAME, cols] = jnp.concatenate([a[:, :HEAD], b[:, :HEAD]], axis=1)
        dqkv[TOK_FRAME:, cols] = jnp.concatenate([a[:, HEAD:], b[:, HEAD:]], axis=1)
        a, b = kv_in[2 * p], kv_in[2 * p + 1]
        dqkv[:, HD + p * LANES : HD + (p + 1) * LANES] = jnp.concatenate(
            [a[:, :HEAD], b[:, :HEAD]], axis=1
        )
        dqkv[:, 2 * HD + p * LANES : 2 * HD + (p + 1) * LANES] = jnp.concatenate(
            [a[:, HEAD:], b[:, HEAD:]], axis=1
        )

    for m in range(TILES):
        gq[m * TILE : (m + 1) * TILE, :] = mm_tn(
            first_in[:, m * TILE : (m + 1) * TILE], dqkv[...]
        ).astype(BF16)
        for k in range(m * plan.nq // TILES, (m + 1) * plan.nq // TILES):
            q_sides(k, start)

    def c_copy(w):
        return remote(csend.at[w], crecv.at[w], c_s.at[w], c_r.at[w], s, sib)

    def y_copy(w):
        return remote(ysend.at[w], yrecv.at[w], y_s.at[w], y_r.at[w], s, across)

    def pass_on(w):
        c_copy(w).wait_recv()
        ysend[w] = (own[w] + crecv[w].astype(F32)).astype(BF16)
        y_copy(w).start()

    for w in range(TILES):
        weights = wq[w * TILE : (w + 1) * TILE, :]
        csend[w] = mm_nt(dqkv[pl.ds(theirs, TOK_FRAME), :], weights).astype(BF16)
        c_copy(w).start()
        own[w] = mm_nt(dqkv[pl.ds(mine, TOK_FRAME), :], weights)
        if w:
            pass_on(w - 1)
    pass_on(TILES - 1)

    for here in (2, 1):
        for zo in range(2):
            if zo != here:
                for i in range(3):
                    late_step(zo, i, here, True, False, False)
    q_chain(True)
    q_chain(False)

    for w in range(TILES):
        y_copy(w).wait_recv()
    row = lambda part: mod[pl.ds(c * 6 + part, 1), :]
    dm[...] = jnp.zeros_like(dm)

    def input_rows(at):
        rows = pl.ds(at, 64)
        tok_rows = pl.ds(mine + at, 64)
        grads = jnp.concatenate(
            [ysend[w, rows].astype(F32) + yrecv[w, rows].astype(F32) for w in range(TILES)], axis=1
        )
        normed, inverse = normalize(tokens[tok_rows, :].astype(F32))
        add_to(dm, 0, grads)
        add_to(dm, 1, grads * normed)
        igrad[tok_rows, :] = dmid[rows, :] + norm_back(grads * (1.0 + row(1)), normed, inverse)

    loop(TOK_FRAME, 64, input_rows)

    def e_copy(base):
        ref = igrad.at[pl.ds(base, TOK_FRAME)]
        return remote(ref, ref, e_s, e_r, s, sib)

    e_copy(mine).start()

    for block in range(6 * D // LANES):
        part, at = block // (D // LANES), block % (D // LANES)
        src = dm if part < 2 else dm4
        lane = slice(at * LANES, (at + 1) * LANES)
        from_row = part if part < 2 else part - 2
        dm3[block // MCOLS, block % MCOLS : block % MCOLS + 1, :] = src[from_row : from_row + 1, lane]
    h_copy = lambda frame: remote(dm3.at[sib], dboth.at[frame], h_s, h_r, s, sib)
    h_copy(c).start()
    dboth[c] = dm3[t]
    h_copy(1 - c).wait_recv()

    def m_copy(src):
        return remote(dboth, dall.at[s], m_s.at[src - plan.first_mod], m_r.at[s], src, t)

    for src in range(plan.first_mod, n):
        @pl.when(s == src)
        def _():
            dall[s] = dboth[...]

        @pl.when(s != src)
        def _():
            m_copy(src).start()

    q_ground(q_turn)
    for i in range(3):
        late_step(1, i, 1, True, True, True)
        late_step(0, i, 0, True, False, True)
    early_units(early_final)
    q_final()

    @pl.when(s >= plan.first_mod)
    def _():
        for d in range(1, n):
            other = lax.rem(s + d, n)
            remote(dboth, dall.at[other], m_s.at[0], m_r.at[other], s, t).wait_recv()

    e_copy(theirs).wait_recv()
    for d in range(1, ZN):
        q_copy(d).wait_send()
        kv_copy(d).wait_send()
    for d in order:
        for e in range(1, rn):
            side_copy(d, e).wait_send()
    late_close()
    early_units(early_done)
    for k in range(plan.nq):
        q_sides(k, done)

    @pl.when(z > 0)
    def _():
        for at in range(4):
            q_down(at, s).wait_send()

    q_ground(lambda k, h: q_last_copy(k, h).wait_send())
    for w in range(TILES):
        c_copy(w).wait_send()
        y_copy(w).wait_send()
    e_copy(mine).wait_send()
    h_copy(c).wait_send()
    for src in range(plan.first_mod, n):
        @pl.when(s != src)
        def _():
            m_copy(src).wait_send()


def tail_part(plan, dq, dkv, first_in, wq, tokens, dmid, mod_rows, dm4, gb, early, cid):
    n, rn = plan.n, plan.r
    rows = F_DEV * TOK_FRAME
    tiles = pltpu.VMEM((TILES, TOK_FRAME, TILE), BF16)
    mods = n - plan.first_mod
    return call(
        functools.partial(tail_kernel, plan),
        (
            jax.ShapeDtypeStruct((rows, D), F32),
            jax.ShapeDtypeStruct((3, plan.uq, QKV), F32),
            jax.ShapeDtypeStruct((3, plan.ub, D), F32),
            jax.ShapeDtypeStruct((n, F_DEV, 16, LANES), F32),
        ),
        [
            pltpu.VMEM((ZN, rows, LANES), BF16),
            pltpu.VMEM((rn - 1, ZN, rows, LANES), BF16),
            pltpu.VMEM((ZN, TOK_FRAME, LANES), BF16),
            pltpu.VMEM((ZN, rows, LANES), BF16),
            pltpu.VMEM((rows, QKV), BF16),
            pltpu.VMEM((D, QKV), BF16),
            pltpu.VMEM((TILES, TOK_FRAME, TILE), F32), tiles, tiles, tiles, tiles,
            pltpu.VMEM((8, D), F32),
            pltpu.VMEM((TP, 16, LANES), F32),
            pltpu.VMEM((F_DEV, 16, LANES), F32),
            pltpu.VMEM((rn - 1, 6, plan.ub, D), BF16),
            pltpu.VMEM((2, 6, plan.ub, D), BF16),
            pltpu.VMEM((plan.ranks, plan.ub, D), BF16),
            pltpu.VMEM((plan.ranks, plan.ub, D), BF16),
            pltpu.VMEM((rn - 1, 4, plan.uq // 2, QKV), BF16),
            pltpu.VMEM((rn - 1, 6, plan.uq // 2, QKV), BF16),
            pltpu.VMEM((4, plan.uq // 2, QKV), BF16),
            pltpu.VMEM((4, plan.uq // 2, QKV), BF16),
            DMA((ZN - 1,)), DMA((ZN,)), DMA((ZN - 1,)), DMA((ZN,)), DMA((ZN, rn - 1)), DMA((ZN, rn - 1)),
            DMA((TILES,)), DMA((TILES,)), DMA((TILES,)), DMA((TILES,)),
            DMA, DMA, DMA, DMA, DMA((mods,)), DMA((n,)),
            DMA((6, rn - 1)), DMA((6, rn - 1)), DMA((6,)), DMA((6, 2)),
            DMA((plan.ranks,)), DMA((plan.ranks,)), DMA((2 * plan.nq,)),
            DMA((rn - 1, 4)), DMA((rn - 1, 6)), DMA((4,)), DMA((4,)),
        ],
        [VM] * 12,
        cid,
        name="tail_part",
    )(dq, dkv, first_in, wq, tokens, dmid, mod_rows, dm4, gb, *early)


def adam_kernel(plan, meta, oq, ob, cond, dmod, master, one, two, average, n_master, n_one, n_two, n_average):
    s = meta[0]
    rate = RATE_FACTOR * D ** (-0.5)
    scale_one = 1.0 / (1.0 - BETA_FIRST**STEP)
    scale_two = 1.0 / (1.0 - BETA_SECOND**STEP)

    def update(rows, grad):
        first = BETA_FIRST * one[rows, :] + (1.0 - BETA_FIRST) * grad
        second = BETA_SECOND * two[rows, :] + (1.0 - BETA_SECOND) * grad * grad
        weight = master[rows, :]
        weight = weight - rate * (
            (first * scale_one) / (jnp.sqrt(second * scale_two) + ADAM_EPSILON)
            + WEIGHT_DECAY * weight
        )
        n_one[rows, :] = first
        n_two[rows, :] = second
        n_master[rows, :] = weight
        n_average[rows, :] = AVERAGE_RATE * average[rows, :] + (1.0 - AVERAGE_RATE) * weight

    for i in range(3):
        k = 3 * s + i
        base = i * plan.flat_rows

        def from_matrix(kind):
            src = oq if kind == "q" else ob
            rows = plan.uq if kind == "q" else plan.ub
            cols = (QKV if kind == "q" else D) // LANES
            for j in range(cols):
                update(
                    pl.ds(base + j, rows, stride=cols), src[i, :, j * LANES : (j + 1) * LANES]
                )

        by_kind(plan, k, from_matrix)

        @pl.when(k >= plan.nb)
        def _():
            at = cond[k - plan.nb]
            for j in range(MCOLS):
                update(
                    pl.ds(base + j, plan.um, stride=MCOLS),
                    mm(at, dmod[pl.ds(j, plan.frames, stride=16), :].astype(BF16)),
                )


def adam(plan, meta, oq, ob, cond_rows, dmod, master, one, two, average):
    shape = jax.ShapeDtypeStruct(master.shape, F32)
    return call(
        functools.partial(adam_kernel, plan),
        (shape,) * 4,
        [],
        [SM] + [VM] * 8,
        name="adam",
    )(meta, oq, ob, cond_rows, dmod, master, one, two, average)


def local(
    tokens,
    grad_out,
    noise_level,
    context_mask,
    frame_clip,
    level_table,
    master,
    moment_one,
    moment_two,
    average,
):
    plan = Plan(lax.axis_size("seq"))
    s = lax.axis_index("seq")
    t = lax.axis_index("tp")
    flat = lambda x: x.reshape(-1, LANES)

    effective = noise_level * (1 - context_mask)
    one_hot = (
        effective[:, None] == jnp.arange(level_table.shape[0], dtype=jnp.int32)[None, :]
    ).astype(BF16)
    condition = jax.nn.silu(mm(one_hot, level_table)).astype(BF16)
    cond_units = condition.reshape(plan.frames, plan.nm, plan.um).transpose(1, 0, 2)

    wq, w_out, w_side, w_early, own_b, mod_rows, first_in, q_mine, kv_all = head_part(
        plan, flat(master), cond_units, tokens, 0
    )
    rn, n = plan.r, plan.n
    w_below = lax.ppermute(own_b, "seq", [(i, i + rn) for i in range(rn, 3 * rn)])
    wo_across = lax.ppermute(
        w_out.reshape(-1, D)[:HD], "tp", [(i, (i + 2) % TP) for i in range(TP)]
    )
    w_beside = jnp.stack(
        [
            lax.ppermute(
                w_side, "seq", [(i, i // rn * rn + (i + d) % rn) for i in range(n)]
            )
            for d in range(1, rn)
        ]
    )
    meta = jnp.concatenate([frame_clip, lax.rem(s, plan.r)[None]]).astype(jnp.int32)
    o_mine, o_rows, lse = attend(plan, meta, q_mine, kv_all)
    result, grads_b, early_sum, do_mine, middle_grad, mod_four = middle_part(
        plan, o_mine, wo_across, (w_out, w_side, w_beside, w_early, w_below),
        tokens, grad_out, mod_rows, 2
    )
    dq_mine, dkv_all = attend_back(plan, meta, q_mine, kv_all, do_mine, o_rows, lse)
    e_above = lax.ppermute(early_sum, "seq", [(i, i - rn) for i in range(3 * rn, n)])
    e_below = lax.ppermute(early_sum, "seq", [(i, i + rn) for i in range(rn)])
    input_grad, own_q, own_b, mod_all = tail_part(
        plan, dq_mine, dkv_all, first_in, wq, tokens, middle_grad, mod_rows, mod_four, grads_b,
        (early_sum, e_above, e_below), 3
    )
    updated = adam(
        plan,
        s[None].astype(jnp.int32),
        own_q,
        own_b,
        cond_units.transpose(0, 2, 1),
        flat(mod_all),
        flat(master),
        flat(moment_one),
        flat(moment_two),
        flat(average),
    )
    new_master, new_one, new_two, new_average = [x.reshape(master.shape) for x in updated]
    return (result, input_grad, new_master, new_one, new_two, new_average)


def solution(mesh):
    token_spec = P("seq", None)
    weight_spec = P("tp", "seq")
    in_specs = (token_spec, token_spec, P(), P(), P(), P()) + (weight_spec,) * 4
    out_specs = (token_spec, token_spec) + (weight_spec,) * 4
    return jax.shard_map(local, mesh=mesh, in_specs=in_specs, out_specs=out_specs, check_vma=False)
```

```python
import functools

import jax
import jax.numpy as jnp
from jax import lax
from jax.experimental import pallas as pl
from jax.experimental.pallas import tpu as pltpu
from jax.sharding import PartitionSpec as P

D = 1024
HEADS = 16
HEAD = 64
FF = 4096
TOK_FRAME = 384
STEP = 7
TP = 4
ZN = 4
HD = HEADS * HEAD // TP
QKV = 3 * HD
FT = FF // TP
MT = 6 * D // TP
F_DEV = 2
BROWS = HD + 2 * FT
LANES = 128
MCOLS = MT // LANES
PACK = TOK_FRAME // 2
TILE = 256
TILES = D // TILE
CUTS = 4

NORM_EPSILON = 1e-06
RATE_FACTOR = 2.5
BETA_FIRST = 0.5
BETA_SECOND = 0.5
ADAM_EPSILON = 1e-08
WEIGHT_DECAY = 0.01
AVERAGE_RATE = 0.9
GELU_A = 0.7978845608028654
GELU_B = 0.044715
MESH = pl.DeviceIdType.MESH
VM = pl.BlockSpec(memory_space=pltpu.VMEM)
SM = pl.BlockSpec(memory_space=pltpu.SMEM)
ANY = pl.BlockSpec(memory_space=pl.ANY)
DMA = pltpu.SemaphoreType.DMA
F32 = jnp.float32
BF16 = jnp.bfloat16
VMEM_LIMIT = 60 * 2**20


def mm(left, right):
    return jnp.dot(left, right, preferred_element_type=F32)


def mm_tn(left, right):
    return lax.dot_general(left, right, (((0,), (0,)), ((), ())), preferred_element_type=F32)


def mm_nt(left, right):
    return lax.dot_general(left, right, (((1,), (1,)), ((), ())), preferred_element_type=F32)


def normalize(rows):
    centred = rows - jnp.mean(rows, axis=1, keepdims=True)
    inverse = lax.rsqrt(jnp.mean(centred * centred, axis=1, keepdims=True) + NORM_EPSILON)
    return (centred * inverse, inverse)


def norm_back(grads, normed, inverse):
    return inverse * (
        grads
        - jnp.mean(grads, axis=1, keepdims=True)
        - normed * jnp.mean(grads * normed, axis=1, keepdims=True)
    )


def loop(count, step, body):
    def turn(i, carry):
        body(pl.multiple_of(i * step, step))
        return carry

    lax.fori_loop(0, count // step, turn, 0)


def add_to(ref, row, values):
    ref[pl.ds(row, 1), :] += jnp.sum(values, axis=0, keepdims=True)


class Plan:
    def __init__(self, seq_count):
        self.n = seq_count
        self.r = seq_count // ZN
        self.shard = (D * QKV + BROWS * D + D * MT) // seq_count
        self.unit = self.shard // 3
        self.uq = self.unit // QKV
        self.ub = self.unit // D
        self.um = self.unit // MT
        self.nq = D // self.uq
        self.nb = self.nq + BROWS // self.ub
        self.nm = D // self.um
        self.first_mod = self.nb // 3
        self.half = (self.nq + self.nb) // 2
        self.flat_rows = self.unit // LANES
        self.frames = seq_count * F_DEV
        self.late = list(range(self.nq, self.half))
        self.early = list(range(self.half, self.nb))
        self.outs = self.late[: -(-HD // self.ub)]
        self.sided = self.late[len(self.outs) :]
        self.rank, self.ranks = self.ranked(self.early)
        self.late_rank, self.late_ranks = self.ranked(self.sided)
        self.grad_rank, self.grad_ranks = self.ranked(self.late)

    def ranked(self, units):
        seen, rank = {}, {}
        for k in units:
            column = self.home(k)[1]
            rank[k] = seen.get(column, 0)
            seen[column] = rank[k] + 1
        return rank, max(seen.values())

    def home(self, k):
        return (k // 3) // self.r, (k // 3) % self.r


def place(plan):
    s = lax.axis_index("seq")
    t = lax.axis_index("tp")
    return s, t, lax.div(s, plan.r), lax.rem(s, plan.r)


def remote(src, dst, send_sem, recv_sem, s, t):
    return pltpu.make_async_remote_copy(
        src_ref=src,
        dst_ref=dst,
        send_sem=send_sem,
        recv_sem=recv_sem,
        device_id=(s, t),
        device_id_type=MESH,
    )


def greet(peers):
    barrier = pltpu.get_barrier_semaphore()
    for s, t in peers:
        pl.semaphore_signal(barrier, inc=1, device_id=(s, t), device_id_type=MESH)
    pl.semaphore_wait(barrier, len(peers))


def by_kind(plan, k, act, low=0, high=None):
    high = plan.nb if high is None else high
    q_high, b_low = min(plan.nq, high), max(plan.nq, low)
    if low < q_high:
        @pl.when((k >= low) & (k < q_high))
        def _():
            act("q")

    if b_low < high:
        @pl.when((k >= b_low) & (k < high))
        def _():
            act("b")


def unit_of(plan, k, kind, wq, wb):
    if kind == "q":
        return wq.at[pl.ds(pl.multiple_of(k * plan.uq, plan.uq), plan.uq)]
    return wb.at[pl.ds(pl.multiple_of((k - plan.nq) * plan.ub, plan.ub), plan.ub)]


def call(kernel, outs, scratch, ins, cid=None, cost=None, name=None, out_specs=None):
    params = dict(vmem_limit_bytes=VMEM_LIMIT)
    if cid is not None:
        params.update(collective_id=cid, has_side_effects=True)
    return pl.pallas_call(
        kernel,
        out_shape=outs,
        in_specs=ins,
        out_specs=out_specs or jax.tree.map(lambda _: VM, outs),
        scratch_shapes=scratch,
        compiler_params=pltpu.CompilerParams(**params),
        cost_estimate=cost,
        name=name,
    )


def head_kernel(
    plan, master, cond, tokens,
    wq, w_out, w_side, w_early, own_b, mods, first_in, q_out, kv_out,
    tile, macc, mpart, mrecv, mod, norm, q_send, kv_send,
    qp_s, qc_s, q_r, wo_s, wo_r, ws_s, ws_r, we_s, we_r, loc_s, m_s, m_r, t_s, t_r, as_, ar, ks, kr, xs, xr,
):
    s, t, z, r = place(plan)
    n, rn = plan.n, plan.r
    greet(
        [(lax.rem(s + d, n), t) for d in range(1, n)]
        + [(s, lax.rem(t + d, TP)) for d in range(1, TP)]
    )
    start = lambda copy: copy.start()
    done = lambda copy: copy.wait_send()
    cut = plan.uq // CUTS

    def q_rows(k, h):
        return wq.at[pl.ds(pl.multiple_of(k * plan.uq + h * cut, cut), cut)]

    def q_copy(k, h, sem, to_s):
        ref = q_rows(k, h)
        return remote(ref, ref, sem, q_r.at[CUTS * k + h], to_s, t)

    def q_arrived(k, h):
        q_copy(k, h, qc_s.at[0, 0], s).wait_recv()

    def column(j):
        return r + rn * lax.rem(j + r, 2)

    def q_own(i, act):
        k = 3 * s + i

        @pl.when(k < plan.nq)
        def _():
            for h in range(CUTS):
                for d in range(1, rn):
                    act(q_copy(k, h, qp_s.at[CUTS * i + h, d - 1], lax.rem(r + d, rn)))

    def q_line(act, wait, whole=False):
        for j in range(2):
            k = column(j)
            for h in range(CUTS):
                if wait:
                    @pl.when((z > 0) | (lax.div(k, 3) != r))
                    def _():
                        q_arrived(k, h)

                @pl.when((z < ZN - 1) & ((z > 0) | (lax.div(k, 3) != r) | whole))
                def _():
                    act(q_copy(k, h, qc_s.at[CUTS * j + h, 0], s + rn))

                @pl.when(z > 0)
                def _():
                    for d in range(1, rn):
                        act(
                            q_copy(
                                k, h, qc_s.at[CUTS * j + h, d], z * rn + lax.rem(r + d, rn)
                            )
                        )

    def slot(k):
        if k in plan.outs:
            at = k - plan.nq
            return w_out.at[at], wo_s.at[at], wo_r.at[at]
        if k in plan.sided:
            at = plan.late_rank[k]
            return w_side.at[at], ws_s.at[at], ws_r.at[at]
        return w_early.at[k - plan.half], we_s.at[plan.rank[k]], we_r.at[k - plan.half]

    def along(k, src, act, up):
        dst, send_sem, recv_sem = slot(k)
        if up and k < plan.half:
            @pl.when(z < ZN - 1)
            def _():
                act(remote(src, dst, send_sem.at[0], recv_sem, s + rn, t))

        if not up:
            @pl.when(z > 0)
            def _():
                act(remote(src, dst, send_sem.at[1], recv_sem, s - rn, t))

    def beside(k, src, act):
        if k in plan.sided:
            return
        dst, send_sem, recv_sem = slot(k)
        for d in range(1, rn):
            act(
                remote(
                    src, dst, send_sem.at[1 + d], recv_sem, z * rn + lax.rem(r + d, rn), t
                )
            )

    def arrived(k):
        dst, send_sem, recv_sem = slot(k)
        remote(own_b.at[0], dst, send_sem.at[0], recv_sem, s, t).wait_recv()

    def keep(k):
        return pltpu.make_async_copy(own_b.at[k % 3], slot(k)[0], loc_s.at[k % 3])

    def owned(units, act):
        for k in units:
            @pl.when(s == k // 3)
            def _():
                act(k, own_b.at[k % 3])

    def pass_along(units, d, act, wait):
        for k in units:
            zo, ro = plan.home(k)
            if k < plan.half and zo + d < ZN:
                @pl.when((r == ro) & (z == zo + d))
                def _():
                    if wait:
                        arrived(k)
                    along(k, slot(k)[0], act, True)
                    beside(k, slot(k)[0], act)

            if zo - d >= 0:
                @pl.when((r == ro) & (z == zo - d))
                def _():
                    if wait:
                        arrived(k)
                    along(k, slot(k)[0], act, False)
                    beside(k, slot(k)[0], act)

    units = plan.late + plan.early
    first_up = [k for k in plan.late if k % 3 == 0 and plan.home(k)[0] > 0]
    later_up = [k for k in plan.late if k not in first_up]

    def fill(i, kind):
        k = 3 * s + i
        base = i * plan.flat_rows
        rows, cols = (plan.uq, QKV // LANES) if kind == "q" else (plan.ub, D // LANES)
        at = pl.multiple_of(k * plan.uq, plan.uq)
        for j in range(cols):
            values = master[pl.ds(base + j, rows, stride=cols), :].astype(BF16)
            if kind == "q":
                wq[pl.ds(at, rows), j * LANES : (j + 1) * LANES] = values
            else:
                own_b[i, :, j * LANES : (j + 1) * LANES] = values

    for away in (True, False):
        for i in range(3):
            k = 3 * s + i

            @pl.when((k < plan.nq) & ((lax.rem(k, rn) != r) == away))
            def _():
                fill(i, "q")
                q_own(i, start)
                if not away:
                    at = lax.div(k, rn)
                    slot_j = lax.rem(at + r, 2)
                    for h in range(CUTS):
                        q_copy(k, h, qc_s.at[CUTS * slot_j + h, 0], s + rn).start()

    for i in range(3):
        @pl.when((3 * s + i >= plan.nq) & (3 * s + i < plan.nb))
        def _():
            fill(i, "b")

    @pl.when(z == 0)
    def _():
        q_line(start, True)

    owned(units, lambda k, src: along(k, src, start, False))
    owned(first_up, lambda k, src: along(k, src, start, True))
    owned(units, lambda k, src: keep(k).start())

    macc[...] = jnp.zeros_like(macc)
    for i in range(3):
        k = 3 * s + i
        base = i * plan.flat_rows

        @pl.when(k >= plan.nb)
        def _():
            for j in range(MCOLS):
                tile[:, j * LANES : (j + 1) * LANES] = master[
                    pl.ds(base + j, plan.um, stride=MCOLS), :
                ].astype(BF16)
            macc[...] += mm(cond[k - plan.nb], tile[...])

    fm = plan.first_mod

    def m_copy(d):
        to = lax.rem(s + d, n)
        return remote(mpart.at[to], mrecv.at[s - fm], m_s.at[d - 1], m_r.at[s - fm], to, t)

    @pl.when(s >= fm)
    def _():
        for f in range(plan.frames):
            for j in range(MCOLS):
                mpart[f // F_DEV, pl.ds((f % F_DEV) * MCOLS + j, 1), :] = macc[
                    pl.ds(f, 1), j * LANES : (j + 1) * LANES
                ]
        mrecv[s - fm] = mpart[s]
        for d in range(1, n):
            m_copy(d).start()

    def norm_rows(at):
        rows = pl.ds(at, 64)
        norm[rows, :] = normalize(tokens[rows, :].astype(F32))[0]

    loop(F_DEV * TOK_FRAME, 64, norm_rows)

    @pl.when(z > 0)
    def _():
        q_line(start, True)

    owned(plan.outs, lambda k, src: along(k, src, start, True))
    owned([k for k in later_up if k not in plan.outs], lambda k, src: along(k, src, start, True))
    owned(units, lambda k, src: beside(k, src, start))
    pass_along(first_up + plan.early, 1, start, True)

    for src in range(fm, n):
        @pl.when(s != src)
        def _():
            remote(mpart.at[0], mrecv.at[src - fm], m_s.at[0], m_r.at[src - fm], s, t).wait_recv()

    total = mrecv[0]
    for src in range(1, n - fm):
        total = total + mrecv[src]
    mod[t] = total

    def t_copy(d):
        return remote(mod.at[t], mod.at[t], t_s.at[d - 1], t_r.at[t], s, lax.rem(t + d, TP))

    for d in range(1, TP):
        t_copy(d).start()
    for d in range(1, TP):
        other = lax.rem(t + d, TP)
        remote(mod.at[t], mod.at[other], t_s.at[0], t_r.at[other], s, t).wait_recv()
    for f in range(F_DEV):
        for block in range(TP * MCOLS):
            part, at = block // (D // LANES), block % (D // LANES)
            mods[f * 6 + part : f * 6 + part + 1, at * LANES : (at + 1) * LANES] = mod[
                block // MCOLS, f * MCOLS + block % MCOLS : f * MCOLS + block % MCOLS + 1, :
            ]

    def affine(f):
        def body(at):
            rows = pl.ds(f * TOK_FRAME + at, 64)
            first_in[rows, :] = (
                norm[rows, :] * (1.0 + mods[f * 6 + 1 : f * 6 + 2, :]) + mods[f * 6 : f * 6 + 1, :]
            ).astype(BF16)

        loop(TOK_FRAME, 64, body)

    for f in range(F_DEV):
        affine(f)

    for k in range(plan.nq):
        for h in range(CUTS):
            if rn > 1:
                at_zero = (z == 0) & (k // 3 != r) & (k % rn != r)

                @pl.when(at_zero | (z > 0) & (k % rn != r))
                def _():
                    q_arrived(k, h)

    keys = mm(first_in[...], wq[:, HD : 2 * HD]).astype(BF16)
    values = mm(first_in[...], wq[:, 2 * HD :]).astype(BF16)
    for h in range(ZN):
        cols = slice(h * HEAD, (h + 1) * HEAD)
        kv_send[h] = jnp.concatenate([keys[:, cols], values[:, cols]], axis=1)

    def kv_copy(d):
        h = lax.rem(z + d, ZN)
        return remote(kv_send.at[h], kv_out.at[s], ks.at[d - 1], kr.at[z], h * rn + r, t)

    def a_copy(d):
        h = lax.rem(z + d, ZN)
        return remote(q_send.at[h], q_out.at[z], as_.at[d - 1], ar.at[z], h * rn + r, t)

    def side_copy(zs, e):
        at = zs * rn + r
        ref = kv_out.at[at]
        return remote(ref, ref, xs.at[zs, e - 1], xr.at[at], z * rn + lax.rem(r + e, rn), t)

    for d in range(1, ZN):
        kv_copy(d).start()
    kv_out[s] = kv_send[z]
    for e in range(1, rn):
        side_copy(z, e).start()
    queries = mm(first_in[...], wq[:, :HD]).astype(BF16)
    for h in range(ZN):
        cols = slice(h * HEAD, (h + 1) * HEAD)
        q_send[h] = jnp.concatenate([queries[:TOK_FRAME, cols], queries[TOK_FRAME:, cols]], axis=1)
    for d in range(1, ZN):
        a_copy(d).start()
    q_out[z] = q_send[z]

    rest = [k for k in plan.sided if k not in first_up]
    pass_along(plan.outs + rest, 1, start, True)
    pass_along(plan.early, 2, start, True)
    for d in range(1, ZN):
        zs = lax.rem(z + d, ZN)
        remote(kv_send.at[0], kv_out.at[zs * rn + r], ks.at[0], kr.at[zs], s, t).wait_recv()
        for e in range(1, rn):
            side_copy(zs, e).start()
        if d > 1:
            pass_along(plan.outs, d, start, True)
    for d in range(2, ZN):
        pass_along(plan.sided, d, start, True)
    pass_along(plan.early, 3, start, True)
    for d in range(1, ZN):
        zs = lax.rem(z + d, ZN)
        remote(q_send.at[0], q_out.at[zs], as_.at[0], ar.at[zs], s, t).wait_recv()
    for e in range(1, rn):
        for zs in range(ZN):
            at = zs * rn + lax.rem(r + e, rn)
            remote(kv_out.at[at], kv_out.at[at], xs.at[0, 0], xr.at[at], s, t).wait_recv()
    for k in plan.outs + plan.early:
        zo, ro = plan.home(k)

        @pl.when((r != ro) & ((z <= zo) | (k in plan.outs)))
        def _():
            arrived(k)


    for i in range(3):
        q_own(i, done)
    q_line(done, False, True)
    owned(units, lambda k, src: along(k, src, done, False))
    owned(plan.late, lambda k, src: along(k, src, done, True))
    owned(units, lambda k, src: beside(k, src, done))
    owned(units, lambda k, src: keep(k).wait())
    for d in range(1, ZN):
        pass_along(units, d, done, False)

    @pl.when(s >= fm)
    def _():
        for d in range(1, n):
            m_copy(d).wait_send()

    for d in range(1, TP):
        t_copy(d).wait_send()
    for d in range(1, ZN):
        kv_copy(d).wait_send()
        a_copy(d).wait_send()
    for zs in range(ZN):
        for e in range(1, rn):
            side_copy(zs, e).wait_send()


def head_part(plan, master, cond_units, tokens, cid):
    n, rn = plan.n, plan.r
    mrows = F_DEV * MCOLS
    rows = F_DEV * TOK_FRAME
    mods = n - plan.first_mod
    return call(
        functools.partial(head_kernel, plan),
        (
            jax.ShapeDtypeStruct((D, QKV), BF16),
            jax.ShapeDtypeStruct((len(plan.outs), plan.ub, D), BF16),
            jax.ShapeDtypeStruct((plan.late_ranks, plan.ub, D), BF16),
            jax.ShapeDtypeStruct((len(plan.early), plan.ub, D), BF16),
            jax.ShapeDtypeStruct((3, plan.ub, D), BF16),
            jax.ShapeDtypeStruct((F_DEV * 6, D), F32),
            jax.ShapeDtypeStruct((rows, D), BF16),
            jax.ShapeDtypeStruct((ZN, TOK_FRAME, LANES), BF16),
            jax.ShapeDtypeStruct((n, rows, LANES), BF16),
        ),
        [
            pltpu.VMEM((plan.um, MT), BF16),
            pltpu.VMEM((plan.frames, MT), F32),
            pltpu.VMEM((n, mrows, LANES), F32),
            pltpu.VMEM((mods, mrows, LANES), F32),
            pltpu.VMEM((TP, mrows, LANES), F32),
            pltpu.VMEM((rows, D), F32),
            pltpu.VMEM((ZN, TOK_FRAME, LANES), BF16),
            pltpu.VMEM((ZN, rows, LANES), BF16),
            DMA((3 * CUTS, rn - 1)), DMA((2 * CUTS, rn)), DMA((CUTS * plan.nq,)),
            DMA((len(plan.outs), rn + 1)), DMA((len(plan.outs),)),
            DMA((plan.late_ranks, 2)), DMA((plan.late_ranks,)),
            DMA((plan.ranks, rn + 1)), DMA((len(plan.early),)), DMA((3,)),
            DMA((n - 1,)), DMA((mods,)), DMA((TP - 1,)), DMA((TP,)),
            DMA((ZN - 1,)), DMA((ZN,)), DMA((ZN - 1,)), DMA((ZN,)), DMA((ZN, rn - 1)), DMA((n,)),
        ],
        [VM] * 3,
        cid,
        out_specs=(VM, ANY, ANY, ANY, VM, VM, VM, VM, VM),
        name="head_part",
    )(master, cond_units, tokens)


def padded(rows, low):
    zero = jnp.zeros_like(rows)
    return jnp.concatenate([rows, zero] if low else [zero, rows], axis=1)


def attend_kernel(plan, meta, q, kv, o, ot, lse, m_ref, l_ref, acc):
    r = meta[plan.frames]
    scale = HEAD ** (-0.5)

    def group(zq, carry):
        for f in range(F_DEV):
            frame = (zq * plan.r + r) * F_DEV + f
            clip = meta[frame]
            pack = q[zq]
            qz = padded(pack[:, f * HEAD : (f + 1) * HEAD], True) * jnp.asarray(scale, BF16)
            m_ref[...] = jnp.full_like(m_ref, -1e30)
            l_ref[...] = jnp.zeros_like(l_ref)
            acc[...] = jnp.zeros_like(acc)

            def block(j, inner):
                @pl.when(meta[j] == clip)
                def _():
                    rows = pl.multiple_of(lax.rem(j, F_DEV) * TOK_FRAME, TOK_FRAME)
                    keys = kv[lax.div(j, F_DEV), pl.ds(rows, TOK_FRAME), :]
                    st = mm_nt(keys, qz)
                    m_old = m_ref[...]
                    m_new = jnp.maximum(m_old, jnp.max(st, axis=0, keepdims=True))
                    p = jnp.exp(st - m_new)
                    alpha = jnp.exp(m_old - m_new)
                    m_ref[...] = m_new
                    l_ref[...] = l_ref[...] * alpha + jnp.sum(p, axis=0, keepdims=True)
                    acc[...] = acc[...] * alpha + mm_tn(keys, p.astype(BF16))

                return inner

            lax.fori_loop(0, frame + 1, block, 0)
            total = l_ref[...]
            out = acc[HEAD:, :] / total
            ot[zq * F_DEV + f] = out
            lse[zq * F_DEV + f] = m_ref[...] + jnp.log(total)
            rows = out.T
            o[zq, f] = jnp.concatenate([rows[:PACK], rows[PACK:]], axis=1).astype(BF16)
        return carry

    lax.fori_loop(0, ZN, group, 0)


def attend(plan, meta, q, kv):
    frames = ZN * F_DEV
    return call(
        functools.partial(attend_kernel, plan),
        (
            jax.ShapeDtypeStruct((ZN, F_DEV, PACK, LANES), BF16),
            jax.ShapeDtypeStruct((frames, HEAD, TOK_FRAME), F32),
            jax.ShapeDtypeStruct((frames, 1, TOK_FRAME), F32),
        ),
        [
            pltpu.VMEM((1, TOK_FRAME), F32),
            pltpu.VMEM((1, TOK_FRAME), F32),
            pltpu.VMEM((LANES, TOK_FRAME), F32),
        ],
        [SM, VM, VM],
        cost=pl.CostEstimate(flops=2 * 10**10, bytes_accessed=6 * 10**7, transcendentals=10**7),
        name="attend",
    )(meta, q, kv)


def middle_kernel(
    plan, o_mine, wo_across, w_out, w_side, w_beside, w_early, w_below, tokens, grad_out, mod,
    result, late_own, late_send, esum, ebuf, do_out, dmid, dmod,
    gb, wb, eside, eend, wo, oall, attended, attn, mid, norm, inv, sin, hidden, dmlp, slopes, dup,
    own, csend, crecv, ysend, yrecv, dattn, dsend, dwo, wsend, wrecv,
    o_s, o_r, f_s, f_r, n_s, n_r, c_s, c_r, y_s, y_r, d_s, d_r, w_s, w_r, e_s, e_r, p_s, p_r, l_s, u_s, u_r, g_s, g_r, j_s, h_s, h_r, i_s, i_r,
):
    s, t, z, r = place(plan)
    rn = plan.r
    y = lax.div(t, 2)
    c = lax.rem(t, 2)
    sib = 2 * y + 1 - c
    across = lax.rem(t + 2, TP)
    mine = pl.multiple_of(c * TOK_FRAME, TOK_FRAME)
    theirs = pl.multiple_of((1 - c) * TOK_FRAME, TOK_FRAME)
    pairs = [(d, e) for d in range(ZN) for e in range(2)][1:]

    def partner(d, e):
        return lax.rem(z + d, ZN), (c if e == 0 else 1 - c)

    greet(
        [(partner(d, e)[0] * rn + r, 2 * y + partner(d, e)[1]) for d, e in pairs]
        + [(s, across)]
        + [(z * rn + lax.rem(r + d, rn), t) for d in range(1, rn)]
    )

    def home(k):
        return (k // 3) // rn, (k // 3) % rn, k - plan.half

    def w_rows(ref, k):
        return ref.at[pl.ds((k - plan.nq) * plan.ub, plan.ub)]

    def late_loads(act):
        for k in plan.late:
            sem = l_s.at[k - plan.nq]
            if k in plan.outs:
                act(pltpu.make_async_copy(w_out.at[k - plan.nq], w_rows(wb, k), sem))
            else:
                zo, ro = plan.home(k)
                rank = plan.late_rank[k]

                @pl.when(r == ro)
                def _():
                    act(pltpu.make_async_copy(w_side.at[rank], w_rows(wb, k), sem))

                @pl.when(r != ro)
                def _():
                    d = lax.rem(r - ro + rn, rn)
                    act(pltpu.make_async_copy(w_beside.at[d - 1, rank], w_rows(wb, k), sem))

    def loads(act):
        for k in plan.early:
            zo, ro, at = home(k)

            @pl.when(z <= zo)
            def _():
                act(pltpu.make_async_copy(w_early.at[at], w_rows(wb, k), l_s.at[len(plan.late) + at]))

            @pl.when((z == zo + 1) & (r == ro))
            def _():
                act(
                    pltpu.make_async_copy(
                        w_below.at[k % 3], w_rows(wb, k), l_s.at[len(plan.late) + at]
                    )
                )

    def rise(k, src, act):
        zo, ro, at = home(k)

        @pl.when(z < ZN - 1)
        def _():
            act(remote(src, w_rows(wb, k), u_s.at[at, 0], u_r.at[at], s + rn, t))

        for d in range(1, rn):
            act(
                remote(
                    src, w_rows(wb, k), u_s.at[at, d], u_r.at[at],
                    z * rn + lax.rem(r + d, rn), t,
                )
            )

    def risen(k):
        remote(w_below.at[0], w_rows(wb, k), u_s.at[0, 0], u_r.at[k - plan.half], s, t).wait_recv()

    def rises(act, first, wait):
        for k in plan.early:
            zo, ro, at = home(k)
            if first:
                @pl.when((z == zo + 1) & (r == ro))
                def _():
                    rise(k, w_below.at[k % 3], act)
            else:
                @pl.when((z > zo + 1) & (r == ro))
                def _():
                    if wait:
                        risen(k)
                    rise(k, w_rows(wb, k), act)

    def o_copy(d, e):
        zd, cd = partner(d, e)
        return remote(
            o_mine.at[zd, cd], oall.at[y * 8 + c * ZN + z], o_s.at[2 * d + e],
            o_r.at[c * ZN + z], zd * rn + r, 2 * y + cd,
        )

    def f_copy(slot):
        ref = oall.at[y * 8 + slot]
        return remote(ref, ref, f_s.at[slot], f_r.at[slot], s, across)

    def p_copy(i, tp):
        ref = wo.at[pl.ds(pl.multiple_of(tp * HD, HD), HD)]
        return remote(ref, ref, p_s.at[i], p_r.at[i], s, sib)

    for d, e in pairs:
        o_copy(d, e).start()
    start = lambda copy: copy.start()
    rises(start, True, False)
    late_loads(start)
    loads(start)
    late_loads(lambda copy: copy.wait())
    wo[pl.ds(pl.multiple_of(t * HD, HD), HD), :] = wb[:HD, :]
    p_copy(0, t).start()
    wo[pl.ds(pl.multiple_of(across * HD, HD), HD), :] = wo_across[...]
    p_copy(1, across).start()
    oall[y * 8 + c * ZN + z] = o_mine[z, c]
    f_copy(c * ZN + z).start()

    def d_mlp(f):
        def body(at):
            rows = pl.ds(f * TOK_FRAME + at, 64)
            dmlp[rows, :] = (grad_out[rows, :].astype(F32) * mod[f * 6 + 5 : f * 6 + 6, :]).astype(
                BF16
            )

        loop(TOK_FRAME, 64, body)

    for f in range(F_DEV):
        d_mlp(f)

    for d, e in pairs:
        zd, cd = partner(d, e)
        slot = cd * ZN + zd
        remote(o_mine.at[0, 0], oall.at[y * 8 + slot], o_s.at[0], o_r.at[slot], s, t).wait_recv()
        f_copy(slot).start()
    for slot in range(8):
        remote(
            oall.at[0], oall.at[(1 - y) * 8 + slot], f_s.at[slot], f_r.at[slot], s, t
        ).wait_recv()
    for m in range(HEADS // 2):
        a, b = oall[2 * m], oall[2 * m + 1]
        cols = slice(m * LANES, (m + 1) * LANES)
        attended[:PACK, cols] = jnp.concatenate([a[:, :HEAD], b[:, :HEAD]], axis=1)
        attended[PACK:, cols] = jnp.concatenate([a[:, HEAD:], b[:, HEAD:]], axis=1)

    p_copy(0, sib).wait_recv()
    p_copy(1, lax.rem(sib + 2, TP)).wait_recv()

    def attn_tile(at):
        attn[:, pl.ds(at, TILE)] = mm(attended[...], wo[:, pl.ds(at, TILE)])

    loop(D, TILE, attn_tile)
    rises(start, False, True)

    row = lambda part: mod[pl.ds(c * 6 + part, 1), :]

    def norm_rows(at):
        rows = pl.ds(at, 64)
        values = tokens[pl.ds(mine + at, 64), :].astype(F32) + row(2) * attn[rows, :]
        mid[rows, :] = values
        normed, inverse = normalize(values)
        norm[rows, :] = normed
        inv[rows, :] = inverse
        sin[pl.ds(mine + at, 64), :] = (normed * (1.0 + row(4)) + row(3)).astype(BF16)

    loop(TOK_FRAME, 64, norm_rows)

    def n_copy(base):
        ref = sin.at[pl.ds(base, TOK_FRAME)]
        return remote(ref, ref, n_s.at[0], n_r.at[0], s, sib)

    n_copy(mine).start()
    loads(lambda copy: copy.wait())
    for k in plan.early:
        zo, ro, at = home(k)

        @pl.when((z > zo) & (r != ro))
        def _():
            risen(k)

    def feed(base):
        rows = pl.ds(base, TOK_FRAME)

        def tile(at):
            cols = pl.ds(at, TILE)
            u = mm(sin[rows, :], wb[HD : HD + FT, cols])
            square = u * u
            inner = GELU_A * u * (1.0 + GELU_B * square)
            th = jnp.tanh(inner)
            half = 0.5 * (1.0 + th)
            hidden[rows, cols] = (u * half).astype(BF16)
            slopes[rows, cols] = half + 0.5 * u * (1.0 - th * th) * (
                GELU_A * (1.0 + 3.0 * GELU_B * square)
            )

        loop(FT, TILE, tile)

    feed(mine)
    n_copy(theirs).wait_recv()
    feed(theirs)

    def d_up(at):
        cols = pl.ds(at, TILE)
        dup[:, cols] = (mm_nt(dmlp[...], wb[pl.ds(HD + FT + at, TILE), :]) * slopes[:, cols]).astype(
            BF16
        )

    loop(FT, TILE, d_up)

    def c_copy(w, n):
        return remote(csend.at[w, n], crecv.at[w, n], c_s.at[w, n], c_r.at[w, n], s, sib)

    def y_copy(w, n):
        return remote(ysend.at[w, n], yrecv.at[w, n], y_s.at[w, n], y_r.at[w, n], s, across)

    def pass_on(w, n):
        c_copy(w, n).wait_recv()
        ysend[w, n] = (own[n] + crecv[w, n].astype(F32)).astype(BF16)
        y_copy(w, n).start()

    def product(w, base, n):
        rows = pl.ds(base, TOK_FRAME)
        if w == 0:
            return mm_nt(dup[rows, :], wb[HD + n * TILE : HD + (n + 1) * TILE, :])
        return mm(hidden[rows, :], wb[HD + FT :, n * TILE : (n + 1) * TILE])

    def products(w):
        for n in range(TILES):
            csend[w, n] = product(w, theirs, n).astype(BF16)
            c_copy(w, n).start()
            own[n] = product(w, mine, n)
            if n:
                pass_on(w, n - 1)
        pass_on(w, TILES - 1)

    def down_grad(at):
        gb[pl.ds(HD + FT + at, TILE), :] = mm_tn(hidden[:, pl.ds(at, TILE)], dmlp[...]).astype(BF16)

    def up_grad(at):
        gb[pl.ds(HD + at, TILE), :] = mm_tn(sin[:, pl.ds(at, TILE)], dup[...]).astype(BF16)

    def early_grad(k, d):
        zo, ro, at = home(k)
        slot = lax.rem(ro - r + rn, rn) - 1 if d is None else d - 1
        return remote(
            w_rows(gb, k), eside.at[slot, plan.rank[k]], g_s.at[at], g_r.at[slot, plan.rank[k]],
            z * rn + ro, t,
        )

    def early_grads(act):
        for k in plan.early:
            zo, ro, at = home(k)

            @pl.when(r != ro)
            def _():
                act(early_grad(k, None))

    def early_hop(rank, act):
        for here, to in ((ZN - 1, s - rn), (0, s + rn)):
            @pl.when(z == here)
            def _():
                act(remote(esum.at[rank], eend.at[rank], h_s.at[rank], h_r.at[rank], to, t))

    def early_total(rank):
        for k in plan.early:
            if plan.rank[k] == rank:
                zo, ro, at = home(k)

                @pl.when(r == ro)
                def _():
                    for d in range(1, rn):
                        early_grad(k, d).wait_recv()

                    def body(at):
                        rows = pl.ds(at, 16)
                        total = gb[pl.ds((k - plan.nq) * plan.ub + at, 16), :].astype(F32)
                        for d in range(1, rn):
                            total = total + eside[d - 1, rank, rows, :].astype(F32)
                        esum[rank, rows, :] = total.astype(BF16)

                    loop(plan.ub, 16, body)
                    early_hop(rank, start)

    def early_pass(rank, to):
        return remote(esum.at[rank], ebuf.at[rank], i_s.at[rank], i_r.at[rank], to, t)

    def early_inner(rank):
        for k in plan.early:
            if plan.rank[k] == rank:
                zo, ro, at = home(k)

                @pl.when((r == ro) & (z > 0) & (z < ZN - 1))
                def _():
                    remote(
                        esum.at[rank], eend.at[rank], h_s.at[rank], h_r.at[rank], s, t
                    ).wait_recv()

                    def body(at):
                        rows = pl.ds(at, 16)
                        esum[rank, rows, :] = (
                            esum[rank, rows, :].astype(F32) + eend[rank, rows, :].astype(F32)
                        ).astype(BF16)

                    loop(plan.ub, 16, body)

                    @pl.when(z != zo)
                    def _():
                        early_pass(rank, s + rn if zo == 2 else s - rn).start()

    def early_close(rank):
        for k in plan.early:
            if plan.rank[k] == rank:
                zo, ro, at = home(k)

                @pl.when((r == ro) & (z == zo))
                def _():
                    early_pass(rank, s).wait_recv()

                @pl.when((r == ro) & (z == 3 - zo))
                def _():
                    early_pass(rank, s).wait_send()

    def early_hops_done(rank):
        for k in plan.early:
            if plan.rank[k] == rank:
                @pl.when(r == home(k)[1])
                def _():
                    early_hop(rank, lambda copy: copy.wait_send())

    loop(FT, TILE, down_grad)
    up_grad(D - TILE)
    early_grads(start)
    products(0)
    products(1)
    loop(D - TILE, TILE, up_grad)
    early_total(0)
    early_total(1)
    early_inner(0)

    dm = dmod
    dm[...] = jnp.zeros_like(dm)
    for n in range(TILES):
        y_copy(0, n).wait_recv()

    def total(w, rows):
        return jnp.concatenate(
            [ysend[w, n, rows].astype(F32) + yrecv[w, n, rows].astype(F32) for n in range(TILES)],
            axis=1,
        )

    def back_rows(at):
        rows = pl.ds(at, 64)
        tok_rows = pl.ds(mine + at, 64)
        grads = total(0, rows)
        normed = norm[rows, :]
        add_to(dm, 1, grads)
        add_to(dm, 2, grads * normed)
        values = grad_out[tok_rows, :].astype(F32) + norm_back(
            grads * (1.0 + row(4)), normed, inv[rows, :]
        )
        dmid[rows, :] = values
        add_to(dm, 0, attn[rows, :] * values)
        dattn[rows, :] = (row(2) * values).astype(BF16)

    loop(TOK_FRAME, 64, back_rows)
    for ch in range(2):
        part = mm_nt(dattn[...], wo[pl.ds(pl.multiple_of((2 * y + ch) * HD, HD), HD), :]).astype(BF16)
        for zh in range(ZN):
            cols = slice(zh * HEAD, (zh + 1) * HEAD)
            dsend[ch * ZN + zh] = jnp.concatenate([part[:PACK, cols], part[PACK:, cols]], axis=1)

    def d_copy(d, e):
        zd, cd = partner(d, e)
        return remote(
            dsend.at[cd * ZN + zd], do_out.at[z, c], d_s.at[2 * d + e], d_r.at[2 * z + c],
            zd * rn + r, 2 * y + cd,
        )

    for d, e in pairs:
        d_copy(d, e).start()
    do_out[z, c] = dsend[c * ZN + z]
    for rank in range(2, plan.ranks):
        early_total(rank)

    def o_grad(head_core):
        cols = pl.ds(pl.multiple_of((2 * y + head_core) * HD, HD), HD)
        return mm_tn(attended[:, cols], dattn[...])

    w_copy = remote(wsend, wrecv, w_s, w_r, s, sib)
    wsend[...] = o_grad(1 - c).astype(BF16)
    w_copy.start()
    dwo[...] = o_grad(c)
    early_inner(1)

    for n in range(TILES):
        y_copy(1, n).wait_recv()

    def result_rows(at):
        rows = pl.ds(at, 64)
        tok_rows = pl.ds(mine + at, 64)
        mlp = total(1, rows)
        add_to(dm, 3, mlp * grad_out[tok_rows, :].astype(F32))
        result[tok_rows, :] = (mid[rows, :] + row(5) * mlp).astype(BF16)

    loop(TOK_FRAME, 64, result_rows)

    def e_copy(base):
        ref = result.at[pl.ds(base, TOK_FRAME)]
        return remote(ref, ref, e_s, e_r, s, sib)

    e_copy(mine).start()
    for rank in range(2, plan.ranks):
        early_inner(rank)
    w_copy.wait_recv()
    gb[:HD, :] = (dwo[...] + wrecv[...].astype(F32)).astype(BF16)

    for d, e in pairs:
        zd, cd = partner(d, e)
        remote(
            dsend.at[0], do_out.at[zd, cd], d_s.at[0], d_r.at[2 * zd + cd], s, t
        ).wait_recv()
    def late_grads(act):
        for k in plan.late:
            zo, ro = plan.home(k)
            rank, sem = plan.grad_rank[k], j_s.at[k - plan.nq]

            @pl.when(r == ro)
            def _():
                act(pltpu.make_async_copy(w_rows(gb, k), late_own.at[rank], sem))

            @pl.when(r != ro)
            def _():
                d = lax.rem(ro - r + rn, rn)
                act(pltpu.make_async_copy(w_rows(gb, k), late_send.at[d - 1, rank], sem))

    late_grads(start)
    for rank in range(plan.ranks):
        early_close(rank)
    e_copy(theirs).wait_recv()
    done = lambda copy: copy.wait_send()
    early_grads(done)
    for rank in range(plan.ranks):
        early_hops_done(rank)
    late_grads(lambda copy: copy.wait())
    rises(done, True, False)
    rises(done, False, False)
    for d, e in pairs:
        o_copy(d, e).wait_send()
        d_copy(d, e).wait_send()
    for slot in range(8):
        f_copy(slot).wait_send()
    n_copy(mine).wait_send()
    p_copy(0, t).wait_send()
    p_copy(1, across).wait_send()
    for w in range(2):
        for n in range(TILES):
            c_copy(w, n).wait_send()
            y_copy(w, n).wait_send()
    w_copy.wait_send()
    e_copy(mine).wait_send()


def middle_part(plan, o_mine, wo_across, weights, tokens, grad_out, mod_rows, cid):
    rn, count = plan.r, len(plan.early)
    rows = F_DEV * TOK_FRAME
    half = lambda dtype: pltpu.VMEM((TOK_FRAME, D), dtype)
    full = lambda dtype: pltpu.VMEM((rows, D), dtype)
    tiles = pltpu.VMEM((2, TILES, TOK_FRAME, TILE), BF16)
    return call(
        functools.partial(middle_kernel, plan),
        (
            jax.ShapeDtypeStruct((rows, D), BF16),
            jax.ShapeDtypeStruct((plan.grad_ranks, plan.ub, D), BF16),
            jax.ShapeDtypeStruct((rn - 1, plan.grad_ranks, plan.ub, D), BF16),
            jax.ShapeDtypeStruct((plan.ranks, plan.ub, D), BF16),
            jax.ShapeDtypeStruct((plan.ranks, plan.ub, D), BF16),
            jax.ShapeDtypeStruct((ZN, F_DEV, PACK, LANES), BF16),
            jax.ShapeDtypeStruct((TOK_FRAME, D), F32),
            jax.ShapeDtypeStruct((8, D), F32),
        ),
        [
            pltpu.VMEM((BROWS, D), BF16),
            pltpu.VMEM((BROWS, D), BF16),
            pltpu.VMEM((rn - 1, plan.ranks, plan.ub, D), BF16),
            pltpu.VMEM((plan.ranks, plan.ub, D), BF16),
            pltpu.VMEM((HEADS * HEAD, D), BF16),
            pltpu.VMEM((HEADS, PACK, LANES), BF16),
            half(BF16), half(F32), half(F32), half(F32), pltpu.VMEM((TOK_FRAME, 1), F32),
            full(BF16), full(BF16), full(BF16), full(F32), full(BF16),
            pltpu.VMEM((TILES, TOK_FRAME, TILE), F32), tiles, tiles, tiles, tiles,
            half(BF16), pltpu.VMEM((8, PACK, LANES), BF16),
            pltpu.VMEM((HD, D), F32), pltpu.VMEM((HD, D), BF16), pltpu.VMEM((HD, D), BF16),
            DMA((8,)), DMA((8,)), DMA((8,)), DMA((8,)), DMA((1,)), DMA((1,)),
            DMA((2, TILES)), DMA((2, TILES)), DMA((2, TILES)), DMA((2, TILES)),
            DMA((8,)), DMA((8,)), DMA, DMA, DMA, DMA, DMA((2,)), DMA((2,)),
            DMA((len(plan.late) + count,)), DMA((count, rn)), DMA((count,)), DMA((count,)), DMA((rn - 1, plan.ranks)),
            DMA((len(plan.late),)), DMA((plan.ranks,)), DMA((plan.ranks,)),
            DMA((plan.ranks,)), DMA((plan.ranks,)),
        ],
        [VM, VM, ANY, ANY, ANY, ANY, ANY, VM, VM, VM],
        cid,
        out_specs=(VM, ANY, ANY, VM, VM, VM, VM, VM),
        name="middle_part",
    )(o_mine, wo_across, *weights, tokens, grad_out, mod_rows)


def tail_kernel(
    plan, meta, q, kv, do, ot, lse, first_in, wq, tokens, dmid, mod, dm4, late_own, late_send, esum, ebuf,
    igrad, oq, ob, dall,
    keys, flipped, qs, gs, qgt, drow, acc, dq_acc, dq, kv_two, lside,
    stage, side, q_in, kv_in, dqkv, gq, own, csend, crecv, ysend, yrecv, dm, dm3, dboth,
    lstage, cb, qside, qpeer, qchain, qstage,
    q_s, q_r, k_s, k_r, x_s, x_r, c_s, c_r, y_s, y_r, e_s, e_r, h_s, h_r, m_s, m_r, t_s, t_r,
    kv_s, ls_s, ls_r, qo_s, qs_r, qp_r, qc_s, qc_r,
):
    s, t, z, r = place(plan)
    n, rn = plan.n, plan.r
    y = lax.div(t, 2)
    c = lax.rem(t, 2)
    sib = 2 * y + 1 - c
    across = lax.rem(t + 2, TP)
    mine = pl.multiple_of(c * TOK_FRAME, TOK_FRAME)
    theirs = pl.multiple_of((1 - c) * TOK_FRAME, TOK_FRAME)
    greet([(lax.rem(s + d, n), t) for d in range(1, n)] + [(s, sib), (s, across)])

    def side_copy(zs, e):
        other = lax.rem(r + e, rn)
        return remote(
            keys.at[zs * rn + other], side.at[e - 1, zs], x_s.at[zs, e - 1], x_r.at[zs, e - 1],
            z * rn + other, t,
        )

    def q_copy(zs):
        return remote(dq.at[zs], q_in.at[z], q_s.at[zs], q_r.at[z], zs * rn + r, t)

    def kv_copy(zs):
        return remote(stage.at[zs], kv_in.at[z], k_s.at[zs], k_r.at[z], zs * rn + r, t)

    def send_q(zs):
        @pl.when(z == zs)
        def _():
            q_in[zs] = dq[zs]

        @pl.when(z != zs)
        def _():
            q_copy(zs).start()

    def send_kv(zs):
        total = keys[zs * rn + r].astype(F32)
        for e in range(1, rn):
            side_copy(zs, e).wait_recv()
            total = total + side[e - 1, zs].astype(F32)
        stage[zs] = total.astype(BF16)

        @pl.when(z == zs)
        def _():
            kv_in[zs] = stage[zs]

        @pl.when(z != zs)
        def _():
            kv_copy(zs).start()

    scale = HEAD ** (-0.5)
    acc[...] = jnp.zeros_like(acc)

    def load(g, slot):
        return pltpu.make_async_copy(kv.at[g], kv_two.at[slot], kv_s.at[slot])

    load(0, 0).start()

    def sort_group(g, carry):
        slot = lax.rem(g, 2)

        @pl.when(g + 1 < n)
        def _():
            load(g + 1, 1 - slot).start()

        load(g, slot).wait()
        first = meta[2 * g] == 0
        a, b = kv_two[slot, :TOK_FRAME, :], kv_two[slot, TOK_FRAME:, :]
        keys[g, 0] = jnp.where(first, a, b)
        keys[g, 1] = jnp.where(first, b, a)
        for kind in range(2):
            flipped[kind, g] = keys[g, kind].T
        return carry

    lax.fori_loop(0, n, sort_group, 0)

    def attend_back_group(zq):
        gq = zq * rn + r
        first = meta[2 * gq] == 0
        clip = meta[2 * gq] + meta[2 * gq + 1]
        parts = []
        for kind in range(2):
            low = first if kind == 0 else jnp.logical_not(first)
            qz = padded(jnp.where(low, q[zq][:, :HEAD], q[zq][:, HEAD:]), True) * jnp.asarray(scale, BF16)
            gpack = jnp.where(low, do[zq, 0], do[zq, 1])
            grads = jnp.concatenate([gpack[:, :HEAD], gpack[:, HEAD:]], axis=0)
            out = jnp.where(low, ot[2 * zq], ot[2 * zq + 1])
            logs = jnp.where(low, lse[2 * zq], lse[2 * zq + 1])
            gz = padded(grads, False)
            qs[...] = qz
            gs[...] = gz
            qgt[:, :TOK_FRAME] = qz.T
            qgt[:, TOK_FRAME:] = gz.T
            drow[...] = jnp.sum(grads.astype(F32).T * out, axis=0, keepdims=True)
            dq_acc[...] = jnp.zeros_like(dq_acc)

            def block(p, inner):
                total = dq_acc[...]
                for e in range(2):
                    g = jnp.minimum(2 * p + e, gq)
                    shown = 2 * p + e <= gq
                    if kind == 1:
                        shown = shown & (meta[2 * g] + meta[2 * g + 1] == clip)
                    off = jnp.where(shown, 0.0, 1e30)
                    key = keys[g, kind]
                    pt = jnp.exp(mm(key, qgt[:, :TOK_FRAME]) - (logs + off))
                    dst = (pt * (mm(key, qgt[:, TOK_FRAME:]) - drow[...])).astype(BF16)
                    acc[kind, g] += mm(dst, qs[...]) + mm(pt.astype(BF16), gs[...])
                    total = total + mm(flipped[kind, g], dst)
                dq_acc[...] = total
                return inner

            lax.fori_loop(0, lax.div(gq + 2, 2), block, 0)
            parts.append((dq_acc[:HEAD, :] * scale).T.astype(BF16))
        dq[zq] = jnp.concatenate(
            [jnp.where(first, parts[0], parts[1]), jnp.where(first, parts[1], parts[0])], axis=1
        )
        for other in range(rn):
            g = zq * rn + other
            low = meta[2 * g] == 0
            a, b = acc[0, g].astype(BF16), acc[1, g].astype(BF16)
            keys[g, 0] = jnp.where(low, a, b)
            keys[g, 1] = jnp.where(low, b, a)

    def late(units, act):
        for k in units:
            zo, ro = plan.home(k)

            @pl.when(r == ro)
            def _():
                act(k, zo, plan.grad_rank[k])

    def late_copy(rank, below, to):
        return remote(lstage.at[rank], cb.at[below, rank], t_s.at[rank], t_r.at[below, rank], to, t)

    def late_side(rank, d):
        return remote(
            late_send.at[d - 1, rank], lside.at[d - 1, rank], ls_s.at[rank, d - 1],
            ls_r.at[rank, d - 1], z * rn + lax.rem(r + d, rn), t,
        )

    def late_sides(rank, act):
        for d in range(1, rn):
            act(late_side(rank, d))

    def late_step(k, zo, rank, here_z, above, below, final):
        @pl.when(z == here_z)
        def _():
            for d in range(1, rn):
                late_side(rank, d).wait_recv()
            if above:
                late_copy(rank, 0, s).wait_recv()
            if below:
                late_copy(rank, 1, s).wait_recv()

            def body(at):
                rows = pl.ds(at, 16)
                total = late_own[rank, rows, :].astype(F32)
                for d in range(1, rn):
                    total = total + lside[d - 1, rank, rows, :].astype(F32)
                if above:
                    total = total + cb[0, rank, rows, :].astype(F32)
                if below:
                    total = total + cb[1, rank, rows, :].astype(F32)
                if final:
                    ob[k % 3, rows, :] = total
                else:
                    lstage[rank, rows, :] = total.astype(BF16)

            loop(plan.ub, 16, body)
            if not final:
                late_copy(
                    rank, 0 if here_z > zo else 1, s - rn if here_z > zo else s + rn
                ).start()

    def late_ends(k, zo, rank):
        late_step(k, zo, rank, ZN - 1, False, False, False)
        if zo > 0:
            late_step(k, zo, rank, 0, False, False, False)

    def late_inner(here):
        def act(k, zo, rank):
            if here > zo:
                late_step(k, zo, rank, here, True, False, False)

        return act

    def late_final(k, zo, rank):
        late_step(k, zo, rank, zo, True, zo > 0, True)

    def late_done(k, zo, rank):
        @pl.when(z != zo)
        def _():
            late_copy(rank, 0, s).wait_send()

    def early_units(act):
        for k in plan.early:
            zo, ro, rank = (k // 3) // rn, (k // 3) % rn, plan.rank[k]

            @pl.when(r == ro)
            def _():
                act(k, zo, rank)

    def early_final(k, zo, rank):
        @pl.when(z == zo)
        def _():
            def body(at):
                rows = pl.ds(at, 16)
                ob[k % 3, rows, :] = esum[rank, rows, :].astype(F32) + ebuf[rank, rows, :].astype(F32)

            loop(plan.ub, 16, body)

    hq = plan.uq // CUTS

    def q_rows(k, h):
        return gq.at[pl.ds(pl.multiple_of(k * plan.uq + h * hq, hq), hq)]

    def q_sides(k, act):
        tc, ro, j = k % rn, k // 3, k // rn
        for h in range(CUTS):
            @pl.when((z > 0) & (r != tc))
            def _():
                slot = lax.rem(tc - r + rn, rn) - 1
                act(
                    remote(
                        q_rows(k, h), qside.at[slot, CUTS * j + h], qo_s.at[CUTS * k + h],
                        qs_r.at[slot, CUTS * j + h], z * rn + tc, t,
                    )
                )

            @pl.when((z == 0) & (r != ro) & (r != tc))
            def _():
                slot = lax.rem(ro - r + rn, rn) - 1
                act(
                    remote(
                        q_rows(k, h), qpeer.at[slot, CUTS * (k % 3) + h], qo_s.at[CUTS * k + h],
                        qp_r.at[slot, CUTS * (k % 3) + h], ro, t,
                    )
                )

    def q_down(at, to):
        return remote(qstage.at[at], qchain.at[at], qc_s.at[at], qc_r.at[at], to, t)

    def q_chain(here, only_j):
        top = here == ZN - 1
        for j in (only_j,):
            k = r + rn * j
            for h in range(CUTS):
                at = CUTS * j + h

                @pl.when(z == here)
                def _():
                    for d in range(1, rn):
                        remote(
                            q_rows(k, h), qside.at[d - 1, at], qo_s.at[0], qs_r.at[d - 1, at], s, t
                        ).wait_recv()
                    if not top:
                        q_down(at, s).wait_recv()
                    unit = q_rows(k, h)

                    def body(row):
                        rows = pl.ds(row, 16)
                        total = unit[rows, :].astype(F32)
                        for d in range(1, rn):
                            total = total + qside[d - 1, at, rows, :].astype(F32)
                        if not top:
                            total = total + qchain[at, rows, :].astype(F32)
                        qstage[at, rows, :] = total.astype(BF16)

                    loop(hq, 16, body)
                    q_down(at, s - rn).start()

    def q_last_copy(k, h):
        tc, ro, j = k % rn, k // 3, k // rn
        slot = (ro - tc + rn) % rn - 1
        return remote(
            qstage.at[CUTS * j + h], qpeer.at[slot, CUTS * (k % 3) + h], qc_s.at[CUTS * j + h],
            qp_r.at[slot, CUTS * (k % 3) + h], ro, t,
        )

    def q_ground(act):
        for k in range(plan.nq):
            if k % rn != k // 3:
                @pl.when((z == 0) & (r == k % rn))
                def _():
                    for h in range(CUTS):
                        act(k, h)

    def q_turn(k, h):
        at = CUTS * (k // rn) + h
        q_down(at, s).wait_recv()
        unit = q_rows(k, h)

        def body(row):
            rows = pl.ds(row, 16)
            qstage[at, rows, :] = (
                unit[rows, :].astype(F32) + qchain[at, rows, :].astype(F32)
            ).astype(BF16)

        loop(hq, 16, body)
        q_last_copy(k, h).start()

    def q_final():
        for k in range(plan.nq):
            @pl.when((z == 0) & (r == k // 3))
            def _():
                straight = k % rn == k // 3
                for h in range(CUTS):
                    at = CUTS * (k // rn) + h
                    if straight:
                        q_down(at, s).wait_recv()
                    for d in range(1, rn):
                        remote(
                            q_rows(k, h), qpeer.at[d - 1, CUTS * (k % 3) + h], qo_s.at[0],
                            qp_r.at[d - 1, CUTS * (k % 3) + h], s, t,
                        ).wait_recv()
                    unit = q_rows(k, h)

                    def body(row):
                        rows = pl.ds(row, 16)
                        total = unit[rows, :].astype(F32)
                        for d in range(1, rn):
                            total = total + qpeer[d - 1, CUTS * (k % 3) + h, rows, :].astype(F32)
                        if straight:
                            total = total + qchain[at, rows, :].astype(F32)
                        oq[k % 3, pl.ds(h * hq + row, 16), :] = total

                    loop(hq, 16, body)

    start = lambda copy: copy.start()
    done = lambda copy: copy.wait_send()
    def only(rank, act):
        return lambda k, zo, own_rank: act(k, zo, own_rank) if own_rank == rank else None

    last = plan.grad_ranks - 1
    late_sides(0, start)
    for zq in range(ZN - 1, -1, -1):
        attend_back_group(zq)
        for e in range(1, rn):
            side_copy(zq, e).start()
        send_q(zq)
        if zq == ZN - 1:
            late(plan.late, only(0, late_ends))
        else:
            send_kv(zq + 1)
    for rank in range(1, plan.grad_ranks):
        late_sides(rank, start)
    send_kv(0)
    late(plan.late, only(0, late_inner(2)))
    late(plan.late, only(0, late_inner(1)))
    late(plan.late, only(1, late_ends))
    for zs in range(ZN):
        @pl.when(z != zs)
        def _():
            remote(dq.at[0], q_in.at[zs], q_s.at[0], q_r.at[zs], s, t).wait_recv()
            remote(stage.at[0], kv_in.at[zs], k_s.at[0], k_r.at[zs], s, t).wait_recv()

    for p in range(2):
        cols = slice(p * LANES, (p + 1) * LANES)
        a, b = q_in[2 * p], q_in[2 * p + 1]
        dqkv[:TOK_FRAME, cols] = jnp.concatenate([a[:, :HEAD], b[:, :HEAD]], axis=1)
        dqkv[TOK_FRAME:, cols] = jnp.concatenate([a[:, HEAD:], b[:, HEAD:]], axis=1)
        a, b = [kv_in[2 * p + i].reshape(F_DEV * TOK_FRAME, LANES) for i in range(2)]
        dqkv[:, HD + p * LANES : HD + (p + 1) * LANES] = jnp.concatenate(
            [a[:, :HEAD], b[:, :HEAD]], axis=1
        )
        dqkv[:, 2 * HD + p * LANES : 2 * HD + (p + 1) * LANES] = jnp.concatenate(
            [a[:, HEAD:], b[:, HEAD:]], axis=1
        )

    for m in range(TILES):
        gq[m * TILE : (m + 1) * TILE, :] = mm_tn(
            first_in[:, m * TILE : (m + 1) * TILE], dqkv[...]
        ).astype(BF16)
        for k in range(m * plan.nq // TILES, (m + 1) * plan.nq // TILES):
            q_sides(k, start)

    def c_copy(w):
        return remote(csend.at[w], crecv.at[w], c_s.at[w], c_r.at[w], s, sib)

    def y_copy(w):
        return remote(ysend.at[w], yrecv.at[w], y_s.at[w], y_r.at[w], s, across)

    def pass_on(w):
        c_copy(w).wait_recv()
        ysend[w] = (own[w] + crecv[w].astype(F32)).astype(BF16)
        y_copy(w).start()

    for w in range(TILES):
        weights = wq[w * TILE : (w + 1) * TILE, :]
        csend[w] = mm_nt(dqkv[pl.ds(theirs, TOK_FRAME), :], weights).astype(BF16)
        c_copy(w).start()
        own[w] = mm_nt(dqkv[pl.ds(mine, TOK_FRAME), :], weights)
        if w:
            pass_on(w - 1)
    pass_on(TILES - 1)

    for rank in range(2, plan.grad_ranks):
        late(plan.late, only(rank, late_ends))
    q_chain(ZN - 1, 0)
    q_chain(ZN - 1, 1)
    late(plan.late, only(1, late_inner(2)))
    q_chain(2, 0)
    late(plan.late, only(last, late_inner(2)))
    q_chain(2, 1)
    q_chain(1, 0)
    late(plan.late, only(1, late_inner(1)))
    q_chain(1, 1)
    late(plan.late, only(last, late_inner(1)))

    for w in range(TILES):
        y_copy(w).wait_recv()
    row = lambda part: mod[pl.ds(c * 6 + part, 1), :]
    dm[...] = jnp.zeros_like(dm)

    def input_rows(at):
        rows = pl.ds(at, 64)
        tok_rows = pl.ds(mine + at, 64)
        grads = jnp.concatenate(
            [ysend[w, rows].astype(F32) + yrecv[w, rows].astype(F32) for w in range(TILES)], axis=1
        )
        normed, inverse = normalize(tokens[tok_rows, :].astype(F32))
        add_to(dm, 0, grads)
        add_to(dm, 1, grads * normed)
        igrad[tok_rows, :] = dmid[rows, :] + norm_back(grads * (1.0 + row(1)), normed, inverse)

    loop(TOK_FRAME, 64, input_rows)

    def e_copy(base):
        ref = igrad.at[pl.ds(base, TOK_FRAME)]
        return remote(ref, ref, e_s, e_r, s, sib)

    e_copy(mine).start()

    for block in range(6 * D // LANES):
        part, at = block // (D // LANES), block % (D // LANES)
        src = dm if part < 2 else dm4
        lane = slice(at * LANES, (at + 1) * LANES)
        from_row = part if part < 2 else part - 2
        dm3[block // MCOLS, block % MCOLS : block % MCOLS + 1, :] = src[from_row : from_row + 1, lane]
    h_copy = lambda frame: remote(dm3.at[sib], dboth.at[frame], h_s, h_r, s, sib)
    h_copy(c).start()
    dboth[c] = dm3[t]
    h_copy(1 - c).wait_recv()

    def m_copy(src):
        return remote(dboth, dall.at[s], m_s.at[src - plan.first_mod], m_r.at[s], src, t)

    for src in range(plan.first_mod, n):
        @pl.when(s == src)
        def _():
            dall[s] = dboth[...]

        @pl.when(s != src)
        def _():
            m_copy(src).start()

    q_ground(q_turn)
    late(plan.late, late_final)
    early_units(early_final)
    q_final()

    @pl.when(s >= plan.first_mod)
    def _():
        for d in range(1, n):
            other = lax.rem(s + d, n)
            remote(dboth, dall.at[other], m_s.at[0], m_r.at[other], s, t).wait_recv()

    e_copy(theirs).wait_recv()
    for zs in range(ZN):
        @pl.when(z != zs)
        def _():
            q_copy(zs).wait_send()
            kv_copy(zs).wait_send()

        for e in range(1, rn):
            side_copy(zs, e).wait_send()
    for rank in range(plan.grad_ranks):
        late_sides(rank, done)
    late(plan.late, late_done)
    for k in range(plan.nq):
        q_sides(k, done)

    @pl.when(z > 0)
    def _():
        for at in range(2 * CUTS):
            q_down(at, s).wait_send()

    q_ground(lambda k, h: q_last_copy(k, h).wait_send())
    for w in range(TILES):
        c_copy(w).wait_send()
        y_copy(w).wait_send()
    e_copy(mine).wait_send()
    h_copy(c).wait_send()
    for src in range(plan.first_mod, n):
        @pl.when(s != src)
        def _():
            m_copy(src).wait_send()


def tail_part(plan, meta, q, kv, do, ot, lse, first_in, wq, tokens, dmid, mod_rows, dm4, late_own, late_send, esum, ebuf, cid):
    n, rn = plan.n, plan.r
    rows = F_DEV * TOK_FRAME
    tiles = pltpu.VMEM((TILES, TOK_FRAME, TILE), BF16)
    mods = n - plan.first_mod
    return call(
        functools.partial(tail_kernel, plan),
        (
            jax.ShapeDtypeStruct((rows, D), F32),
            jax.ShapeDtypeStruct((3, plan.uq, QKV), F32),
            jax.ShapeDtypeStruct((3, plan.ub, D), F32),
            jax.ShapeDtypeStruct((n, F_DEV, 16, LANES), F32),
        ),
        [
            pltpu.VMEM((n, 2, TOK_FRAME, LANES), BF16),
            pltpu.VMEM((2, n, LANES, TOK_FRAME), BF16),
            pltpu.VMEM((TOK_FRAME, LANES), BF16),
            pltpu.VMEM((TOK_FRAME, LANES), BF16),
            pltpu.VMEM((LANES, 2 * TOK_FRAME), BF16),
            pltpu.VMEM((1, TOK_FRAME), F32),
            pltpu.VMEM((2, n, TOK_FRAME, LANES), F32),
            pltpu.VMEM((LANES, TOK_FRAME), F32),
            pltpu.VMEM((ZN, TOK_FRAME, LANES), BF16),
            pltpu.VMEM((2, rows, LANES), BF16),
            pltpu.VMEM((rn - 1, plan.grad_ranks, plan.ub, D), BF16),
            pltpu.VMEM((ZN, 2, TOK_FRAME, LANES), BF16),
            pltpu.VMEM((rn - 1, ZN, 2, TOK_FRAME, LANES), BF16),
            pltpu.VMEM((ZN, TOK_FRAME, LANES), BF16),
            pltpu.VMEM((ZN, 2, TOK_FRAME, LANES), BF16),
            pltpu.VMEM((rows, QKV), BF16),
            pltpu.VMEM((D, QKV), BF16),
            pltpu.VMEM((TILES, TOK_FRAME, TILE), F32), tiles, tiles, tiles, tiles,
            pltpu.VMEM((8, D), F32),
            pltpu.VMEM((TP, 16, LANES), F32),
            pltpu.VMEM((F_DEV, 16, LANES), F32),
            pltpu.VMEM((plan.grad_ranks, plan.ub, D), BF16),
            pltpu.VMEM((2, plan.grad_ranks, plan.ub, D), BF16),
            pltpu.VMEM((rn - 1, 2 * CUTS, plan.uq // CUTS, QKV), BF16),
            pltpu.VMEM((rn - 1, 3 * CUTS, plan.uq // CUTS, QKV), BF16),
            pltpu.VMEM((2 * CUTS, plan.uq // CUTS, QKV), BF16),
            pltpu.VMEM((2 * CUTS, plan.uq // CUTS, QKV), BF16),
            DMA((ZN,)), DMA((ZN,)), DMA((ZN,)), DMA((ZN,)), DMA((ZN, rn - 1)), DMA((ZN, rn - 1)),
            DMA((TILES,)), DMA((TILES,)), DMA((TILES,)), DMA((TILES,)),
            DMA, DMA, DMA, DMA, DMA((mods,)), DMA((n,)),
            DMA((plan.grad_ranks,)), DMA((2, plan.grad_ranks)),
            DMA((2,)), DMA((plan.grad_ranks, rn - 1)), DMA((plan.grad_ranks, rn - 1)),
            DMA((CUTS * plan.nq,)),
            DMA((rn - 1, 2 * CUTS)), DMA((rn - 1, 3 * CUTS)), DMA((2 * CUTS,)), DMA((2 * CUTS,)),
        ],
        [SM, VM, ANY] + [VM] * 10 + [ANY, VM, VM],
        cid,
        name="tail_part",
    )(meta, q, kv, do, ot, lse, first_in, wq, tokens, dmid, mod_rows, dm4, late_own, late_send, esum, ebuf)


def adam_kernel(plan, meta, oq, ob, cond, dmod, master, one, two, average, n_master, n_one, n_two, n_average):
    s = meta[0]
    rate = RATE_FACTOR * D ** (-0.5)
    scale_one = 1.0 / (1.0 - BETA_FIRST**STEP)
    scale_two = 1.0 / (1.0 - BETA_SECOND**STEP)

    def update(rows, grad):
        first = BETA_FIRST * one[rows, :] + (1.0 - BETA_FIRST) * grad
        second = BETA_SECOND * two[rows, :] + (1.0 - BETA_SECOND) * grad * grad
        weight = master[rows, :]
        weight = weight - rate * (
            (first * scale_one) / (jnp.sqrt(second * scale_two) + ADAM_EPSILON)
            + WEIGHT_DECAY * weight
        )
        n_one[rows, :] = first
        n_two[rows, :] = second
        n_master[rows, :] = weight
        n_average[rows, :] = AVERAGE_RATE * average[rows, :] + (1.0 - AVERAGE_RATE) * weight

    if True:
        k = 3 * s + pl.program_id(0)
        base = 0

        def from_matrix(kind):
            src = oq if kind == "q" else ob
            rows = plan.uq if kind == "q" else plan.ub
            cols = (QKV if kind == "q" else D) // LANES
            for j in range(cols):
                update(
                    pl.ds(base + j, rows, stride=cols), src[0, :, j * LANES : (j + 1) * LANES]
                )

        by_kind(plan, k, from_matrix)

        @pl.when(k >= plan.nb)
        def _():
            at = cond[k - plan.nb]
            for j in range(MCOLS):
                update(
                    pl.ds(base + j, plan.um, stride=MCOLS),
                    mm(at, dmod[pl.ds(j, plan.frames, stride=16), :].astype(BF16)),
                )


def adam(plan, meta, oq, ob, cond_rows, dmod, master, one, two, average):
    shape = jax.ShapeDtypeStruct(master.shape, F32)
    flat = pl.BlockSpec((plan.flat_rows, LANES), lambda i: (i, 0))
    unit = lambda rows, cols: pl.BlockSpec((1, rows, cols), lambda i: (i, 0, 0))
    whole = lambda x: pl.BlockSpec(x.shape, lambda i: (0,) * x.ndim)
    return pl.pallas_call(
        functools.partial(adam_kernel, plan),
        out_shape=(shape,) * 4,
        grid=(3,),
        in_specs=[SM, unit(plan.uq, QKV), unit(plan.ub, D), whole(cond_rows), whole(dmod)] + [flat] * 4,
        out_specs=(flat,) * 4,
        compiler_params=pltpu.CompilerParams(vmem_limit_bytes=VMEM_LIMIT),
        name="adam",
    )(meta, oq, ob, cond_rows, dmod, master, one, two, average)


def local(
    tokens,
    grad_out,
    noise_level,
    context_mask,
    frame_clip,
    level_table,
    master,
    moment_one,
    moment_two,
    average,
):
    plan = Plan(lax.axis_size("seq"))
    s = lax.axis_index("seq")
    t = lax.axis_index("tp")
    flat = lambda x: x.reshape(-1, LANES)

    effective = noise_level * (1 - context_mask)
    one_hot = (
        effective[:, None] == jnp.arange(level_table.shape[0], dtype=jnp.int32)[None, :]
    ).astype(BF16)
    condition = jax.nn.silu(mm(one_hot, level_table)).astype(BF16)
    cond_units = condition.reshape(plan.frames, plan.nm, plan.um).transpose(1, 0, 2)

    wq, w_out, w_side, w_early, own_b, mod_rows, first_in, q_mine, kv_all = head_part(
        plan, flat(master), cond_units, tokens, 0
    )
    rn, n = plan.r, plan.n
    w_below = lax.ppermute(own_b, "seq", [(i, i + rn) for i in range(rn, 3 * rn)])
    wo_across = lax.ppermute(
        w_out.reshape(-1, D)[:HD], "tp", [(i, (i + 2) % TP) for i in range(TP)]
    )
    w_beside = jnp.stack(
        [
            lax.ppermute(
                w_side, "seq", [(i, i // rn * rn + (i + d) % rn) for i in range(n)]
            )
            for d in range(1, rn)
        ]
    )
    meta = jnp.concatenate([frame_clip, lax.rem(s, plan.r)[None]]).astype(jnp.int32)
    o_mine, o_rows, lse = attend(plan, meta, q_mine, kv_all)
    result, late_own, late_send, early_sum, early_in, do_mine, middle_grad, mod_four = middle_part(
        plan, o_mine, wo_across, (w_out, w_side, w_beside, w_early, w_below),
        tokens, grad_out, mod_rows, 2
    )
    input_grad, own_q, own_b, mod_all = tail_part(
        plan, meta, q_mine, kv_all, do_mine, o_rows, lse, first_in, wq, tokens, middle_grad,
        mod_rows, mod_four, late_own, late_send, early_sum, early_in, 3,
    )
    updated = adam(
        plan,
        s[None].astype(jnp.int32),
        own_q,
        own_b,
        cond_units.transpose(0, 2, 1),
        flat(mod_all),
        flat(master),
        flat(moment_one),
        flat(moment_two),
        flat(average),
    )
    new_master, new_one, new_two, new_average = [x.reshape(master.shape) for x in updated]
    return (result, input_grad, new_master, new_one, new_two, new_average)


def solution(mesh):
    token_spec = P("seq", None)
    weight_spec = P("tp", "seq")
    in_specs = (token_spec, token_spec, P(), P(), P(), P()) + (weight_spec,) * 4
    out_specs = (token_spec, token_spec) + (weight_spec,) * 4
    return jax.shard_map(local, mesh=mesh, in_specs=in_specs, out_specs=out_specs, check_vma=False)
```

```python
import functools

import jax
import jax.numpy as jnp
from jax import lax
from jax.experimental import pallas as pl
from jax.experimental.pallas import tpu as pltpu
from jax.sharding import PartitionSpec as P

D = 1024
HEADS = 16
HEAD = 64
FF = 4096
TOK_FRAME = 384
STEP = 7
TP = 4
ZN = 4
HD = HEADS * HEAD // TP
QKV = 3 * HD
FT = FF // TP
MT = 6 * D // TP
F_DEV = 2
BROWS = HD + 2 * FT
LANES = 128
MCOLS = MT // LANES
PACK = TOK_FRAME // 2
TILE = 256
TILES = D // TILE
CUTS = 4

NORM_EPSILON = 1e-06
RATE_FACTOR = 2.5
BETA_FIRST = 0.5
BETA_SECOND = 0.5
ADAM_EPSILON = 1e-08
WEIGHT_DECAY = 0.01
AVERAGE_RATE = 0.9
GELU_A = 0.7978845608028654
GELU_B = 0.044715
MESH = pl.DeviceIdType.MESH
VM = pl.BlockSpec(memory_space=pltpu.VMEM)
SM = pl.BlockSpec(memory_space=pltpu.SMEM)
ANY = pl.BlockSpec(memory_space=pl.ANY)
DMA = pltpu.SemaphoreType.DMA
F32 = jnp.float32
BF16 = jnp.bfloat16
VMEM_LIMIT = 60 * 2**20


def mm(left, right):
    return jnp.dot(left, right, preferred_element_type=F32)


def mm_tn(left, right):
    return lax.dot_general(left, right, (((0,), (0,)), ((), ())), preferred_element_type=F32)


def mm_nt(left, right):
    return lax.dot_general(left, right, (((1,), (1,)), ((), ())), preferred_element_type=F32)


def normalize(rows):
    centred = rows - jnp.mean(rows, axis=1, keepdims=True)
    inverse = lax.rsqrt(jnp.mean(centred * centred, axis=1, keepdims=True) + NORM_EPSILON)
    return (centred * inverse, inverse)


def norm_back(grads, normed, inverse):
    return inverse * (
        grads
        - jnp.mean(grads, axis=1, keepdims=True)
        - normed * jnp.mean(grads * normed, axis=1, keepdims=True)
    )


def loop(count, step, body):
    def turn(i, carry):
        body(pl.multiple_of(i * step, step))
        return carry

    lax.fori_loop(0, count // step, turn, 0)


def add_to(ref, row, values):
    ref[pl.ds(row, 1), :] += jnp.sum(values, axis=0, keepdims=True)


class Plan:
    def __init__(self, seq_count):
        self.n = seq_count
        self.r = seq_count // ZN
        self.shard = (D * QKV + BROWS * D + D * MT) // seq_count
        self.unit = self.shard // 3
        self.uq = self.unit // QKV
        self.ub = self.unit // D
        self.um = self.unit // MT
        self.nq = D // self.uq
        self.nb = self.nq + BROWS // self.ub
        self.nm = D // self.um
        self.first_mod = self.nb // 3
        self.half = (self.nq + self.nb) // 2
        self.flat_rows = self.unit // LANES
        self.frames = seq_count * F_DEV
        self.late = list(range(self.nq, self.half))
        self.early = list(range(self.half, self.nb))
        self.outs = self.late[: -(-HD // self.ub)]
        self.sided = self.late[len(self.outs) :]
        self.rank, self.ranks = self.ranked(self.early)
        self.late_rank, self.late_ranks = self.ranked(self.sided)
        self.grad_rank, self.grad_ranks = self.ranked(self.late)

    def ranked(self, units):
        seen, rank = {}, {}
        for k in units:
            column = self.home(k)[1]
            rank[k] = seen.get(column, 0)
            seen[column] = rank[k] + 1
        return rank, max(seen.values())

    def home(self, k):
        return (k // 3) // self.r, (k // 3) % self.r


def place(plan):
    s = lax.axis_index("seq")
    t = lax.axis_index("tp")
    return s, t, lax.div(s, plan.r), lax.rem(s, plan.r)


def remote(src, dst, send_sem, recv_sem, s, t):
    return pltpu.make_async_remote_copy(
        src_ref=src,
        dst_ref=dst,
        send_sem=send_sem,
        recv_sem=recv_sem,
        device_id=(s, t),
        device_id_type=MESH,
    )


def greet(peers):
    barrier = pltpu.get_barrier_semaphore()
    for s, t in peers:
        pl.semaphore_signal(barrier, inc=1, device_id=(s, t), device_id_type=MESH)
    pl.semaphore_wait(barrier, len(peers))


def by_kind(plan, k, act, low=0, high=None):
    high = plan.nb if high is None else high
    q_high, b_low = min(plan.nq, high), max(plan.nq, low)
    if low < q_high:
        @pl.when((k >= low) & (k < q_high))
        def _():
            act("q")

    if b_low < high:
        @pl.when((k >= b_low) & (k < high))
        def _():
            act("b")


def unit_of(plan, k, kind, wq, wb):
    if kind == "q":
        return wq.at[pl.ds(pl.multiple_of(k * plan.uq, plan.uq), plan.uq)]
    return wb.at[pl.ds(pl.multiple_of((k - plan.nq) * plan.ub, plan.ub), plan.ub)]


def call(kernel, outs, scratch, ins, cid=None, cost=None, name=None, out_specs=None):
    params = dict(vmem_limit_bytes=VMEM_LIMIT)
    if cid is not None:
        params.update(collective_id=cid, has_side_effects=True)
    return pl.pallas_call(
        kernel,
        out_shape=outs,
        in_specs=ins,
        out_specs=out_specs or jax.tree.map(lambda _: VM, outs),
        scratch_shapes=scratch,
        compiler_params=pltpu.CompilerParams(**params),
        cost_estimate=cost,
        name=name,
    )


def head_kernel(
    plan, meta, master, cond, tokens,
    wq, w_out, w_side, w_early, w_below, w_beside, wo_across, mods, first_in, q_out, kv_out, o, ot, lse,
    own_b, pool, flipped, qt, m_ref, l_ref, acc, tile, macc, mpart, mrecv, mod, norm, q_send, kv_send,
    qp_s, qc_s, q_r, wo_s, wo_r, ws_s, ws_r, we_s, we_r, loc_s, m_s, m_r, t_s, t_r, as_, ar, ks, kr, xs, xr,
    bl_s, bl_r, bs_s, bs_r, oa_s, oa_r,
):
    s, t, z, r = place(plan)
    n, rn = plan.n, plan.r
    greet(
        [(lax.rem(s + d, n), t) for d in range(1, n)]
        + [(s, lax.rem(t + d, TP)) for d in range(1, TP)]
    )
    start = lambda copy: copy.start()
    done = lambda copy: copy.wait_send()
    cut = plan.uq // CUTS

    def q_rows(k, h):
        return wq.at[pl.ds(pl.multiple_of(k * plan.uq + h * cut, cut), cut)]

    def q_copy(k, h, sem, to_s):
        ref = q_rows(k, h)
        return remote(ref, ref, sem, q_r.at[CUTS * k + h], to_s, t)

    def q_arrived(k, h):
        q_copy(k, h, qc_s.at[0, 0], s).wait_recv()

    def column(j):
        return r + rn * lax.rem(j + r, 2)

    def q_own(i, act):
        k = 3 * s + i

        @pl.when(k < plan.nq)
        def _():
            for h in range(CUTS):
                for d in range(1, rn):
                    act(q_copy(k, h, qp_s.at[CUTS * i + h, d - 1], lax.rem(r + d, rn)))

    def q_line(act, wait, whole=False):
        for j in range(2):
            k = column(j)
            for h in range(CUTS):
                if wait:
                    @pl.when((z > 0) | (lax.div(k, 3) != r))
                    def _():
                        q_arrived(k, h)

                @pl.when((z < ZN - 1) & ((z > 0) | (lax.div(k, 3) != r) | whole))
                def _():
                    act(q_copy(k, h, qc_s.at[CUTS * j + h, 0], s + rn))

                @pl.when(z > 0)
                def _():
                    for d in range(1, rn):
                        act(
                            q_copy(
                                k, h, qc_s.at[CUTS * j + h, d], z * rn + lax.rem(r + d, rn)
                            )
                        )

    def slot(k):
        if k in plan.outs:
            at = k - plan.nq
            return w_out.at[at], wo_s.at[at], wo_r.at[at]
        if k in plan.sided:
            at = plan.late_rank[k]
            return w_side.at[at], ws_s.at[at], ws_r.at[at]
        return w_early.at[k - plan.half], we_s.at[plan.rank[k]], we_r.at[k - plan.half]

    def along(k, src, act, up):
        dst, send_sem, recv_sem = slot(k)
        if up and k < plan.half:
            @pl.when(z < ZN - 1)
            def _():
                act(remote(src, dst, send_sem.at[0], recv_sem, s + rn, t))

        if not up:
            @pl.when(z > 0)
            def _():
                act(remote(src, dst, send_sem.at[1], recv_sem, s - rn, t))

    def beside(k, src, act):
        if k in plan.sided:
            return
        dst, send_sem, recv_sem = slot(k)
        for d in range(1, rn):
            act(
                remote(
                    src, dst, send_sem.at[1 + d], recv_sem, z * rn + lax.rem(r + d, rn), t
                )
            )

    def arrived(k):
        dst, send_sem, recv_sem = slot(k)
        remote(own_b.at[0], dst, send_sem.at[0], recv_sem, s, t).wait_recv()

    def keep(k):
        return pltpu.make_async_copy(own_b.at[k % 3], slot(k)[0], loc_s.at[k % 3])

    def owned(units, act):
        for k in units:
            @pl.when(s == k // 3)
            def _():
                act(k, own_b.at[k % 3])

    def pass_along(units, d, act, wait):
        for k in units:
            zo, ro = plan.home(k)
            if k < plan.half and zo + d < (ZN - 1 if k in plan.sided else ZN):
                @pl.when((r == ro) & (z == zo + d))
                def _():
                    if wait:
                        arrived(k)
                    along(k, slot(k)[0], act, True)
                    beside(k, slot(k)[0], act)

            if zo - d >= (1 if k in plan.sided or d > 1 else 0):
                @pl.when((r == ro) & (z == zo - d))
                def _():
                    if wait:
                        arrived(k)
                    along(k, slot(k)[0], act, False)
                    beside(k, slot(k)[0], act)

    def settle(k, low):
        zo, ro = plan.home(k)

        @pl.when((r == ro) & ((z == 0) & (zo > 0) if low else (z == ZN - 1) & (zo < ZN - 1)))
        def _():
            arrived(k)

    def hop(k, act):
        zo, ro = plan.home(k)

        @pl.when(s == k // 3)
        def _():
            act(remote(own_b.at[k % 3], w_below.at[k % 3], bl_s.at[k % 3], bl_r.at[k % 3], s + rn, t))

    def hopped(k):
        zo, ro = plan.home(k)

        @pl.when((r == ro) & (z == zo + 1))
        def _():
            remote(own_b.at[0], w_below.at[k % 3], bl_s.at[0], bl_r.at[k % 3], s, t).wait_recv()

    def share(k, act, low=None):
        rank = plan.late_rank[k]
        part = True if low is None else (z <= 1) == low

        @pl.when((r == plan.home(k)[1]) & part)
        def _():
            for d in range(1, rn):
                act(
                    remote(
                        w_side.at[rank], w_beside.at[d - 1, rank], bs_s.at[rank, d - 1],
                        bs_r.at[d - 1, rank], z * rn + lax.rem(r + d, rn), t,
                    )
                )

    def shared(k):
        rank = plan.late_rank[k]

        @pl.when(r != plan.home(k)[1])
        def _():
            d = lax.rem(r - plan.home(k)[1] + rn, rn)
            remote(
                w_side.at[0], w_beside.at[d - 1, rank], bs_s.at[0, 0], bs_r.at[d - 1, rank], s, t
            ).wait_recv()

    def out_copy(w):
        count = min(plan.ub, HD - w * plan.ub)
        return remote(
            w_out.at[w].at[pl.ds(0, count)], wo_across.at[pl.ds(w * plan.ub, count)],
            oa_s.at[w], oa_r.at[w], s, lax.rem(t + 2, TP),
        )

    def sort_group(g):
        first = meta[2 * g] == 0
        a, b = kv_out[g, :TOK_FRAME, :], kv_out[g, TOK_FRAME:, :]
        pool[g, 0] = jnp.where(first, a, b)
        pool[g, 1] = jnp.where(first, b, a)
        for kind in range(2):
            flipped[kind, g] = pool[g, kind].T

    def attend_group(zq):
        gq = zq * rn + r
        first = meta[2 * gq] == 0
        clip = meta[2 * gq] + meta[2 * gq + 1]
        parts = []
        for kind in range(2):
            low = first if kind == 0 else jnp.logical_not(first)
            rows = jnp.where(low, q_out[zq][:, :HEAD], q_out[zq][:, HEAD:])
            qt[...] = (padded(rows, True) * jnp.asarray(HEAD ** (-0.5), BF16)).T
            m_ref[...] = jnp.full_like(m_ref, -1e30)
            l_ref[...] = jnp.zeros_like(l_ref)
            acc[...] = jnp.zeros_like(acc)

            def block(p, inner):
                pair = []
                m_old = m_ref[...]
                m_new = m_old
                for e in range(2):
                    g = jnp.minimum(2 * p + e, gq)
                    shown = 2 * p + e <= gq
                    if kind == 1:
                        shown = shown & (meta[2 * g] + meta[2 * g + 1] == clip)
                    off = jnp.where(shown, 0.0, 1e30)
                    st = mm(pool[g, kind], qt[...])
                    m_new = jnp.maximum(m_new, jnp.max(st, axis=0, keepdims=True) - off)
                    pair.append((g, st, off))
                alpha = jnp.exp(m_old - m_new)
                total, out = l_ref[...] * alpha, acc[...] * alpha
                for g, st, off in pair:
                    weights = jnp.exp(st - (m_new + off))
                    total = total + jnp.sum(weights, axis=0, keepdims=True)
                    out = out + mm(flipped[kind, g], weights.astype(BF16))
                m_ref[...] = m_new
                l_ref[...] = total
                acc[...] = out
                return inner

            lax.fori_loop(0, lax.div(gq + 2, 2), block, 0)
            total = l_ref[...]
            out = acc[HEAD:, :] / total
            ot[2 * zq + kind] = out
            lse[2 * zq + kind] = m_ref[...] + jnp.log(total)
            rows = out.T
            parts.append(jnp.concatenate([rows[:PACK], rows[PACK:]], axis=1).astype(BF16))
        o[zq, 0] = jnp.where(first, parts[0], parts[1])
        o[zq, 1] = jnp.where(first, parts[1], parts[0])

    units = plan.late + plan.early
    first_up = [k for k in plan.late if k % 3 == 0 and plan.home(k)[0] > 0]
    later_up = [k for k in plan.late if k not in first_up]

    def fill(i, kind):
        k = 3 * s + i
        base = i * plan.flat_rows
        rows, cols = (plan.uq, QKV // LANES) if kind == "q" else (plan.ub, D // LANES)
        at = pl.multiple_of(k * plan.uq, plan.uq)
        for j in range(cols):
            values = master[pl.ds(base + j, rows, stride=cols), :].astype(BF16)
            if kind == "q":
                wq[pl.ds(at, rows), j * LANES : (j + 1) * LANES] = values
            else:
                own_b[i, :, j * LANES : (j + 1) * LANES] = values

    for away in (True, False):
        for i in range(3):
            k = 3 * s + i

            @pl.when((k < plan.nq) & ((lax.rem(k, rn) != r) == away))
            def _():
                fill(i, "q")
                q_own(i, start)
                if not away:
                    at = lax.div(k, rn)
                    slot_j = lax.rem(at + r, 2)
                    for h in range(CUTS):
                        q_copy(k, h, qc_s.at[CUTS * slot_j + h, 0], s + rn).start()

    for i in range(3):
        @pl.when((3 * s + i >= plan.nq) & (3 * s + i < plan.nb))
        def _():
            fill(i, "b")

    @pl.when(z == 0)
    def _():
        q_line(start, True)

    owned(units, lambda k, src: along(k, src, start, False))
    owned(first_up, lambda k, src: along(k, src, start, True))
    owned(units, lambda k, src: keep(k).start())

    macc[...] = jnp.zeros_like(macc)
    for i in range(3):
        k = 3 * s + i
        base = i * plan.flat_rows

        @pl.when(k >= plan.nb)
        def _():
            for j in range(MCOLS):
                tile[:, j * LANES : (j + 1) * LANES] = master[
                    pl.ds(base + j, plan.um, stride=MCOLS), :
                ].astype(BF16)
            macc[...] += mm(cond[k - plan.nb], tile[...])

    fm = plan.first_mod

    def m_copy(d):
        to = lax.rem(s + d, n)
        return remote(mpart.at[to], mrecv.at[s - fm], m_s.at[d - 1], m_r.at[s - fm], to, t)

    @pl.when(s >= fm)
    def _():
        for f in range(plan.frames):
            for j in range(MCOLS):
                mpart[f // F_DEV, pl.ds((f % F_DEV) * MCOLS + j, 1), :] = macc[
                    pl.ds(f, 1), j * LANES : (j + 1) * LANES
                ]
        mrecv[s - fm] = mpart[s]
        for d in range(1, n):
            m_copy(d).start()

    def norm_rows(at):
        rows = pl.ds(at, 64)
        norm[rows, :] = normalize(tokens[rows, :].astype(F32))[0]

    loop(F_DEV * TOK_FRAME, 64, norm_rows)

    @pl.when(z > 0)
    def _():
        q_line(start, True)

    owned(plan.outs, lambda k, src: along(k, src, start, True))
    owned([k for k in later_up if k not in plan.outs], lambda k, src: along(k, src, start, True))
    owned(units, lambda k, src: beside(k, src, start))
    pass_along(first_up + plan.early, 1, start, True)

    for src in range(fm, n):
        @pl.when(s != src)
        def _():
            remote(mpart.at[0], mrecv.at[src - fm], m_s.at[0], m_r.at[src - fm], s, t).wait_recv()

    total = mrecv[0]
    for src in range(1, n - fm):
        total = total + mrecv[src]
    mod[t] = total

    def t_copy(d):
        return remote(mod.at[t], mod.at[t], t_s.at[d - 1], t_r.at[t], s, lax.rem(t + d, TP))

    for d in range(1, TP):
        t_copy(d).start()
    for d in range(1, TP):
        other = lax.rem(t + d, TP)
        remote(mod.at[t], mod.at[other], t_s.at[0], t_r.at[other], s, t).wait_recv()
    for f in range(F_DEV):
        for block in range(TP * MCOLS):
            part, at = block // (D // LANES), block % (D // LANES)
            mods[f * 6 + part : f * 6 + part + 1, at * LANES : (at + 1) * LANES] = mod[
                block // MCOLS, f * MCOLS + block % MCOLS : f * MCOLS + block % MCOLS + 1, :
            ]

    def affine(f):
        def body(at):
            rows = pl.ds(f * TOK_FRAME + at, 64)
            first_in[rows, :] = (
                norm[rows, :] * (1.0 + mods[f * 6 + 1 : f * 6 + 2, :]) + mods[f * 6 : f * 6 + 1, :]
            ).astype(BF16)

        loop(TOK_FRAME, 64, body)

    for f in range(F_DEV):
        affine(f)

    for k in range(plan.nq):
        for h in range(CUTS):
            if rn > 1:
                at_zero = (z == 0) & (k // 3 != r) & (k % rn != r)

                @pl.when(at_zero | (z > 0) & (k % rn != r))
                def _():
                    q_arrived(k, h)

    keys = mm(first_in[...], wq[:, HD : 2 * HD]).astype(BF16)
    values = mm(first_in[...], wq[:, 2 * HD :]).astype(BF16)
    for h in range(ZN):
        cols = slice(h * HEAD, (h + 1) * HEAD)
        kv_send[h] = jnp.concatenate([keys[:, cols], values[:, cols]], axis=1)

    def kv_copy(d):
        h = lax.rem(z + d, ZN)
        return remote(kv_send.at[h], kv_out.at[s], ks.at[d - 1], kr.at[z], h * rn + r, t)

    def a_copy(d):
        h = lax.rem(z + d, ZN)
        return remote(q_send.at[h], q_out.at[z], as_.at[d - 1], ar.at[z], h * rn + r, t)

    def side_copy(zs, e):
        at = zs * rn + r
        ref = kv_out.at[at]
        return remote(ref, ref, xs.at[zs, e - 1], xr.at[at], z * rn + lax.rem(r + e, rn), t)

    for d in range(1, ZN):
        kv_copy(d).start()
    kv_out[s] = kv_send[z]
    for e in range(1, rn):
        side_copy(z, e).start()
    queries = mm(first_in[...], wq[:, :HD]).astype(BF16)
    for h in range(ZN):
        cols = slice(h * HEAD, (h + 1) * HEAD)
        q_send[h] = jnp.concatenate([queries[:TOK_FRAME, cols], queries[TOK_FRAME:, cols]], axis=1)
    for d in range(1, ZN):
        a_copy(d).start()
    q_out[z] = q_send[z]

    rest = [k for k in plan.sided if k not in first_up]
    pass_along(plan.outs + rest, 1, start, True)
    for k in plan.early:
        hop(k, start)
    owned(units, lambda k, src: keep(k).wait())
    for k in plan.sided:
        settle(k, True)
        share(k, start, True)

    def kv_come(zs):
        @pl.when(z != zs)
        def _():
            remote(kv_send.at[0], kv_out.at[zs * rn + r], ks.at[0], kr.at[zs], s, t).wait_recv()
            for e in range(1, rn):
                side_copy(zs, e).start()

    def ready(zq):
        for e in range(1, rn):
            at = zq * rn + lax.rem(r + e, rn)
            remote(kv_out.at[at], kv_out.at[at], xs.at[0, 0], xr.at[at], s, t).wait_recv()
        for other in range(rn):
            sort_group(zq * rn + other)

        @pl.when(z != zq)
        def _():
            remote(q_send.at[0], q_out.at[zq], as_.at[0], ar.at[zq], s, t).wait_recv()

    kv_come(0)
    kv_come(1)
    pass_along(plan.outs, 2, start, True)
    ready(0)
    attend_group(0)
    kv_come(2)
    kv_come(3)
    pass_along(plan.outs, 3, start, True)
    ready(1)
    attend_group(1)
    for d in range(2, ZN):
        pass_along(plan.sided, d, start, True)
    for k in plan.sided:
        settle(k, False)
        share(k, start, False)
    ready(2)
    attend_group(2)
    for k in plan.outs:
        @pl.when(r != plan.home(k)[1])
        def _():
            arrived(k)

    for w in range(len(plan.outs)):
        out_copy(w).start()
    ready(3)
    attend_group(3)
    for k in plan.early:
        hopped(k)
        zo, ro = plan.home(k)
        if zo > 1:
            @pl.when((r == ro) & (z == 0))
            def _():
                arrived(k)

    for k in plan.sided:
        shared(k)
    for w in range(len(plan.outs)):
        out_copy(w).wait()

    for k in plan.early:
        zo, ro = plan.home(k)

        @pl.when((r != ro) & (z <= zo) & (z >= zo - 1))
        def _():
            arrived(k)

        hop(k, done)
    for k in plan.sided:
        share(k, done)
    for i in range(3):
        q_own(i, done)
    q_line(done, False, True)
    owned(units, lambda k, src: along(k, src, done, False))
    owned(plan.late, lambda k, src: along(k, src, done, True))
    owned(units, lambda k, src: beside(k, src, done))
    for d in range(1, ZN):
        pass_along(units, d, done, False)

    @pl.when(s >= fm)
    def _():
        for d in range(1, n):
            m_copy(d).wait_send()

    for d in range(1, TP):
        t_copy(d).wait_send()
    for d in range(1, ZN):
        kv_copy(d).wait_send()
        a_copy(d).wait_send()
    for zs in range(ZN):
        for e in range(1, rn):
            side_copy(zs, e).wait_send()


def head_part(plan, meta, master, cond_units, tokens, cid):
    n, rn = plan.n, plan.r
    mrows = F_DEV * MCOLS
    rows = F_DEV * TOK_FRAME
    mods = n - plan.first_mod
    return call(
        functools.partial(head_kernel, plan),
        (
            jax.ShapeDtypeStruct((D, QKV), BF16),
            jax.ShapeDtypeStruct((len(plan.outs), plan.ub, D), BF16),
            jax.ShapeDtypeStruct((plan.late_ranks, plan.ub, D), BF16),
            jax.ShapeDtypeStruct((len(plan.early), plan.ub, D), BF16),
            jax.ShapeDtypeStruct((3, plan.ub, D), BF16),
            jax.ShapeDtypeStruct((rn - 1, plan.late_ranks, plan.ub, D), BF16),
            jax.ShapeDtypeStruct((HD, D), BF16),
            jax.ShapeDtypeStruct((F_DEV * 6, D), F32),
            jax.ShapeDtypeStruct((rows, D), BF16),
            jax.ShapeDtypeStruct((ZN, TOK_FRAME, LANES), BF16),
            jax.ShapeDtypeStruct((n, rows, LANES), BF16),
            jax.ShapeDtypeStruct((ZN, F_DEV, PACK, LANES), BF16),
            jax.ShapeDtypeStruct((ZN * F_DEV, HEAD, TOK_FRAME), F32),
            jax.ShapeDtypeStruct((ZN * F_DEV, 1, TOK_FRAME), F32),
        ),
        [
            pltpu.VMEM((3, plan.ub, D), BF16),
            pltpu.VMEM((n, 2, TOK_FRAME, LANES), BF16),
            pltpu.VMEM((2, n, LANES, TOK_FRAME), BF16),
            pltpu.VMEM((LANES, TOK_FRAME), BF16),
            pltpu.VMEM((1, TOK_FRAME), F32),
            pltpu.VMEM((1, TOK_FRAME), F32),
            pltpu.VMEM((LANES, TOK_FRAME), F32),
            pltpu.VMEM((plan.um, MT), BF16),
            pltpu.VMEM((plan.frames, MT), F32),
            pltpu.VMEM((n, mrows, LANES), F32),
            pltpu.VMEM((mods, mrows, LANES), F32),
            pltpu.VMEM((TP, mrows, LANES), F32),
            pltpu.VMEM((rows, D), F32),
            pltpu.VMEM((ZN, TOK_FRAME, LANES), BF16),
            pltpu.VMEM((ZN, rows, LANES), BF16),
            DMA((3 * CUTS, rn - 1)), DMA((2 * CUTS, rn)), DMA((CUTS * plan.nq,)),
            DMA((len(plan.outs), rn + 1)), DMA((len(plan.outs),)),
            DMA((plan.late_ranks, 2)), DMA((plan.late_ranks,)),
            DMA((plan.ranks, rn + 1)), DMA((len(plan.early),)), DMA((3,)),
            DMA((n - 1,)), DMA((mods,)), DMA((TP - 1,)), DMA((TP,)),
            DMA((ZN - 1,)), DMA((ZN,)), DMA((ZN - 1,)), DMA((ZN,)), DMA((ZN, rn - 1)), DMA((n,)),
            DMA((3,)), DMA((3,)), DMA((plan.late_ranks, rn - 1)), DMA((rn - 1, plan.late_ranks)),
            DMA((len(plan.outs),)), DMA((len(plan.outs),)),
        ],
        [SM] + [VM] * 3,
        cid,
        out_specs=(VM,) + (ANY,) * 6 + (VM,) * 7,
        name="head_part",
    )(meta, master, cond_units, tokens)


def padded(rows, low):
    zero = jnp.zeros_like(rows)
    return jnp.concatenate([rows, zero] if low else [zero, rows], axis=1)


def middle_kernel(
    plan, o_mine, wo_across, w_out, w_side, w_beside, w_early, w_below, tokens, grad_out, mod,
    result, late_own, late_send, esum, ebuf, do_out, dmid, dmod,
    gb, wb, eside, eend, wo, oall, attended, attn, mid, norm, inv, sin, hidden, dmlp, slopes, dup,
    own, csend, crecv, ysend, yrecv, dattn, dsend, dwo, wsend, wrecv,
    o_s, o_r, f_s, f_r, n_s, n_r, c_s, c_r, y_s, y_r, d_s, d_r, w_s, w_r, e_s, e_r, p_s, p_r, l_s, u_s, u_r, g_s, g_r, j_s, h_s, h_r, i_s, i_r,
):
    s, t, z, r = place(plan)
    rn = plan.r
    y = lax.div(t, 2)
    c = lax.rem(t, 2)
    sib = 2 * y + 1 - c
    across = lax.rem(t + 2, TP)
    mine = pl.multiple_of(c * TOK_FRAME, TOK_FRAME)
    theirs = pl.multiple_of((1 - c) * TOK_FRAME, TOK_FRAME)
    pairs = [(d, e) for d in range(ZN) for e in range(2)][1:]

    def partner(d, e):
        return lax.rem(z + d, ZN), (c if e == 0 else 1 - c)

    greet(
        [(partner(d, e)[0] * rn + r, 2 * y + partner(d, e)[1]) for d, e in pairs]
        + [(s, across)]
        + [(z * rn + lax.rem(r + d, rn), t) for d in range(1, rn)]
    )

    def home(k):
        return (k // 3) // rn, (k // 3) % rn, k - plan.half

    def w_rows(ref, k):
        return ref.at[pl.ds((k - plan.nq) * plan.ub, plan.ub)]

    def late_loads(act):
        for k in plan.late:
            sem = l_s.at[k - plan.nq]
            if k in plan.outs:
                act(pltpu.make_async_copy(w_out.at[k - plan.nq], w_rows(wb, k), sem))
            else:
                zo, ro = plan.home(k)
                rank = plan.late_rank[k]

                @pl.when(r == ro)
                def _():
                    act(pltpu.make_async_copy(w_side.at[rank], w_rows(wb, k), sem))

                @pl.when(r != ro)
                def _():
                    d = lax.rem(r - ro + rn, rn)
                    act(pltpu.make_async_copy(w_beside.at[d - 1, rank], w_rows(wb, k), sem))

    def loads(act):
        for k in plan.early:
            zo, ro, at = home(k)

            @pl.when((z <= zo) & ((z >= zo - 1) | (r == ro)))
            def _():
                act(pltpu.make_async_copy(w_early.at[at], w_rows(wb, k), l_s.at[len(plan.late) + at]))

            @pl.when((z == zo + 1) & (r == ro))
            def _():
                act(
                    pltpu.make_async_copy(
                        w_below.at[k % 3], w_rows(wb, k), l_s.at[len(plan.late) + at]
                    )
                )

    def rise(k, src, act):
        zo, ro, at = home(k)

        @pl.when((z < ZN - 1) & (z > zo))
        def _():
            act(remote(src, w_rows(wb, k), u_s.at[at, 0], u_r.at[at], s + rn, t))

        for d in range(1, rn):
            act(
                remote(
                    src, w_rows(wb, k), u_s.at[at, d], u_r.at[at],
                    z * rn + lax.rem(r + d, rn), t,
                )
            )

    def risen(k):
        remote(w_below.at[0], w_rows(wb, k), u_s.at[0, 0], u_r.at[k - plan.half], s, t).wait_recv()

    def rises(act, first, wait):
        for k in plan.early:
            zo, ro, at = home(k)
            if first:
                @pl.when((z == zo + 1) & (r == ro))
                def _():
                    rise(k, w_below.at[k % 3], act)

                if zo > 1:
                    @pl.when((z < zo - 1) & (r == ro))
                    def _():
                        rise(k, w_early.at[at], act)

            else:
                @pl.when((z > zo + 1) & (r == ro))
                def _():
                    if wait:
                        risen(k)
                    rise(k, w_rows(wb, k), act)

    def o_copy(d, e):
        zd, cd = partner(d, e)
        return remote(
            o_mine.at[zd, cd], oall.at[y * 8 + c * ZN + z], o_s.at[2 * d + e],
            o_r.at[c * ZN + z], zd * rn + r, 2 * y + cd,
        )

    def f_copy(slot):
        ref = oall.at[y * 8 + slot]
        return remote(ref, ref, f_s.at[slot], f_r.at[slot], s, across)

    def p_copy(i, tp):
        ref = wo.at[pl.ds(pl.multiple_of(tp * HD, HD), HD)]
        return remote(ref, ref, p_s.at[i], p_r.at[i], s, sib)

    for d, e in pairs:
        o_copy(d, e).start()
    start = lambda copy: copy.start()
    rises(start, True, False)
    late_loads(start)
    loads(start)
    late_loads(lambda copy: copy.wait())
    wo[pl.ds(pl.multiple_of(t * HD, HD), HD), :] = wb[:HD, :]
    p_copy(0, t).start()
    wo[pl.ds(pl.multiple_of(across * HD, HD), HD), :] = wo_across[...]
    p_copy(1, across).start()
    oall[y * 8 + c * ZN + z] = o_mine[z, c]
    f_copy(c * ZN + z).start()

    def d_mlp(f):
        def body(at):
            rows = pl.ds(f * TOK_FRAME + at, 64)
            dmlp[rows, :] = (grad_out[rows, :].astype(F32) * mod[f * 6 + 5 : f * 6 + 6, :]).astype(
                BF16
            )

        loop(TOK_FRAME, 64, body)

    for f in range(F_DEV):
        d_mlp(f)

    for d, e in pairs:
        zd, cd = partner(d, e)
        slot = cd * ZN + zd
        remote(o_mine.at[0, 0], oall.at[y * 8 + slot], o_s.at[0], o_r.at[slot], s, t).wait_recv()
        f_copy(slot).start()
    for slot in range(8):
        remote(
            oall.at[0], oall.at[(1 - y) * 8 + slot], f_s.at[slot], f_r.at[slot], s, t
        ).wait_recv()
    for m in range(HEADS // 2):
        a, b = oall[2 * m], oall[2 * m + 1]
        cols = slice(m * LANES, (m + 1) * LANES)
        attended[:PACK, cols] = jnp.concatenate([a[:, :HEAD], b[:, :HEAD]], axis=1)
        attended[PACK:, cols] = jnp.concatenate([a[:, HEAD:], b[:, HEAD:]], axis=1)

    p_copy(0, sib).wait_recv()
    p_copy(1, lax.rem(sib + 2, TP)).wait_recv()

    def attn_tile(at):
        attn[:, pl.ds(at, TILE)] = mm(attended[...], wo[:, pl.ds(at, TILE)])

    loop(D, TILE, attn_tile)
    rises(start, False, True)

    row = lambda part: mod[pl.ds(c * 6 + part, 1), :]

    def norm_rows(at):
        rows = pl.ds(at, 64)
        values = tokens[pl.ds(mine + at, 64), :].astype(F32) + row(2) * attn[rows, :]
        mid[rows, :] = values
        normed, inverse = normalize(values)
        norm[rows, :] = normed
        inv[rows, :] = inverse
        sin[pl.ds(mine + at, 64), :] = (normed * (1.0 + row(4)) + row(3)).astype(BF16)

    loop(TOK_FRAME, 64, norm_rows)

    def n_copy(base):
        ref = sin.at[pl.ds(base, TOK_FRAME)]
        return remote(ref, ref, n_s.at[0], n_r.at[0], s, sib)

    n_copy(mine).start()
    loads(lambda copy: copy.wait())
    for k in plan.early:
        zo, ro, at = home(k)

        @pl.when(((z > zo) | (z < zo - 1)) & (r != ro))
        def _():
            risen(k)

    def feed(base):
        rows = pl.ds(base, TOK_FRAME)

        def tile(at):
            cols = pl.ds(at, TILE)
            u = mm(sin[rows, :], wb[HD : HD + FT, cols])
            square = u * u
            inner = GELU_A * u * (1.0 + GELU_B * square)
            th = jnp.tanh(inner)
            half = 0.5 * (1.0 + th)
            hidden[rows, cols] = (u * half).astype(BF16)
            slopes[rows, cols] = half + 0.5 * u * (1.0 - th * th) * (
                GELU_A * (1.0 + 3.0 * GELU_B * square)
            )

        loop(FT, TILE, tile)

    feed(mine)
    n_copy(theirs).wait_recv()
    feed(theirs)

    def d_up(at):
        cols = pl.ds(at, TILE)
        dup[:, cols] = (mm_nt(dmlp[...], wb[pl.ds(HD + FT + at, TILE), :]) * slopes[:, cols]).astype(
            BF16
        )

    loop(FT, TILE, d_up)

    def c_copy(w, n):
        return remote(csend.at[w, n], crecv.at[w, n], c_s.at[w, n], c_r.at[w, n], s, sib)

    def y_copy(w, n):
        return remote(ysend.at[w, n], yrecv.at[w, n], y_s.at[w, n], y_r.at[w, n], s, across)

    def pass_on(w, n):
        c_copy(w, n).wait_recv()
        ysend[w, n] = (own[n] + crecv[w, n].astype(F32)).astype(BF16)
        y_copy(w, n).start()

    def product(w, base, n):
        rows = pl.ds(base, TOK_FRAME)
        if w == 0:
            return mm_nt(dup[rows, :], wb[HD + n * TILE : HD + (n + 1) * TILE, :])
        return mm(hidden[rows, :], wb[HD + FT :, n * TILE : (n + 1) * TILE])

    def products(w):
        for n in range(TILES):
            csend[w, n] = product(w, theirs, n).astype(BF16)
            c_copy(w, n).start()
            own[n] = product(w, mine, n)
            if n:
                pass_on(w, n - 1)
        pass_on(w, TILES - 1)

    def down_grad(at):
        gb[pl.ds(HD + FT + at, TILE), :] = mm_tn(hidden[:, pl.ds(at, TILE)], dmlp[...]).astype(BF16)

    def up_grad(at):
        gb[pl.ds(HD + at, TILE), :] = mm_tn(sin[:, pl.ds(at, TILE)], dup[...]).astype(BF16)

    def early_grad(k, d):
        zo, ro, at = home(k)
        slot = lax.rem(ro - r + rn, rn) - 1 if d is None else d - 1
        return remote(
            w_rows(gb, k), eside.at[slot, plan.rank[k]], g_s.at[at], g_r.at[slot, plan.rank[k]],
            z * rn + ro, t,
        )

    def early_grads(act):
        for k in plan.early:
            zo, ro, at = home(k)

            @pl.when(r != ro)
            def _():
                act(early_grad(k, None))

    def early_hop(rank, act):
        for here, to in ((ZN - 1, s - rn), (0, s + rn)):
            @pl.when(z == here)
            def _():
                act(remote(esum.at[rank], eend.at[rank], h_s.at[rank], h_r.at[rank], to, t))

    def early_total(rank):
        for k in plan.early:
            if plan.rank[k] == rank:
                zo, ro, at = home(k)

                @pl.when(r == ro)
                def _():
                    for d in range(1, rn):
                        early_grad(k, d).wait_recv()

                    def body(at):
                        rows = pl.ds(at, 16)
                        total = gb[pl.ds((k - plan.nq) * plan.ub + at, 16), :].astype(F32)
                        for d in range(1, rn):
                            total = total + eside[d - 1, rank, rows, :].astype(F32)
                        esum[rank, rows, :] = total.astype(BF16)

                    loop(plan.ub, 16, body)
                    early_hop(rank, start)

    def early_pass(rank, to):
        return remote(esum.at[rank], ebuf.at[rank], i_s.at[rank], i_r.at[rank], to, t)

    def early_inner(rank):
        for k in plan.early:
            if plan.rank[k] == rank:
                zo, ro, at = home(k)

                @pl.when((r == ro) & (z > 0) & (z < ZN - 1))
                def _():
                    remote(
                        esum.at[rank], eend.at[rank], h_s.at[rank], h_r.at[rank], s, t
                    ).wait_recv()

                    def body(at):
                        rows = pl.ds(at, 16)
                        esum[rank, rows, :] = (
                            esum[rank, rows, :].astype(F32) + eend[rank, rows, :].astype(F32)
                        ).astype(BF16)

                    loop(plan.ub, 16, body)

                    @pl.when(z != zo)
                    def _():
                        early_pass(rank, s + rn if zo == 2 else s - rn).start()

    def early_close(rank):
        for k in plan.early:
            if plan.rank[k] == rank:
                zo, ro, at = home(k)

                @pl.when((r == ro) & (z == zo))
                def _():
                    early_pass(rank, s).wait_recv()

                @pl.when((r == ro) & (z == 3 - zo))
                def _():
                    early_pass(rank, s).wait_send()

    def early_hops_done(rank):
        for k in plan.early:
            if plan.rank[k] == rank:
                @pl.when(r == home(k)[1])
                def _():
                    early_hop(rank, lambda copy: copy.wait_send())

    loop(FT, TILE, down_grad)
    up_grad(D - TILE)
    early_grads(start)
    products(0)
    products(1)
    loop(D - TILE, TILE, up_grad)
    early_total(0)
    early_total(1)
    early_inner(0)

    dm = dmod
    dm[...] = jnp.zeros_like(dm)
    for n in range(TILES):
        y_copy(0, n).wait_recv()

    def total(w, rows):
        return jnp.concatenate(
            [ysend[w, n, rows].astype(F32) + yrecv[w, n, rows].astype(F32) for n in range(TILES)],
            axis=1,
        )

    def back_rows(at):
        rows = pl.ds(at, 64)
        tok_rows = pl.ds(mine + at, 64)
        grads = total(0, rows)
        normed = norm[rows, :]
        add_to(dm, 1, grads)
        add_to(dm, 2, grads * normed)
        values = grad_out[tok_rows, :].astype(F32) + norm_back(
            grads * (1.0 + row(4)), normed, inv[rows, :]
        )
        dmid[rows, :] = values
        add_to(dm, 0, attn[rows, :] * values)
        dattn[rows, :] = (row(2) * values).astype(BF16)

    loop(TOK_FRAME, 64, back_rows)
    for ch in range(2):
        part = mm_nt(dattn[...], wo[pl.ds(pl.multiple_of((2 * y + ch) * HD, HD), HD), :]).astype(BF16)
        for zh in range(ZN):
            cols = slice(zh * HEAD, (zh + 1) * HEAD)
            dsend[ch * ZN + zh] = jnp.concatenate([part[:PACK, cols], part[PACK:, cols]], axis=1)

    def d_copy(d, e):
        zd, cd = partner(d, e)
        return remote(
            dsend.at[cd * ZN + zd], do_out.at[z, c], d_s.at[2 * d + e], d_r.at[2 * z + c],
            zd * rn + r, 2 * y + cd,
        )

    for d, e in pairs:
        d_copy(d, e).start()
    do_out[z, c] = dsend[c * ZN + z]
    for rank in range(2, plan.ranks):
        early_total(rank)

    def o_grad(head_core):
        cols = pl.ds(pl.multiple_of((2 * y + head_core) * HD, HD), HD)
        return mm_tn(attended[:, cols], dattn[...])

    w_copy = remote(wsend, wrecv, w_s, w_r, s, sib)
    wsend[...] = o_grad(1 - c).astype(BF16)
    w_copy.start()
    dwo[...] = o_grad(c)
    early_inner(1)

    for n in range(TILES):
        y_copy(1, n).wait_recv()

    def result_rows(at):
        rows = pl.ds(at, 64)
        tok_rows = pl.ds(mine + at, 64)
        mlp = total(1, rows)
        add_to(dm, 3, mlp * grad_out[tok_rows, :].astype(F32))
        result[tok_rows, :] = (mid[rows, :] + row(5) * mlp).astype(BF16)

    loop(TOK_FRAME, 64, result_rows)

    def e_copy(base):
        ref = result.at[pl.ds(base, TOK_FRAME)]
        return remote(ref, ref, e_s, e_r, s, sib)

    e_copy(mine).start()
    for rank in range(2, plan.ranks):
        early_inner(rank)
    w_copy.wait_recv()
    gb[:HD, :] = (dwo[...] + wrecv[...].astype(F32)).astype(BF16)

    for d, e in pairs:
        zd, cd = partner(d, e)
        remote(
            dsend.at[0], do_out.at[zd, cd], d_s.at[0], d_r.at[2 * zd + cd], s, t
        ).wait_recv()
    def late_grads(act):
        for k in plan.late:
            zo, ro = plan.home(k)
            rank, sem = plan.grad_rank[k], j_s.at[k - plan.nq]

            @pl.when(r == ro)
            def _():
                act(pltpu.make_async_copy(w_rows(gb, k), late_own.at[rank], sem))

            @pl.when(r != ro)
            def _():
                d = lax.rem(ro - r + rn, rn)
                act(pltpu.make_async_copy(w_rows(gb, k), late_send.at[d - 1, rank], sem))

    late_grads(start)
    for rank in range(plan.ranks):
        early_close(rank)
    e_copy(theirs).wait_recv()
    done = lambda copy: copy.wait_send()
    early_grads(done)
    for rank in range(plan.ranks):
        early_hops_done(rank)
    late_grads(lambda copy: copy.wait())
    rises(done, True, False)
    rises(done, False, False)
    for d, e in pairs:
        o_copy(d, e).wait_send()
        d_copy(d, e).wait_send()
    for slot in range(8):
        f_copy(slot).wait_send()
    n_copy(mine).wait_send()
    p_copy(0, t).wait_send()
    p_copy(1, across).wait_send()
    for w in range(2):
        for n in range(TILES):
            c_copy(w, n).wait_send()
            y_copy(w, n).wait_send()
    w_copy.wait_send()
    e_copy(mine).wait_send()


def middle_part(plan, o_mine, wo_across, weights, tokens, grad_out, mod_rows, cid):
    rn, count = plan.r, len(plan.early)
    rows = F_DEV * TOK_FRAME
    half = lambda dtype: pltpu.VMEM((TOK_FRAME, D), dtype)
    full = lambda dtype: pltpu.VMEM((rows, D), dtype)
    tiles = pltpu.VMEM((2, TILES, TOK_FRAME, TILE), BF16)
    return call(
        functools.partial(middle_kernel, plan),
        (
            jax.ShapeDtypeStruct((rows, D), BF16),
            jax.ShapeDtypeStruct((plan.grad_ranks, plan.ub, D), BF16),
            jax.ShapeDtypeStruct((rn - 1, plan.grad_ranks, plan.ub, D), BF16),
            jax.ShapeDtypeStruct((plan.ranks, plan.ub, D), BF16),
            jax.ShapeDtypeStruct((plan.ranks, plan.ub, D), BF16),
            jax.ShapeDtypeStruct((ZN, F_DEV, PACK, LANES), BF16),
            jax.ShapeDtypeStruct((TOK_FRAME, D), F32),
            jax.ShapeDtypeStruct((8, D), F32),
        ),
        [
            pltpu.VMEM((BROWS, D), BF16),
            pltpu.VMEM((BROWS, D), BF16),
            pltpu.VMEM((rn - 1, plan.ranks, plan.ub, D), BF16),
            pltpu.VMEM((plan.ranks, plan.ub, D), BF16),
            pltpu.VMEM((HEADS * HEAD, D), BF16),
            pltpu.VMEM((HEADS, PACK, LANES), BF16),
            half(BF16), half(F32), half(F32), half(F32), pltpu.VMEM((TOK_FRAME, 1), F32),
            full(BF16), full(BF16), full(BF16), full(F32), full(BF16),
            pltpu.VMEM((TILES, TOK_FRAME, TILE), F32), tiles, tiles, tiles, tiles,
            half(BF16), pltpu.VMEM((8, PACK, LANES), BF16),
            pltpu.VMEM((HD, D), F32), pltpu.VMEM((HD, D), BF16), pltpu.VMEM((HD, D), BF16),
            DMA((8,)), DMA((8,)), DMA((8,)), DMA((8,)), DMA((1,)), DMA((1,)),
            DMA((2, TILES)), DMA((2, TILES)), DMA((2, TILES)), DMA((2, TILES)),
            DMA((8,)), DMA((8,)), DMA, DMA, DMA, DMA, DMA((2,)), DMA((2,)),
            DMA((len(plan.late) + count,)), DMA((count, rn)), DMA((count,)), DMA((count,)), DMA((rn - 1, plan.ranks)),
            DMA((len(plan.late),)), DMA((plan.ranks,)), DMA((plan.ranks,)),
            DMA((plan.ranks,)), DMA((plan.ranks,)),
        ],
        [VM, VM, ANY, ANY, ANY, ANY, ANY, VM, VM, VM],
        cid,
        out_specs=(VM, ANY, ANY, VM, VM, VM, VM, VM),
        name="middle_part",
    )(o_mine, wo_across, *weights, tokens, grad_out, mod_rows)


def tail_kernel(
    plan, meta, q, kv, do, ot, lse, first_in, wq, tokens, dmid, mod, dm4, late_own, late_send, esum, ebuf,
    igrad, oq, ob, dall,
    keys, flipped, qs, gs, qgt, drow, acc, dq_acc, dq, kv_two, lside,
    stage, side, q_in, kv_in, dqkv, gq, own, csend, crecv, ysend, yrecv, dm, dm3, dboth,
    lstage, cb, qside, qpeer, qchain, qstage,
    q_s, q_r, k_s, k_r, x_s, x_r, c_s, c_r, y_s, y_r, e_s, e_r, h_s, h_r, m_s, m_r, t_s, t_r,
    kv_s, ls_s, ls_r, qo_s, qs_r, qp_r, qc_s, qc_r,
):
    s, t, z, r = place(plan)
    n, rn = plan.n, plan.r
    y = lax.div(t, 2)
    c = lax.rem(t, 2)
    sib = 2 * y + 1 - c
    across = lax.rem(t + 2, TP)
    mine = pl.multiple_of(c * TOK_FRAME, TOK_FRAME)
    theirs = pl.multiple_of((1 - c) * TOK_FRAME, TOK_FRAME)
    greet([(lax.rem(s + d, n), t) for d in range(1, n)] + [(s, sib), (s, across)])

    def side_copy(zs, e):
        other = lax.rem(r + e, rn)
        return remote(
            keys.at[zs * rn + other], side.at[e - 1, zs], x_s.at[zs, e - 1], x_r.at[zs, e - 1],
            z * rn + other, t,
        )

    def q_copy(zs):
        return remote(dq.at[zs], q_in.at[z], q_s.at[zs], q_r.at[z], zs * rn + r, t)

    def kv_copy(zs):
        return remote(stage.at[zs], kv_in.at[z], k_s.at[zs], k_r.at[z], zs * rn + r, t)

    def send_q(zs):
        @pl.when(z == zs)
        def _():
            q_in[zs] = dq[zs]

        @pl.when(z != zs)
        def _():
            q_copy(zs).start()

    def send_kv(zs):
        total = keys[zs * rn + r].astype(F32)
        for e in range(1, rn):
            side_copy(zs, e).wait_recv()
            total = total + side[e - 1, zs].astype(F32)
        stage[zs] = total.astype(BF16)

        @pl.when(z == zs)
        def _():
            kv_in[zs] = stage[zs]

        @pl.when(z != zs)
        def _():
            kv_copy(zs).start()

    scale = HEAD ** (-0.5)
    acc[...] = jnp.zeros_like(acc)

    def load(g, slot):
        return pltpu.make_async_copy(kv.at[g], kv_two.at[slot], kv_s.at[slot])

    load(0, 0).start()

    def sort_group(g, carry):
        slot = lax.rem(g, 2)

        @pl.when(g + 1 < n)
        def _():
            load(g + 1, 1 - slot).start()

        load(g, slot).wait()
        first = meta[2 * g] == 0
        a, b = kv_two[slot, :TOK_FRAME, :], kv_two[slot, TOK_FRAME:, :]
        keys[g, 0] = jnp.where(first, a, b)
        keys[g, 1] = jnp.where(first, b, a)
        for kind in range(2):
            flipped[kind, g] = keys[g, kind].T
        return carry

    lax.fori_loop(0, n, sort_group, 0)

    def attend_back_group(zq):
        gq = zq * rn + r
        first = meta[2 * gq] == 0
        clip = meta[2 * gq] + meta[2 * gq + 1]
        parts = []
        for kind in range(2):
            low = first if kind == 0 else jnp.logical_not(first)
            qz = padded(jnp.where(low, q[zq][:, :HEAD], q[zq][:, HEAD:]), True) * jnp.asarray(scale, BF16)
            gpack = jnp.where(low, do[zq, 0], do[zq, 1])
            grads = jnp.concatenate([gpack[:, :HEAD], gpack[:, HEAD:]], axis=0)
            out = ot[2 * zq + kind]
            logs = lse[2 * zq + kind]
            gz = padded(grads, False)
            qs[...] = qz
            gs[...] = gz
            qgt[:, :TOK_FRAME] = qz.T
            qgt[:, TOK_FRAME:] = gz.T
            drow[...] = jnp.sum(grads.astype(F32).T * out, axis=0, keepdims=True)
            dq_acc[...] = jnp.zeros_like(dq_acc)

            def block(p, inner):
                total = dq_acc[...]
                for e in range(2):
                    g = jnp.minimum(2 * p + e, gq)
                    shown = 2 * p + e <= gq
                    if kind == 1:
                        shown = shown & (meta[2 * g] + meta[2 * g + 1] == clip)
                    off = jnp.where(shown, 0.0, 1e30)
                    key = keys[g, kind]
                    pt = jnp.exp(mm(key, qgt[:, :TOK_FRAME]) - (logs + off))
                    dst = (pt * (mm(key, qgt[:, TOK_FRAME:]) - drow[...])).astype(BF16)
                    acc[kind, g] += mm(dst, qs[...]) + mm(pt.astype(BF16), gs[...])
                    total = total + mm(flipped[kind, g], dst)
                dq_acc[...] = total
                return inner

            lax.fori_loop(0, lax.div(gq + 2, 2), block, 0)
            parts.append((dq_acc[:HEAD, :] * scale).T.astype(BF16))
        dq[zq] = jnp.concatenate(
            [jnp.where(first, parts[0], parts[1]), jnp.where(first, parts[1], parts[0])], axis=1
        )
        for other in range(rn):
            g = zq * rn + other
            low = meta[2 * g] == 0
            a, b = acc[0, g].astype(BF16), acc[1, g].astype(BF16)
            keys[g, 0] = jnp.where(low, a, b)
            keys[g, 1] = jnp.where(low, b, a)

    def late(units, act):
        for k in units:
            zo, ro = plan.home(k)

            @pl.when(r == ro)
            def _():
                act(k, zo, plan.grad_rank[k])

    def late_copy(rank, below, to):
        return remote(lstage.at[rank], cb.at[below, rank], t_s.at[rank], t_r.at[below, rank], to, t)

    def late_side(rank, d):
        return remote(
            late_send.at[d - 1, rank], lside.at[d - 1, rank], ls_s.at[rank, d - 1],
            ls_r.at[rank, d - 1], z * rn + lax.rem(r + d, rn), t,
        )

    def late_sides(rank, act):
        for d in range(1, rn):
            act(late_side(rank, d))

    def late_step(k, zo, rank, here_z, above, below, final):
        @pl.when(z == here_z)
        def _():
            for d in range(1, rn):
                late_side(rank, d).wait_recv()
            if above:
                late_copy(rank, 0, s).wait_recv()
            if below:
                late_copy(rank, 1, s).wait_recv()

            def body(at):
                rows = pl.ds(at, 16)
                total = late_own[rank, rows, :].astype(F32)
                for d in range(1, rn):
                    total = total + lside[d - 1, rank, rows, :].astype(F32)
                if above:
                    total = total + cb[0, rank, rows, :].astype(F32)
                if below:
                    total = total + cb[1, rank, rows, :].astype(F32)
                if final:
                    ob[k % 3, rows, :] = total
                else:
                    lstage[rank, rows, :] = total.astype(BF16)

            loop(plan.ub, 16, body)
            if not final:
                late_copy(
                    rank, 0 if here_z > zo else 1, s - rn if here_z > zo else s + rn
                ).start()

    def late_ends(k, zo, rank):
        late_step(k, zo, rank, ZN - 1, False, False, False)
        if zo > 0:
            late_step(k, zo, rank, 0, False, False, False)

    def late_inner(here):
        def act(k, zo, rank):
            if here > zo:
                late_step(k, zo, rank, here, True, False, False)

        return act

    def late_final(k, zo, rank):
        late_step(k, zo, rank, zo, True, zo > 0, True)

    def late_done(k, zo, rank):
        @pl.when(z != zo)
        def _():
            late_copy(rank, 0, s).wait_send()

    def early_units(act):
        for k in plan.early:
            zo, ro, rank = (k // 3) // rn, (k // 3) % rn, plan.rank[k]

            @pl.when(r == ro)
            def _():
                act(k, zo, rank)

    def early_final(k, zo, rank):
        @pl.when(z == zo)
        def _():
            def body(at):
                rows = pl.ds(at, 16)
                ob[k % 3, rows, :] = esum[rank, rows, :].astype(F32) + ebuf[rank, rows, :].astype(F32)

            loop(plan.ub, 16, body)

    hq = plan.uq // CUTS

    def q_rows(k, h):
        return gq.at[pl.ds(pl.multiple_of(k * plan.uq + h * hq, hq), hq)]

    def q_sides(k, act):
        tc, ro, j = k % rn, k // 3, k // rn
        for h in range(CUTS):
            @pl.when((z > 0) & (r != tc))
            def _():
                slot = lax.rem(tc - r + rn, rn) - 1
                act(
                    remote(
                        q_rows(k, h), qside.at[slot, CUTS * j + h], qo_s.at[CUTS * k + h],
                        qs_r.at[slot, CUTS * j + h], z * rn + tc, t,
                    )
                )

            @pl.when((z == 0) & (r != ro) & (r != tc))
            def _():
                slot = lax.rem(ro - r + rn, rn) - 1
                act(
                    remote(
                        q_rows(k, h), qpeer.at[slot, CUTS * (k % 3) + h], qo_s.at[CUTS * k + h],
                        qp_r.at[slot, CUTS * (k % 3) + h], ro, t,
                    )
                )

    def q_down(at, to):
        return remote(qstage.at[at], qchain.at[at], qc_s.at[at], qc_r.at[at], to, t)

    def q_chain(here, only_j):
        top = here == ZN - 1
        for j in (only_j,):
            k = r + rn * j
            for h in range(CUTS):
                at = CUTS * j + h

                @pl.when(z == here)
                def _():
                    for d in range(1, rn):
                        remote(
                            q_rows(k, h), qside.at[d - 1, at], qo_s.at[0], qs_r.at[d - 1, at], s, t
                        ).wait_recv()
                    if not top:
                        q_down(at, s).wait_recv()
                    unit = q_rows(k, h)

                    def body(row):
                        rows = pl.ds(row, 16)
                        total = unit[rows, :].astype(F32)
                        for d in range(1, rn):
                            total = total + qside[d - 1, at, rows, :].astype(F32)
                        if not top:
                            total = total + qchain[at, rows, :].astype(F32)
                        qstage[at, rows, :] = total.astype(BF16)

                    loop(hq, 16, body)
                    q_down(at, s - rn).start()

    def q_last_copy(k, h):
        tc, ro, j = k % rn, k // 3, k // rn
        slot = (ro - tc + rn) % rn - 1
        return remote(
            qstage.at[CUTS * j + h], qpeer.at[slot, CUTS * (k % 3) + h], qc_s.at[CUTS * j + h],
            qp_r.at[slot, CUTS * (k % 3) + h], ro, t,
        )

    def q_ground(act):
        for k in range(plan.nq):
            if k % rn != k // 3:
                @pl.when((z == 0) & (r == k % rn))
                def _():
                    for h in range(CUTS):
                        act(k, h)

    def q_turn(k, h):
        at = CUTS * (k // rn) + h
        q_down(at, s).wait_recv()
        unit = q_rows(k, h)

        def body(row):
            rows = pl.ds(row, 16)
            qstage[at, rows, :] = (
                unit[rows, :].astype(F32) + qchain[at, rows, :].astype(F32)
            ).astype(BF16)

        loop(hq, 16, body)
        q_last_copy(k, h).start()

    def q_final():
        for k in range(plan.nq):
            @pl.when((z == 0) & (r == k // 3))
            def _():
                straight = k % rn == k // 3
                for h in range(CUTS):
                    at = CUTS * (k // rn) + h
                    if straight:
                        q_down(at, s).wait_recv()
                    for d in range(1, rn):
                        remote(
                            q_rows(k, h), qpeer.at[d - 1, CUTS * (k % 3) + h], qo_s.at[0],
                            qp_r.at[d - 1, CUTS * (k % 3) + h], s, t,
                        ).wait_recv()
                    unit = q_rows(k, h)

                    def body(row):
                        rows = pl.ds(row, 16)
                        total = unit[rows, :].astype(F32)
                        for d in range(1, rn):
                            total = total + qpeer[d - 1, CUTS * (k % 3) + h, rows, :].astype(F32)
                        if straight:
                            total = total + qchain[at, rows, :].astype(F32)
                        oq[k % 3, pl.ds(h * hq + row, 16), :] = total

                    loop(hq, 16, body)

    start = lambda copy: copy.start()
    done = lambda copy: copy.wait_send()
    def only(rank, act):
        return lambda k, zo, own_rank: act(k, zo, own_rank) if own_rank == rank else None

    last = plan.grad_ranks - 1
    late_sides(0, start)
    for zq in range(ZN - 1, -1, -1):
        attend_back_group(zq)
        for e in range(1, rn):
            side_copy(zq, e).start()
        send_q(zq)
        if zq == ZN - 1:
            late(plan.late, only(0, late_ends))
        else:
            send_kv(zq + 1)
    for rank in range(1, plan.grad_ranks):
        late_sides(rank, start)
    send_kv(0)
    late(plan.late, only(0, late_inner(2)))
    late(plan.late, only(0, late_inner(1)))
    late(plan.late, only(1, late_ends))
    for zs in range(ZN):
        @pl.when(z != zs)
        def _():
            remote(dq.at[0], q_in.at[zs], q_s.at[0], q_r.at[zs], s, t).wait_recv()
            remote(stage.at[0], kv_in.at[zs], k_s.at[0], k_r.at[zs], s, t).wait_recv()

    for p in range(2):
        cols = slice(p * LANES, (p + 1) * LANES)
        a, b = q_in[2 * p], q_in[2 * p + 1]
        dqkv[:TOK_FRAME, cols] = jnp.concatenate([a[:, :HEAD], b[:, :HEAD]], axis=1)
        dqkv[TOK_FRAME:, cols] = jnp.concatenate([a[:, HEAD:], b[:, HEAD:]], axis=1)
        a, b = [kv_in[2 * p + i].reshape(F_DEV * TOK_FRAME, LANES) for i in range(2)]
        dqkv[:, HD + p * LANES : HD + (p + 1) * LANES] = jnp.concatenate(
            [a[:, :HEAD], b[:, :HEAD]], axis=1
        )
        dqkv[:, 2 * HD + p * LANES : 2 * HD + (p + 1) * LANES] = jnp.concatenate(
            [a[:, HEAD:], b[:, HEAD:]], axis=1
        )

    for m in range(TILES):
        gq[m * TILE : (m + 1) * TILE, :] = mm_tn(
            first_in[:, m * TILE : (m + 1) * TILE], dqkv[...]
        ).astype(BF16)
        for k in range(m * plan.nq // TILES, (m + 1) * plan.nq // TILES):
            q_sides(k, start)

    def c_copy(w):
        return remote(csend.at[w], crecv.at[w], c_s.at[w], c_r.at[w], s, sib)

    def y_copy(w):
        return remote(ysend.at[w], yrecv.at[w], y_s.at[w], y_r.at[w], s, across)

    def pass_on(w):
        c_copy(w).wait_recv()
        ysend[w] = (own[w] + crecv[w].astype(F32)).astype(BF16)
        y_copy(w).start()

    for w in range(TILES):
        weights = wq[w * TILE : (w + 1) * TILE, :]
        csend[w] = mm_nt(dqkv[pl.ds(theirs, TOK_FRAME), :], weights).astype(BF16)
        c_copy(w).start()
        own[w] = mm_nt(dqkv[pl.ds(mine, TOK_FRAME), :], weights)
        if w:
            pass_on(w - 1)
    pass_on(TILES - 1)

    for rank in range(2, plan.grad_ranks):
        late(plan.late, only(rank, late_ends))
    q_chain(ZN - 1, 0)
    q_chain(ZN - 1, 1)
    late(plan.late, only(1, late_inner(2)))
    q_chain(2, 0)
    late(plan.late, only(last, late_inner(2)))
    q_chain(2, 1)
    q_chain(1, 0)
    late(plan.late, only(1, late_inner(1)))
    q_chain(1, 1)
    late(plan.late, only(last, late_inner(1)))

    for w in range(TILES):
        y_copy(w).wait_recv()
    row = lambda part: mod[pl.ds(c * 6 + part, 1), :]
    dm[...] = jnp.zeros_like(dm)

    def input_rows(at):
        rows = pl.ds(at, 64)
        tok_rows = pl.ds(mine + at, 64)
        grads = jnp.concatenate(
            [ysend[w, rows].astype(F32) + yrecv[w, rows].astype(F32) for w in range(TILES)], axis=1
        )
        normed, inverse = normalize(tokens[tok_rows, :].astype(F32))
        add_to(dm, 0, grads)
        add_to(dm, 1, grads * normed)
        igrad[tok_rows, :] = dmid[rows, :] + norm_back(grads * (1.0 + row(1)), normed, inverse)

    loop(TOK_FRAME, 64, input_rows)

    def e_copy(base):
        ref = igrad.at[pl.ds(base, TOK_FRAME)]
        return remote(ref, ref, e_s, e_r, s, sib)

    e_copy(mine).start()

    for block in range(6 * D // LANES):
        part, at = block // (D // LANES), block % (D // LANES)
        src = dm if part < 2 else dm4
        lane = slice(at * LANES, (at + 1) * LANES)
        from_row = part if part < 2 else part - 2
        dm3[block // MCOLS, block % MCOLS : block % MCOLS + 1, :] = src[from_row : from_row + 1, lane]
    h_copy = lambda frame: remote(dm3.at[sib], dboth.at[frame], h_s, h_r, s, sib)
    h_copy(c).start()
    dboth[c] = dm3[t]
    h_copy(1 - c).wait_recv()

    def m_copy(src):
        return remote(dboth, dall.at[s], m_s.at[src - plan.first_mod], m_r.at[s], src, t)

    for src in range(plan.first_mod, n):
        @pl.when(s == src)
        def _():
            dall[s] = dboth[...]

        @pl.when(s != src)
        def _():
            m_copy(src).start()

    q_ground(q_turn)
    late(plan.late, late_final)
    early_units(early_final)
    q_final()

    @pl.when(s >= plan.first_mod)
    def _():
        for d in range(1, n):
            other = lax.rem(s + d, n)
            remote(dboth, dall.at[other], m_s.at[0], m_r.at[other], s, t).wait_recv()

    e_copy(theirs).wait_recv()
    for zs in range(ZN):
        @pl.when(z != zs)
        def _():
            q_copy(zs).wait_send()
            kv_copy(zs).wait_send()

        for e in range(1, rn):
            side_copy(zs, e).wait_send()
    for rank in range(plan.grad_ranks):
        late_sides(rank, done)
    late(plan.late, late_done)
    for k in range(plan.nq):
        q_sides(k, done)

    @pl.when(z > 0)
    def _():
        for at in range(2 * CUTS):
            q_down(at, s).wait_send()

    q_ground(lambda k, h: q_last_copy(k, h).wait_send())
    for w in range(TILES):
        c_copy(w).wait_send()
        y_copy(w).wait_send()
    e_copy(mine).wait_send()
    h_copy(c).wait_send()
    for src in range(plan.first_mod, n):
        @pl.when(s != src)
        def _():
            m_copy(src).wait_send()


def tail_part(plan, meta, q, kv, do, ot, lse, first_in, wq, tokens, dmid, mod_rows, dm4, late_own, late_send, esum, ebuf, cid):
    n, rn = plan.n, plan.r
    rows = F_DEV * TOK_FRAME
    tiles = pltpu.VMEM((TILES, TOK_FRAME, TILE), BF16)
    mods = n - plan.first_mod
    return call(
        functools.partial(tail_kernel, plan),
        (
            jax.ShapeDtypeStruct((rows, D), F32),
            jax.ShapeDtypeStruct((3, plan.uq, QKV), F32),
            jax.ShapeDtypeStruct((3, plan.ub, D), F32),
            jax.ShapeDtypeStruct((n, F_DEV, 16, LANES), F32),
        ),
        [
            pltpu.VMEM((n, 2, TOK_FRAME, LANES), BF16),
            pltpu.VMEM((2, n, LANES, TOK_FRAME), BF16),
            pltpu.VMEM((TOK_FRAME, LANES), BF16),
            pltpu.VMEM((TOK_FRAME, LANES), BF16),
            pltpu.VMEM((LANES, 2 * TOK_FRAME), BF16),
            pltpu.VMEM((1, TOK_FRAME), F32),
            pltpu.VMEM((2, n, TOK_FRAME, LANES), F32),
            pltpu.VMEM((LANES, TOK_FRAME), F32),
            pltpu.VMEM((ZN, TOK_FRAME, LANES), BF16),
            pltpu.VMEM((2, rows, LANES), BF16),
            pltpu.VMEM((rn - 1, plan.grad_ranks, plan.ub, D), BF16),
            pltpu.VMEM((ZN, 2, TOK_FRAME, LANES), BF16),
            pltpu.VMEM((rn - 1, ZN, 2, TOK_FRAME, LANES), BF16),
            pltpu.VMEM((ZN, TOK_FRAME, LANES), BF16),
            pltpu.VMEM((ZN, 2, TOK_FRAME, LANES), BF16),
            pltpu.VMEM((rows, QKV), BF16),
            pltpu.VMEM((D, QKV), BF16),
            pltpu.VMEM((TILES, TOK_FRAME, TILE), F32), tiles, tiles, tiles, tiles,
            pltpu.VMEM((8, D), F32),
            pltpu.VMEM((TP, 16, LANES), F32),
            pltpu.VMEM((F_DEV, 16, LANES), F32),
            pltpu.VMEM((plan.grad_ranks, plan.ub, D), BF16),
            pltpu.VMEM((2, plan.grad_ranks, plan.ub, D), BF16),
            pltpu.VMEM((rn - 1, 2 * CUTS, plan.uq // CUTS, QKV), BF16),
            pltpu.VMEM((rn - 1, 3 * CUTS, plan.uq // CUTS, QKV), BF16),
            pltpu.VMEM((2 * CUTS, plan.uq // CUTS, QKV), BF16),
            pltpu.VMEM((2 * CUTS, plan.uq // CUTS, QKV), BF16),
            DMA((ZN,)), DMA((ZN,)), DMA((ZN,)), DMA((ZN,)), DMA((ZN, rn - 1)), DMA((ZN, rn - 1)),
            DMA((TILES,)), DMA((TILES,)), DMA((TILES,)), DMA((TILES,)),
            DMA, DMA, DMA, DMA, DMA((mods,)), DMA((n,)),
            DMA((plan.grad_ranks,)), DMA((2, plan.grad_ranks)),
            DMA((2,)), DMA((plan.grad_ranks, rn - 1)), DMA((plan.grad_ranks, rn - 1)),
            DMA((CUTS * plan.nq,)),
            DMA((rn - 1, 2 * CUTS)), DMA((rn - 1, 3 * CUTS)), DMA((2 * CUTS,)), DMA((2 * CUTS,)),
        ],
        [SM, VM, ANY] + [VM] * 10 + [ANY, VM, VM],
        cid,
        name="tail_part",
    )(meta, q, kv, do, ot, lse, first_in, wq, tokens, dmid, mod_rows, dm4, late_own, late_send, esum, ebuf)


def adam_kernel(plan, meta, oq, ob, cond, dmod, master, one, two, average, n_master, n_one, n_two, n_average):
    s = meta[0]
    rate = RATE_FACTOR * D ** (-0.5)
    scale_one = 1.0 / (1.0 - BETA_FIRST**STEP)
    scale_two = 1.0 / (1.0 - BETA_SECOND**STEP)

    def update(rows, grad):
        first = BETA_FIRST * one[rows, :] + (1.0 - BETA_FIRST) * grad
        second = BETA_SECOND * two[rows, :] + (1.0 - BETA_SECOND) * grad * grad
        weight = master[rows, :]
        weight = weight - rate * (
            (first * scale_one) / (jnp.sqrt(second * scale_two) + ADAM_EPSILON)
            + WEIGHT_DECAY * weight
        )
        n_one[rows, :] = first
        n_two[rows, :] = second
        n_master[rows, :] = weight
        n_average[rows, :] = AVERAGE_RATE * average[rows, :] + (1.0 - AVERAGE_RATE) * weight

    if True:
        k = 3 * s + pl.program_id(0)
        base = 0

        def from_matrix(kind):
            src = oq if kind == "q" else ob
            rows = plan.uq if kind == "q" else plan.ub
            cols = (QKV if kind == "q" else D) // LANES
            for j in range(cols):
                update(
                    pl.ds(base + j, rows, stride=cols), src[0, :, j * LANES : (j + 1) * LANES]
                )

        by_kind(plan, k, from_matrix)

        @pl.when(k >= plan.nb)
        def _():
            at = cond[k - plan.nb]
            for j in range(MCOLS):
                update(
                    pl.ds(base + j, plan.um, stride=MCOLS),
                    mm(at, dmod[pl.ds(j, plan.frames, stride=16), :].astype(BF16)),
                )


def adam(plan, meta, oq, ob, cond_rows, dmod, master, one, two, average):
    shape = jax.ShapeDtypeStruct(master.shape, F32)
    flat = pl.BlockSpec((plan.flat_rows, LANES), lambda i: (i, 0))
    unit = lambda rows, cols: pl.BlockSpec((1, rows, cols), lambda i: (i, 0, 0))
    whole = lambda x: pl.BlockSpec(x.shape, lambda i: (0,) * x.ndim)
    return pl.pallas_call(
        functools.partial(adam_kernel, plan),
        out_shape=(shape,) * 4,
        grid=(3,),
        in_specs=[SM, unit(plan.uq, QKV), unit(plan.ub, D), whole(cond_rows), whole(dmod)] + [flat] * 4,
        out_specs=(flat,) * 4,
        compiler_params=pltpu.CompilerParams(vmem_limit_bytes=VMEM_LIMIT),
        name="adam",
    )(meta, oq, ob, cond_rows, dmod, master, one, two, average)


def local(
    tokens,
    grad_out,
    noise_level,
    context_mask,
    frame_clip,
    level_table,
    master,
    moment_one,
    moment_two,
    average,
):
    plan = Plan(lax.axis_size("seq"))
    s = lax.axis_index("seq")
    t = lax.axis_index("tp")
    flat = lambda x: x.reshape(-1, LANES)

    effective = noise_level * (1 - context_mask)
    one_hot = (
        effective[:, None] == jnp.arange(level_table.shape[0], dtype=jnp.int32)[None, :]
    ).astype(BF16)
    condition = jax.nn.silu(mm(one_hot, level_table)).astype(BF16)
    cond_units = condition.reshape(plan.frames, plan.nm, plan.um).transpose(1, 0, 2)

    meta = frame_clip.astype(jnp.int32)
    (
        wq, w_out, w_side, w_early, w_below, w_beside, wo_across, mod_rows, first_in, q_mine, kv_all,
        o_mine, o_rows, lse,
    ) = head_part(plan, meta, flat(master), cond_units, tokens, 0)
    result, late_own, late_send, early_sum, early_in, do_mine, middle_grad, mod_four = middle_part(
        plan, o_mine, wo_across, (w_out, w_side, w_beside, w_early, w_below),
        tokens, grad_out, mod_rows, 2
    )
    input_grad, own_q, own_b, mod_all = tail_part(
        plan, meta, q_mine, kv_all, do_mine, o_rows, lse, first_in, wq, tokens, middle_grad,
        mod_rows, mod_four, late_own, late_send, early_sum, early_in, 3,
    )
    updated = adam(
        plan,
        s[None].astype(jnp.int32),
        own_q,
        own_b,
        cond_units.transpose(0, 2, 1),
        flat(mod_all),
        flat(master),
        flat(moment_one),
        flat(moment_two),
        flat(average),
    )
    new_master, new_one, new_two, new_average = [x.reshape(master.shape) for x in updated]
    return (result, input_grad, new_master, new_one, new_two, new_average)


def solution(mesh):
    token_spec = P("seq", None)
    weight_spec = P("tp", "seq")
    in_specs = (token_spec, token_spec, P(), P(), P(), P()) + (weight_spec,) * 4
    out_specs = (token_spec, token_spec) + (weight_spec,) * 4
    return jax.shard_map(local, mesh=mesh, in_specs=in_specs, out_specs=out_specs, check_vma=False)
```

```python
import functools

import jax
import jax.numpy as jnp
from jax import lax
from jax.experimental import pallas as pl
from jax.experimental.pallas import tpu as pltpu
from jax.sharding import PartitionSpec as P

D = 1024
HEADS = 16
HEAD = 64
FF = 4096
TOK_FRAME = 384
STEP = 7
TP = 4
ZN = 4
HD = HEADS * HEAD // TP
QKV = 3 * HD
FT = FF // TP
MT = 6 * D // TP
F_DEV = 2
BROWS = HD + 2 * FT
LANES = 128
MCOLS = MT // LANES
PACK = TOK_FRAME // 2
TILE = 256
TILES = D // TILE
CUTS = 4

NORM_EPSILON = 1e-06
RATE_FACTOR = 2.5
BETA_FIRST = 0.5
BETA_SECOND = 0.5
ADAM_EPSILON = 1e-08
WEIGHT_DECAY = 0.01
AVERAGE_RATE = 0.9
GELU_A = 0.7978845608028654
GELU_B = 0.044715
MESH = pl.DeviceIdType.MESH
VM = pl.BlockSpec(memory_space=pltpu.VMEM)
SM = pl.BlockSpec(memory_space=pltpu.SMEM)
ANY = pl.BlockSpec(memory_space=pl.ANY)
DMA = pltpu.SemaphoreType.DMA
F32 = jnp.float32
BF16 = jnp.bfloat16
VMEM_LIMIT = 60 * 2**20


def mm(left, right):
    return jnp.dot(left, right, preferred_element_type=F32)


def mm_tn(left, right):
    return lax.dot_general(left, right, (((0,), (0,)), ((), ())), preferred_element_type=F32)


def mm_nt(left, right):
    return lax.dot_general(left, right, (((1,), (1,)), ((), ())), preferred_element_type=F32)


def normalize(rows):
    centred = rows - jnp.mean(rows, axis=1, keepdims=True)
    inverse = lax.rsqrt(jnp.mean(centred * centred, axis=1, keepdims=True) + NORM_EPSILON)
    return (centred * inverse, inverse)


def norm_back(grads, normed, inverse):
    return inverse * (
        grads
        - jnp.mean(grads, axis=1, keepdims=True)
        - normed * jnp.mean(grads * normed, axis=1, keepdims=True)
    )


def loop(count, step, body):
    def turn(i, carry):
        body(pl.multiple_of(i * step, step))
        return carry

    lax.fori_loop(0, count // step, turn, 0)


def add_to(ref, row, values):
    ref[pl.ds(row, 1), :] += jnp.sum(values, axis=0, keepdims=True)


class Plan:
    def __init__(self, seq_count):
        self.n = seq_count
        self.r = seq_count // ZN
        self.shard = (D * QKV + BROWS * D + D * MT) // seq_count
        self.unit = self.shard // 3
        self.uq = self.unit // QKV
        self.ub = self.unit // D
        self.um = self.unit // MT
        self.nq = D // self.uq
        self.nb = self.nq + BROWS // self.ub
        self.nm = D // self.um
        self.first_mod = self.nb // 3
        self.half = (self.nq + self.nb) // 2
        self.flat_rows = self.unit // LANES
        self.frames = seq_count * F_DEV
        self.late = list(range(self.nq, self.half))
        self.early = list(range(self.half, self.nb))
        self.outs = self.late[: -(-HD // self.ub)]
        self.sided = self.late[len(self.outs) :]
        self.rank, self.ranks = self.ranked(self.early)
        self.late_rank, self.late_ranks = self.ranked(self.sided)
        self.grad_rank, self.grad_ranks = self.ranked(self.late)

    def ranked(self, units):
        seen, rank = {}, {}
        for k in units:
            column = self.home(k)[1]
            rank[k] = seen.get(column, 0)
            seen[column] = rank[k] + 1
        return rank, max(seen.values())

    def home(self, k):
        return (k // 3) // self.r, (k // 3) % self.r


def place(plan):
    s = lax.axis_index("seq")
    t = lax.axis_index("tp")
    return s, t, lax.div(s, plan.r), lax.rem(s, plan.r)


def remote(src, dst, send_sem, recv_sem, s, t):
    return pltpu.make_async_remote_copy(
        src_ref=src,
        dst_ref=dst,
        send_sem=send_sem,
        recv_sem=recv_sem,
        device_id=(s, t),
        device_id_type=MESH,
    )


def greet(peers):
    barrier = pltpu.get_barrier_semaphore()
    for s, t in peers:
        pl.semaphore_signal(barrier, inc=1, device_id=(s, t), device_id_type=MESH)
    pl.semaphore_wait(barrier, len(peers))


def by_kind(plan, k, act, low=0, high=None):
    high = plan.nb if high is None else high
    q_high, b_low = min(plan.nq, high), max(plan.nq, low)
    if low < q_high:
        @pl.when((k >= low) & (k < q_high))
        def _():
            act("q")

    if b_low < high:
        @pl.when((k >= b_low) & (k < high))
        def _():
            act("b")


def unit_of(plan, k, kind, wq, wb):
    if kind == "q":
        return wq.at[pl.ds(pl.multiple_of(k * plan.uq, plan.uq), plan.uq)]
    return wb.at[pl.ds(pl.multiple_of((k - plan.nq) * plan.ub, plan.ub), plan.ub)]


def call(kernel, outs, scratch, ins, cid=None, cost=None, name=None, out_specs=None):
    params = dict(vmem_limit_bytes=VMEM_LIMIT)
    if cid is not None:
        params.update(collective_id=cid, has_side_effects=True)
    return pl.pallas_call(
        kernel,
        out_shape=outs,
        in_specs=ins,
        out_specs=out_specs or jax.tree.map(lambda _: VM, outs),
        scratch_shapes=scratch,
        compiler_params=pltpu.CompilerParams(**params),
        cost_estimate=cost,
        name=name,
    )


def head_kernel(
    plan, meta, master, cond, tokens,
    wq, w_out, w_side, w_early, w_below, w_beside, wo_across, mods, first_in, q_out, kv_out, o, ot, lse,
    own_b, pool, flipped, qt, m_ref, l_ref, acc, tile, macc, mpart, mrecv, mod, norm, q_send, kv_send,
    qp_s, qc_s, q_r, wo_s, wo_r, ws_s, ws_r, we_s, we_r, loc_s, m_s, m_r, t_s, t_r, as_, ar, ks, kr, xs, xr,
    bl_s, bl_r, bs_s, bs_r, oa_s, oa_r,
):
    s, t, z, r = place(plan)
    n, rn = plan.n, plan.r
    greet(
        [(lax.rem(s + d, n), t) for d in range(1, n)]
        + [(s, lax.rem(t + d, TP)) for d in range(1, TP)]
    )
    start = lambda copy: copy.start()
    done = lambda copy: copy.wait_send()
    cut = plan.uq // CUTS

    def q_rows(k, h):
        return wq.at[pl.ds(pl.multiple_of(k * plan.uq + h * cut, cut), cut)]

    def q_copy(k, h, sem, to_s):
        ref = q_rows(k, h)
        return remote(ref, ref, sem, q_r.at[CUTS * k + h], to_s, t)

    def q_arrived(k, h):
        q_copy(k, h, qc_s.at[0, 0], s).wait_recv()

    def column(j):
        return r + rn * lax.rem(j + r, 2)

    def q_own(i, act):
        k = 3 * s + i

        @pl.when(k < plan.nq)
        def _():
            for h in range(CUTS):
                for d in range(1, rn):
                    act(q_copy(k, h, qp_s.at[CUTS * i + h, d - 1], lax.rem(r + d, rn)))

    def q_line(act, wait, whole=False):
        for j in range(2):
            k = column(j)
            for h in range(CUTS):
                if wait:
                    @pl.when((z > 0) | (lax.div(k, 3) != r))
                    def _():
                        q_arrived(k, h)

                @pl.when((z < ZN - 1) & ((z > 0) | (lax.div(k, 3) != r) | whole))
                def _():
                    act(q_copy(k, h, qc_s.at[CUTS * j + h, 0], s + rn))

                @pl.when(z > 0)
                def _():
                    for d in range(1, rn):
                        act(
                            q_copy(
                                k, h, qc_s.at[CUTS * j + h, d], z * rn + lax.rem(r + d, rn)
                            )
                        )

    def slot(k):
        if k in plan.outs:
            at = k - plan.nq
            return w_out.at[at], wo_s.at[at], wo_r.at[at]
        if k in plan.sided:
            at = plan.late_rank[k]
            return w_side.at[at], ws_s.at[at], ws_r.at[at]
        return w_early.at[k - plan.half], we_s.at[plan.rank[k]], we_r.at[k - plan.half]

    def along(k, src, act, up):
        dst, send_sem, recv_sem = slot(k)
        if up and k < plan.half:
            @pl.when(z < ZN - 1)
            def _():
                act(remote(src, dst, send_sem.at[0], recv_sem, s + rn, t))

        if not up:
            @pl.when(z > 0)
            def _():
                act(remote(src, dst, send_sem.at[1], recv_sem, s - rn, t))

    def beside(k, src, act):
        if k not in plan.outs:
            return
        dst, send_sem, recv_sem = slot(k)
        for d in range(1, rn):
            act(
                remote(
                    src, dst, send_sem.at[1 + d], recv_sem, z * rn + lax.rem(r + d, rn), t
                )
            )

    def arrived(k):
        dst, send_sem, recv_sem = slot(k)
        remote(own_b.at[0], dst, send_sem.at[0], recv_sem, s, t).wait_recv()

    def keep(k):
        return pltpu.make_async_copy(own_b.at[k % 3], slot(k)[0], loc_s.at[k % 3])

    def owned(units, act):
        for k in units:
            @pl.when(s == k // 3)
            def _():
                act(k, own_b.at[k % 3])

    def pass_along(units, d, act, wait):
        for k in units:
            zo, ro = plan.home(k)
            if k < plan.half and zo + d < (ZN - 1 if k in plan.sided else ZN):
                @pl.when((r == ro) & (z == zo + d))
                def _():
                    if wait:
                        arrived(k)
                    along(k, slot(k)[0], act, True)
                    beside(k, slot(k)[0], act)

            if zo - d >= (0 if k in plan.outs else 1):
                @pl.when((r == ro) & (z == zo - d))
                def _():
                    if wait:
                        arrived(k)
                    along(k, slot(k)[0], act, False)
                    beside(k, slot(k)[0], act)

    def settle(k, low):
        zo, ro = plan.home(k)

        @pl.when((r == ro) & ((z == 0) & (zo > 0) if low else (z == ZN - 1) & (zo < ZN - 1)))
        def _():
            arrived(k)

    def hop(k, act):
        zo, ro = plan.home(k)

        @pl.when(s == k // 3)
        def _():
            act(remote(own_b.at[k % 3], w_below.at[k % 3], bl_s.at[k % 3], bl_r.at[k % 3], s + rn, t))

    def hopped(k):
        zo, ro = plan.home(k)

        @pl.when((r == ro) & (z == zo + 1))
        def _():
            remote(own_b.at[0], w_below.at[k % 3], bl_s.at[0], bl_r.at[k % 3], s, t).wait_recv()

    def share(k, act, low=None):
        rank = plan.late_rank[k]
        part = True if low is None else (z <= 1) == low

        @pl.when((r == plan.home(k)[1]) & part)
        def _():
            for d in range(1, rn):
                act(
                    remote(
                        w_side.at[rank], w_beside.at[d - 1, rank], bs_s.at[rank, d - 1],
                        bs_r.at[d - 1, rank], z * rn + lax.rem(r + d, rn), t,
                    )
                )

    def shared(k):
        rank = plan.late_rank[k]

        @pl.when(r != plan.home(k)[1])
        def _():
            d = lax.rem(r - plan.home(k)[1] + rn, rn)
            remote(
                w_side.at[0], w_beside.at[d - 1, rank], bs_s.at[0, 0], bs_r.at[d - 1, rank], s, t
            ).wait_recv()

    def out_copy(w):
        count = min(plan.ub, HD - w * plan.ub)
        return remote(
            w_out.at[w].at[pl.ds(0, count)], wo_across.at[pl.ds(w * plan.ub, count)],
            oa_s.at[w], oa_r.at[w], s, lax.rem(t + 2, TP),
        )

    def sort_group(g):
        first = meta[2 * g] == 0
        a, b = kv_out[g, :TOK_FRAME, :], kv_out[g, TOK_FRAME:, :]
        pool[g, 0] = jnp.where(first, a, b)
        pool[g, 1] = jnp.where(first, b, a)
        for kind in range(2):
            flipped[kind, g] = pool[g, kind].T

    def attend_group(zq):
        gq = zq * rn + r
        first = meta[2 * gq] == 0
        clip = meta[2 * gq] + meta[2 * gq + 1]
        parts = []
        for kind in range(2):
            low = first if kind == 0 else jnp.logical_not(first)
            rows = jnp.where(low, q_out[zq][:, :HEAD], q_out[zq][:, HEAD:])
            qt[...] = (padded(rows, True) * jnp.asarray(HEAD ** (-0.5), BF16)).T
            m_ref[...] = jnp.full_like(m_ref, -1e30)
            l_ref[...] = jnp.zeros_like(l_ref)
            acc[...] = jnp.zeros_like(acc)

            def block(p, inner):
                pair = []
                m_old = m_ref[...]
                m_new = m_old
                for e in range(2):
                    g = jnp.minimum(2 * p + e, gq)
                    shown = 2 * p + e <= gq
                    if kind == 1:
                        shown = shown & (meta[2 * g] + meta[2 * g + 1] == clip)
                    off = jnp.where(shown, 0.0, 1e30)
                    st = mm(pool[g, kind], qt[...])
                    m_new = jnp.maximum(m_new, jnp.max(st, axis=0, keepdims=True) - off)
                    pair.append((g, st, off))
                alpha = jnp.exp(m_old - m_new)
                total, out = l_ref[...] * alpha, acc[...] * alpha
                for g, st, off in pair:
                    weights = jnp.exp(st - (m_new + off))
                    total = total + jnp.sum(weights, axis=0, keepdims=True)
                    out = out + mm(flipped[kind, g], weights.astype(BF16))
                m_ref[...] = m_new
                l_ref[...] = total
                acc[...] = out
                return inner

            lax.fori_loop(0, lax.div(gq + 2, 2), block, 0)
            total = l_ref[...]
            out = acc[HEAD:, :] / total
            ot[2 * zq + kind] = out
            lse[2 * zq + kind] = m_ref[...] + jnp.log(total)
            rows = out.T
            parts.append(jnp.concatenate([rows[:PACK], rows[PACK:]], axis=1).astype(BF16))
        o[zq, 0] = jnp.where(first, parts[0], parts[1])
        o[zq, 1] = jnp.where(first, parts[1], parts[0])

    units = plan.late + plan.early
    first_up = [k for k in plan.late if k % 3 == 0 and plan.home(k)[0] > 0]
    later_up = [k for k in plan.late if k not in first_up]

    def fill(i, kind):
        k = 3 * s + i
        base = i * plan.flat_rows
        rows, cols = (plan.uq, QKV // LANES) if kind == "q" else (plan.ub, D // LANES)
        at = pl.multiple_of(k * plan.uq, plan.uq)
        for j in range(cols):
            values = master[pl.ds(base + j, rows, stride=cols), :].astype(BF16)
            if kind == "q":
                wq[pl.ds(at, rows), j * LANES : (j + 1) * LANES] = values
            else:
                own_b[i, :, j * LANES : (j + 1) * LANES] = values

    for away in (True, False):
        for i in range(3):
            k = 3 * s + i

            @pl.when((k < plan.nq) & ((lax.rem(k, rn) != r) == away))
            def _():
                fill(i, "q")
                q_own(i, start)
                if not away:
                    at = lax.div(k, rn)
                    slot_j = lax.rem(at + r, 2)
                    for h in range(CUTS):
                        q_copy(k, h, qc_s.at[CUTS * slot_j + h, 0], s + rn).start()

    for i in range(3):
        @pl.when((3 * s + i >= plan.nq) & (3 * s + i < plan.nb))
        def _():
            fill(i, "b")

    @pl.when(z == 0)
    def _():
        q_line(start, True)

    owned(units, lambda k, src: along(k, src, start, False))
    owned(first_up, lambda k, src: along(k, src, start, True))
    owned(units, lambda k, src: keep(k).start())

    macc[...] = jnp.zeros_like(macc)
    for i in range(3):
        k = 3 * s + i
        base = i * plan.flat_rows

        @pl.when(k >= plan.nb)
        def _():
            for j in range(MCOLS):
                tile[:, j * LANES : (j + 1) * LANES] = master[
                    pl.ds(base + j, plan.um, stride=MCOLS), :
                ].astype(BF16)
            macc[...] += mm(cond[k - plan.nb], tile[...])

    fm = plan.first_mod

    def m_copy(d):
        to = lax.rem(s + d, n)
        return remote(mpart.at[to], mrecv.at[s - fm], m_s.at[d - 1], m_r.at[s - fm], to, t)

    @pl.when(s >= fm)
    def _():
        for f in range(plan.frames):
            for j in range(MCOLS):
                mpart[f // F_DEV, pl.ds((f % F_DEV) * MCOLS + j, 1), :] = macc[
                    pl.ds(f, 1), j * LANES : (j + 1) * LANES
                ]
        mrecv[s - fm] = mpart[s]
        for d in range(1, n):
            m_copy(d).start()

    def norm_rows(at):
        rows = pl.ds(at, 64)
        norm[rows, :] = normalize(tokens[rows, :].astype(F32))[0]

    loop(F_DEV * TOK_FRAME, 64, norm_rows)

    @pl.when(z > 0)
    def _():
        q_line(start, True)

    owned(plan.outs, lambda k, src: along(k, src, start, True))
    owned([k for k in later_up if k not in plan.outs], lambda k, src: along(k, src, start, True))
    owned(units, lambda k, src: beside(k, src, start))
    pass_along(first_up + plan.early, 1, start, True)

    for src in range(fm, n):
        @pl.when(s != src)
        def _():
            remote(mpart.at[0], mrecv.at[src - fm], m_s.at[0], m_r.at[src - fm], s, t).wait_recv()

    total = mrecv[0]
    for src in range(1, n - fm):
        total = total + mrecv[src]
    mod[t] = total

    def t_copy(d):
        return remote(mod.at[t], mod.at[t], t_s.at[d - 1], t_r.at[t], s, lax.rem(t + d, TP))

    for d in range(1, TP):
        t_copy(d).start()
    for d in range(1, TP):
        other = lax.rem(t + d, TP)
        remote(mod.at[t], mod.at[other], t_s.at[0], t_r.at[other], s, t).wait_recv()
    for f in range(F_DEV):
        for block in range(TP * MCOLS):
            part, at = block // (D // LANES), block % (D // LANES)
            mods[f * 6 + part : f * 6 + part + 1, at * LANES : (at + 1) * LANES] = mod[
                block // MCOLS, f * MCOLS + block % MCOLS : f * MCOLS + block % MCOLS + 1, :
            ]

    def affine(f):
        def body(at):
            rows = pl.ds(f * TOK_FRAME + at, 64)
            first_in[rows, :] = (
                norm[rows, :] * (1.0 + mods[f * 6 + 1 : f * 6 + 2, :]) + mods[f * 6 : f * 6 + 1, :]
            ).astype(BF16)

        loop(TOK_FRAME, 64, body)

    for f in range(F_DEV):
        affine(f)

    for k in range(plan.nq):
        for h in range(CUTS):
            if rn > 1:
                at_zero = (z == 0) & (k // 3 != r) & (k % rn != r)

                @pl.when(at_zero | (z > 0) & (k % rn != r))
                def _():
                    q_arrived(k, h)

    keys = mm(first_in[...], wq[:, HD : 2 * HD]).astype(BF16)
    values = mm(first_in[...], wq[:, 2 * HD :]).astype(BF16)
    for h in range(ZN):
        cols = slice(h * HEAD, (h + 1) * HEAD)
        kv_send[h] = jnp.concatenate([keys[:, cols], values[:, cols]], axis=1)

    def kv_copy(d):
        h = lax.rem(z + d, ZN)
        return remote(kv_send.at[h], kv_out.at[s], ks.at[d - 1], kr.at[z], h * rn + r, t)

    def a_copy(d):
        h = lax.rem(z + d, ZN)
        return remote(q_send.at[h], q_out.at[z], as_.at[d - 1], ar.at[z], h * rn + r, t)

    def side_copy(zs, e):
        at = zs * rn + r
        ref = kv_out.at[at]
        return remote(ref, ref, xs.at[zs, e - 1], xr.at[at], z * rn + lax.rem(r + e, rn), t)

    for d in range(1, ZN):
        kv_copy(d).start()
    kv_out[s] = kv_send[z]
    for e in range(1, rn):
        side_copy(z, e).start()
    queries = mm(first_in[...], wq[:, :HD]).astype(BF16)
    for h in range(ZN):
        cols = slice(h * HEAD, (h + 1) * HEAD)
        q_send[h] = jnp.concatenate([queries[:TOK_FRAME, cols], queries[TOK_FRAME:, cols]], axis=1)
    for d in range(1, ZN):
        a_copy(d).start()
    q_out[z] = q_send[z]

    rest = [k for k in plan.sided if k not in first_up]
    pass_along(plan.outs + rest, 1, start, True)
    for k in plan.early:
        hop(k, start)
    owned(units, lambda k, src: keep(k).wait())
    for k in plan.sided:
        settle(k, True)
        share(k, start, True)

    def kv_come(zs):
        @pl.when(z != zs)
        def _():
            remote(kv_send.at[0], kv_out.at[zs * rn + r], ks.at[0], kr.at[zs], s, t).wait_recv()
            for e in range(1, rn):
                side_copy(zs, e).start()

    def ready(zq):
        for e in range(1, rn):
            at = zq * rn + lax.rem(r + e, rn)
            remote(kv_out.at[at], kv_out.at[at], xs.at[0, 0], xr.at[at], s, t).wait_recv()
        for other in range(rn):
            sort_group(zq * rn + other)

        @pl.when(z != zq)
        def _():
            remote(q_send.at[0], q_out.at[zq], as_.at[0], ar.at[zq], s, t).wait_recv()

    kv_come(0)
    kv_come(1)
    pass_along(plan.outs, 2, start, True)
    ready(0)
    attend_group(0)
    kv_come(2)
    kv_come(3)
    pass_along(plan.outs, 3, start, True)
    ready(1)
    attend_group(1)
    for d in range(2, ZN):
        pass_along(plan.sided, d, start, True)
    for k in plan.sided:
        settle(k, False)
        share(k, start, False)
    ready(2)
    attend_group(2)
    for k in plan.outs:
        @pl.when(r != plan.home(k)[1])
        def _():
            arrived(k)

    for w in range(len(plan.outs)):
        out_copy(w).start()
    ready(3)
    attend_group(3)
    for k in plan.early:
        hopped(k)
        zo, ro = plan.home(k)
        if zo > 0:
            @pl.when((r == ro) & (z == 0))
            def _():
                arrived(k)

    for k in plan.sided:
        shared(k)
    for w in range(len(plan.outs)):
        out_copy(w).wait()

    for k in plan.early:
        hop(k, done)
    for k in plan.sided:
        share(k, done)
    for i in range(3):
        q_own(i, done)
    q_line(done, False, True)
    owned(units, lambda k, src: along(k, src, done, False))
    owned(plan.late, lambda k, src: along(k, src, done, True))
    owned(units, lambda k, src: beside(k, src, done))
    for d in range(1, ZN):
        pass_along(units, d, done, False)

    @pl.when(s >= fm)
    def _():
        for d in range(1, n):
            m_copy(d).wait_send()

    for d in range(1, TP):
        t_copy(d).wait_send()
    for d in range(1, ZN):
        kv_copy(d).wait_send()
        a_copy(d).wait_send()
    for zs in range(ZN):
        for e in range(1, rn):
            side_copy(zs, e).wait_send()


def head_part(plan, meta, master, cond_units, tokens, cid):
    n, rn = plan.n, plan.r
    mrows = F_DEV * MCOLS
    rows = F_DEV * TOK_FRAME
    mods = n - plan.first_mod
    return call(
        functools.partial(head_kernel, plan),
        (
            jax.ShapeDtypeStruct((D, QKV), BF16),
            jax.ShapeDtypeStruct((len(plan.outs), plan.ub, D), BF16),
            jax.ShapeDtypeStruct((plan.late_ranks, plan.ub, D), BF16),
            jax.ShapeDtypeStruct((len(plan.early), plan.ub, D), BF16),
            jax.ShapeDtypeStruct((3, plan.ub, D), BF16),
            jax.ShapeDtypeStruct((rn - 1, plan.late_ranks, plan.ub, D), BF16),
            jax.ShapeDtypeStruct((HD, D), BF16),
            jax.ShapeDtypeStruct((F_DEV * 6, D), F32),
            jax.ShapeDtypeStruct((rows, D), BF16),
            jax.ShapeDtypeStruct((ZN, TOK_FRAME, LANES), BF16),
            jax.ShapeDtypeStruct((n, rows, LANES), BF16),
            jax.ShapeDtypeStruct((ZN, F_DEV, PACK, LANES), BF16),
            jax.ShapeDtypeStruct((ZN * F_DEV, HEAD, TOK_FRAME), F32),
            jax.ShapeDtypeStruct((ZN * F_DEV, 1, TOK_FRAME), F32),
        ),
        [
            pltpu.VMEM((3, plan.ub, D), BF16),
            pltpu.VMEM((n, 2, TOK_FRAME, LANES), BF16),
            pltpu.VMEM((2, n, LANES, TOK_FRAME), BF16),
            pltpu.VMEM((LANES, TOK_FRAME), BF16),
            pltpu.VMEM((1, TOK_FRAME), F32),
            pltpu.VMEM((1, TOK_FRAME), F32),
            pltpu.VMEM((LANES, TOK_FRAME), F32),
            pltpu.VMEM((plan.um, MT), BF16),
            pltpu.VMEM((plan.frames, MT), F32),
            pltpu.VMEM((n, mrows, LANES), F32),
            pltpu.VMEM((mods, mrows, LANES), F32),
            pltpu.VMEM((TP, mrows, LANES), F32),
            pltpu.VMEM((rows, D), F32),
            pltpu.VMEM((ZN, TOK_FRAME, LANES), BF16),
            pltpu.VMEM((ZN, rows, LANES), BF16),
            DMA((3 * CUTS, rn - 1)), DMA((2 * CUTS, rn)), DMA((CUTS * plan.nq,)),
            DMA((len(plan.outs), rn + 1)), DMA((len(plan.outs),)),
            DMA((plan.late_ranks, 2)), DMA((plan.late_ranks,)),
            DMA((plan.ranks, rn + 1)), DMA((len(plan.early),)), DMA((3,)),
            DMA((n - 1,)), DMA((mods,)), DMA((TP - 1,)), DMA((TP,)),
            DMA((ZN - 1,)), DMA((ZN,)), DMA((ZN - 1,)), DMA((ZN,)), DMA((ZN, rn - 1)), DMA((n,)),
            DMA((3,)), DMA((3,)), DMA((plan.late_ranks, rn - 1)), DMA((rn - 1, plan.late_ranks)),
            DMA((len(plan.outs),)), DMA((len(plan.outs),)),
        ],
        [SM] + [VM] * 3,
        cid,
        out_specs=(VM,) + (ANY,) * 6 + (VM,) * 7,
        name="head_part",
    )(meta, master, cond_units, tokens)


def padded(rows, low):
    zero = jnp.zeros_like(rows)
    return jnp.concatenate([rows, zero] if low else [zero, rows], axis=1)


def middle_kernel(
    plan, o_mine, wo_across, w_out, w_side, w_beside, w_early, w_below, tokens, grad_out, mod,
    result, late_own, late_send, esum, ebuf, do_out, dmid, dmod,
    gb, wb, eside, eend, wo, oall, attended, attn, mid, norm, inv, sin, hidden, dmlp, slopes, dup,
    own, csend, crecv, ysend, yrecv, dattn, dsend, dwo, wsend, wrecv,
    o_s, o_r, f_s, f_r, n_s, n_r, c_s, c_r, y_s, y_r, d_s, d_r, w_s, w_r, e_s, e_r, p_s, p_r, l_s, u_s, u_r, g_s, g_r, j_s, h_s, h_r, i_s, i_r,
):
    s, t, z, r = place(plan)
    rn = plan.r
    y = lax.div(t, 2)
    c = lax.rem(t, 2)
    sib = 2 * y + 1 - c
    across = lax.rem(t + 2, TP)
    mine = pl.multiple_of(c * TOK_FRAME, TOK_FRAME)
    theirs = pl.multiple_of((1 - c) * TOK_FRAME, TOK_FRAME)
    pairs = [(d, e) for d in range(ZN) for e in range(2)][1:]

    def partner(d, e):
        return lax.rem(z + d, ZN), (c if e == 0 else 1 - c)

    greet(
        [(partner(d, e)[0] * rn + r, 2 * y + partner(d, e)[1]) for d, e in pairs]
        + [(s, across)]
        + [(z * rn + lax.rem(r + d, rn), t) for d in range(1, rn)]
    )

    def home(k):
        return (k // 3) // rn, (k // 3) % rn, k - plan.half

    def w_rows(ref, k):
        return ref.at[pl.ds((k - plan.nq) * plan.ub, plan.ub)]

    def late_loads(act):
        for k in plan.late:
            sem = l_s.at[k - plan.nq]
            if k in plan.outs:
                act(pltpu.make_async_copy(w_out.at[k - plan.nq], w_rows(wb, k), sem))
            else:
                zo, ro = plan.home(k)
                rank = plan.late_rank[k]

                @pl.when(r == ro)
                def _():
                    act(pltpu.make_async_copy(w_side.at[rank], w_rows(wb, k), sem))

                @pl.when(r != ro)
                def _():
                    d = lax.rem(r - ro + rn, rn)
                    act(pltpu.make_async_copy(w_beside.at[d - 1, rank], w_rows(wb, k), sem))

    def loads(act):
        for k in plan.early:
            zo, ro, at = home(k)

            @pl.when((z <= zo) & (r == ro))
            def _():
                act(pltpu.make_async_copy(w_early.at[at], w_rows(wb, k), l_s.at[len(plan.late) + at]))

            @pl.when((z == zo + 1) & (r == ro))
            def _():
                act(
                    pltpu.make_async_copy(
                        w_below.at[k % 3], w_rows(wb, k), l_s.at[len(plan.late) + at]
                    )
                )

    def rise(k, src, act):
        zo, ro, at = home(k)

        @pl.when((z < ZN - 1) & (z > zo))
        def _():
            act(remote(src, w_rows(wb, k), u_s.at[at, 0], u_r.at[at], s + rn, t))

        for d in range(1, rn):
            act(
                remote(
                    src, w_rows(wb, k), u_s.at[at, d], u_r.at[at],
                    z * rn + lax.rem(r + d, rn), t,
                )
            )

    def risen(k):
        remote(w_below.at[0], w_rows(wb, k), u_s.at[0, 0], u_r.at[k - plan.half], s, t).wait_recv()

    def rises(act, first, wait):
        for k in plan.early:
            zo, ro, at = home(k)
            if first:
                @pl.when((z == zo + 1) & (r == ro))
                def _():
                    rise(k, w_below.at[k % 3], act)

                @pl.when((z <= zo) & (r == ro))
                def _():
                    rise(k, w_early.at[at], act)

            else:
                @pl.when((z > zo + 1) & (r == ro))
                def _():
                    if wait:
                        risen(k)
                    rise(k, w_rows(wb, k), act)

    def o_copy(d, e):
        zd, cd = partner(d, e)
        return remote(
            o_mine.at[zd, cd], oall.at[y * 8 + c * ZN + z], o_s.at[2 * d + e],
            o_r.at[c * ZN + z], zd * rn + r, 2 * y + cd,
        )

    def f_copy(slot):
        ref = oall.at[y * 8 + slot]
        return remote(ref, ref, f_s.at[slot], f_r.at[slot], s, across)

    def p_copy(i, tp):
        ref = wo.at[pl.ds(pl.multiple_of(tp * HD, HD), HD)]
        return remote(ref, ref, p_s.at[i], p_r.at[i], s, sib)

    for d, e in pairs:
        o_copy(d, e).start()
    start = lambda copy: copy.start()
    rises(start, True, False)
    late_loads(start)
    loads(start)
    late_loads(lambda copy: copy.wait())
    wo[pl.ds(pl.multiple_of(t * HD, HD), HD), :] = wb[:HD, :]
    p_copy(0, t).start()
    wo[pl.ds(pl.multiple_of(across * HD, HD), HD), :] = wo_across[...]
    p_copy(1, across).start()
    oall[y * 8 + c * ZN + z] = o_mine[z, c]
    f_copy(c * ZN + z).start()

    def d_mlp(f):
        def body(at):
            rows = pl.ds(f * TOK_FRAME + at, 64)
            dmlp[rows, :] = (grad_out[rows, :].astype(F32) * mod[f * 6 + 5 : f * 6 + 6, :]).astype(
                BF16
            )

        loop(TOK_FRAME, 64, body)

    for f in range(F_DEV):
        d_mlp(f)

    for d, e in pairs:
        zd, cd = partner(d, e)
        slot = cd * ZN + zd
        remote(o_mine.at[0, 0], oall.at[y * 8 + slot], o_s.at[0], o_r.at[slot], s, t).wait_recv()
        f_copy(slot).start()
    for slot in range(8):
        remote(
            oall.at[0], oall.at[(1 - y) * 8 + slot], f_s.at[slot], f_r.at[slot], s, t
        ).wait_recv()
    for m in range(HEADS // 2):
        a, b = oall[2 * m], oall[2 * m + 1]
        cols = slice(m * LANES, (m + 1) * LANES)
        attended[:PACK, cols] = jnp.concatenate([a[:, :HEAD], b[:, :HEAD]], axis=1)
        attended[PACK:, cols] = jnp.concatenate([a[:, HEAD:], b[:, HEAD:]], axis=1)

    p_copy(0, sib).wait_recv()
    p_copy(1, lax.rem(sib + 2, TP)).wait_recv()

    def attn_tile(at):
        attn[:, pl.ds(at, TILE)] = mm(attended[...], wo[:, pl.ds(at, TILE)])

    loop(D, TILE, attn_tile)
    rises(start, False, True)

    row = lambda part: mod[pl.ds(c * 6 + part, 1), :]

    def norm_rows(at):
        rows = pl.ds(at, 64)
        values = tokens[pl.ds(mine + at, 64), :].astype(F32) + row(2) * attn[rows, :]
        mid[rows, :] = values
        normed, inverse = normalize(values)
        norm[rows, :] = normed
        inv[rows, :] = inverse
        sin[pl.ds(mine + at, 64), :] = (normed * (1.0 + row(4)) + row(3)).astype(BF16)

    loop(TOK_FRAME, 64, norm_rows)

    def n_copy(base):
        ref = sin.at[pl.ds(base, TOK_FRAME)]
        return remote(ref, ref, n_s.at[0], n_r.at[0], s, sib)

    n_copy(mine).start()
    loads(lambda copy: copy.wait())
    for k in plan.early:
        zo, ro, at = home(k)

        @pl.when(r != ro)
        def _():
            risen(k)

    def feed(base):
        rows = pl.ds(base, TOK_FRAME)

        def tile(at):
            cols = pl.ds(at, TILE)
            u = mm(sin[rows, :], wb[HD : HD + FT, cols])
            square = u * u
            inner = GELU_A * u * (1.0 + GELU_B * square)
            th = jnp.tanh(inner)
            half = 0.5 * (1.0 + th)
            hidden[rows, cols] = (u * half).astype(BF16)
            slopes[rows, cols] = half + 0.5 * u * (1.0 - th * th) * (
                GELU_A * (1.0 + 3.0 * GELU_B * square)
            )

        loop(FT, TILE, tile)

    feed(mine)
    n_copy(theirs).wait_recv()
    feed(theirs)

    def d_up(at):
        cols = pl.ds(at, TILE)
        dup[:, cols] = (mm_nt(dmlp[...], wb[pl.ds(HD + FT + at, TILE), :]) * slopes[:, cols]).astype(
            BF16
        )

    loop(FT, TILE, d_up)

    def c_copy(w, n):
        return remote(csend.at[w, n], crecv.at[w, n], c_s.at[w, n], c_r.at[w, n], s, sib)

    def y_copy(w, n):
        return remote(ysend.at[w, n], yrecv.at[w, n], y_s.at[w, n], y_r.at[w, n], s, across)

    def pass_on(w, n):
        c_copy(w, n).wait_recv()
        ysend[w, n] = (own[n] + crecv[w, n].astype(F32)).astype(BF16)
        y_copy(w, n).start()

    def product(w, base, n):
        rows = pl.ds(base, TOK_FRAME)
        if w == 0:
            return mm_nt(dup[rows, :], wb[HD + n * TILE : HD + (n + 1) * TILE, :])
        return mm(hidden[rows, :], wb[HD + FT :, n * TILE : (n + 1) * TILE])

    def products(w):
        for n in range(TILES):
            csend[w, n] = product(w, theirs, n).astype(BF16)
            c_copy(w, n).start()
            own[n] = product(w, mine, n)
            if n:
                pass_on(w, n - 1)
        pass_on(w, TILES - 1)

    def down_grad(at):
        gb[pl.ds(HD + FT + at, TILE), :] = mm_tn(hidden[:, pl.ds(at, TILE)], dmlp[...]).astype(BF16)

    def up_grad(at):
        gb[pl.ds(HD + at, TILE), :] = mm_tn(sin[:, pl.ds(at, TILE)], dup[...]).astype(BF16)

    def early_grad(k, d):
        zo, ro, at = home(k)
        slot = lax.rem(ro - r + rn, rn) - 1 if d is None else d - 1
        return remote(
            w_rows(gb, k), eside.at[slot, plan.rank[k]], g_s.at[at], g_r.at[slot, plan.rank[k]],
            z * rn + ro, t,
        )

    def early_grads(act):
        for k in plan.early:
            zo, ro, at = home(k)

            @pl.when(r != ro)
            def _():
                act(early_grad(k, None))

    def early_hop(rank, act):
        for here, to in ((ZN - 1, s - rn), (0, s + rn)):
            @pl.when(z == here)
            def _():
                act(remote(esum.at[rank], eend.at[rank], h_s.at[rank], h_r.at[rank], to, t))

    def early_total(rank):
        for k in plan.early:
            if plan.rank[k] == rank:
                zo, ro, at = home(k)

                @pl.when(r == ro)
                def _():
                    for d in range(1, rn):
                        early_grad(k, d).wait_recv()

                    def body(at):
                        rows = pl.ds(at, 16)
                        total = gb[pl.ds((k - plan.nq) * plan.ub + at, 16), :].astype(F32)
                        for d in range(1, rn):
                            total = total + eside[d - 1, rank, rows, :].astype(F32)
                        esum[rank, rows, :] = total.astype(BF16)

                    loop(plan.ub, 16, body)
                    early_hop(rank, start)

    def early_pass(rank, to):
        return remote(esum.at[rank], ebuf.at[rank], i_s.at[rank], i_r.at[rank], to, t)

    def early_inner(rank):
        for k in plan.early:
            if plan.rank[k] == rank:
                zo, ro, at = home(k)

                @pl.when((r == ro) & (z > 0) & (z < ZN - 1))
                def _():
                    remote(
                        esum.at[rank], eend.at[rank], h_s.at[rank], h_r.at[rank], s, t
                    ).wait_recv()

                    def body(at):
                        rows = pl.ds(at, 16)
                        esum[rank, rows, :] = (
                            esum[rank, rows, :].astype(F32) + eend[rank, rows, :].astype(F32)
                        ).astype(BF16)

                    loop(plan.ub, 16, body)

                    @pl.when(z != zo)
                    def _():
                        early_pass(rank, s + rn if zo == 2 else s - rn).start()

    def early_close(rank):
        for k in plan.early:
            if plan.rank[k] == rank:
                zo, ro, at = home(k)

                @pl.when((r == ro) & (z == zo))
                def _():
                    early_pass(rank, s).wait_recv()

                @pl.when((r == ro) & (z == 3 - zo))
                def _():
                    early_pass(rank, s).wait_send()

    def early_hops_done(rank):
        for k in plan.early:
            if plan.rank[k] == rank:
                @pl.when(r == home(k)[1])
                def _():
                    early_hop(rank, lambda copy: copy.wait_send())

    loop(FT, TILE, down_grad)
    up_grad(D - TILE)
    early_grads(start)
    products(0)
    products(1)
    loop(D - TILE, TILE, up_grad)
    early_total(0)
    early_total(1)
    early_inner(0)

    dm = dmod
    dm[...] = jnp.zeros_like(dm)
    for n in range(TILES):
        y_copy(0, n).wait_recv()

    def total(w, rows):
        return jnp.concatenate(
            [ysend[w, n, rows].astype(F32) + yrecv[w, n, rows].astype(F32) for n in range(TILES)],
            axis=1,
        )

    def back_rows(at):
        rows = pl.ds(at, 64)
        tok_rows = pl.ds(mine + at, 64)
        grads = total(0, rows)
        normed = norm[rows, :]
        add_to(dm, 1, grads)
        add_to(dm, 2, grads * normed)
        values = grad_out[tok_rows, :].astype(F32) + norm_back(
            grads * (1.0 + row(4)), normed, inv[rows, :]
        )
        dmid[rows, :] = values
        add_to(dm, 0, attn[rows, :] * values)
        dattn[rows, :] = (row(2) * values).astype(BF16)

    loop(TOK_FRAME, 64, back_rows)
    for ch in range(2):
        part = mm_nt(dattn[...], wo[pl.ds(pl.multiple_of((2 * y + ch) * HD, HD), HD), :]).astype(BF16)
        for zh in range(ZN):
            cols = slice(zh * HEAD, (zh + 1) * HEAD)
            dsend[ch * ZN + zh] = jnp.concatenate([part[:PACK, cols], part[PACK:, cols]], axis=1)

    def d_copy(d, e):
        zd, cd = partner(d, e)
        return remote(
            dsend.at[cd * ZN + zd], do_out.at[z, c], d_s.at[2 * d + e], d_r.at[2 * z + c],
            zd * rn + r, 2 * y + cd,
        )

    for d, e in pairs:
        d_copy(d, e).start()
    do_out[z, c] = dsend[c * ZN + z]
    for rank in range(2, plan.ranks):
        early_total(rank)

    def o_grad(head_core):
        cols = pl.ds(pl.multiple_of((2 * y + head_core) * HD, HD), HD)
        return mm_tn(attended[:, cols], dattn[...])

    w_copy = remote(wsend, wrecv, w_s, w_r, s, sib)
    wsend[...] = o_grad(1 - c).astype(BF16)
    w_copy.start()
    dwo[...] = o_grad(c)
    early_inner(1)

    for n in range(TILES):
        y_copy(1, n).wait_recv()

    def result_rows(at):
        rows = pl.ds(at, 64)
        tok_rows = pl.ds(mine + at, 64)
        mlp = total(1, rows)
        add_to(dm, 3, mlp * grad_out[tok_rows, :].astype(F32))
        result[tok_rows, :] = (mid[rows, :] + row(5) * mlp).astype(BF16)

    loop(TOK_FRAME, 64, result_rows)

    def e_copy(base):
        ref = result.at[pl.ds(base, TOK_FRAME)]
        return remote(ref, ref, e_s, e_r, s, sib)

    e_copy(mine).start()
    for rank in range(2, plan.ranks):
        early_inner(rank)
    w_copy.wait_recv()
    gb[:HD, :] = (dwo[...] + wrecv[...].astype(F32)).astype(BF16)

    for d, e in pairs:
        zd, cd = partner(d, e)
        remote(
            dsend.at[0], do_out.at[zd, cd], d_s.at[0], d_r.at[2 * zd + cd], s, t
        ).wait_recv()
    def late_grads(act):
        for k in plan.late:
            zo, ro = plan.home(k)
            rank, sem = plan.grad_rank[k], j_s.at[k - plan.nq]

            @pl.when(r == ro)
            def _():
                act(pltpu.make_async_copy(w_rows(gb, k), late_own.at[rank], sem))

            @pl.when(r != ro)
            def _():
                d = lax.rem(ro - r + rn, rn)
                act(pltpu.make_async_copy(w_rows(gb, k), late_send.at[d - 1, rank], sem))

    late_grads(start)
    for rank in range(plan.ranks):
        early_close(rank)
    e_copy(theirs).wait_recv()
    done = lambda copy: copy.wait_send()
    early_grads(done)
    for rank in range(plan.ranks):
        early_hops_done(rank)
    late_grads(lambda copy: copy.wait())
    rises(done, True, False)
    rises(done, False, False)
    for d, e in pairs:
        o_copy(d, e).wait_send()
        d_copy(d, e).wait_send()
    for slot in range(8):
        f_copy(slot).wait_send()
    n_copy(mine).wait_send()
    p_copy(0, t).wait_send()
    p_copy(1, across).wait_send()
    for w in range(2):
        for n in range(TILES):
            c_copy(w, n).wait_send()
            y_copy(w, n).wait_send()
    w_copy.wait_send()
    e_copy(mine).wait_send()


def middle_part(plan, o_mine, wo_across, weights, tokens, grad_out, mod_rows, cid):
    rn, count = plan.r, len(plan.early)
    rows = F_DEV * TOK_FRAME
    half = lambda dtype: pltpu.VMEM((TOK_FRAME, D), dtype)
    full = lambda dtype: pltpu.VMEM((rows, D), dtype)
    tiles = pltpu.VMEM((2, TILES, TOK_FRAME, TILE), BF16)
    return call(
        functools.partial(middle_kernel, plan),
        (
            jax.ShapeDtypeStruct((rows, D), BF16),
            jax.ShapeDtypeStruct((plan.grad_ranks, plan.ub, D), BF16),
            jax.ShapeDtypeStruct((rn - 1, plan.grad_ranks, plan.ub, D), BF16),
            jax.ShapeDtypeStruct((plan.ranks, plan.ub, D), BF16),
            jax.ShapeDtypeStruct((plan.ranks, plan.ub, D), BF16),
            jax.ShapeDtypeStruct((ZN, F_DEV, PACK, LANES), BF16),
            jax.ShapeDtypeStruct((TOK_FRAME, D), F32),
            jax.ShapeDtypeStruct((8, D), F32),
        ),
        [
            pltpu.VMEM((BROWS, D), BF16),
            pltpu.VMEM((BROWS, D), BF16),
            pltpu.VMEM((rn - 1, plan.ranks, plan.ub, D), BF16),
            pltpu.VMEM((plan.ranks, plan.ub, D), BF16),
            pltpu.VMEM((HEADS * HEAD, D), BF16),
            pltpu.VMEM((HEADS, PACK, LANES), BF16),
            half(BF16), half(F32), half(F32), half(F32), pltpu.VMEM((TOK_FRAME, 1), F32),
            full(BF16), full(BF16), full(BF16), full(F32), full(BF16),
            pltpu.VMEM((TILES, TOK_FRAME, TILE), F32), tiles, tiles, tiles, tiles,
            half(BF16), pltpu.VMEM((8, PACK, LANES), BF16),
            pltpu.VMEM((HD, D), F32), pltpu.VMEM((HD, D), BF16), pltpu.VMEM((HD, D), BF16),
            DMA((8,)), DMA((8,)), DMA((8,)), DMA((8,)), DMA((1,)), DMA((1,)),
            DMA((2, TILES)), DMA((2, TILES)), DMA((2, TILES)), DMA((2, TILES)),
            DMA((8,)), DMA((8,)), DMA, DMA, DMA, DMA, DMA((2,)), DMA((2,)),
            DMA((len(plan.late) + count,)), DMA((count, rn)), DMA((count,)), DMA((count,)), DMA((rn - 1, plan.ranks)),
            DMA((len(plan.late),)), DMA((plan.ranks,)), DMA((plan.ranks,)),
            DMA((plan.ranks,)), DMA((plan.ranks,)),
        ],
        [VM, VM, ANY, ANY, ANY, ANY, ANY, VM, VM, VM],
        cid,
        out_specs=(VM, ANY, ANY, VM, VM, VM, VM, VM),
        name="middle_part",
    )(o_mine, wo_across, *weights, tokens, grad_out, mod_rows)


def tail_kernel(
    plan, meta, q, kv, do, ot, lse, first_in, wq, tokens, dmid, mod, dm4, late_own, late_send, esum, ebuf,
    igrad, oq, ob, dall,
    keys, flipped, qs, gs, qgt, drow, acc, dq_acc, dq, kv_two, lside,
    stage, side, q_in, kv_in, dqkv, gq, own, csend, crecv, ysend, yrecv, dm, dm3, dboth,
    lstage, cb, qside, qpeer, qchain, qstage,
    q_s, q_r, k_s, k_r, x_s, x_r, c_s, c_r, y_s, y_r, e_s, e_r, h_s, h_r, m_s, m_r, t_s, t_r,
    kv_s, ls_s, ls_r, qo_s, qs_r, qp_r, qc_s, qc_r,
):
    s, t, z, r = place(plan)
    n, rn = plan.n, plan.r
    y = lax.div(t, 2)
    c = lax.rem(t, 2)
    sib = 2 * y + 1 - c
    across = lax.rem(t + 2, TP)
    mine = pl.multiple_of(c * TOK_FRAME, TOK_FRAME)
    theirs = pl.multiple_of((1 - c) * TOK_FRAME, TOK_FRAME)
    greet([(lax.rem(s + d, n), t) for d in range(1, n)] + [(s, sib), (s, across)])

    def side_copy(zs, e):
        other = lax.rem(r + e, rn)
        return remote(
            keys.at[zs * rn + other], side.at[e - 1, zs], x_s.at[zs, e - 1], x_r.at[zs, e - 1],
            z * rn + other, t,
        )

    def q_copy(zs):
        return remote(dq.at[zs], q_in.at[z], q_s.at[zs], q_r.at[z], zs * rn + r, t)

    def kv_copy(zs):
        return remote(stage.at[zs], kv_in.at[z], k_s.at[zs], k_r.at[z], zs * rn + r, t)

    def send_q(zs):
        @pl.when(z == zs)
        def _():
            q_in[zs] = dq[zs]

        @pl.when(z != zs)
        def _():
            q_copy(zs).start()

    def send_kv(zs):
        total = keys[zs * rn + r].astype(F32)
        for e in range(1, rn):
            side_copy(zs, e).wait_recv()
            total = total + side[e - 1, zs].astype(F32)
        stage[zs] = total.astype(BF16)

        @pl.when(z == zs)
        def _():
            kv_in[zs] = stage[zs]

        @pl.when(z != zs)
        def _():
            kv_copy(zs).start()

    scale = HEAD ** (-0.5)
    acc[...] = jnp.zeros_like(acc)

    def load(g, slot):
        return pltpu.make_async_copy(kv.at[g], kv_two.at[slot], kv_s.at[slot])

    load(0, 0).start()

    def sort_group(g, carry):
        slot = lax.rem(g, 2)

        @pl.when(g + 1 < n)
        def _():
            load(g + 1, 1 - slot).start()

        load(g, slot).wait()
        first = meta[2 * g] == 0
        a, b = kv_two[slot, :TOK_FRAME, :], kv_two[slot, TOK_FRAME:, :]
        keys[g, 0] = jnp.where(first, a, b)
        keys[g, 1] = jnp.where(first, b, a)
        for kind in range(2):
            flipped[kind, g] = keys[g, kind].T
        return carry

    lax.fori_loop(0, n, sort_group, 0)

    def attend_back_group(zq):
        gq = zq * rn + r
        first = meta[2 * gq] == 0
        clip = meta[2 * gq] + meta[2 * gq + 1]
        parts = []
        for kind in range(2):
            low = first if kind == 0 else jnp.logical_not(first)
            qz = padded(jnp.where(low, q[zq][:, :HEAD], q[zq][:, HEAD:]), True) * jnp.asarray(scale, BF16)
            gpack = jnp.where(low, do[zq, 0], do[zq, 1])
            grads = jnp.concatenate([gpack[:, :HEAD], gpack[:, HEAD:]], axis=0)
            out = ot[2 * zq + kind]
            logs = lse[2 * zq + kind]
            gz = padded(grads, False)
            qs[...] = qz
            gs[...] = gz
            qgt[:, :TOK_FRAME] = qz.T
            qgt[:, TOK_FRAME:] = gz.T
            drow[...] = jnp.sum(grads.astype(F32).T * out, axis=0, keepdims=True)
            dq_acc[...] = jnp.zeros_like(dq_acc)

            def block(p, inner):
                total = dq_acc[...]
                for e in range(2):
                    g = jnp.minimum(2 * p + e, gq)
                    shown = 2 * p + e <= gq
                    if kind == 1:
                        shown = shown & (meta[2 * g] + meta[2 * g + 1] == clip)
                    off = jnp.where(shown, 0.0, 1e30)
                    key = keys[g, kind]
                    pt = jnp.exp(mm(key, qgt[:, :TOK_FRAME]) - (logs + off))
                    dst = (pt * (mm(key, qgt[:, TOK_FRAME:]) - drow[...])).astype(BF16)
                    acc[kind, g] += mm(dst, qs[...]) + mm(pt.astype(BF16), gs[...])
                    total = total + mm(flipped[kind, g], dst)
                dq_acc[...] = total
                return inner

            lax.fori_loop(0, lax.div(gq + 2, 2), block, 0)
            parts.append((dq_acc[:HEAD, :] * scale).T.astype(BF16))
        dq[zq] = jnp.concatenate(
            [jnp.where(first, parts[0], parts[1]), jnp.where(first, parts[1], parts[0])], axis=1
        )
        for other in range(rn):
            g = zq * rn + other
            low = meta[2 * g] == 0
            a, b = acc[0, g].astype(BF16), acc[1, g].astype(BF16)
            keys[g, 0] = jnp.where(low, a, b)
            keys[g, 1] = jnp.where(low, b, a)

    def late(units, act):
        for k in units:
            zo, ro = plan.home(k)

            @pl.when(r == ro)
            def _():
                act(k, zo, plan.grad_rank[k])

    def late_copy(rank, below, to):
        return remote(lstage.at[rank], cb.at[below, rank], t_s.at[rank], t_r.at[below, rank], to, t)

    def late_side(rank, d):
        return remote(
            late_send.at[d - 1, rank], lside.at[d - 1, rank], ls_s.at[rank, d - 1],
            ls_r.at[rank, d - 1], z * rn + lax.rem(r + d, rn), t,
        )

    def late_sides(rank, act):
        for d in range(1, rn):
            act(late_side(rank, d))

    def late_step(k, zo, rank, here_z, above, below, final):
        @pl.when(z == here_z)
        def _():
            for d in range(1, rn):
                late_side(rank, d).wait_recv()
            if above:
                late_copy(rank, 0, s).wait_recv()
            if below:
                late_copy(rank, 1, s).wait_recv()

            def body(at):
                rows = pl.ds(at, 16)
                total = late_own[rank, rows, :].astype(F32)
                for d in range(1, rn):
                    total = total + lside[d - 1, rank, rows, :].astype(F32)
                if above:
                    total = total + cb[0, rank, rows, :].astype(F32)
                if below:
                    total = total + cb[1, rank, rows, :].astype(F32)
                if final:
                    ob[k % 3, rows, :] = total
                else:
                    lstage[rank, rows, :] = total.astype(BF16)

            loop(plan.ub, 16, body)
            if not final:
                late_copy(
                    rank, 0 if here_z > zo else 1, s - rn if here_z > zo else s + rn
                ).start()

    def late_ends(k, zo, rank):
        late_step(k, zo, rank, ZN - 1, False, False, False)
        if zo > 0:
            late_step(k, zo, rank, 0, False, False, False)

    def late_inner(here):
        def act(k, zo, rank):
            if here > zo:
                late_step(k, zo, rank, here, True, False, False)

        return act

    def late_final(k, zo, rank):
        late_step(k, zo, rank, zo, True, zo > 0, True)

    def late_done(k, zo, rank):
        @pl.when(z != zo)
        def _():
            late_copy(rank, 0, s).wait_send()

    def early_units(act):
        for k in plan.early:
            zo, ro, rank = (k // 3) // rn, (k // 3) % rn, plan.rank[k]

            @pl.when(r == ro)
            def _():
                act(k, zo, rank)

    def early_final(k, zo, rank):
        @pl.when(z == zo)
        def _():
            def body(at):
                rows = pl.ds(at, 16)
                ob[k % 3, rows, :] = esum[rank, rows, :].astype(F32) + ebuf[rank, rows, :].astype(F32)

            loop(plan.ub, 16, body)

    hq = plan.uq // CUTS

    def q_rows(k, h):
        return gq.at[pl.ds(pl.multiple_of(k * plan.uq + h * hq, hq), hq)]

    def q_sides(k, act):
        tc, ro, j = k % rn, k // 3, k // rn
        for h in range(CUTS):
            @pl.when((z > 0) & (r != tc))
            def _():
                slot = lax.rem(tc - r + rn, rn) - 1
                act(
                    remote(
                        q_rows(k, h), qside.at[slot, CUTS * j + h], qo_s.at[CUTS * k + h],
                        qs_r.at[slot, CUTS * j + h], z * rn + tc, t,
                    )
                )

            @pl.when((z == 0) & (r != ro) & (r != tc))
            def _():
                slot = lax.rem(ro - r + rn, rn) - 1
                act(
                    remote(
                        q_rows(k, h), qpeer.at[slot, CUTS * (k % 3) + h], qo_s.at[CUTS * k + h],
                        qp_r.at[slot, CUTS * (k % 3) + h], ro, t,
                    )
                )

    def q_down(at, to):
        return remote(qstage.at[at], qchain.at[at], qc_s.at[at], qc_r.at[at], to, t)

    def q_chain(here, only_j):
        top = here == ZN - 1
        for j in (only_j,):
            k = r + rn * j
            for h in range(CUTS):
                at = CUTS * j + h

                @pl.when(z == here)
                def _():
                    for d in range(1, rn):
                        remote(
                            q_rows(k, h), qside.at[d - 1, at], qo_s.at[0], qs_r.at[d - 1, at], s, t
                        ).wait_recv()
                    if not top:
                        q_down(at, s).wait_recv()
                    unit = q_rows(k, h)

                    def body(row):
                        rows = pl.ds(row, 16)
                        total = unit[rows, :].astype(F32)
                        for d in range(1, rn):
                            total = total + qside[d - 1, at, rows, :].astype(F32)
                        if not top:
                            total = total + qchain[at, rows, :].astype(F32)
                        qstage[at, rows, :] = total.astype(BF16)

                    loop(hq, 16, body)
                    q_down(at, s - rn).start()

    def q_last_copy(k, h):
        tc, ro, j = k % rn, k // 3, k // rn
        slot = (ro - tc + rn) % rn - 1
        return remote(
            qstage.at[CUTS * j + h], qpeer.at[slot, CUTS * (k % 3) + h], qc_s.at[CUTS * j + h],
            qp_r.at[slot, CUTS * (k % 3) + h], ro, t,
        )

    def q_ground(act):
        for k in range(plan.nq):
            if k % rn != k // 3:
                @pl.when((z == 0) & (r == k % rn))
                def _():
                    for h in range(CUTS):
                        act(k, h)

    def q_turn(k, h):
        at = CUTS * (k // rn) + h
        q_down(at, s).wait_recv()
        unit = q_rows(k, h)

        def body(row):
            rows = pl.ds(row, 16)
            qstage[at, rows, :] = (
                unit[rows, :].astype(F32) + qchain[at, rows, :].astype(F32)
            ).astype(BF16)

        loop(hq, 16, body)
        q_last_copy(k, h).start()

    def q_final():
        for k in range(plan.nq):
            @pl.when((z == 0) & (r == k // 3))
            def _():
                straight = k % rn == k // 3
                for h in range(CUTS):
                    at = CUTS * (k // rn) + h
                    if straight:
                        q_down(at, s).wait_recv()
                    for d in range(1, rn):
                        remote(
                            q_rows(k, h), qpeer.at[d - 1, CUTS * (k % 3) + h], qo_s.at[0],
                            qp_r.at[d - 1, CUTS * (k % 3) + h], s, t,
                        ).wait_recv()
                    unit = q_rows(k, h)

                    def body(row):
                        rows = pl.ds(row, 16)
                        total = unit[rows, :].astype(F32)
                        for d in range(1, rn):
                            total = total + qpeer[d - 1, CUTS * (k % 3) + h, rows, :].astype(F32)
                        if straight:
                            total = total + qchain[at, rows, :].astype(F32)
                        oq[k % 3, pl.ds(h * hq + row, 16), :] = total

                    loop(hq, 16, body)

    start = lambda copy: copy.start()
    done = lambda copy: copy.wait_send()
    def only(rank, act):
        return lambda k, zo, own_rank: act(k, zo, own_rank) if own_rank == rank else None

    last = plan.grad_ranks - 1
    late_sides(0, start)
    for zq in range(ZN - 1, -1, -1):
        attend_back_group(zq)
        for e in range(1, rn):
            side_copy(zq, e).start()
        send_q(zq)
        if zq == ZN - 1:
            late(plan.late, only(0, late_ends))
        else:
            send_kv(zq + 1)
    for rank in range(1, plan.grad_ranks):
        late_sides(rank, start)
    send_kv(0)
    late(plan.late, only(0, late_inner(2)))
    late(plan.late, only(0, late_inner(1)))
    late(plan.late, only(1, late_ends))
    for zs in range(ZN):
        @pl.when(z != zs)
        def _():
            remote(dq.at[0], q_in.at[zs], q_s.at[0], q_r.at[zs], s, t).wait_recv()
            remote(stage.at[0], kv_in.at[zs], k_s.at[0], k_r.at[zs], s, t).wait_recv()

    for p in range(2):
        cols = slice(p * LANES, (p + 1) * LANES)
        a, b = q_in[2 * p], q_in[2 * p + 1]
        dqkv[:TOK_FRAME, cols] = jnp.concatenate([a[:, :HEAD], b[:, :HEAD]], axis=1)
        dqkv[TOK_FRAME:, cols] = jnp.concatenate([a[:, HEAD:], b[:, HEAD:]], axis=1)
        a, b = [kv_in[2 * p + i].reshape(F_DEV * TOK_FRAME, LANES) for i in range(2)]
        dqkv[:, HD + p * LANES : HD + (p + 1) * LANES] = jnp.concatenate(
            [a[:, :HEAD], b[:, :HEAD]], axis=1
        )
        dqkv[:, 2 * HD + p * LANES : 2 * HD + (p + 1) * LANES] = jnp.concatenate(
            [a[:, HEAD:], b[:, HEAD:]], axis=1
        )

    for m in range(TILES):
        gq[m * TILE : (m + 1) * TILE, :] = mm_tn(
            first_in[:, m * TILE : (m + 1) * TILE], dqkv[...]
        ).astype(BF16)
        for k in range(m * plan.nq // TILES, (m + 1) * plan.nq // TILES):
            q_sides(k, start)

    def c_copy(w):
        return remote(csend.at[w], crecv.at[w], c_s.at[w], c_r.at[w], s, sib)

    def y_copy(w):
        return remote(ysend.at[w], yrecv.at[w], y_s.at[w], y_r.at[w], s, across)

    def pass_on(w):
        c_copy(w).wait_recv()
        ysend[w] = (own[w] + crecv[w].astype(F32)).astype(BF16)
        y_copy(w).start()

    for w in range(TILES):
        weights = wq[w * TILE : (w + 1) * TILE, :]
        csend[w] = mm_nt(dqkv[pl.ds(theirs, TOK_FRAME), :], weights).astype(BF16)
        c_copy(w).start()
        own[w] = mm_nt(dqkv[pl.ds(mine, TOK_FRAME), :], weights)
        if w:
            pass_on(w - 1)
    pass_on(TILES - 1)

    for rank in range(2, plan.grad_ranks):
        late(plan.late, only(rank, late_ends))
    q_chain(ZN - 1, 0)
    q_chain(ZN - 1, 1)
    late(plan.late, only(1, late_inner(2)))
    q_chain(2, 0)
    late(plan.late, only(last, late_inner(2)))
    q_chain(2, 1)
    q_chain(1, 0)
    late(plan.late, only(1, late_inner(1)))
    q_chain(1, 1)
    late(plan.late, only(last, late_inner(1)))

    for w in range(TILES):
        y_copy(w).wait_recv()
    row = lambda part: mod[pl.ds(c * 6 + part, 1), :]
    dm[...] = jnp.zeros_like(dm)

    def input_rows(at):
        rows = pl.ds(at, 64)
        tok_rows = pl.ds(mine + at, 64)
        grads = jnp.concatenate(
            [ysend[w, rows].astype(F32) + yrecv[w, rows].astype(F32) for w in range(TILES)], axis=1
        )
        normed, inverse = normalize(tokens[tok_rows, :].astype(F32))
        add_to(dm, 0, grads)
        add_to(dm, 1, grads * normed)
        igrad[tok_rows, :] = dmid[rows, :] + norm_back(grads * (1.0 + row(1)), normed, inverse)

    loop(TOK_FRAME, 64, input_rows)

    def e_copy(base):
        ref = igrad.at[pl.ds(base, TOK_FRAME)]
        return remote(ref, ref, e_s, e_r, s, sib)

    e_copy(mine).start()

    for block in range(6 * D // LANES):
        part, at = block // (D // LANES), block % (D // LANES)
        src = dm if part < 2 else dm4
        lane = slice(at * LANES, (at + 1) * LANES)
        from_row = part if part < 2 else part - 2
        dm3[block // MCOLS, block % MCOLS : block % MCOLS + 1, :] = src[from_row : from_row + 1, lane]
    h_copy = lambda frame: remote(dm3.at[sib], dboth.at[frame], h_s, h_r, s, sib)
    h_copy(c).start()
    dboth[c] = dm3[t]
    h_copy(1 - c).wait_recv()

    def m_copy(src):
        return remote(dboth, dall.at[s], m_s.at[src - plan.first_mod], m_r.at[s], src, t)

    for src in range(plan.first_mod, n):
        @pl.when(s == src)
        def _():
            dall[s] = dboth[...]

        @pl.when(s != src)
        def _():
            m_copy(src).start()

    q_ground(q_turn)
    late(plan.late, late_final)
    early_units(early_final)
    q_final()

    @pl.when(s >= plan.first_mod)
    def _():
        for d in range(1, n):
            other = lax.rem(s + d, n)
            remote(dboth, dall.at[other], m_s.at[0], m_r.at[other], s, t).wait_recv()

    e_copy(theirs).wait_recv()
    for zs in range(ZN):
        @pl.when(z != zs)
        def _():
            q_copy(zs).wait_send()
            kv_copy(zs).wait_send()

        for e in range(1, rn):
            side_copy(zs, e).wait_send()
    for rank in range(plan.grad_ranks):
        late_sides(rank, done)
    late(plan.late, late_done)
    for k in range(plan.nq):
        q_sides(k, done)

    @pl.when(z > 0)
    def _():
        for at in range(2 * CUTS):
            q_down(at, s).wait_send()

    q_ground(lambda k, h: q_last_copy(k, h).wait_send())
    for w in range(TILES):
        c_copy(w).wait_send()
        y_copy(w).wait_send()
    e_copy(mine).wait_send()
    h_copy(c).wait_send()
    for src in range(plan.first_mod, n):
        @pl.when(s != src)
        def _():
            m_copy(src).wait_send()


def tail_part(plan, meta, q, kv, do, ot, lse, first_in, wq, tokens, dmid, mod_rows, dm4, late_own, late_send, esum, ebuf, cid):
    n, rn = plan.n, plan.r
    rows = F_DEV * TOK_FRAME
    tiles = pltpu.VMEM((TILES, TOK_FRAME, TILE), BF16)
    mods = n - plan.first_mod
    return call(
        functools.partial(tail_kernel, plan),
        (
            jax.ShapeDtypeStruct((rows, D), F32),
            jax.ShapeDtypeStruct((3, plan.uq, QKV), F32),
            jax.ShapeDtypeStruct((3, plan.ub, D), F32),
            jax.ShapeDtypeStruct((n, F_DEV, 16, LANES), F32),
        ),
        [
            pltpu.VMEM((n, 2, TOK_FRAME, LANES), BF16),
            pltpu.VMEM((2, n, LANES, TOK_FRAME), BF16),
            pltpu.VMEM((TOK_FRAME, LANES), BF16),
            pltpu.VMEM((TOK_FRAME, LANES), BF16),
            pltpu.VMEM((LANES, 2 * TOK_FRAME), BF16),
            pltpu.VMEM((1, TOK_FRAME), F32),
            pltpu.VMEM((2, n, TOK_FRAME, LANES), F32),
            pltpu.VMEM((LANES, TOK_FRAME), F32),
            pltpu.VMEM((ZN, TOK_FRAME, LANES), BF16),
            pltpu.VMEM((2, rows, LANES), BF16),
            pltpu.VMEM((rn - 1, plan.grad_ranks, plan.ub, D), BF16),
            pltpu.VMEM((ZN, 2, TOK_FRAME, LANES), BF16),
            pltpu.VMEM((rn - 1, ZN, 2, TOK_FRAME, LANES), BF16),
            pltpu.VMEM((ZN, TOK_FRAME, LANES), BF16),
            pltpu.VMEM((ZN, 2, TOK_FRAME, LANES), BF16),
            pltpu.VMEM((rows, QKV), BF16),
            pltpu.VMEM((D, QKV), BF16),
            pltpu.VMEM((TILES, TOK_FRAME, TILE), F32), tiles, tiles, tiles, tiles,
            pltpu.VMEM((8, D), F32),
            pltpu.VMEM((TP, 16, LANES), F32),
            pltpu.VMEM((F_DEV, 16, LANES), F32),
            pltpu.VMEM((plan.grad_ranks, plan.ub, D), BF16),
            pltpu.VMEM((2, plan.grad_ranks, plan.ub, D), BF16),
            pltpu.VMEM((rn - 1, 2 * CUTS, plan.uq // CUTS, QKV), BF16),
            pltpu.VMEM((rn - 1, 3 * CUTS, plan.uq // CUTS, QKV), BF16),
            pltpu.VMEM((2 * CUTS, plan.uq // CUTS, QKV), BF16),
            pltpu.VMEM((2 * CUTS, plan.uq // CUTS, QKV), BF16),
            DMA((ZN,)), DMA((ZN,)), DMA((ZN,)), DMA((ZN,)), DMA((ZN, rn - 1)), DMA((ZN, rn - 1)),
            DMA((TILES,)), DMA((TILES,)), DMA((TILES,)), DMA((TILES,)),
            DMA, DMA, DMA, DMA, DMA((mods,)), DMA((n,)),
            DMA((plan.grad_ranks,)), DMA((2, plan.grad_ranks)),
            DMA((2,)), DMA((plan.grad_ranks, rn - 1)), DMA((plan.grad_ranks, rn - 1)),
            DMA((CUTS * plan.nq,)),
            DMA((rn - 1, 2 * CUTS)), DMA((rn - 1, 3 * CUTS)), DMA((2 * CUTS,)), DMA((2 * CUTS,)),
        ],
        [SM, VM, ANY] + [VM] * 10 + [ANY, VM, VM],
        cid,
        name="tail_part",
    )(meta, q, kv, do, ot, lse, first_in, wq, tokens, dmid, mod_rows, dm4, late_own, late_send, esum, ebuf)


def adam_kernel(plan, meta, oq, ob, cond, dmod, master, one, two, average, n_master, n_one, n_two, n_average):
    s = meta[0]
    rate = RATE_FACTOR * D ** (-0.5)
    scale_one = 1.0 / (1.0 - BETA_FIRST**STEP)
    scale_two = 1.0 / (1.0 - BETA_SECOND**STEP)

    def update(rows, grad):
        first = BETA_FIRST * one[rows, :] + (1.0 - BETA_FIRST) * grad
        second = BETA_SECOND * two[rows, :] + (1.0 - BETA_SECOND) * grad * grad
        weight = master[rows, :]
        weight = weight - rate * (
            (first * scale_one) / (jnp.sqrt(second * scale_two) + ADAM_EPSILON)
            + WEIGHT_DECAY * weight
        )
        n_one[rows, :] = first
        n_two[rows, :] = second
        n_master[rows, :] = weight
        n_average[rows, :] = AVERAGE_RATE * average[rows, :] + (1.0 - AVERAGE_RATE) * weight

    if True:
        k = 3 * s + pl.program_id(0)
        base = 0

        def from_matrix(kind):
            src = oq if kind == "q" else ob
            rows = plan.uq if kind == "q" else plan.ub
            cols = (QKV if kind == "q" else D) // LANES
            for j in range(cols):
                update(
                    pl.ds(base + j, rows, stride=cols), src[0, :, j * LANES : (j + 1) * LANES]
                )

        by_kind(plan, k, from_matrix)

        @pl.when(k >= plan.nb)
        def _():
            at = cond[k - plan.nb]
            for j in range(MCOLS):
                update(
                    pl.ds(base + j, plan.um, stride=MCOLS),
                    mm(at, dmod[pl.ds(j, plan.frames, stride=16), :].astype(BF16)),
                )


def adam(plan, meta, oq, ob, cond_rows, dmod, master, one, two, average):
    shape = jax.ShapeDtypeStruct(master.shape, F32)
    flat = pl.BlockSpec((plan.flat_rows, LANES), lambda i: (i, 0))
    unit = lambda rows, cols: pl.BlockSpec((1, rows, cols), lambda i: (i, 0, 0))
    whole = lambda x: pl.BlockSpec(x.shape, lambda i: (0,) * x.ndim)
    return pl.pallas_call(
        functools.partial(adam_kernel, plan),
        out_shape=(shape,) * 4,
        grid=(3,),
        in_specs=[SM, unit(plan.uq, QKV), unit(plan.ub, D), whole(cond_rows), whole(dmod)] + [flat] * 4,
        out_specs=(flat,) * 4,
        compiler_params=pltpu.CompilerParams(vmem_limit_bytes=VMEM_LIMIT),
        name="adam",
    )(meta, oq, ob, cond_rows, dmod, master, one, two, average)


def local(
    tokens,
    grad_out,
    noise_level,
    context_mask,
    frame_clip,
    level_table,
    master,
    moment_one,
    moment_two,
    average,
):
    plan = Plan(lax.axis_size("seq"))
    s = lax.axis_index("seq")
    t = lax.axis_index("tp")
    flat = lambda x: x.reshape(-1, LANES)

    effective = noise_level * (1 - context_mask)
    one_hot = (
        effective[:, None] == jnp.arange(level_table.shape[0], dtype=jnp.int32)[None, :]
    ).astype(BF16)
    condition = jax.nn.silu(mm(one_hot, level_table)).astype(BF16)
    cond_units = condition.reshape(plan.frames, plan.nm, plan.um).transpose(1, 0, 2)

    meta = frame_clip.astype(jnp.int32)
    (
        wq, w_out, w_side, w_early, w_below, w_beside, wo_across, mod_rows, first_in, q_mine, kv_all,
        o_mine, o_rows, lse,
    ) = head_part(plan, meta, flat(master), cond_units, tokens, 0)
    result, late_own, late_send, early_sum, early_in, do_mine, middle_grad, mod_four = middle_part(
        plan, o_mine, wo_across, (w_out, w_side, w_beside, w_early, w_below),
        tokens, grad_out, mod_rows, 2
    )
    input_grad, own_q, own_b, mod_all = tail_part(
        plan, meta, q_mine, kv_all, do_mine, o_rows, lse, first_in, wq, tokens, middle_grad,
        mod_rows, mod_four, late_own, late_send, early_sum, early_in, 3,
    )
    updated = adam(
        plan,
        s[None].astype(jnp.int32),
        own_q,
        own_b,
        cond_units.transpose(0, 2, 1),
        flat(mod_all),
        flat(master),
        flat(moment_one),
        flat(moment_two),
        flat(average),
    )
    new_master, new_one, new_two, new_average = [x.reshape(master.shape) for x in updated]
    return (result, input_grad, new_master, new_one, new_two, new_average)


def solution(mesh):
    token_spec = P("seq", None)
    weight_spec = P("tp", "seq")
    in_specs = (token_spec, token_spec, P(), P(), P(), P()) + (weight_spec,) * 4
    out_specs = (token_spec, token_spec) + (weight_spec,) * 4
    return jax.shard_map(local, mesh=mesh, in_specs=in_specs, out_specs=out_specs, check_vma=False)
```

```python
import functools

import jax
import jax.numpy as jnp
from jax import lax
from jax.experimental import pallas as pl
from jax.experimental.pallas import tpu as pltpu
from jax.sharding import PartitionSpec as P

D = 1024
HEADS = 16
HEAD = 64
FF = 4096
TOK_FRAME = 384
STEP = 7
TP = 4
ZN = 4
HD = HEADS * HEAD // TP
QKV = 3 * HD
FT = FF // TP
MT = 6 * D // TP
F_DEV = 2
BROWS = HD + 2 * FT
LANES = 128
MCOLS = MT // LANES
PACK = TOK_FRAME // 2
TILE = 256
TILES = D // TILE
CUTS = 4
ADAM_CUTS = 2

NORM_EPSILON = 1e-06
RATE_FACTOR = 2.5
BETA_FIRST = 0.5
BETA_SECOND = 0.5
ADAM_EPSILON = 1e-08
WEIGHT_DECAY = 0.01
AVERAGE_RATE = 0.9
GELU_A = 0.7978845608028654
GELU_B = 0.044715
MESH = pl.DeviceIdType.MESH
VM = pl.BlockSpec(memory_space=pltpu.VMEM)
SM = pl.BlockSpec(memory_space=pltpu.SMEM)
ANY = pl.BlockSpec(memory_space=pl.ANY)
DMA = pltpu.SemaphoreType.DMA
F32 = jnp.float32
BF16 = jnp.bfloat16
VMEM_LIMIT = 60 * 2**20


def mm(left, right):
    return jnp.dot(left, right, preferred_element_type=F32)


def mm_tn(left, right):
    return lax.dot_general(left, right, (((0,), (0,)), ((), ())), preferred_element_type=F32)


def mm_nt(left, right):
    return lax.dot_general(left, right, (((1,), (1,)), ((), ())), preferred_element_type=F32)


def normalize(rows):
    centred = rows - jnp.mean(rows, axis=1, keepdims=True)
    inverse = lax.rsqrt(jnp.mean(centred * centred, axis=1, keepdims=True) + NORM_EPSILON)
    return (centred * inverse, inverse)


def norm_back(grads, normed, inverse):
    return inverse * (
        grads
        - jnp.mean(grads, axis=1, keepdims=True)
        - normed * jnp.mean(grads * normed, axis=1, keepdims=True)
    )


def loop(count, step, body):
    def turn(i, carry):
        body(pl.multiple_of(i * step, step))
        return carry

    lax.fori_loop(0, count // step, turn, 0)


def add_to(ref, row, values):
    ref[pl.ds(row, 1), :] += jnp.sum(values, axis=0, keepdims=True)


class Plan:
    def __init__(self, seq_count):
        self.n = seq_count
        self.r = seq_count // ZN
        self.shard = (D * QKV + BROWS * D + D * MT) // seq_count
        self.unit = self.shard // 3
        self.uq = self.unit // QKV
        self.ub = self.unit // D
        self.um = self.unit // MT
        self.nq = D // self.uq
        self.nb = self.nq + BROWS // self.ub
        self.nm = D // self.um
        self.first_mod = self.nb // 3
        self.half = (self.nq + self.nb) // 2
        self.flat_rows = self.unit // LANES
        self.frames = seq_count * F_DEV
        self.late = list(range(self.nq, self.half))
        self.early = list(range(self.half, self.nb))
        self.outs = self.late[: -(-HD // self.ub)]
        self.sided = self.late[len(self.outs) :]
        self.rank, self.ranks = self.ranked(self.early)
        self.late_rank, self.late_ranks = self.ranked(self.sided)
        self.grad_rank, self.grad_ranks = self.ranked(self.late)

    def ranked(self, units):
        seen, rank = {}, {}
        for k in units:
            column = self.home(k)[1]
            rank[k] = seen.get(column, 0)
            seen[column] = rank[k] + 1
        return rank, max(seen.values())

    def home(self, k):
        return (k // 3) // self.r, (k // 3) % self.r


def place(plan):
    s = lax.axis_index("seq")
    t = lax.axis_index("tp")
    return s, t, lax.div(s, plan.r), lax.rem(s, plan.r)


def remote(src, dst, send_sem, recv_sem, s, t):
    return pltpu.make_async_remote_copy(
        src_ref=src,
        dst_ref=dst,
        send_sem=send_sem,
        recv_sem=recv_sem,
        device_id=(s, t),
        device_id_type=MESH,
    )


def greet(peers):
    barrier = pltpu.get_barrier_semaphore()
    for s, t in peers:
        pl.semaphore_signal(barrier, inc=1, device_id=(s, t), device_id_type=MESH)
    pl.semaphore_wait(barrier, len(peers))


def by_kind(plan, k, act, low=0, high=None):
    high = plan.nb if high is None else high
    q_high, b_low = min(plan.nq, high), max(plan.nq, low)
    if low < q_high:
        @pl.when((k >= low) & (k < q_high))
        def _():
            act("q")

    if b_low < high:
        @pl.when((k >= b_low) & (k < high))
        def _():
            act("b")


def unit_of(plan, k, kind, wq, wb):
    if kind == "q":
        return wq.at[pl.ds(pl.multiple_of(k * plan.uq, plan.uq), plan.uq)]
    return wb.at[pl.ds(pl.multiple_of((k - plan.nq) * plan.ub, plan.ub), plan.ub)]


def call(kernel, outs, scratch, ins, cid=None, cost=None, name=None, out_specs=None):
    params = dict(vmem_limit_bytes=VMEM_LIMIT)
    if cid is not None:
        params.update(collective_id=cid, has_side_effects=True)
    return pl.pallas_call(
        kernel,
        out_shape=outs,
        in_specs=ins,
        out_specs=out_specs or jax.tree.map(lambda _: VM, outs),
        scratch_shapes=scratch,
        compiler_params=pltpu.CompilerParams(**params),
        cost_estimate=cost,
        name=name,
    )


def head_kernel(
    plan, meta, master, cond, tokens,
    wq, w_out, w_side, w_early, w_below, w_beside, wo_across, mods, first_in, q_out, kv_out, o, ot, lse,
    own_b, pool, flipped, qt, m_ref, l_ref, acc, tile, macc, mpart, mrecv, mod, norm, q_send, kv_send,
    qp_s, qc_s, q_r, wo_s, wo_r, ws_s, ws_r, we_s, we_r, loc_s, m_s, m_r, t_s, t_r, as_, ar, ks, kr, xs, xr,
    bl_s, bl_r, bs_s, bs_r, oa_s, oa_r,
):
    s, t, z, r = place(plan)
    n, rn = plan.n, plan.r
    greet(
        [(lax.rem(s + d, n), t) for d in range(1, n)]
        + [(s, lax.rem(t + d, TP)) for d in range(1, TP)]
    )
    start = lambda copy: copy.start()
    done = lambda copy: copy.wait_send()
    cut = plan.uq // CUTS

    def q_rows(k, h):
        return wq.at[pl.ds(pl.multiple_of(k * plan.uq + h * cut, cut), cut)]

    def q_copy(k, h, sem, to_s):
        ref = q_rows(k, h)
        return remote(ref, ref, sem, q_r.at[CUTS * k + h], to_s, t)

    def q_arrived(k, h):
        q_copy(k, h, qc_s.at[0, 0], s).wait_recv()

    def column(j):
        return r + rn * lax.rem(j + r, 2)

    def q_own(i, act):
        k = 3 * s + i

        @pl.when(k < plan.nq)
        def _():
            for h in range(CUTS):
                for d in range(1, rn):
                    act(q_copy(k, h, qp_s.at[CUTS * i + h, d - 1], lax.rem(r + d, rn)))

    def q_line(act, wait, whole=False):
        for j in range(2):
            k = column(j)
            for h in range(CUTS):
                if wait:
                    @pl.when((z > 0) | (lax.div(k, 3) != r))
                    def _():
                        q_arrived(k, h)

                @pl.when((z < ZN - 1) & ((z > 0) | (lax.div(k, 3) != r) | whole))
                def _():
                    act(q_copy(k, h, qc_s.at[CUTS * j + h, 0], s + rn))

                @pl.when(z > 0)
                def _():
                    for d in range(1, rn):
                        act(
                            q_copy(
                                k, h, qc_s.at[CUTS * j + h, d], z * rn + lax.rem(r + d, rn)
                            )
                        )

    def slot(k):
        if k in plan.outs:
            at = k - plan.nq
            return w_out.at[at], wo_s.at[at], wo_r.at[at]
        if k in plan.sided:
            at = plan.late_rank[k]
            return w_side.at[at], ws_s.at[at], ws_r.at[at]
        return w_early.at[k - plan.half], we_s.at[plan.rank[k]], we_r.at[k - plan.half]

    def along(k, src, act, up):
        dst, send_sem, recv_sem = slot(k)
        if up and k < plan.half:
            @pl.when(z < ZN - 1)
            def _():
                act(remote(src, dst, send_sem.at[0], recv_sem, s + rn, t))

        if not up:
            @pl.when(z > 0)
            def _():
                act(remote(src, dst, send_sem.at[1], recv_sem, s - rn, t))

    def beside(k, src, act):
        if k not in plan.outs:
            return
        dst, send_sem, recv_sem = slot(k)
        for d in range(1, rn):
            act(
                remote(
                    src, dst, send_sem.at[1 + d], recv_sem, z * rn + lax.rem(r + d, rn), t
                )
            )

    def arrived(k):
        dst, send_sem, recv_sem = slot(k)
        remote(own_b.at[0], dst, send_sem.at[0], recv_sem, s, t).wait_recv()

    def keep(k):
        return pltpu.make_async_copy(own_b.at[k % 3], slot(k)[0], loc_s.at[k % 3])

    def owned(units, act):
        for k in units:
            @pl.when(s == k // 3)
            def _():
                act(k, own_b.at[k % 3])

    def pass_along(units, d, act, wait):
        for k in units:
            zo, ro = plan.home(k)
            if k < plan.half and zo + d < (ZN - 1 if k in plan.sided else ZN):
                @pl.when((r == ro) & (z == zo + d))
                def _():
                    if wait:
                        arrived(k)
                    along(k, slot(k)[0], act, True)
                    beside(k, slot(k)[0], act)

            if zo - d >= (0 if k in plan.outs else 1):
                @pl.when((r == ro) & (z == zo - d))
                def _():
                    if wait:
                        arrived(k)
                    along(k, slot(k)[0], act, False)
                    beside(k, slot(k)[0], act)

    def settle(k, low):
        zo, ro = plan.home(k)

        @pl.when((r == ro) & ((z == 0) & (zo > 0) if low else (z == ZN - 1) & (zo < ZN - 1)))
        def _():
            arrived(k)

    def hop(k, act):
        zo, ro = plan.home(k)

        @pl.when(s == k // 3)
        def _():
            act(remote(own_b.at[k % 3], w_below.at[k % 3], bl_s.at[k % 3], bl_r.at[k % 3], s + rn, t))

    def hopped(k):
        zo, ro = plan.home(k)

        @pl.when((r == ro) & (z == zo + 1))
        def _():
            remote(own_b.at[0], w_below.at[k % 3], bl_s.at[0], bl_r.at[k % 3], s, t).wait_recv()

    def share(k, act, low=None):
        rank = plan.late_rank[k]
        part = True if low is None else (z <= 1) == low

        @pl.when((r == plan.home(k)[1]) & part)
        def _():
            for d in range(1, rn):
                act(
                    remote(
                        w_side.at[rank], w_beside.at[d - 1, rank], bs_s.at[rank, d - 1],
                        bs_r.at[d - 1, rank], z * rn + lax.rem(r + d, rn), t,
                    )
                )

    def shared(k):
        rank = plan.late_rank[k]

        @pl.when(r != plan.home(k)[1])
        def _():
            d = lax.rem(r - plan.home(k)[1] + rn, rn)
            remote(
                w_side.at[0], w_beside.at[d - 1, rank], bs_s.at[0, 0], bs_r.at[d - 1, rank], s, t
            ).wait_recv()

    def out_copy(w):
        count = min(plan.ub, HD - w * plan.ub)
        return remote(
            w_out.at[w].at[pl.ds(0, count)], wo_across.at[pl.ds(w * plan.ub, count)],
            oa_s.at[w], oa_r.at[w], s, lax.rem(t + 2, TP),
        )

    def sort_group(g):
        first = meta[2 * g] == 0
        a, b = kv_out[g, :TOK_FRAME, :], kv_out[g, TOK_FRAME:, :]
        pool[g, 0] = jnp.where(first, a, b)
        pool[g, 1] = jnp.where(first, b, a)
        for kind in range(2):
            flipped[kind, g] = pool[g, kind].T

    def attend_group(zq):
        gq = zq * rn + r
        first = meta[2 * gq] == 0
        clip = meta[2 * gq] + meta[2 * gq + 1]
        parts = []
        for kind in range(2):
            low = first if kind == 0 else jnp.logical_not(first)
            rows = jnp.where(low, q_out[zq][:, :HEAD], q_out[zq][:, HEAD:])
            qt[...] = (padded(rows, True) * jnp.asarray(HEAD ** (-0.5), BF16)).T
            m_ref[...] = jnp.full_like(m_ref, -1e30)
            l_ref[...] = jnp.zeros_like(l_ref)
            acc[...] = jnp.zeros_like(acc)

            def block(p, inner):
                pair = []
                m_old = m_ref[...]
                m_new = m_old
                for e in range(2):
                    g = jnp.minimum(2 * p + e, gq)
                    shown = 2 * p + e <= gq
                    if kind == 1:
                        shown = shown & (meta[2 * g] + meta[2 * g + 1] == clip)
                    off = jnp.where(shown, 0.0, 1e30)
                    st = mm(pool[g, kind], qt[...])
                    m_new = jnp.maximum(m_new, jnp.max(st, axis=0, keepdims=True) - off)
                    pair.append((g, st, off))
                alpha = jnp.exp(m_old - m_new)
                total, out = l_ref[...] * alpha, acc[...] * alpha
                for g, st, off in pair:
                    weights = jnp.exp(st - (m_new + off))
                    total = total + jnp.sum(weights, axis=0, keepdims=True)
                    out = out + mm(flipped[kind, g], weights.astype(BF16))
                m_ref[...] = m_new
                l_ref[...] = total
                acc[...] = out
                return inner

            lax.fori_loop(0, lax.div(gq + 2, 2), block, 0)
            total = l_ref[...]
            out = acc[HEAD:, :] / total
            ot[2 * zq + kind] = out
            lse[2 * zq + kind] = m_ref[...] + jnp.log(total)
            rows = out.T
            parts.append(jnp.concatenate([rows[:PACK], rows[PACK:]], axis=1).astype(BF16))
        o[zq, 0] = jnp.where(first, parts[0], parts[1])
        o[zq, 1] = jnp.where(first, parts[1], parts[0])

    units = plan.late + plan.early
    first_up = [k for k in plan.late if k % 3 == 0 and plan.home(k)[0] > 0]
    later_up = [k for k in plan.late if k not in first_up]

    def fill(i, kind):
        k = 3 * s + i
        base = i * plan.flat_rows
        rows, cols = (plan.uq, QKV // LANES) if kind == "q" else (plan.ub, D // LANES)
        at = pl.multiple_of(k * plan.uq, plan.uq)
        for j in range(cols):
            values = master[pl.ds(base + j, rows, stride=cols), :].astype(BF16)
            if kind == "q":
                wq[pl.ds(at, rows), j * LANES : (j + 1) * LANES] = values
            else:
                own_b[i, :, j * LANES : (j + 1) * LANES] = values

    for away in (True, False):
        for i in range(3):
            k = 3 * s + i

            @pl.when((k < plan.nq) & ((lax.rem(k, rn) != r) == away))
            def _():
                fill(i, "q")
                q_own(i, start)
                if not away:
                    at = lax.div(k, rn)
                    slot_j = lax.rem(at + r, 2)
                    for h in range(CUTS):
                        q_copy(k, h, qc_s.at[CUTS * slot_j + h, 0], s + rn).start()

    for i in range(3):
        @pl.when((3 * s + i >= plan.nq) & (3 * s + i < plan.nb))
        def _():
            fill(i, "b")

    @pl.when(z == 0)
    def _():
        q_line(start, True)

    owned(units, lambda k, src: along(k, src, start, False))
    owned(first_up, lambda k, src: along(k, src, start, True))
    owned(units, lambda k, src: keep(k).start())

    macc[...] = jnp.zeros_like(macc)
    for i in range(3):
        k = 3 * s + i
        base = i * plan.flat_rows

        @pl.when(k >= plan.nb)
        def _():
            for j in range(MCOLS):
                tile[:, j * LANES : (j + 1) * LANES] = master[
                    pl.ds(base + j, plan.um, stride=MCOLS), :
                ].astype(BF16)
            macc[...] += mm(cond[k - plan.nb], tile[...])

    fm = plan.first_mod

    def m_copy(d):
        to = lax.rem(s + d, n)
        return remote(mpart.at[to], mrecv.at[s - fm], m_s.at[d - 1], m_r.at[s - fm], to, t)

    @pl.when(s >= fm)
    def _():
        for f in range(plan.frames):
            for j in range(MCOLS):
                mpart[f // F_DEV, pl.ds((f % F_DEV) * MCOLS + j, 1), :] = macc[
                    pl.ds(f, 1), j * LANES : (j + 1) * LANES
                ]
        mrecv[s - fm] = mpart[s]
        for d in range(1, n):
            m_copy(d).start()

    def norm_rows(at):
        rows = pl.ds(at, 64)
        norm[rows, :] = normalize(tokens[rows, :].astype(F32))[0]

    loop(F_DEV * TOK_FRAME, 64, norm_rows)

    @pl.when(z > 0)
    def _():
        q_line(start, True)

    owned(plan.outs, lambda k, src: along(k, src, start, True))
    owned([k for k in later_up if k not in plan.outs], lambda k, src: along(k, src, start, True))
    owned(units, lambda k, src: beside(k, src, start))
    pass_along(first_up + plan.early, 1, start, True)

    for src in range(fm, n):
        @pl.when(s != src)
        def _():
            remote(mpart.at[0], mrecv.at[src - fm], m_s.at[0], m_r.at[src - fm], s, t).wait_recv()

    total = mrecv[0]
    for src in range(1, n - fm):
        total = total + mrecv[src]
    mod[t] = total

    def t_copy(d):
        return remote(mod.at[t], mod.at[t], t_s.at[d - 1], t_r.at[t], s, lax.rem(t + d, TP))

    for d in range(1, TP):
        t_copy(d).start()
    for d in range(1, TP):
        other = lax.rem(t + d, TP)
        remote(mod.at[t], mod.at[other], t_s.at[0], t_r.at[other], s, t).wait_recv()
    for f in range(F_DEV):
        for block in range(TP * MCOLS):
            part, at = block // (D // LANES), block % (D // LANES)
            mods[f * 6 + part : f * 6 + part + 1, at * LANES : (at + 1) * LANES] = mod[
                block // MCOLS, f * MCOLS + block % MCOLS : f * MCOLS + block % MCOLS + 1, :
            ]

    def affine(f):
        def body(at):
            rows = pl.ds(f * TOK_FRAME + at, 64)
            first_in[rows, :] = (
                norm[rows, :] * (1.0 + mods[f * 6 + 1 : f * 6 + 2, :]) + mods[f * 6 : f * 6 + 1, :]
            ).astype(BF16)

        loop(TOK_FRAME, 64, body)

    for f in range(F_DEV):
        affine(f)

    for k in range(plan.nq):
        for h in range(CUTS):
            if rn > 1:
                at_zero = (z == 0) & (k // 3 != r) & (k % rn != r)

                @pl.when(at_zero | (z > 0) & (k % rn != r))
                def _():
                    q_arrived(k, h)

    keys = mm(first_in[...], wq[:, HD : 2 * HD]).astype(BF16)
    values = mm(first_in[...], wq[:, 2 * HD :]).astype(BF16)
    for h in range(ZN):
        cols = slice(h * HEAD, (h + 1) * HEAD)
        kv_send[h] = jnp.concatenate([keys[:, cols], values[:, cols]], axis=1)

    def kv_copy(d):
        h = lax.rem(z + d, ZN)
        return remote(kv_send.at[h], kv_out.at[s], ks.at[d - 1], kr.at[z], h * rn + r, t)

    def a_copy(d):
        h = lax.rem(z + d, ZN)
        return remote(q_send.at[h], q_out.at[z], as_.at[d - 1], ar.at[z], h * rn + r, t)

    def side_copy(zs, e):
        at = zs * rn + r
        ref = kv_out.at[at]
        return remote(ref, ref, xs.at[zs, e - 1], xr.at[at], z * rn + lax.rem(r + e, rn), t)

    for d in range(1, ZN):
        kv_copy(d).start()
    kv_out[s] = kv_send[z]
    for e in range(1, rn):
        side_copy(z, e).start()
    queries = mm(first_in[...], wq[:, :HD]).astype(BF16)
    for h in range(ZN):
        cols = slice(h * HEAD, (h + 1) * HEAD)
        q_send[h] = jnp.concatenate([queries[:TOK_FRAME, cols], queries[TOK_FRAME:, cols]], axis=1)
    for d in range(1, ZN):
        a_copy(d).start()
    q_out[z] = q_send[z]

    rest = [k for k in plan.sided if k not in first_up]
    pass_along(plan.outs + rest, 1, start, True)
    owned(units, lambda k, src: keep(k).wait())
    for k in plan.sided:
        settle(k, True)
        share(k, start, True)

    def kv_come(zs):
        @pl.when(z != zs)
        def _():
            remote(kv_send.at[0], kv_out.at[zs * rn + r], ks.at[0], kr.at[zs], s, t).wait_recv()
            for e in range(1, rn):
                side_copy(zs, e).start()

    def ready(zq):
        for e in range(1, rn):
            at = zq * rn + lax.rem(r + e, rn)
            remote(kv_out.at[at], kv_out.at[at], xs.at[0, 0], xr.at[at], s, t).wait_recv()
        for other in range(rn):
            sort_group(zq * rn + other)

        @pl.when(z != zq)
        def _():
            remote(q_send.at[0], q_out.at[zq], as_.at[0], ar.at[zq], s, t).wait_recv()

    kv_come(0)
    kv_come(1)
    pass_along(plan.outs, 2, start, True)
    for k in plan.early:
        hop(k, start)
    ready(0)
    attend_group(0)
    kv_come(2)
    kv_come(3)
    pass_along(plan.outs, 3, start, True)
    ready(1)
    attend_group(1)
    for d in range(2, ZN):
        pass_along(plan.sided, d, start, True)
    for k in plan.sided:
        settle(k, False)
        share(k, start, False)
    ready(2)
    attend_group(2)
    for k in plan.outs:
        @pl.when(r != plan.home(k)[1])
        def _():
            arrived(k)

    for w in range(len(plan.outs)):
        out_copy(w).start()
    ready(3)
    attend_group(3)
    for k in plan.early:
        hopped(k)
        zo, ro = plan.home(k)
        if zo > 0:
            @pl.when((r == ro) & (z == 0))
            def _():
                arrived(k)

    for k in plan.sided:
        shared(k)
    for w in range(len(plan.outs)):
        out_copy(w).wait()

    for k in plan.early:
        hop(k, done)
    for k in plan.sided:
        share(k, done)
    for i in range(3):
        q_own(i, done)
    q_line(done, False, True)
    owned(units, lambda k, src: along(k, src, done, False))
    owned(plan.late, lambda k, src: along(k, src, done, True))
    owned(units, lambda k, src: beside(k, src, done))
    for d in range(1, ZN):
        pass_along(units, d, done, False)

    @pl.when(s >= fm)
    def _():
        for d in range(1, n):
            m_copy(d).wait_send()

    for d in range(1, TP):
        t_copy(d).wait_send()
    for d in range(1, ZN):
        kv_copy(d).wait_send()
        a_copy(d).wait_send()
    for zs in range(ZN):
        for e in range(1, rn):
            side_copy(zs, e).wait_send()


def head_part(plan, meta, master, cond_units, tokens, cid):
    n, rn = plan.n, plan.r
    mrows = F_DEV * MCOLS
    rows = F_DEV * TOK_FRAME
    mods = n - plan.first_mod
    return call(
        functools.partial(head_kernel, plan),
        (
            jax.ShapeDtypeStruct((D, QKV), BF16),
            jax.ShapeDtypeStruct((len(plan.outs), plan.ub, D), BF16),
            jax.ShapeDtypeStruct((plan.late_ranks, plan.ub, D), BF16),
            jax.ShapeDtypeStruct((len(plan.early), plan.ub, D), BF16),
            jax.ShapeDtypeStruct((3, plan.ub, D), BF16),
            jax.ShapeDtypeStruct((rn - 1, plan.late_ranks, plan.ub, D), BF16),
            jax.ShapeDtypeStruct((HD, D), BF16),
            jax.ShapeDtypeStruct((F_DEV * 6, D), F32),
            jax.ShapeDtypeStruct((rows, D), BF16),
            jax.ShapeDtypeStruct((ZN, TOK_FRAME, LANES), BF16),
            jax.ShapeDtypeStruct((n, rows, LANES), BF16),
            jax.ShapeDtypeStruct((ZN, F_DEV, PACK, LANES), BF16),
            jax.ShapeDtypeStruct((ZN * F_DEV, HEAD, TOK_FRAME), F32),
            jax.ShapeDtypeStruct((ZN * F_DEV, 1, TOK_FRAME), F32),
        ),
        [
            pltpu.VMEM((3, plan.ub, D), BF16),
            pltpu.VMEM((n, 2, TOK_FRAME, LANES), BF16),
            pltpu.VMEM((2, n, LANES, TOK_FRAME), BF16),
            pltpu.VMEM((LANES, TOK_FRAME), BF16),
            pltpu.VMEM((1, TOK_FRAME), F32),
            pltpu.VMEM((1, TOK_FRAME), F32),
            pltpu.VMEM((LANES, TOK_FRAME), F32),
            pltpu.VMEM((plan.um, MT), BF16),
            pltpu.VMEM((plan.frames, MT), F32),
            pltpu.VMEM((n, mrows, LANES), F32),
            pltpu.VMEM((mods, mrows, LANES), F32),
            pltpu.VMEM((TP, mrows, LANES), F32),
            pltpu.VMEM((rows, D), F32),
            pltpu.VMEM((ZN, TOK_FRAME, LANES), BF16),
            pltpu.VMEM((ZN, rows, LANES), BF16),
            DMA((3 * CUTS, rn - 1)), DMA((2 * CUTS, rn)), DMA((CUTS * plan.nq,)),
            DMA((len(plan.outs), rn + 1)), DMA((len(plan.outs),)),
            DMA((plan.late_ranks, 2)), DMA((plan.late_ranks,)),
            DMA((plan.ranks, rn + 1)), DMA((len(plan.early),)), DMA((3,)),
            DMA((n - 1,)), DMA((mods,)), DMA((TP - 1,)), DMA((TP,)),
            DMA((ZN - 1,)), DMA((ZN,)), DMA((ZN - 1,)), DMA((ZN,)), DMA((ZN, rn - 1)), DMA((n,)),
            DMA((3,)), DMA((3,)), DMA((plan.late_ranks, rn - 1)), DMA((rn - 1, plan.late_ranks)),
            DMA((len(plan.outs),)), DMA((len(plan.outs),)),
        ],
        [SM] + [VM] * 3,
        cid,
        out_specs=(VM,) + (ANY,) * 6 + (VM,) * 7,
        name="head_part",
    )(meta, master, cond_units, tokens)


def padded(rows, low):
    zero = jnp.zeros_like(rows)
    return jnp.concatenate([rows, zero] if low else [zero, rows], axis=1)


def middle_kernel(
    plan, o_mine, wo_across, w_out, w_side, w_beside, w_early, w_below, tokens, grad_out, mod,
    result, late_own, late_send, esum, ebuf, do_out, dmid, dmod,
    gb, wb, eside, eend, wo, oall, attended, attn, mid, norm, inv, sin, hidden, dmlp, slopes, dup,
    own, csend, crecv, ysend, yrecv, dattn, dsend, dwo, wsend, wrecv,
    o_s, o_r, f_s, f_r, n_s, n_r, c_s, c_r, y_s, y_r, d_s, d_r, w_s, w_r, e_s, e_r, p_s, p_r, l_s, u_s, u_r, g_s, g_r, j_s, h_s, h_r, i_s, i_r,
):
    s, t, z, r = place(plan)
    rn = plan.r
    y = lax.div(t, 2)
    c = lax.rem(t, 2)
    sib = 2 * y + 1 - c
    across = lax.rem(t + 2, TP)
    mine = pl.multiple_of(c * TOK_FRAME, TOK_FRAME)
    theirs = pl.multiple_of((1 - c) * TOK_FRAME, TOK_FRAME)
    pairs = [(d, e) for d in range(ZN) for e in range(2)][1:]

    def partner(d, e):
        return lax.rem(z + d, ZN), (c if e == 0 else 1 - c)

    greet(
        [(partner(d, e)[0] * rn + r, 2 * y + partner(d, e)[1]) for d, e in pairs]
        + [(s, across)]
        + [(z * rn + lax.rem(r + d, rn), t) for d in range(1, rn)]
    )

    def home(k):
        return (k // 3) // rn, (k // 3) % rn, k - plan.half

    def w_rows(ref, k):
        return ref.at[pl.ds((k - plan.nq) * plan.ub, plan.ub)]

    def late_loads(act):
        for k in plan.late:
            sem = l_s.at[k - plan.nq]
            if k in plan.outs:
                act(pltpu.make_async_copy(w_out.at[k - plan.nq], w_rows(wb, k), sem))
            else:
                zo, ro = plan.home(k)
                rank = plan.late_rank[k]

                @pl.when(r == ro)
                def _():
                    act(pltpu.make_async_copy(w_side.at[rank], w_rows(wb, k), sem))

                @pl.when(r != ro)
                def _():
                    d = lax.rem(r - ro + rn, rn)
                    act(pltpu.make_async_copy(w_beside.at[d - 1, rank], w_rows(wb, k), sem))

    def loads(act):
        for k in plan.early:
            zo, ro, at = home(k)

            @pl.when((z <= zo) & (r == ro))
            def _():
                act(pltpu.make_async_copy(w_early.at[at], w_rows(wb, k), l_s.at[len(plan.late) + at]))

            @pl.when((z == zo + 1) & (r == ro))
            def _():
                act(
                    pltpu.make_async_copy(
                        w_below.at[k % 3], w_rows(wb, k), l_s.at[len(plan.late) + at]
                    )
                )

    def rise(k, src, act):
        zo, ro, at = home(k)

        @pl.when((z < ZN - 1) & (z > zo))
        def _():
            act(remote(src, w_rows(wb, k), u_s.at[at, 0], u_r.at[at], s + rn, t))

        for d in range(1, rn):
            act(
                remote(
                    src, w_rows(wb, k), u_s.at[at, d], u_r.at[at],
                    z * rn + lax.rem(r + d, rn), t,
                )
            )

    def risen(k):
        remote(w_below.at[0], w_rows(wb, k), u_s.at[0, 0], u_r.at[k - plan.half], s, t).wait_recv()

    def rises(act, first, wait):
        for k in plan.early:
            zo, ro, at = home(k)
            if first:
                @pl.when((z == zo + 1) & (r == ro))
                def _():
                    rise(k, w_below.at[k % 3], act)

                @pl.when((z <= zo) & (r == ro))
                def _():
                    rise(k, w_early.at[at], act)

            else:
                @pl.when((z > zo + 1) & (r == ro))
                def _():
                    if wait:
                        risen(k)
                    rise(k, w_rows(wb, k), act)

    def o_copy(d, e):
        zd, cd = partner(d, e)
        return remote(
            o_mine.at[zd, cd], oall.at[y * 8 + c * ZN + z], o_s.at[2 * d + e],
            o_r.at[c * ZN + z], zd * rn + r, 2 * y + cd,
        )

    def f_copy(slot):
        ref = oall.at[y * 8 + slot]
        return remote(ref, ref, f_s.at[slot], f_r.at[slot], s, across)

    def p_copy(i, tp):
        ref = wo.at[pl.ds(pl.multiple_of(tp * HD, HD), HD)]
        return remote(ref, ref, p_s.at[i], p_r.at[i], s, sib)

    for d, e in pairs:
        o_copy(d, e).start()
    start = lambda copy: copy.start()
    rises(start, True, False)
    late_loads(start)
    loads(start)
    late_loads(lambda copy: copy.wait())
    wo[pl.ds(pl.multiple_of(t * HD, HD), HD), :] = wb[:HD, :]
    p_copy(0, t).start()
    wo[pl.ds(pl.multiple_of(across * HD, HD), HD), :] = wo_across[...]
    p_copy(1, across).start()
    oall[y * 8 + c * ZN + z] = o_mine[z, c]
    f_copy(c * ZN + z).start()

    def d_mlp(f):
        def body(at):
            rows = pl.ds(f * TOK_FRAME + at, 64)
            dmlp[rows, :] = (grad_out[rows, :].astype(F32) * mod[f * 6 + 5 : f * 6 + 6, :]).astype(
                BF16
            )

        loop(TOK_FRAME, 64, body)

    for f in range(F_DEV):
        d_mlp(f)

    for d, e in pairs:
        zd, cd = partner(d, e)
        slot = cd * ZN + zd
        remote(o_mine.at[0, 0], oall.at[y * 8 + slot], o_s.at[0], o_r.at[slot], s, t).wait_recv()
        f_copy(slot).start()
    for slot in range(8):
        remote(
            oall.at[0], oall.at[(1 - y) * 8 + slot], f_s.at[slot], f_r.at[slot], s, t
        ).wait_recv()
    for m in range(HEADS // 2):
        a, b = oall[2 * m], oall[2 * m + 1]
        cols = slice(m * LANES, (m + 1) * LANES)
        attended[:PACK, cols] = jnp.concatenate([a[:, :HEAD], b[:, :HEAD]], axis=1)
        attended[PACK:, cols] = jnp.concatenate([a[:, HEAD:], b[:, HEAD:]], axis=1)

    p_copy(0, sib).wait_recv()
    p_copy(1, lax.rem(sib + 2, TP)).wait_recv()

    def attn_tile(at):
        attn[:, pl.ds(at, TILE)] = mm(attended[...], wo[:, pl.ds(at, TILE)])

    loop(D, TILE, attn_tile)
    rises(start, False, True)

    row = lambda part: mod[pl.ds(c * 6 + part, 1), :]

    def norm_rows(at):
        rows = pl.ds(at, 64)
        values = tokens[pl.ds(mine + at, 64), :].astype(F32) + row(2) * attn[rows, :]
        mid[rows, :] = values
        normed, inverse = normalize(values)
        norm[rows, :] = normed
        inv[rows, :] = inverse
        sin[pl.ds(mine + at, 64), :] = (normed * (1.0 + row(4)) + row(3)).astype(BF16)

    loop(TOK_FRAME, 64, norm_rows)

    def n_copy(base):
        ref = sin.at[pl.ds(base, TOK_FRAME)]
        return remote(ref, ref, n_s.at[0], n_r.at[0], s, sib)

    n_copy(mine).start()
    loads(lambda copy: copy.wait())
    for k in plan.early:
        zo, ro, at = home(k)

        @pl.when(r != ro)
        def _():
            risen(k)

    def feed(base):
        rows = pl.ds(base, TOK_FRAME)

        def tile(at):
            cols = pl.ds(at, TILE)
            u = mm(sin[rows, :], wb[HD : HD + FT, cols])
            square = u * u
            inner = GELU_A * u * (1.0 + GELU_B * square)
            th = jnp.tanh(inner)
            half = 0.5 * (1.0 + th)
            hidden[rows, cols] = (u * half).astype(BF16)
            slopes[rows, cols] = half + 0.5 * u * (1.0 - th * th) * (
                GELU_A * (1.0 + 3.0 * GELU_B * square)
            )

        loop(FT, TILE, tile)

    feed(mine)
    n_copy(theirs).wait_recv()
    feed(theirs)

    def d_up(at):
        cols = pl.ds(at, TILE)
        dup[:, cols] = (mm_nt(dmlp[...], wb[pl.ds(HD + FT + at, TILE), :]) * slopes[:, cols]).astype(
            BF16
        )

    loop(FT, TILE, d_up)

    def c_copy(w, n):
        return remote(csend.at[w, n], crecv.at[w, n], c_s.at[w, n], c_r.at[w, n], s, sib)

    def y_copy(w, n):
        return remote(ysend.at[w, n], yrecv.at[w, n], y_s.at[w, n], y_r.at[w, n], s, across)

    def pass_on(w, n):
        c_copy(w, n).wait_recv()
        ysend[w, n] = (own[n] + crecv[w, n].astype(F32)).astype(BF16)
        y_copy(w, n).start()

    def product(w, base, n):
        rows = pl.ds(base, TOK_FRAME)
        if w == 0:
            return mm_nt(dup[rows, :], wb[HD + n * TILE : HD + (n + 1) * TILE, :])
        return mm(hidden[rows, :], wb[HD + FT :, n * TILE : (n + 1) * TILE])

    def products(w):
        for n in range(TILES):
            csend[w, n] = product(w, theirs, n).astype(BF16)
            c_copy(w, n).start()
            own[n] = product(w, mine, n)
            if n:
                pass_on(w, n - 1)
        pass_on(w, TILES - 1)

    def down_grad(at):
        gb[pl.ds(HD + FT + at, TILE), :] = mm_tn(hidden[:, pl.ds(at, TILE)], dmlp[...]).astype(BF16)

    def up_grad(at):
        gb[pl.ds(HD + at, TILE), :] = mm_tn(sin[:, pl.ds(at, TILE)], dup[...]).astype(BF16)

    def early_grad(k, d):
        zo, ro, at = home(k)
        slot = lax.rem(ro - r + rn, rn) - 1 if d is None else d - 1
        return remote(
            w_rows(gb, k), eside.at[slot, plan.rank[k]], g_s.at[at], g_r.at[slot, plan.rank[k]],
            z * rn + ro, t,
        )

    def early_grads(act):
        for k in plan.early:
            zo, ro, at = home(k)

            @pl.when(r != ro)
            def _():
                act(early_grad(k, None))

    def early_hop(rank, act):
        for here, to in ((ZN - 1, s - rn), (0, s + rn)):
            @pl.when(z == here)
            def _():
                act(remote(esum.at[rank], eend.at[rank], h_s.at[rank], h_r.at[rank], to, t))

    def early_total(rank):
        for k in plan.early:
            if plan.rank[k] == rank:
                zo, ro, at = home(k)

                @pl.when(r == ro)
                def _():
                    for d in range(1, rn):
                        early_grad(k, d).wait_recv()

                    def body(at):
                        rows = pl.ds(at, 16)
                        total = gb[pl.ds((k - plan.nq) * plan.ub + at, 16), :].astype(F32)
                        for d in range(1, rn):
                            total = total + eside[d - 1, rank, rows, :].astype(F32)
                        esum[rank, rows, :] = total.astype(BF16)

                    loop(plan.ub, 16, body)
                    early_hop(rank, start)

    def early_pass(rank, to):
        return remote(esum.at[rank], ebuf.at[rank], i_s.at[rank], i_r.at[rank], to, t)

    def early_inner(rank):
        for k in plan.early:
            if plan.rank[k] == rank:
                zo, ro, at = home(k)

                @pl.when((r == ro) & (z > 0) & (z < ZN - 1))
                def _():
                    remote(
                        esum.at[rank], eend.at[rank], h_s.at[rank], h_r.at[rank], s, t
                    ).wait_recv()

                    def body(at):
                        rows = pl.ds(at, 16)
                        esum[rank, rows, :] = (
                            esum[rank, rows, :].astype(F32) + eend[rank, rows, :].astype(F32)
                        ).astype(BF16)

                    loop(plan.ub, 16, body)

                    @pl.when(z != zo)
                    def _():
                        early_pass(rank, s + rn if zo == 2 else s - rn).start()

    def early_close(rank):
        for k in plan.early:
            if plan.rank[k] == rank:
                zo, ro, at = home(k)

                @pl.when((r == ro) & (z == zo))
                def _():
                    early_pass(rank, s).wait_recv()

                @pl.when((r == ro) & (z == 3 - zo))
                def _():
                    early_pass(rank, s).wait_send()

    def early_hops_done(rank):
        for k in plan.early:
            if plan.rank[k] == rank:
                @pl.when(r == home(k)[1])
                def _():
                    early_hop(rank, lambda copy: copy.wait_send())

    loop(FT, TILE, down_grad)
    up_grad(D - TILE)
    early_grads(start)
    products(0)
    products(1)
    loop(D - TILE, TILE, up_grad)
    early_total(0)
    early_total(1)
    early_inner(0)

    dm = dmod
    dm[...] = jnp.zeros_like(dm)
    for n in range(TILES):
        y_copy(0, n).wait_recv()

    def total(w, rows):
        return jnp.concatenate(
            [ysend[w, n, rows].astype(F32) + yrecv[w, n, rows].astype(F32) for n in range(TILES)],
            axis=1,
        )

    def back_rows(at):
        rows = pl.ds(at, 64)
        tok_rows = pl.ds(mine + at, 64)
        grads = total(0, rows)
        normed = norm[rows, :]
        add_to(dm, 1, grads)
        add_to(dm, 2, grads * normed)
        values = grad_out[tok_rows, :].astype(F32) + norm_back(
            grads * (1.0 + row(4)), normed, inv[rows, :]
        )
        dmid[rows, :] = values
        add_to(dm, 0, attn[rows, :] * values)
        dattn[rows, :] = (row(2) * values).astype(BF16)

    loop(TOK_FRAME, 64, back_rows)
    for ch in range(2):
        part = mm_nt(dattn[...], wo[pl.ds(pl.multiple_of((2 * y + ch) * HD, HD), HD), :]).astype(BF16)
        for zh in range(ZN):
            cols = slice(zh * HEAD, (zh + 1) * HEAD)
            dsend[ch * ZN + zh] = jnp.concatenate([part[:PACK, cols], part[PACK:, cols]], axis=1)

    def d_copy(d, e):
        zd, cd = partner(d, e)
        return remote(
            dsend.at[cd * ZN + zd], do_out.at[z, c], d_s.at[2 * d + e], d_r.at[2 * z + c],
            zd * rn + r, 2 * y + cd,
        )

    for d, e in pairs:
        d_copy(d, e).start()
    do_out[z, c] = dsend[c * ZN + z]
    for rank in range(2, plan.ranks):
        early_total(rank)

    def o_grad(head_core):
        cols = pl.ds(pl.multiple_of((2 * y + head_core) * HD, HD), HD)
        return mm_tn(attended[:, cols], dattn[...])

    w_copy = remote(wsend, wrecv, w_s, w_r, s, sib)
    wsend[...] = o_grad(1 - c).astype(BF16)
    w_copy.start()
    dwo[...] = o_grad(c)
    early_inner(1)

    for n in range(TILES):
        y_copy(1, n).wait_recv()

    def result_rows(at):
        rows = pl.ds(at, 64)
        tok_rows = pl.ds(mine + at, 64)
        mlp = total(1, rows)
        add_to(dm, 3, mlp * grad_out[tok_rows, :].astype(F32))
        result[tok_rows, :] = (mid[rows, :] + row(5) * mlp).astype(BF16)

    loop(TOK_FRAME, 64, result_rows)

    def e_copy(base):
        ref = result.at[pl.ds(base, TOK_FRAME)]
        return remote(ref, ref, e_s, e_r, s, sib)

    e_copy(mine).start()
    for rank in range(2, plan.ranks):
        early_inner(rank)
    w_copy.wait_recv()
    gb[:HD, :] = (dwo[...] + wrecv[...].astype(F32)).astype(BF16)

    for d, e in pairs:
        zd, cd = partner(d, e)
        remote(
            dsend.at[0], do_out.at[zd, cd], d_s.at[0], d_r.at[2 * zd + cd], s, t
        ).wait_recv()
    def late_grads(act):
        for k in plan.late:
            zo, ro = plan.home(k)
            rank, sem = plan.grad_rank[k], j_s.at[k - plan.nq]

            @pl.when(r == ro)
            def _():
                act(pltpu.make_async_copy(w_rows(gb, k), late_own.at[rank], sem))

            @pl.when(r != ro)
            def _():
                d = lax.rem(ro - r + rn, rn)
                act(pltpu.make_async_copy(w_rows(gb, k), late_send.at[d - 1, rank], sem))

    late_grads(start)
    for rank in range(plan.ranks):
        early_close(rank)
    e_copy(theirs).wait_recv()
    done = lambda copy: copy.wait_send()
    early_grads(done)
    for rank in range(plan.ranks):
        early_hops_done(rank)
    late_grads(lambda copy: copy.wait())
    rises(done, True, False)
    rises(done, False, False)
    for d, e in pairs:
        o_copy(d, e).wait_send()
        d_copy(d, e).wait_send()
    for slot in range(8):
        f_copy(slot).wait_send()
    n_copy(mine).wait_send()
    p_copy(0, t).wait_send()
    p_copy(1, across).wait_send()
    for w in range(2):
        for n in range(TILES):
            c_copy(w, n).wait_send()
            y_copy(w, n).wait_send()
    w_copy.wait_send()
    e_copy(mine).wait_send()


def middle_part(plan, o_mine, wo_across, weights, tokens, grad_out, mod_rows, cid):
    rn, count = plan.r, len(plan.early)
    rows = F_DEV * TOK_FRAME
    half = lambda dtype: pltpu.VMEM((TOK_FRAME, D), dtype)
    full = lambda dtype: pltpu.VMEM((rows, D), dtype)
    tiles = pltpu.VMEM((2, TILES, TOK_FRAME, TILE), BF16)
    return call(
        functools.partial(middle_kernel, plan),
        (
            jax.ShapeDtypeStruct((rows, D), BF16),
            jax.ShapeDtypeStruct((plan.grad_ranks, plan.ub, D), BF16),
            jax.ShapeDtypeStruct((rn - 1, plan.grad_ranks, plan.ub, D), BF16),
            jax.ShapeDtypeStruct((plan.ranks, plan.ub, D), BF16),
            jax.ShapeDtypeStruct((plan.ranks, plan.ub, D), BF16),
            jax.ShapeDtypeStruct((ZN, F_DEV, PACK, LANES), BF16),
            jax.ShapeDtypeStruct((TOK_FRAME, D), F32),
            jax.ShapeDtypeStruct((8, D), F32),
        ),
        [
            pltpu.VMEM((BROWS, D), BF16),
            pltpu.VMEM((BROWS, D), BF16),
            pltpu.VMEM((rn - 1, plan.ranks, plan.ub, D), BF16),
            pltpu.VMEM((plan.ranks, plan.ub, D), BF16),
            pltpu.VMEM((HEADS * HEAD, D), BF16),
            pltpu.VMEM((HEADS, PACK, LANES), BF16),
            half(BF16), half(F32), half(F32), half(F32), pltpu.VMEM((TOK_FRAME, 1), F32),
            full(BF16), full(BF16), full(BF16), full(F32), full(BF16),
            pltpu.VMEM((TILES, TOK_FRAME, TILE), F32), tiles, tiles, tiles, tiles,
            half(BF16), pltpu.VMEM((8, PACK, LANES), BF16),
            pltpu.VMEM((HD, D), F32), pltpu.VMEM((HD, D), BF16), pltpu.VMEM((HD, D), BF16),
            DMA((8,)), DMA((8,)), DMA((8,)), DMA((8,)), DMA((1,)), DMA((1,)),
            DMA((2, TILES)), DMA((2, TILES)), DMA((2, TILES)), DMA((2, TILES)),
            DMA((8,)), DMA((8,)), DMA, DMA, DMA, DMA, DMA((2,)), DMA((2,)),
            DMA((len(plan.late) + count,)), DMA((count, rn)), DMA((count,)), DMA((count,)), DMA((rn - 1, plan.ranks)),
            DMA((len(plan.late),)), DMA((plan.ranks,)), DMA((plan.ranks,)),
            DMA((plan.ranks,)), DMA((plan.ranks,)),
        ],
        [VM, VM, ANY, ANY, ANY, ANY, ANY, VM, VM, VM],
        cid,
        out_specs=(VM, ANY, ANY, VM, VM, VM, VM, VM),
        name="middle_part",
    )(o_mine, wo_across, *weights, tokens, grad_out, mod_rows)


def tail_kernel(
    plan, meta, q, kv, do, ot, lse, first_in, wq, tokens, dmid, mod, dm4, late_own, late_send, esum, ebuf,
    igrad, oq, ob, dall,
    keys, flipped, qs, gs, qgt, drow, acc, dq_acc, dq, kv_two, lside,
    stage, side, q_in, kv_in, dqkv, gq, own, csend, crecv, ysend, yrecv, dm, dm3, dboth,
    lstage, cb, qside, qpeer, qchain, qstage,
    q_s, q_r, k_s, k_r, x_s, x_r, c_s, c_r, y_s, y_r, e_s, e_r, h_s, h_r, m_s, m_r, t_s, t_r,
    kv_s, ls_s, ls_r, qo_s, qs_r, qp_r, qc_s, qc_r,
):
    s, t, z, r = place(plan)
    n, rn = plan.n, plan.r
    y = lax.div(t, 2)
    c = lax.rem(t, 2)
    sib = 2 * y + 1 - c
    across = lax.rem(t + 2, TP)
    mine = pl.multiple_of(c * TOK_FRAME, TOK_FRAME)
    theirs = pl.multiple_of((1 - c) * TOK_FRAME, TOK_FRAME)
    greet([(lax.rem(s + d, n), t) for d in range(1, n)] + [(s, sib), (s, across)])

    def side_copy(zs, e):
        other = lax.rem(r + e, rn)
        return remote(
            keys.at[zs * rn + other], side.at[e - 1, zs], x_s.at[zs, e - 1], x_r.at[zs, e - 1],
            z * rn + other, t,
        )

    def q_copy(zs):
        return remote(dq.at[zs], q_in.at[z], q_s.at[zs], q_r.at[z], zs * rn + r, t)

    def kv_copy(zs):
        return remote(stage.at[zs], kv_in.at[z], k_s.at[zs], k_r.at[z], zs * rn + r, t)

    def send_q(zs):
        @pl.when(z == zs)
        def _():
            q_in[zs] = dq[zs]

        @pl.when(z != zs)
        def _():
            q_copy(zs).start()

    def send_kv(zs):
        total = keys[zs * rn + r].astype(F32)
        for e in range(1, rn):
            side_copy(zs, e).wait_recv()
            total = total + side[e - 1, zs].astype(F32)
        stage[zs] = total.astype(BF16)

        @pl.when(z == zs)
        def _():
            kv_in[zs] = stage[zs]

        @pl.when(z != zs)
        def _():
            kv_copy(zs).start()

    scale = HEAD ** (-0.5)
    acc[...] = jnp.zeros_like(acc)

    def load(g, slot):
        return pltpu.make_async_copy(kv.at[g], kv_two.at[slot], kv_s.at[slot])

    load(0, 0).start()

    def sort_group(g, carry):
        slot = lax.rem(g, 2)

        @pl.when(g + 1 < n)
        def _():
            load(g + 1, 1 - slot).start()

        load(g, slot).wait()
        first = meta[2 * g] == 0
        a, b = kv_two[slot, :TOK_FRAME, :], kv_two[slot, TOK_FRAME:, :]
        keys[g, 0] = jnp.where(first, a, b)
        keys[g, 1] = jnp.where(first, b, a)
        for kind in range(2):
            flipped[kind, g] = keys[g, kind].T
        return carry

    lax.fori_loop(0, n, sort_group, 0)

    def attend_back_group(zq):
        gq = zq * rn + r
        first = meta[2 * gq] == 0
        clip = meta[2 * gq] + meta[2 * gq + 1]
        parts = []
        for kind in range(2):
            low = first if kind == 0 else jnp.logical_not(first)
            qz = padded(jnp.where(low, q[zq][:, :HEAD], q[zq][:, HEAD:]), True) * jnp.asarray(scale, BF16)
            gpack = jnp.where(low, do[zq, 0], do[zq, 1])
            grads = jnp.concatenate([gpack[:, :HEAD], gpack[:, HEAD:]], axis=0)
            out = ot[2 * zq + kind]
            logs = lse[2 * zq + kind]
            gz = padded(grads, False)
            qs[...] = qz
            gs[...] = gz
            qgt[:, :TOK_FRAME] = qz.T
            qgt[:, TOK_FRAME:] = gz.T
            drow[...] = jnp.sum(grads.astype(F32).T * out, axis=0, keepdims=True)
            dq_acc[...] = jnp.zeros_like(dq_acc)

            def block(p, inner):
                total = dq_acc[...]
                for e in range(2):
                    g = jnp.minimum(2 * p + e, gq)
                    shown = 2 * p + e <= gq
                    if kind == 1:
                        shown = shown & (meta[2 * g] + meta[2 * g + 1] == clip)
                    off = jnp.where(shown, 0.0, 1e30)
                    key = keys[g, kind]
                    pt = jnp.exp(mm(key, qgt[:, :TOK_FRAME]) - (logs + off))
                    dst = (pt * (mm(key, qgt[:, TOK_FRAME:]) - drow[...])).astype(BF16)
                    acc[kind, g] += mm(dst, qs[...]) + mm(pt.astype(BF16), gs[...])
                    total = total + mm(flipped[kind, g], dst)
                dq_acc[...] = total
                return inner

            lax.fori_loop(0, lax.div(gq + 2, 2), block, 0)
            parts.append((dq_acc[:HEAD, :] * scale).T.astype(BF16))
        dq[zq] = jnp.concatenate(
            [jnp.where(first, parts[0], parts[1]), jnp.where(first, parts[1], parts[0])], axis=1
        )
        for other in range(rn):
            g = zq * rn + other
            low = meta[2 * g] == 0
            a, b = acc[0, g].astype(BF16), acc[1, g].astype(BF16)
            keys[g, 0] = jnp.where(low, a, b)
            keys[g, 1] = jnp.where(low, b, a)

    def late(units, act):
        for k in units:
            zo, ro = plan.home(k)

            @pl.when(r == ro)
            def _():
                act(k, zo, plan.grad_rank[k])

    def late_copy(rank, below, to):
        return remote(lstage.at[rank], cb.at[below, rank], t_s.at[rank], t_r.at[below, rank], to, t)

    def late_side(rank, d):
        return remote(
            late_send.at[d - 1, rank], lside.at[d - 1, rank], ls_s.at[rank, d - 1],
            ls_r.at[rank, d - 1], z * rn + lax.rem(r + d, rn), t,
        )

    def late_sides(rank, act):
        for d in range(1, rn):
            act(late_side(rank, d))

    def late_step(k, zo, rank, here_z, above, below, final):
        @pl.when(z == here_z)
        def _():
            for d in range(1, rn):
                late_side(rank, d).wait_recv()
            if above:
                late_copy(rank, 0, s).wait_recv()
            if below:
                late_copy(rank, 1, s).wait_recv()

            def body(at):
                rows = pl.ds(at, 16)
                total = late_own[rank, rows, :].astype(F32)
                for d in range(1, rn):
                    total = total + lside[d - 1, rank, rows, :].astype(F32)
                if above:
                    total = total + cb[0, rank, rows, :].astype(F32)
                if below:
                    total = total + cb[1, rank, rows, :].astype(F32)
                if final:
                    ob[k % 3, rows, :] = total
                else:
                    lstage[rank, rows, :] = total.astype(BF16)

            loop(plan.ub, 16, body)
            if not final:
                late_copy(
                    rank, 0 if here_z > zo else 1, s - rn if here_z > zo else s + rn
                ).start()

    def late_ends(k, zo, rank):
        late_step(k, zo, rank, ZN - 1, False, False, False)
        if zo > 0:
            late_step(k, zo, rank, 0, False, False, False)

    def late_inner(here):
        def act(k, zo, rank):
            if here > zo:
                late_step(k, zo, rank, here, True, False, False)

        return act

    def late_final(k, zo, rank):
        late_step(k, zo, rank, zo, True, zo > 0, True)

    def late_done(k, zo, rank):
        @pl.when(z != zo)
        def _():
            late_copy(rank, 0, s).wait_send()

    def early_units(act):
        for k in plan.early:
            zo, ro, rank = (k // 3) // rn, (k // 3) % rn, plan.rank[k]

            @pl.when(r == ro)
            def _():
                act(k, zo, rank)

    def early_final(k, zo, rank):
        @pl.when(z == zo)
        def _():
            def body(at):
                rows = pl.ds(at, 16)
                ob[k % 3, rows, :] = esum[rank, rows, :].astype(F32) + ebuf[rank, rows, :].astype(F32)

            loop(plan.ub, 16, body)

    hq = plan.uq // CUTS

    def q_rows(k, h):
        return gq.at[pl.ds(pl.multiple_of(k * plan.uq + h * hq, hq), hq)]

    def q_sides(k, act):
        tc, ro, j = k % rn, k // 3, k // rn
        for h in range(CUTS):
            @pl.when((z > 0) & (r != tc))
            def _():
                slot = lax.rem(tc - r + rn, rn) - 1
                act(
                    remote(
                        q_rows(k, h), qside.at[slot, CUTS * j + h], qo_s.at[CUTS * k + h],
                        qs_r.at[slot, CUTS * j + h], z * rn + tc, t,
                    )
                )

            @pl.when((z == 0) & (r != ro) & (r != tc))
            def _():
                slot = lax.rem(ro - r + rn, rn) - 1
                act(
                    remote(
                        q_rows(k, h), qpeer.at[slot, CUTS * (k % 3) + h], qo_s.at[CUTS * k + h],
                        qp_r.at[slot, CUTS * (k % 3) + h], ro, t,
                    )
                )

    def q_down(at, to):
        return remote(qstage.at[at], qchain.at[at], qc_s.at[at], qc_r.at[at], to, t)

    def q_chain(here, only_j):
        top = here == ZN - 1
        for j in (only_j,):
            k = r + rn * j
            for h in range(CUTS):
                at = CUTS * j + h

                @pl.when(z == here)
                def _():
                    for d in range(1, rn):
                        remote(
                            q_rows(k, h), qside.at[d - 1, at], qo_s.at[0], qs_r.at[d - 1, at], s, t
                        ).wait_recv()
                    if not top:
                        q_down(at, s).wait_recv()
                    unit = q_rows(k, h)

                    def body(row):
                        rows = pl.ds(row, 16)
                        total = unit[rows, :].astype(F32)
                        for d in range(1, rn):
                            total = total + qside[d - 1, at, rows, :].astype(F32)
                        if not top:
                            total = total + qchain[at, rows, :].astype(F32)
                        qstage[at, rows, :] = total.astype(BF16)

                    loop(hq, 16, body)
                    q_down(at, s - rn).start()

    def q_last_copy(k, h):
        tc, ro, j = k % rn, k // 3, k // rn
        slot = (ro - tc + rn) % rn - 1
        return remote(
            qstage.at[CUTS * j + h], qpeer.at[slot, CUTS * (k % 3) + h], qc_s.at[CUTS * j + h],
            qp_r.at[slot, CUTS * (k % 3) + h], ro, t,
        )

    def q_ground(act):
        for k in range(plan.nq):
            if k % rn != k // 3:
                @pl.when((z == 0) & (r == k % rn))
                def _():
                    for h in range(CUTS):
                        act(k, h)

    def q_turn(k, h):
        at = CUTS * (k // rn) + h
        q_down(at, s).wait_recv()
        unit = q_rows(k, h)

        def body(row):
            rows = pl.ds(row, 16)
            qstage[at, rows, :] = (
                unit[rows, :].astype(F32) + qchain[at, rows, :].astype(F32)
            ).astype(BF16)

        loop(hq, 16, body)
        q_last_copy(k, h).start()

    def q_final():
        for k in range(plan.nq):
            @pl.when((z == 0) & (r == k // 3))
            def _():
                straight = k % rn == k // 3
                for h in range(CUTS):
                    at = CUTS * (k // rn) + h
                    if straight:
                        q_down(at, s).wait_recv()
                    for d in range(1, rn):
                        remote(
                            q_rows(k, h), qpeer.at[d - 1, CUTS * (k % 3) + h], qo_s.at[0],
                            qp_r.at[d - 1, CUTS * (k % 3) + h], s, t,
                        ).wait_recv()
                    unit = q_rows(k, h)

                    def body(row):
                        rows = pl.ds(row, 16)
                        total = unit[rows, :].astype(F32)
                        for d in range(1, rn):
                            total = total + qpeer[d - 1, CUTS * (k % 3) + h, rows, :].astype(F32)
                        if straight:
                            total = total + qchain[at, rows, :].astype(F32)
                        oq[k % 3, pl.ds(h * hq + row, 16), :] = total

                    loop(hq, 16, body)

    start = lambda copy: copy.start()
    done = lambda copy: copy.wait_send()
    def only(rank, act):
        return lambda k, zo, own_rank: act(k, zo, own_rank) if own_rank == rank else None

    last = plan.grad_ranks - 1
    late_sides(0, start)
    for zq in range(ZN - 1, -1, -1):
        attend_back_group(zq)
        for e in range(1, rn):
            side_copy(zq, e).start()
        send_q(zq)
        if zq == ZN - 1:
            late(plan.late, only(0, late_ends))
        else:
            send_kv(zq + 1)
    for rank in range(1, plan.grad_ranks):
        late_sides(rank, start)
    send_kv(0)
    late(plan.late, only(0, late_inner(2)))
    late(plan.late, only(0, late_inner(1)))
    late(plan.late, only(1, late_ends))
    for zs in range(ZN):
        @pl.when(z != zs)
        def _():
            remote(dq.at[0], q_in.at[zs], q_s.at[0], q_r.at[zs], s, t).wait_recv()
            remote(stage.at[0], kv_in.at[zs], k_s.at[0], k_r.at[zs], s, t).wait_recv()

    for p in range(2):
        cols = slice(p * LANES, (p + 1) * LANES)
        a, b = q_in[2 * p], q_in[2 * p + 1]
        dqkv[:TOK_FRAME, cols] = jnp.concatenate([a[:, :HEAD], b[:, :HEAD]], axis=1)
        dqkv[TOK_FRAME:, cols] = jnp.concatenate([a[:, HEAD:], b[:, HEAD:]], axis=1)
        a, b = [kv_in[2 * p + i].reshape(F_DEV * TOK_FRAME, LANES) for i in range(2)]
        dqkv[:, HD + p * LANES : HD + (p + 1) * LANES] = jnp.concatenate(
            [a[:, :HEAD], b[:, :HEAD]], axis=1
        )
        dqkv[:, 2 * HD + p * LANES : 2 * HD + (p + 1) * LANES] = jnp.concatenate(
            [a[:, HEAD:], b[:, HEAD:]], axis=1
        )

    for m in range(TILES):
        gq[m * TILE : (m + 1) * TILE, :] = mm_tn(
            first_in[:, m * TILE : (m + 1) * TILE], dqkv[...]
        ).astype(BF16)
        for k in range(m * plan.nq // TILES, (m + 1) * plan.nq // TILES):
            q_sides(k, start)

    def c_copy(w):
        return remote(csend.at[w], crecv.at[w], c_s.at[w], c_r.at[w], s, sib)

    def y_copy(w):
        return remote(ysend.at[w], yrecv.at[w], y_s.at[w], y_r.at[w], s, across)

    def pass_on(w):
        c_copy(w).wait_recv()
        ysend[w] = (own[w] + crecv[w].astype(F32)).astype(BF16)
        y_copy(w).start()

    for w in range(TILES):
        weights = wq[w * TILE : (w + 1) * TILE, :]
        csend[w] = mm_nt(dqkv[pl.ds(theirs, TOK_FRAME), :], weights).astype(BF16)
        c_copy(w).start()
        own[w] = mm_nt(dqkv[pl.ds(mine, TOK_FRAME), :], weights)
        if w:
            pass_on(w - 1)
    pass_on(TILES - 1)

    for rank in range(2, plan.grad_ranks):
        late(plan.late, only(rank, late_ends))
    q_chain(ZN - 1, 0)
    q_chain(ZN - 1, 1)
    late(plan.late, only(1, late_inner(2)))
    q_chain(2, 0)
    late(plan.late, only(last, late_inner(2)))
    q_chain(2, 1)
    q_chain(1, 0)
    late(plan.late, only(1, late_inner(1)))
    q_chain(1, 1)
    late(plan.late, only(last, late_inner(1)))

    for w in range(TILES):
        y_copy(w).wait_recv()
    row = lambda part: mod[pl.ds(c * 6 + part, 1), :]
    dm[...] = jnp.zeros_like(dm)

    def input_rows(at):
        rows = pl.ds(at, 64)
        tok_rows = pl.ds(mine + at, 64)
        grads = jnp.concatenate(
            [ysend[w, rows].astype(F32) + yrecv[w, rows].astype(F32) for w in range(TILES)], axis=1
        )
        normed, inverse = normalize(tokens[tok_rows, :].astype(F32))
        add_to(dm, 0, grads)
        add_to(dm, 1, grads * normed)
        igrad[tok_rows, :] = dmid[rows, :] + norm_back(grads * (1.0 + row(1)), normed, inverse)

    loop(TOK_FRAME, 64, input_rows)

    def e_copy(base):
        ref = igrad.at[pl.ds(base, TOK_FRAME)]
        return remote(ref, ref, e_s, e_r, s, sib)

    e_copy(mine).start()

    for block in range(6 * D // LANES):
        part, at = block // (D // LANES), block % (D // LANES)
        src = dm if part < 2 else dm4
        lane = slice(at * LANES, (at + 1) * LANES)
        from_row = part if part < 2 else part - 2
        dm3[block // MCOLS, block % MCOLS : block % MCOLS + 1, :] = src[from_row : from_row + 1, lane]
    h_copy = lambda frame: remote(dm3.at[sib], dboth.at[frame], h_s, h_r, s, sib)
    h_copy(c).start()
    dboth[c] = dm3[t]
    h_copy(1 - c).wait_recv()

    def m_copy(src):
        return remote(dboth, dall.at[s], m_s.at[src - plan.first_mod], m_r.at[s], src, t)

    for src in range(plan.first_mod, n):
        @pl.when(s == src)
        def _():
            dall[s] = dboth[...]

        @pl.when(s != src)
        def _():
            m_copy(src).start()

    q_ground(q_turn)
    late(plan.late, late_final)
    early_units(early_final)
    q_final()

    @pl.when(s >= plan.first_mod)
    def _():
        for d in range(1, n):
            other = lax.rem(s + d, n)
            remote(dboth, dall.at[other], m_s.at[0], m_r.at[other], s, t).wait_recv()

    e_copy(theirs).wait_recv()
    for zs in range(ZN):
        @pl.when(z != zs)
        def _():
            q_copy(zs).wait_send()
            kv_copy(zs).wait_send()

        for e in range(1, rn):
            side_copy(zs, e).wait_send()
    for rank in range(plan.grad_ranks):
        late_sides(rank, done)
    late(plan.late, late_done)
    for k in range(plan.nq):
        q_sides(k, done)

    @pl.when(z > 0)
    def _():
        for at in range(2 * CUTS):
            q_down(at, s).wait_send()

    q_ground(lambda k, h: q_last_copy(k, h).wait_send())
    for w in range(TILES):
        c_copy(w).wait_send()
        y_copy(w).wait_send()
    e_copy(mine).wait_send()
    h_copy(c).wait_send()
    for src in range(plan.first_mod, n):
        @pl.when(s != src)
        def _():
            m_copy(src).wait_send()


def tail_part(plan, meta, q, kv, do, ot, lse, first_in, wq, tokens, dmid, mod_rows, dm4, late_own, late_send, esum, ebuf, cid):
    n, rn = plan.n, plan.r
    rows = F_DEV * TOK_FRAME
    tiles = pltpu.VMEM((TILES, TOK_FRAME, TILE), BF16)
    mods = n - plan.first_mod
    return call(
        functools.partial(tail_kernel, plan),
        (
            jax.ShapeDtypeStruct((rows, D), F32),
            jax.ShapeDtypeStruct((3, plan.uq, QKV), F32),
            jax.ShapeDtypeStruct((3, plan.ub, D), F32),
            jax.ShapeDtypeStruct((n, F_DEV, 16, LANES), F32),
        ),
        [
            pltpu.VMEM((n, 2, TOK_FRAME, LANES), BF16),
            pltpu.VMEM((2, n, LANES, TOK_FRAME), BF16),
            pltpu.VMEM((TOK_FRAME, LANES), BF16),
            pltpu.VMEM((TOK_FRAME, LANES), BF16),
            pltpu.VMEM((LANES, 2 * TOK_FRAME), BF16),
            pltpu.VMEM((1, TOK_FRAME), F32),
            pltpu.VMEM((2, n, TOK_FRAME, LANES), F32),
            pltpu.VMEM((LANES, TOK_FRAME), F32),
            pltpu.VMEM((ZN, TOK_FRAME, LANES), BF16),
            pltpu.VMEM((2, rows, LANES), BF16),
            pltpu.VMEM((rn - 1, plan.grad_ranks, plan.ub, D), BF16),
            pltpu.VMEM((ZN, 2, TOK_FRAME, LANES), BF16),
            pltpu.VMEM((rn - 1, ZN, 2, TOK_FRAME, LANES), BF16),
            pltpu.VMEM((ZN, TOK_FRAME, LANES), BF16),
            pltpu.VMEM((ZN, 2, TOK_FRAME, LANES), BF16),
            pltpu.VMEM((rows, QKV), BF16),
            pltpu.VMEM((D, QKV), BF16),
            pltpu.VMEM((TILES, TOK_FRAME, TILE), F32), tiles, tiles, tiles, tiles,
            pltpu.VMEM((8, D), F32),
            pltpu.VMEM((TP, 16, LANES), F32),
            pltpu.VMEM((F_DEV, 16, LANES), F32),
            pltpu.VMEM((plan.grad_ranks, plan.ub, D), BF16),
            pltpu.VMEM((2, plan.grad_ranks, plan.ub, D), BF16),
            pltpu.VMEM((rn - 1, 2 * CUTS, plan.uq // CUTS, QKV), BF16),
            pltpu.VMEM((rn - 1, 3 * CUTS, plan.uq // CUTS, QKV), BF16),
            pltpu.VMEM((2 * CUTS, plan.uq // CUTS, QKV), BF16),
            pltpu.VMEM((2 * CUTS, plan.uq // CUTS, QKV), BF16),
            DMA((ZN,)), DMA((ZN,)), DMA((ZN,)), DMA((ZN,)), DMA((ZN, rn - 1)), DMA((ZN, rn - 1)),
            DMA((TILES,)), DMA((TILES,)), DMA((TILES,)), DMA((TILES,)),
            DMA, DMA, DMA, DMA, DMA((mods,)), DMA((n,)),
            DMA((plan.grad_ranks,)), DMA((2, plan.grad_ranks)),
            DMA((2,)), DMA((plan.grad_ranks, rn - 1)), DMA((plan.grad_ranks, rn - 1)),
            DMA((CUTS * plan.nq,)),
            DMA((rn - 1, 2 * CUTS)), DMA((rn - 1, 3 * CUTS)), DMA((2 * CUTS,)), DMA((2 * CUTS,)),
        ],
        [SM, VM, ANY] + [VM] * 10 + [ANY, VM, VM],
        cid,
        name="tail_part",
    )(meta, q, kv, do, ot, lse, first_in, wq, tokens, dmid, mod_rows, dm4, late_own, late_send, esum, ebuf)


def adam_kernel(plan, meta, oq, ob, cond, dmod, master, one, two, average, n_master, n_one, n_two, n_average):
    s = meta[0]
    rate = RATE_FACTOR * D ** (-0.5)
    scale_one = 1.0 / (1.0 - BETA_FIRST**STEP)
    scale_two = 1.0 / (1.0 - BETA_SECOND**STEP)

    def update(rows, grad):
        first = BETA_FIRST * one[rows, :] + (1.0 - BETA_FIRST) * grad
        second = BETA_SECOND * two[rows, :] + (1.0 - BETA_SECOND) * grad * grad
        weight = master[rows, :]
        weight = weight - rate * (
            (first * scale_one) / (jnp.sqrt(second * scale_two) + ADAM_EPSILON)
            + WEIGHT_DECAY * weight
        )
        n_one[rows, :] = first
        n_two[rows, :] = second
        n_master[rows, :] = weight
        n_average[rows, :] = AVERAGE_RATE * average[rows, :] + (1.0 - AVERAGE_RATE) * weight

    if True:
        k = 3 * s + lax.div(pl.program_id(0), ADAM_CUTS)
        base = 0

        def from_matrix(kind):
            src = oq if kind == "q" else ob
            rows = (plan.uq if kind == "q" else plan.ub) // ADAM_CUTS
            cols = (QKV if kind == "q" else D) // LANES
            for j in range(cols):
                update(
                    pl.ds(base + j, rows, stride=cols), src[0, :, j * LANES : (j + 1) * LANES]
                )

        by_kind(plan, k, from_matrix)

        @pl.when(k >= plan.nb)
        def _():
            count = plan.um // ADAM_CUTS
            part = pl.multiple_of(lax.rem(pl.program_id(0), ADAM_CUTS) * count, count)
            at = cond[k - plan.nb, pl.ds(part, count), :]
            for j in range(MCOLS):
                update(
                    pl.ds(base + j, count, stride=MCOLS),
                    mm(at, dmod[pl.ds(j, plan.frames, stride=16), :].astype(BF16)),
                )


def adam(plan, meta, oq, ob, cond_rows, dmod, master, one, two, average):
    shape = jax.ShapeDtypeStruct(master.shape, F32)
    flat = pl.BlockSpec((plan.flat_rows // ADAM_CUTS, LANES), lambda i: (i, 0))
    unit = lambda rows, cols: pl.BlockSpec(
        (1, rows // ADAM_CUTS, cols), lambda i: (lax.div(i, ADAM_CUTS), lax.rem(i, ADAM_CUTS), 0)
    )
    whole = lambda x: pl.BlockSpec(x.shape, lambda i: (0,) * x.ndim)
    return pl.pallas_call(
        functools.partial(adam_kernel, plan),
        out_shape=(shape,) * 4,
        grid=(3 * ADAM_CUTS,),
        in_specs=[SM, unit(plan.uq, QKV), unit(plan.ub, D), whole(cond_rows), whole(dmod)] + [flat] * 4,
        out_specs=(flat,) * 4,
        compiler_params=pltpu.CompilerParams(vmem_limit_bytes=VMEM_LIMIT),
        name="adam",
    )(meta, oq, ob, cond_rows, dmod, master, one, two, average)


def local(
    tokens,
    grad_out,
    noise_level,
    context_mask,
    frame_clip,
    level_table,
    master,
    moment_one,
    moment_two,
    average,
):
    plan = Plan(lax.axis_size("seq"))
    s = lax.axis_index("seq")
    t = lax.axis_index("tp")
    flat = lambda x: x.reshape(-1, LANES)

    effective = noise_level * (1 - context_mask)
    one_hot = (
        effective[:, None] == jnp.arange(level_table.shape[0], dtype=jnp.int32)[None, :]
    ).astype(BF16)
    condition = jax.nn.silu(mm(one_hot, level_table)).astype(BF16)
    cond_units = condition.reshape(plan.frames, plan.nm, plan.um).transpose(1, 0, 2)

    meta = frame_clip.astype(jnp.int32)
    (
        wq, w_out, w_side, w_early, w_below, w_beside, wo_across, mod_rows, first_in, q_mine, kv_all,
        o_mine, o_rows, lse,
    ) = head_part(plan, meta, flat(master), cond_units, tokens, 0)
    result, late_own, late_send, early_sum, early_in, do_mine, middle_grad, mod_four = middle_part(
        plan, o_mine, wo_across, (w_out, w_side, w_beside, w_early, w_below),
        tokens, grad_out, mod_rows, 2
    )
    input_grad, own_q, own_b, mod_all = tail_part(
        plan, meta, q_mine, kv_all, do_mine, o_rows, lse, first_in, wq, tokens, middle_grad,
        mod_rows, mod_four, late_own, late_send, early_sum, early_in, 3,
    )
    updated = adam(
        plan,
        s[None].astype(jnp.int32),
        own_q,
        own_b,
        cond_units.transpose(0, 2, 1),
        flat(mod_all),
        flat(master),
        flat(moment_one),
        flat(moment_two),
        flat(average),
    )
    new_master, new_one, new_two, new_average = [x.reshape(master.shape) for x in updated]
    return (result, input_grad, new_master, new_one, new_two, new_average)


def solution(mesh):
    token_spec = P("seq", None)
    weight_spec = P("tp", "seq")
    in_specs = (token_spec, token_spec, P(), P(), P(), P()) + (weight_spec,) * 4
    out_specs = (token_spec, token_spec) + (weight_spec,) * 4
    return jax.shard_map(local, mesh=mesh, in_specs=in_specs, out_specs=out_specs, check_vma=False)
```

```python
import functools

import jax
import jax.numpy as jnp
from jax import lax
from jax.experimental import pallas as pl
from jax.experimental.pallas import tpu as pltpu
from jax.sharding import PartitionSpec as P

D = 1024
HEADS = 16
HEAD = 64
FF = 4096
TOK_FRAME = 384
STEP = 7
TP = 4
ZN = 4
HD = HEADS * HEAD // TP
QKV = 3 * HD
FT = FF // TP
MT = 6 * D // TP
F_DEV = 2
BROWS = HD + 2 * FT
LANES = 128
MCOLS = MT // LANES
PACK = TOK_FRAME // 2
TILE = 256
TILES = D // TILE
CUTS = 4
ADAM_CUTS = 2

NORM_EPSILON = 1e-06
RATE_FACTOR = 2.5
BETA_FIRST = 0.5
BETA_SECOND = 0.5
ADAM_EPSILON = 1e-08
WEIGHT_DECAY = 0.01
AVERAGE_RATE = 0.9
GELU_A = 0.7978845608028654
GELU_B = 0.044715
MESH = pl.DeviceIdType.MESH
VM = pl.BlockSpec(memory_space=pltpu.VMEM)
SM = pl.BlockSpec(memory_space=pltpu.SMEM)
ANY = pl.BlockSpec(memory_space=pl.ANY)
DMA = pltpu.SemaphoreType.DMA
F32 = jnp.float32
BF16 = jnp.bfloat16
VMEM_LIMIT = 60 * 2**20


def mm(left, right):
    return jnp.dot(left, right, preferred_element_type=F32)


def mm_tn(left, right):
    return lax.dot_general(left, right, (((0,), (0,)), ((), ())), preferred_element_type=F32)


def mm_nt(left, right):
    return lax.dot_general(left, right, (((1,), (1,)), ((), ())), preferred_element_type=F32)


def normalize(rows):
    centred = rows - jnp.mean(rows, axis=1, keepdims=True)
    inverse = lax.rsqrt(jnp.mean(centred * centred, axis=1, keepdims=True) + NORM_EPSILON)
    return (centred * inverse, inverse)


def norm_back(grads, normed, inverse):
    return inverse * (
        grads
        - jnp.mean(grads, axis=1, keepdims=True)
        - normed * jnp.mean(grads * normed, axis=1, keepdims=True)
    )


def loop(count, step, body):
    def turn(i, carry):
        body(pl.multiple_of(i * step, step))
        return carry

    lax.fori_loop(0, count // step, turn, 0)


def add_to(ref, row, values):
    ref[pl.ds(row, 1), :] += jnp.sum(values, axis=0, keepdims=True)


class Plan:
    def __init__(self, seq_count):
        self.n = seq_count
        self.r = seq_count // ZN
        self.shard = (D * QKV + BROWS * D + D * MT) // seq_count
        self.unit = self.shard // 3
        self.uq = self.unit // QKV
        self.ub = self.unit // D
        self.um = self.unit // MT
        self.nq = D // self.uq
        self.nb = self.nq + BROWS // self.ub
        self.nm = D // self.um
        self.first_mod = self.nb // 3
        self.half = (self.nq + self.nb) // 2
        self.flat_rows = self.unit // LANES
        self.frames = seq_count * F_DEV
        self.late = list(range(self.nq, self.half))
        self.early = list(range(self.half, self.nb))
        self.outs = self.late[: -(-HD // self.ub)]
        self.sided = self.late[len(self.outs) :]
        self.rank, self.ranks = self.ranked(self.early)
        self.late_rank, self.late_ranks = self.ranked(self.sided)
        self.grad_rank, self.grad_ranks = self.ranked(self.late)

    def ranked(self, units):
        seen, rank = {}, {}
        for k in units:
            column = self.home(k)[1]
            rank[k] = seen.get(column, 0)
            seen[column] = rank[k] + 1
        return rank, max(seen.values())

    def home(self, k):
        return (k // 3) // self.r, (k // 3) % self.r


def place(plan):
    s = lax.axis_index("seq")
    t = lax.axis_index("tp")
    return s, t, lax.div(s, plan.r), lax.rem(s, plan.r)


def remote(src, dst, send_sem, recv_sem, s, t):
    return pltpu.make_async_remote_copy(
        src_ref=src,
        dst_ref=dst,
        send_sem=send_sem,
        recv_sem=recv_sem,
        device_id=(s, t),
        device_id_type=MESH,
    )


def greet(peers):
    barrier = pltpu.get_barrier_semaphore()
    for s, t in peers:
        pl.semaphore_signal(barrier, inc=1, device_id=(s, t), device_id_type=MESH)
    pl.semaphore_wait(barrier, len(peers))


def by_kind(plan, k, act, low=0, high=None):
    high = plan.nb if high is None else high
    q_high, b_low = min(plan.nq, high), max(plan.nq, low)
    if low < q_high:
        @pl.when((k >= low) & (k < q_high))
        def _():
            act("q")

    if b_low < high:
        @pl.when((k >= b_low) & (k < high))
        def _():
            act("b")


def unit_of(plan, k, kind, wq, wb):
    if kind == "q":
        return wq.at[pl.ds(pl.multiple_of(k * plan.uq, plan.uq), plan.uq)]
    return wb.at[pl.ds(pl.multiple_of((k - plan.nq) * plan.ub, plan.ub), plan.ub)]


def call(kernel, outs, scratch, ins, cid=None, cost=None, name=None, out_specs=None):
    params = dict(vmem_limit_bytes=VMEM_LIMIT)
    if cid is not None:
        params.update(collective_id=cid, has_side_effects=True)
    return pl.pallas_call(
        kernel,
        out_shape=outs,
        in_specs=ins,
        out_specs=out_specs or jax.tree.map(lambda _: VM, outs),
        scratch_shapes=scratch,
        compiler_params=pltpu.CompilerParams(**params),
        cost_estimate=cost,
        name=name,
    )


def head_kernel(
    plan, meta, master, cond, tokens,
    wq, w_out, w_side, w_early, w_below, w_beside, wo_across, mods, first_in, q_out, kv_out, o, ot, lse,
    own_b, pool, flipped, qt, m_ref, l_ref, acc, tile, macc, mpart, mrecv, mod, norm, q_send, kv_send,
    qp_s, qc_s, q_r, wo_s, wo_r, ws_s, ws_r, we_s, we_r, loc_s, m_s, m_r, t_s, t_r, as_, ar, ks, kr, xs, xr,
    bl_s, bl_r, bs_s, bs_r, oa_s, oa_r,
):
    s, t, z, r = place(plan)
    n, rn = plan.n, plan.r
    greet(
        [(lax.rem(s + d, n), t) for d in range(1, n)]
        + [(s, lax.rem(t + d, TP)) for d in range(1, TP)]
    )
    start = lambda copy: copy.start()
    done = lambda copy: copy.wait_send()
    cut = plan.uq // CUTS

    def q_rows(k, h):
        return wq.at[pl.ds(pl.multiple_of(k * plan.uq + h * cut, cut), cut)]

    def q_copy(k, h, sem, to_s):
        ref = q_rows(k, h)
        return remote(ref, ref, sem, q_r.at[CUTS * k + h], to_s, t)

    def q_arrived(k, h):
        q_copy(k, h, qc_s.at[0, 0], s).wait_recv()

    def column(j):
        return r + rn * lax.rem(j + r, 2)

    def q_own(i, act):
        k = 3 * s + i

        @pl.when(k < plan.nq)
        def _():
            for h in range(CUTS):
                for d in range(1, rn):
                    act(q_copy(k, h, qp_s.at[CUTS * i + h, d - 1], lax.rem(r + d, rn)))

    def q_line(act, wait, whole=False):
        for j in range(2):
            k = column(j)
            for h in range(CUTS):
                if wait:
                    @pl.when((z > 0) | (lax.div(k, 3) != r))
                    def _():
                        q_arrived(k, h)

                @pl.when((z < ZN - 1) & ((z > 0) | (lax.div(k, 3) != r) | whole))
                def _():
                    act(q_copy(k, h, qc_s.at[CUTS * j + h, 0], s + rn))

                @pl.when(z > 0)
                def _():
                    for d in range(1, rn):
                        act(
                            q_copy(
                                k, h, qc_s.at[CUTS * j + h, d], z * rn + lax.rem(r + d, rn)
                            )
                        )

    def slot(k):
        if k in plan.outs:
            at = k - plan.nq
            return w_out.at[at], wo_s.at[at], wo_r.at[at]
        if k in plan.sided:
            at = plan.late_rank[k]
            return w_side.at[at], ws_s.at[at], ws_r.at[at]
        return w_early.at[k - plan.half], we_s.at[plan.rank[k]], we_r.at[k - plan.half]

    def along(k, src, act, up):
        dst, send_sem, recv_sem = slot(k)
        if up and k < plan.half:
            @pl.when(z < ZN - 1)
            def _():
                act(remote(src, dst, send_sem.at[0], recv_sem, s + rn, t))

        if not up:
            @pl.when(z > 0)
            def _():
                act(remote(src, dst, send_sem.at[1], recv_sem, s - rn, t))

    def beside(k, src, act):
        if k not in plan.outs:
            return
        dst, send_sem, recv_sem = slot(k)
        for d in range(1, rn):
            act(
                remote(
                    src, dst, send_sem.at[1 + d], recv_sem, z * rn + lax.rem(r + d, rn), t
                )
            )

    def arrived(k):
        dst, send_sem, recv_sem = slot(k)
        remote(own_b.at[0], dst, send_sem.at[0], recv_sem, s, t).wait_recv()

    def keep(k):
        return pltpu.make_async_copy(own_b.at[k % 3], slot(k)[0], loc_s.at[k % 3])

    def owned(units, act):
        for k in units:
            @pl.when(s == k // 3)
            def _():
                act(k, own_b.at[k % 3])

    def pass_along(units, d, act, wait):
        for k in units:
            zo, ro = plan.home(k)
            if k < plan.half and zo + d < (ZN - 1 if k in plan.sided else ZN):
                @pl.when((r == ro) & (z == zo + d))
                def _():
                    if wait:
                        arrived(k)
                    along(k, slot(k)[0], act, True)
                    beside(k, slot(k)[0], act)

            if zo - d >= (0 if k in plan.outs else 1):
                @pl.when((r == ro) & (z == zo - d))
                def _():
                    if wait:
                        arrived(k)
                    along(k, slot(k)[0], act, False)
                    beside(k, slot(k)[0], act)

    def settle(k, low):
        zo, ro = plan.home(k)

        @pl.when((r == ro) & ((z == 0) & (zo > 0) if low else (z == ZN - 1) & (zo < ZN - 1)))
        def _():
            arrived(k)

    def hop(k, act):
        zo, ro = plan.home(k)

        @pl.when(s == k // 3)
        def _():
            act(remote(own_b.at[k % 3], w_below.at[k % 3], bl_s.at[k % 3], bl_r.at[k % 3], s + rn, t))

    def hopped(k):
        zo, ro = plan.home(k)

        @pl.when((r == ro) & (z == zo + 1))
        def _():
            remote(own_b.at[0], w_below.at[k % 3], bl_s.at[0], bl_r.at[k % 3], s, t).wait_recv()

    def share(k, act, low=None):
        rank = plan.late_rank[k]
        part = True if low is None else (z <= 1) == low

        @pl.when((r == plan.home(k)[1]) & part)
        def _():
            for d in range(1, rn):
                act(
                    remote(
                        w_side.at[rank], w_beside.at[d - 1, rank], bs_s.at[rank, d - 1],
                        bs_r.at[d - 1, rank], z * rn + lax.rem(r + d, rn), t,
                    )
                )

    def shared(k):
        rank = plan.late_rank[k]

        @pl.when(r != plan.home(k)[1])
        def _():
            d = lax.rem(r - plan.home(k)[1] + rn, rn)
            remote(
                w_side.at[0], w_beside.at[d - 1, rank], bs_s.at[0, 0], bs_r.at[d - 1, rank], s, t
            ).wait_recv()

    def out_copy(w):
        count = min(plan.ub, HD - w * plan.ub)
        return remote(
            w_out.at[w].at[pl.ds(0, count)], wo_across.at[pl.ds(w * plan.ub, count)],
            oa_s.at[w], oa_r.at[w], s, lax.rem(t + 2, TP),
        )

    def sort_group(g):
        first = meta[2 * g] == 0
        a, b = kv_out[g, :TOK_FRAME, :], kv_out[g, TOK_FRAME:, :]
        pool[g, 0] = jnp.where(first, a, b)
        pool[g, 1] = jnp.where(first, b, a)
        for kind in range(2):
            flipped[kind, g] = pool[g, kind].T

    def attend_group(zq):
        gq = zq * rn + r
        first = meta[2 * gq] == 0
        clip = meta[2 * gq] + meta[2 * gq + 1]
        parts = []
        for kind in range(2):
            low = first if kind == 0 else jnp.logical_not(first)
            rows = jnp.where(low, q_out[zq][:, :HEAD], q_out[zq][:, HEAD:])
            qt[...] = (padded(rows, True) * jnp.asarray(HEAD ** (-0.5), BF16)).T
            m_ref[...] = jnp.full_like(m_ref, -1e30)
            l_ref[...] = jnp.zeros_like(l_ref)
            acc[...] = jnp.zeros_like(acc)

            def block(p, inner):
                pair = []
                m_old = m_ref[...]
                m_new = m_old
                for e in range(2):
                    g = jnp.minimum(2 * p + e, gq)
                    shown = 2 * p + e <= gq
                    if kind == 1:
                        shown = shown & (meta[2 * g] + meta[2 * g + 1] == clip)
                    off = jnp.where(shown, 0.0, 1e30)
                    st = mm(pool[g, kind], qt[...])
                    m_new = jnp.maximum(m_new, jnp.max(st, axis=0, keepdims=True) - off)
                    pair.append((g, st, off))
                alpha = jnp.exp(m_old - m_new)
                total, out = l_ref[...] * alpha, acc[...] * alpha
                for g, st, off in pair:
                    weights = jnp.exp(st - (m_new + off))
                    total = total + jnp.sum(weights, axis=0, keepdims=True)
                    out = out + mm(flipped[kind, g], weights.astype(BF16))
                m_ref[...] = m_new
                l_ref[...] = total
                acc[...] = out
                return inner

            lax.fori_loop(0, lax.div(gq + 2, 2), block, 0)
            total = l_ref[...]
            out = acc[HEAD:, :] / total
            ot[2 * zq + kind] = out
            lse[2 * zq + kind] = m_ref[...] + jnp.log(total)
            rows = out.T
            parts.append(jnp.concatenate([rows[:PACK], rows[PACK:]], axis=1).astype(BF16))
        o[zq, 0] = jnp.where(first, parts[0], parts[1])
        o[zq, 1] = jnp.where(first, parts[1], parts[0])

    units = plan.late + plan.early
    first_up = [k for k in plan.late if k % 3 == 0 and plan.home(k)[0] > 0]
    later_up = [k for k in plan.late if k not in first_up]

    def fill(i, kind):
        k = 3 * s + i
        base = i * plan.flat_rows
        rows, cols = (plan.uq, QKV // LANES) if kind == "q" else (plan.ub, D // LANES)
        at = pl.multiple_of(k * plan.uq, plan.uq)
        for j in range(cols):
            values = master[pl.ds(base + j, rows, stride=cols), :].astype(BF16)
            if kind == "q":
                wq[pl.ds(at, rows), j * LANES : (j + 1) * LANES] = values
            else:
                own_b[i, :, j * LANES : (j + 1) * LANES] = values

    for away in (True, False):
        for i in range(3):
            k = 3 * s + i

            @pl.when((k < plan.nq) & ((lax.rem(k, rn) != r) == away))
            def _():
                fill(i, "q")
                q_own(i, start)
                if not away:
                    at = lax.div(k, rn)
                    slot_j = lax.rem(at + r, 2)
                    for h in range(CUTS):
                        q_copy(k, h, qc_s.at[CUTS * slot_j + h, 0], s + rn).start()

    for i in range(3):
        @pl.when((3 * s + i >= plan.nq) & (3 * s + i < plan.nb))
        def _():
            fill(i, "b")

    @pl.when(z == 0)
    def _():
        q_line(start, True)

    owned(units, lambda k, src: along(k, src, start, False))
    owned(first_up, lambda k, src: along(k, src, start, True))
    owned(units, lambda k, src: keep(k).start())

    macc[...] = jnp.zeros_like(macc)
    for i in range(3):
        k = 3 * s + i
        base = i * plan.flat_rows

        @pl.when(k >= plan.nb)
        def _():
            for j in range(MCOLS):
                tile[:, j * LANES : (j + 1) * LANES] = master[
                    pl.ds(base + j, plan.um, stride=MCOLS), :
                ].astype(BF16)
            macc[...] += mm(cond[k - plan.nb], tile[...])

    fm = plan.first_mod

    def m_copy(d):
        to = lax.rem(s + d, n)
        return remote(mpart.at[to], mrecv.at[s - fm], m_s.at[d - 1], m_r.at[s - fm], to, t)

    @pl.when(s >= fm)
    def _():
        for f in range(plan.frames):
            for j in range(MCOLS):
                mpart[f // F_DEV, pl.ds((f % F_DEV) * MCOLS + j, 1), :] = macc[
                    pl.ds(f, 1), j * LANES : (j + 1) * LANES
                ]
        mrecv[s - fm] = mpart[s]
        for d in range(1, n):
            m_copy(d).start()

    def norm_rows(at):
        rows = pl.ds(at, 64)
        norm[rows, :] = normalize(tokens[rows, :].astype(F32))[0]

    loop(F_DEV * TOK_FRAME, 64, norm_rows)

    @pl.when(z > 0)
    def _():
        q_line(start, True)

    owned(plan.outs, lambda k, src: along(k, src, start, True))
    owned([k for k in later_up if k not in plan.outs], lambda k, src: along(k, src, start, True))
    owned(units, lambda k, src: beside(k, src, start))
    pass_along(first_up + plan.early, 1, start, True)

    for src in range(fm, n):
        @pl.when(s != src)
        def _():
            remote(mpart.at[0], mrecv.at[src - fm], m_s.at[0], m_r.at[src - fm], s, t).wait_recv()

    total = mrecv[0]
    for src in range(1, n - fm):
        total = total + mrecv[src]
    mod[t] = total

    def t_copy(d):
        return remote(mod.at[t], mod.at[t], t_s.at[d - 1], t_r.at[t], s, lax.rem(t + d, TP))

    for d in range(1, TP):
        t_copy(d).start()
    for d in range(1, TP):
        other = lax.rem(t + d, TP)
        remote(mod.at[t], mod.at[other], t_s.at[0], t_r.at[other], s, t).wait_recv()
    for f in range(F_DEV):
        for block in range(TP * MCOLS):
            part, at = block // (D // LANES), block % (D // LANES)
            mods[f * 6 + part : f * 6 + part + 1, at * LANES : (at + 1) * LANES] = mod[
                block // MCOLS, f * MCOLS + block % MCOLS : f * MCOLS + block % MCOLS + 1, :
            ]

    def affine(f):
        def body(at):
            rows = pl.ds(f * TOK_FRAME + at, 64)
            first_in[rows, :] = (
                norm[rows, :] * (1.0 + mods[f * 6 + 1 : f * 6 + 2, :]) + mods[f * 6 : f * 6 + 1, :]
            ).astype(BF16)

        loop(TOK_FRAME, 64, body)

    for f in range(F_DEV):
        affine(f)

    for k in range(plan.nq):
        for h in range(CUTS):
            if rn > 1:
                at_zero = (z == 0) & (k // 3 != r) & (k % rn != r)

                @pl.when(at_zero | (z > 0) & (k % rn != r))
                def _():
                    q_arrived(k, h)

    keys = mm(first_in[...], wq[:, HD : 2 * HD]).astype(BF16)
    values = mm(first_in[...], wq[:, 2 * HD :]).astype(BF16)
    for h in range(ZN):
        cols = slice(h * HEAD, (h + 1) * HEAD)
        kv_send[h] = jnp.concatenate([keys[:, cols], values[:, cols]], axis=1)

    def kv_copy(d):
        h = lax.rem(z + d, ZN)
        return remote(kv_send.at[h], kv_out.at[s], ks.at[d - 1], kr.at[z], h * rn + r, t)

    def a_copy(d):
        h = lax.rem(z + d, ZN)
        return remote(q_send.at[h], q_out.at[z], as_.at[d - 1], ar.at[z], h * rn + r, t)

    def side_copy(zs, e):
        at = zs * rn + r
        ref = kv_out.at[at]
        return remote(ref, ref, xs.at[zs, e - 1], xr.at[at], z * rn + lax.rem(r + e, rn), t)

    for d in range(1, ZN):
        kv_copy(d).start()
    kv_out[s] = kv_send[z]
    for e in range(1, rn):
        side_copy(z, e).start()
    queries = mm(first_in[...], wq[:, :HD]).astype(BF16)
    for h in range(ZN):
        cols = slice(h * HEAD, (h + 1) * HEAD)
        q_send[h] = jnp.concatenate([queries[:TOK_FRAME, cols], queries[TOK_FRAME:, cols]], axis=1)
    for d in range(1, ZN):
        a_copy(d).start()
    q_out[z] = q_send[z]

    rest = [k for k in plan.sided if k not in first_up]
    pass_along(plan.outs + rest, 1, start, True)
    owned(units, lambda k, src: keep(k).wait())
    for k in plan.sided:
        settle(k, True)
        share(k, start, True)

    def kv_come(zs):
        @pl.when(z != zs)
        def _():
            remote(kv_send.at[0], kv_out.at[zs * rn + r], ks.at[0], kr.at[zs], s, t).wait_recv()
            for e in range(1, rn):
                side_copy(zs, e).start()

    def ready(zq):
        for e in range(1, rn):
            at = zq * rn + lax.rem(r + e, rn)
            remote(kv_out.at[at], kv_out.at[at], xs.at[0, 0], xr.at[at], s, t).wait_recv()
        for other in range(rn):
            sort_group(zq * rn + other)

        @pl.when(z != zq)
        def _():
            remote(q_send.at[0], q_out.at[zq], as_.at[0], ar.at[zq], s, t).wait_recv()

    kv_come(0)
    kv_come(1)
    pass_along(plan.outs, 2, start, True)
    for k in plan.early:
        hop(k, start)
    ready(0)
    attend_group(0)
    kv_come(2)
    kv_come(3)
    pass_along(plan.outs, 3, start, True)
    ready(1)
    attend_group(1)
    for d in range(2, ZN):
        pass_along(plan.sided, d, start, True)
    for k in plan.sided:
        settle(k, False)
        share(k, start, False)
    ready(2)
    attend_group(2)
    for k in plan.outs:
        @pl.when(r != plan.home(k)[1])
        def _():
            arrived(k)

    for w in range(len(plan.outs)):
        out_copy(w).start()
    ready(3)
    attend_group(3)
    for k in plan.early:
        hopped(k)
        zo, ro = plan.home(k)
        if zo > 0:
            @pl.when((r == ro) & (z == 0))
            def _():
                arrived(k)

    for k in plan.sided:
        shared(k)
    for w in range(len(plan.outs)):
        out_copy(w).wait()

    for k in plan.early:
        hop(k, done)
    for k in plan.sided:
        share(k, done)
    for i in range(3):
        q_own(i, done)
    q_line(done, False, True)
    owned(units, lambda k, src: along(k, src, done, False))
    owned(plan.late, lambda k, src: along(k, src, done, True))
    owned(units, lambda k, src: beside(k, src, done))
    for d in range(1, ZN):
        pass_along(units, d, done, False)

    @pl.when(s >= fm)
    def _():
        for d in range(1, n):
            m_copy(d).wait_send()

    for d in range(1, TP):
        t_copy(d).wait_send()
    for d in range(1, ZN):
        kv_copy(d).wait_send()
        a_copy(d).wait_send()
    for zs in range(ZN):
        for e in range(1, rn):
            side_copy(zs, e).wait_send()


def head_part(plan, meta, master, cond_units, tokens, cid):
    n, rn = plan.n, plan.r
    mrows = F_DEV * MCOLS
    rows = F_DEV * TOK_FRAME
    mods = n - plan.first_mod
    return call(
        functools.partial(head_kernel, plan),
        (
            jax.ShapeDtypeStruct((D, QKV), BF16),
            jax.ShapeDtypeStruct((len(plan.outs), plan.ub, D), BF16),
            jax.ShapeDtypeStruct((plan.late_ranks, plan.ub, D), BF16),
            jax.ShapeDtypeStruct((len(plan.early), plan.ub, D), BF16),
            jax.ShapeDtypeStruct((3, plan.ub, D), BF16),
            jax.ShapeDtypeStruct((rn - 1, plan.late_ranks, plan.ub, D), BF16),
            jax.ShapeDtypeStruct((HD, D), BF16),
            jax.ShapeDtypeStruct((F_DEV * 6, D), F32),
            jax.ShapeDtypeStruct((rows, D), BF16),
            jax.ShapeDtypeStruct((ZN, TOK_FRAME, LANES), BF16),
            jax.ShapeDtypeStruct((n, rows, LANES), BF16),
            jax.ShapeDtypeStruct((ZN, F_DEV, PACK, LANES), BF16),
            jax.ShapeDtypeStruct((ZN * F_DEV, HEAD, TOK_FRAME), F32),
            jax.ShapeDtypeStruct((ZN * F_DEV, 1, TOK_FRAME), F32),
        ),
        [
            pltpu.VMEM((3, plan.ub, D), BF16),
            pltpu.VMEM((n, 2, TOK_FRAME, LANES), BF16),
            pltpu.VMEM((2, n, LANES, TOK_FRAME), BF16),
            pltpu.VMEM((LANES, TOK_FRAME), BF16),
            pltpu.VMEM((1, TOK_FRAME), F32),
            pltpu.VMEM((1, TOK_FRAME), F32),
            pltpu.VMEM((LANES, TOK_FRAME), F32),
            pltpu.VMEM((plan.um, MT), BF16),
            pltpu.VMEM((plan.frames, MT), F32),
            pltpu.VMEM((n, mrows, LANES), F32),
            pltpu.VMEM((mods, mrows, LANES), F32),
            pltpu.VMEM((TP, mrows, LANES), F32),
            pltpu.VMEM((rows, D), F32),
            pltpu.VMEM((ZN, TOK_FRAME, LANES), BF16),
            pltpu.VMEM((ZN, rows, LANES), BF16),
            DMA((3 * CUTS, rn - 1)), DMA((2 * CUTS, rn)), DMA((CUTS * plan.nq,)),
            DMA((len(plan.outs), rn + 1)), DMA((len(plan.outs),)),
            DMA((plan.late_ranks, 2)), DMA((plan.late_ranks,)),
            DMA((plan.ranks, rn + 1)), DMA((len(plan.early),)), DMA((3,)),
            DMA((n - 1,)), DMA((mods,)), DMA((TP - 1,)), DMA((TP,)),
            DMA((ZN - 1,)), DMA((ZN,)), DMA((ZN - 1,)), DMA((ZN,)), DMA((ZN, rn - 1)), DMA((n,)),
            DMA((3,)), DMA((3,)), DMA((plan.late_ranks, rn - 1)), DMA((rn - 1, plan.late_ranks)),
            DMA((len(plan.outs),)), DMA((len(plan.outs),)),
        ],
        [SM] + [VM] * 3,
        cid,
        out_specs=(VM,) + (ANY,) * 6 + (VM,) * 7,
        name="head_part",
    )(meta, master, cond_units, tokens)


def padded(rows, low):
    zero = jnp.zeros_like(rows)
    return jnp.concatenate([rows, zero] if low else [zero, rows], axis=1)


def middle_kernel(
    plan, o_mine, wo_across, w_out, w_side, w_beside, w_early, w_below, tokens, grad_out, mod,
    result, late_own, late_send, esum, ebuf, do_out, dmid, dmod,
    gb, wb, eside, eend, wo, oall, attended, attn, mid, norm, inv, sin, hidden, dmlp, slopes, dup,
    own, csend, crecv, ysend, yrecv, dattn, dsend, dwo, wsend, wrecv,
    o_s, o_r, f_s, f_r, n_s, n_r, c_s, c_r, y_s, y_r, d_s, d_r, w_s, w_r, e_s, e_r, p_s, p_r, l_s, u_s, u_r, g_s, g_r, j_s, h_s, h_r, i_s, i_r,
):
    s, t, z, r = place(plan)
    rn = plan.r
    y = lax.div(t, 2)
    c = lax.rem(t, 2)
    sib = 2 * y + 1 - c
    across = lax.rem(t + 2, TP)
    mine = pl.multiple_of(c * TOK_FRAME, TOK_FRAME)
    theirs = pl.multiple_of((1 - c) * TOK_FRAME, TOK_FRAME)
    pairs = [(d, e) for d in range(ZN) for e in range(2)][1:]

    def partner(d, e):
        return lax.rem(z + d, ZN), (c if e == 0 else 1 - c)

    greet(
        [(partner(d, e)[0] * rn + r, 2 * y + partner(d, e)[1]) for d, e in pairs]
        + [(s, across)]
        + [(z * rn + lax.rem(r + d, rn), t) for d in range(1, rn)]
    )

    def home(k):
        return (k // 3) // rn, (k // 3) % rn, k - plan.half

    def w_rows(ref, k):
        return ref.at[pl.ds((k - plan.nq) * plan.ub, plan.ub)]

    def late_loads(act):
        for k in plan.late:
            sem = l_s.at[k - plan.nq]
            if k in plan.outs:
                act(pltpu.make_async_copy(w_out.at[k - plan.nq], w_rows(wb, k), sem))
            else:
                zo, ro = plan.home(k)
                rank = plan.late_rank[k]

                @pl.when(r == ro)
                def _():
                    act(pltpu.make_async_copy(w_side.at[rank], w_rows(wb, k), sem))

                @pl.when(r != ro)
                def _():
                    d = lax.rem(r - ro + rn, rn)
                    act(pltpu.make_async_copy(w_beside.at[d - 1, rank], w_rows(wb, k), sem))

    def loads(act):
        for k in plan.early:
            zo, ro, at = home(k)

            @pl.when((z <= zo) & (r == ro))
            def _():
                act(pltpu.make_async_copy(w_early.at[at], w_rows(wb, k), l_s.at[len(plan.late) + at]))

            @pl.when((z == zo + 1) & (r == ro))
            def _():
                act(
                    pltpu.make_async_copy(
                        w_below.at[k % 3], w_rows(wb, k), l_s.at[len(plan.late) + at]
                    )
                )

    def rise(k, src, act):
        zo, ro, at = home(k)

        @pl.when((z < ZN - 1) & (z > zo))
        def _():
            act(remote(src, w_rows(wb, k), u_s.at[at, 0], u_r.at[at], s + rn, t))

        for d in range(1, rn):
            act(
                remote(
                    src, w_rows(wb, k), u_s.at[at, d], u_r.at[at],
                    z * rn + lax.rem(r + d, rn), t,
                )
            )

    def risen(k):
        remote(w_below.at[0], w_rows(wb, k), u_s.at[0, 0], u_r.at[k - plan.half], s, t).wait_recv()

    def rises(act, first, wait):
        for k in plan.early:
            zo, ro, at = home(k)
            if first:
                @pl.when((z == zo + 1) & (r == ro))
                def _():
                    rise(k, w_below.at[k % 3], act)

                @pl.when((z <= zo) & (r == ro))
                def _():
                    rise(k, w_early.at[at], act)

            else:
                @pl.when((z > zo + 1) & (r == ro))
                def _():
                    if wait:
                        risen(k)
                    rise(k, w_rows(wb, k), act)

    def o_copy(d, e):
        zd, cd = partner(d, e)
        return remote(
            o_mine.at[zd, cd], oall.at[y * 8 + c * ZN + z], o_s.at[2 * d + e],
            o_r.at[c * ZN + z], zd * rn + r, 2 * y + cd,
        )

    def f_copy(slot):
        ref = oall.at[y * 8 + slot]
        return remote(ref, ref, f_s.at[slot], f_r.at[slot], s, across)

    def p_copy(i, tp):
        ref = wo.at[pl.ds(pl.multiple_of(tp * HD, HD), HD)]
        return remote(ref, ref, p_s.at[i], p_r.at[i], s, sib)

    for d, e in pairs:
        o_copy(d, e).start()
    start = lambda copy: copy.start()
    rises(start, True, False)
    late_loads(start)
    loads(start)
    late_loads(lambda copy: copy.wait())
    wo[pl.ds(pl.multiple_of(t * HD, HD), HD), :] = wb[:HD, :]
    p_copy(0, t).start()
    wo[pl.ds(pl.multiple_of(across * HD, HD), HD), :] = wo_across[...]
    p_copy(1, across).start()
    oall[y * 8 + c * ZN + z] = o_mine[z, c]
    f_copy(c * ZN + z).start()

    def d_mlp(f):
        def body(at):
            rows = pl.ds(f * TOK_FRAME + at, 64)
            dmlp[rows, :] = (grad_out[rows, :].astype(F32) * mod[f * 6 + 5 : f * 6 + 6, :]).astype(
                BF16
            )

        loop(TOK_FRAME, 64, body)

    for f in range(F_DEV):
        d_mlp(f)

    for d, e in pairs:
        zd, cd = partner(d, e)
        slot = cd * ZN + zd
        remote(o_mine.at[0, 0], oall.at[y * 8 + slot], o_s.at[0], o_r.at[slot], s, t).wait_recv()
        f_copy(slot).start()
    for slot in range(8):
        remote(
            oall.at[0], oall.at[(1 - y) * 8 + slot], f_s.at[slot], f_r.at[slot], s, t
        ).wait_recv()
    for m in range(HEADS // 2):
        a, b = oall[2 * m], oall[2 * m + 1]
        cols = slice(m * LANES, (m + 1) * LANES)
        attended[:PACK, cols] = jnp.concatenate([a[:, :HEAD], b[:, :HEAD]], axis=1)
        attended[PACK:, cols] = jnp.concatenate([a[:, HEAD:], b[:, HEAD:]], axis=1)

    p_copy(0, sib).wait_recv()
    p_copy(1, lax.rem(sib + 2, TP)).wait_recv()

    def attn_tile(at):
        attn[:, pl.ds(at, TILE)] = mm(attended[...], wo[:, pl.ds(at, TILE)])

    loop(D, TILE, attn_tile)
    rises(start, False, True)

    row = lambda part: mod[pl.ds(c * 6 + part, 1), :]

    def norm_rows(at):
        rows = pl.ds(at, 64)
        values = tokens[pl.ds(mine + at, 64), :].astype(F32) + row(2) * attn[rows, :]
        mid[rows, :] = values
        normed, inverse = normalize(values)
        norm[rows, :] = normed
        inv[rows, :] = inverse
        sin[pl.ds(mine + at, 64), :] = (normed * (1.0 + row(4)) + row(3)).astype(BF16)

    loop(TOK_FRAME, 64, norm_rows)

    def n_copy(base):
        ref = sin.at[pl.ds(base, TOK_FRAME)]
        return remote(ref, ref, n_s.at[0], n_r.at[0], s, sib)

    n_copy(mine).start()
    loads(lambda copy: copy.wait())
    for k in plan.early:
        zo, ro, at = home(k)

        @pl.when(r != ro)
        def _():
            risen(k)

    def feed(base):
        rows = pl.ds(base, TOK_FRAME)

        def tile(at):
            cols = pl.ds(at, TILE)
            u = mm(sin[rows, :], wb[HD : HD + FT, cols])
            square = u * u
            inner = GELU_A * u * (1.0 + GELU_B * square)
            th = jnp.tanh(inner)
            half = 0.5 * (1.0 + th)
            hidden[rows, cols] = (u * half).astype(BF16)
            slopes[rows, cols] = half + 0.5 * u * (1.0 - th * th) * (
                GELU_A * (1.0 + 3.0 * GELU_B * square)
            )

        loop(FT, TILE, tile)

    feed(mine)
    n_copy(theirs).wait_recv()
    feed(theirs)

    def d_up(at):
        cols = pl.ds(at, TILE)
        dup[:, cols] = (mm_nt(dmlp[...], wb[pl.ds(HD + FT + at, TILE), :]) * slopes[:, cols]).astype(
            BF16
        )

    loop(FT, TILE, d_up)

    def c_copy(w, n):
        return remote(csend.at[w, n], crecv.at[w, n], c_s.at[w, n], c_r.at[w, n], s, sib)

    def y_copy(w, n):
        return remote(ysend.at[w, n], yrecv.at[w, n], y_s.at[w, n], y_r.at[w, n], s, across)

    def pass_on(w, n):
        c_copy(w, n).wait_recv()
        ysend[w, n] = (own[n] + crecv[w, n].astype(F32)).astype(BF16)
        y_copy(w, n).start()

    def product(w, base, n):
        rows = pl.ds(base, TOK_FRAME)
        if w == 0:
            return mm_nt(dup[rows, :], wb[HD + n * TILE : HD + (n + 1) * TILE, :])
        return mm(hidden[rows, :], wb[HD + FT :, n * TILE : (n + 1) * TILE])

    def products(w):
        for n in range(TILES):
            csend[w, n] = product(w, theirs, n).astype(BF16)
            c_copy(w, n).start()
            own[n] = product(w, mine, n)
            if n:
                pass_on(w, n - 1)
        pass_on(w, TILES - 1)

    def down_grad(at):
        gb[pl.ds(HD + FT + at, TILE), :] = mm_tn(hidden[:, pl.ds(at, TILE)], dmlp[...]).astype(BF16)

    def up_grad(at):
        gb[pl.ds(HD + at, TILE), :] = mm_tn(sin[:, pl.ds(at, TILE)], dup[...]).astype(BF16)

    def early_grad(k, d):
        zo, ro, at = home(k)
        slot = lax.rem(ro - r + rn, rn) - 1 if d is None else d - 1
        return remote(
            w_rows(gb, k), eside.at[slot, plan.rank[k]], g_s.at[at], g_r.at[slot, plan.rank[k]],
            z * rn + ro, t,
        )

    def early_grads(act):
        for k in plan.early:
            zo, ro, at = home(k)

            @pl.when(r != ro)
            def _():
                act(early_grad(k, None))

    def early_hop(rank, act):
        for here, to in ((ZN - 1, s - rn), (0, s + rn)):
            @pl.when(z == here)
            def _():
                act(remote(esum.at[rank], eend.at[rank], h_s.at[rank], h_r.at[rank], to, t))

    def early_total(rank):
        for k in plan.early:
            if plan.rank[k] == rank:
                zo, ro, at = home(k)

                @pl.when(r == ro)
                def _():
                    for d in range(1, rn):
                        early_grad(k, d).wait_recv()

                    def body(at):
                        rows = pl.ds(at, 16)
                        total = gb[pl.ds((k - plan.nq) * plan.ub + at, 16), :].astype(F32)
                        for d in range(1, rn):
                            total = total + eside[d - 1, rank, rows, :].astype(F32)
                        esum[rank, rows, :] = total.astype(BF16)

                    loop(plan.ub, 16, body)
                    early_hop(rank, start)

    def early_pass(rank, to):
        return remote(esum.at[rank], ebuf.at[rank], i_s.at[rank], i_r.at[rank], to, t)

    def early_inner(rank):
        for k in plan.early:
            if plan.rank[k] == rank:
                zo, ro, at = home(k)

                @pl.when((r == ro) & (z > 0) & (z < ZN - 1))
                def _():
                    remote(
                        esum.at[rank], eend.at[rank], h_s.at[rank], h_r.at[rank], s, t
                    ).wait_recv()

                    def body(at):
                        rows = pl.ds(at, 16)
                        esum[rank, rows, :] = (
                            esum[rank, rows, :].astype(F32) + eend[rank, rows, :].astype(F32)
                        ).astype(BF16)

                    loop(plan.ub, 16, body)

                    @pl.when(z != zo)
                    def _():
                        early_pass(rank, s + rn if zo == 2 else s - rn).start()

    def early_close(rank):
        for k in plan.early:
            if plan.rank[k] == rank:
                zo, ro, at = home(k)

                @pl.when((r == ro) & (z == zo))
                def _():
                    early_pass(rank, s).wait_recv()

                @pl.when((r == ro) & (z == 3 - zo))
                def _():
                    early_pass(rank, s).wait_send()

    def early_hops_done(rank):
        for k in plan.early:
            if plan.rank[k] == rank:
                @pl.when(r == home(k)[1])
                def _():
                    early_hop(rank, lambda copy: copy.wait_send())

    loop(FT, TILE, down_grad)
    up_grad(D - TILE)
    early_grads(start)
    products(0)
    products(1)
    loop(D - TILE, TILE, up_grad)
    early_total(0)
    early_total(1)
    early_inner(0)

    dm = dmod
    dm[...] = jnp.zeros_like(dm)
    for n in range(TILES):
        y_copy(0, n).wait_recv()

    def total(w, rows):
        return jnp.concatenate(
            [ysend[w, n, rows].astype(F32) + yrecv[w, n, rows].astype(F32) for n in range(TILES)],
            axis=1,
        )

    def back_rows(at):
        rows = pl.ds(at, 64)
        tok_rows = pl.ds(mine + at, 64)
        grads = total(0, rows)
        normed = norm[rows, :]
        add_to(dm, 1, grads)
        add_to(dm, 2, grads * normed)
        values = grad_out[tok_rows, :].astype(F32) + norm_back(
            grads * (1.0 + row(4)), normed, inv[rows, :]
        )
        dmid[rows, :] = values
        add_to(dm, 0, attn[rows, :] * values)
        dattn[rows, :] = (row(2) * values).astype(BF16)

    loop(TOK_FRAME, 64, back_rows)
    for ch in range(2):
        part = mm_nt(dattn[...], wo[pl.ds(pl.multiple_of((2 * y + ch) * HD, HD), HD), :]).astype(BF16)
        for zh in range(ZN):
            cols = slice(zh * HEAD, (zh + 1) * HEAD)
            dsend[ch * ZN + zh] = jnp.concatenate([part[:PACK, cols], part[PACK:, cols]], axis=1)

    def d_copy(d, e):
        zd, cd = partner(d, e)
        return remote(
            dsend.at[cd * ZN + zd], do_out.at[z, c], d_s.at[2 * d + e], d_r.at[2 * z + c],
            zd * rn + r, 2 * y + cd,
        )

    for d, e in pairs:
        d_copy(d, e).start()
    do_out[z, c] = dsend[c * ZN + z]
    for rank in range(2, plan.ranks):
        early_total(rank)

    def o_grad(head_core):
        cols = pl.ds(pl.multiple_of((2 * y + head_core) * HD, HD), HD)
        return mm_tn(attended[:, cols], dattn[...])

    w_copy = remote(wsend, wrecv, w_s, w_r, s, sib)
    wsend[...] = o_grad(1 - c).astype(BF16)
    w_copy.start()
    dwo[...] = o_grad(c)
    early_inner(1)

    for n in range(TILES):
        y_copy(1, n).wait_recv()

    def result_rows(at):
        rows = pl.ds(at, 64)
        tok_rows = pl.ds(mine + at, 64)
        mlp = total(1, rows)
        add_to(dm, 3, mlp * grad_out[tok_rows, :].astype(F32))
        result[tok_rows, :] = (mid[rows, :] + row(5) * mlp).astype(BF16)

    loop(TOK_FRAME, 64, result_rows)

    def e_copy(base):
        ref = result.at[pl.ds(base, TOK_FRAME)]
        return remote(ref, ref, e_s, e_r, s, sib)

    e_copy(mine).start()
    for rank in range(2, plan.ranks):
        early_inner(rank)
    w_copy.wait_recv()
    gb[:HD, :] = (dwo[...] + wrecv[...].astype(F32)).astype(BF16)

    for d, e in pairs:
        zd, cd = partner(d, e)
        remote(
            dsend.at[0], do_out.at[zd, cd], d_s.at[0], d_r.at[2 * zd + cd], s, t
        ).wait_recv()
    def late_grads(act):
        for k in plan.late:
            zo, ro = plan.home(k)
            rank, sem = plan.grad_rank[k], j_s.at[k - plan.nq]

            @pl.when(r == ro)
            def _():
                act(pltpu.make_async_copy(w_rows(gb, k), late_own.at[rank], sem))

            @pl.when(r != ro)
            def _():
                d = lax.rem(ro - r + rn, rn)
                act(pltpu.make_async_copy(w_rows(gb, k), late_send.at[d - 1, rank], sem))

    late_grads(start)
    for rank in range(plan.ranks):
        early_close(rank)
    e_copy(theirs).wait_recv()
    done = lambda copy: copy.wait_send()
    early_grads(done)
    for rank in range(plan.ranks):
        early_hops_done(rank)
    late_grads(lambda copy: copy.wait())
    rises(done, True, False)
    rises(done, False, False)
    for d, e in pairs:
        o_copy(d, e).wait_send()
        d_copy(d, e).wait_send()
    for slot in range(8):
        f_copy(slot).wait_send()
    n_copy(mine).wait_send()
    p_copy(0, t).wait_send()
    p_copy(1, across).wait_send()
    for w in range(2):
        for n in range(TILES):
            c_copy(w, n).wait_send()
            y_copy(w, n).wait_send()
    w_copy.wait_send()
    e_copy(mine).wait_send()


def middle_part(plan, o_mine, wo_across, weights, tokens, grad_out, mod_rows, cid):
    rn, count = plan.r, len(plan.early)
    rows = F_DEV * TOK_FRAME
    half = lambda dtype: pltpu.VMEM((TOK_FRAME, D), dtype)
    full = lambda dtype: pltpu.VMEM((rows, D), dtype)
    tiles = pltpu.VMEM((2, TILES, TOK_FRAME, TILE), BF16)
    return call(
        functools.partial(middle_kernel, plan),
        (
            jax.ShapeDtypeStruct((rows, D), BF16),
            jax.ShapeDtypeStruct((plan.grad_ranks, plan.ub, D), BF16),
            jax.ShapeDtypeStruct((rn - 1, plan.grad_ranks, plan.ub, D), BF16),
            jax.ShapeDtypeStruct((plan.ranks, plan.ub, D), BF16),
            jax.ShapeDtypeStruct((plan.ranks, plan.ub, D), BF16),
            jax.ShapeDtypeStruct((ZN, F_DEV, PACK, LANES), BF16),
            jax.ShapeDtypeStruct((TOK_FRAME, D), F32),
            jax.ShapeDtypeStruct((8, D), F32),
        ),
        [
            pltpu.VMEM((BROWS, D), BF16),
            pltpu.VMEM((BROWS, D), BF16),
            pltpu.VMEM((rn - 1, plan.ranks, plan.ub, D), BF16),
            pltpu.VMEM((plan.ranks, plan.ub, D), BF16),
            pltpu.VMEM((HEADS * HEAD, D), BF16),
            pltpu.VMEM((HEADS, PACK, LANES), BF16),
            half(BF16), half(F32), half(F32), half(F32), pltpu.VMEM((TOK_FRAME, 1), F32),
            full(BF16), full(BF16), full(BF16), full(F32), full(BF16),
            pltpu.VMEM((TILES, TOK_FRAME, TILE), F32), tiles, tiles, tiles, tiles,
            half(BF16), pltpu.VMEM((8, PACK, LANES), BF16),
            pltpu.VMEM((HD, D), F32), pltpu.VMEM((HD, D), BF16), pltpu.VMEM((HD, D), BF16),
            DMA((8,)), DMA((8,)), DMA((8,)), DMA((8,)), DMA((1,)), DMA((1,)),
            DMA((2, TILES)), DMA((2, TILES)), DMA((2, TILES)), DMA((2, TILES)),
            DMA((8,)), DMA((8,)), DMA, DMA, DMA, DMA, DMA((2,)), DMA((2,)),
            DMA((len(plan.late) + count,)), DMA((count, rn)), DMA((count,)), DMA((count,)), DMA((rn - 1, plan.ranks)),
            DMA((len(plan.late),)), DMA((plan.ranks,)), DMA((plan.ranks,)),
            DMA((plan.ranks,)), DMA((plan.ranks,)),
        ],
        [VM, VM, ANY, ANY, ANY, ANY, ANY, VM, VM, VM],
        cid,
        out_specs=(VM, ANY, ANY, VM, VM, VM, VM, VM),
        name="middle_part",
    )(o_mine, wo_across, *weights, tokens, grad_out, mod_rows)


def tail_kernel(
    plan, meta, q, kv, do, ot, lse, first_in, wq, tokens, dmid, mod, dm4, late_own, late_send, esum, ebuf,
    igrad, oq, ob, dall,
    keys, flipped, qs, gs, qgt, drow, acc, dq_acc, dq, kv_two, lside,
    stage, side, q_in, kv_in, dqkv, gq, own, csend, crecv, ysend, yrecv, dm, dm3, dboth,
    lstage, cb, qside, qpeer, qchain, qstage,
    q_s, q_r, k_s, k_r, x_s, x_r, c_s, c_r, y_s, y_r, e_s, e_r, h_s, h_r, m_s, m_r, t_s, t_r,
    kv_s, ls_s, ls_r, qo_s, qs_r, qp_r, qc_s, qc_r,
):
    s, t, z, r = place(plan)
    n, rn = plan.n, plan.r
    y = lax.div(t, 2)
    c = lax.rem(t, 2)
    sib = 2 * y + 1 - c
    across = lax.rem(t + 2, TP)
    mine = pl.multiple_of(c * TOK_FRAME, TOK_FRAME)
    theirs = pl.multiple_of((1 - c) * TOK_FRAME, TOK_FRAME)
    greet([(lax.rem(s + d, n), t) for d in range(1, n)] + [(s, sib), (s, across)])

    def side_copy(zs, e):
        other = lax.rem(r + e, rn)
        return remote(
            keys.at[zs * rn + other], side.at[e - 1, zs], x_s.at[zs, e - 1], x_r.at[zs, e - 1],
            z * rn + other, t,
        )

    def q_copy(zs):
        return remote(dq.at[zs], q_in.at[z], q_s.at[zs], q_r.at[z], zs * rn + r, t)

    def kv_copy(zs):
        return remote(stage.at[zs], kv_in.at[z], k_s.at[zs], k_r.at[z], zs * rn + r, t)

    def send_q(zs):
        @pl.when(z == zs)
        def _():
            q_in[zs] = dq[zs]

        @pl.when(z != zs)
        def _():
            q_copy(zs).start()

    def send_kv(zs):
        total = keys[zs * rn + r].astype(F32)
        for e in range(1, rn):
            side_copy(zs, e).wait_recv()
            total = total + side[e - 1, zs].astype(F32)
        stage[zs] = total.astype(BF16)

        @pl.when(z == zs)
        def _():
            kv_in[zs] = stage[zs]

        @pl.when(z != zs)
        def _():
            kv_copy(zs).start()

    scale = HEAD ** (-0.5)
    acc[...] = jnp.zeros_like(acc)

    def load(g, slot):
        return pltpu.make_async_copy(kv.at[g], kv_two.at[slot], kv_s.at[slot])

    load(0, 0).start()

    def sort_group(g, carry):
        slot = lax.rem(g, 2)

        @pl.when(g + 1 < n)
        def _():
            load(g + 1, 1 - slot).start()

        load(g, slot).wait()
        first = meta[2 * g] == 0
        a, b = kv_two[slot, :TOK_FRAME, :], kv_two[slot, TOK_FRAME:, :]
        keys[g, 0] = jnp.where(first, a, b)
        keys[g, 1] = jnp.where(first, b, a)
        for kind in range(2):
            flipped[kind, g] = keys[g, kind].T
        return carry

    lax.fori_loop(0, n, sort_group, 0)

    def attend_back_group(zq):
        gq = zq * rn + r
        first = meta[2 * gq] == 0
        clip = meta[2 * gq] + meta[2 * gq + 1]
        parts = []
        for kind in range(2):
            low = first if kind == 0 else jnp.logical_not(first)
            qz = padded(jnp.where(low, q[zq][:, :HEAD], q[zq][:, HEAD:]), True) * jnp.asarray(scale, BF16)
            gpack = jnp.where(low, do[zq, 0], do[zq, 1])
            grads = jnp.concatenate([gpack[:, :HEAD], gpack[:, HEAD:]], axis=0)
            out = ot[2 * zq + kind]
            logs = lse[2 * zq + kind]
            gz = padded(grads, False)
            qs[...] = qz
            gs[...] = gz
            qgt[:, :TOK_FRAME] = qz.T
            qgt[:, TOK_FRAME:] = gz.T
            drow[...] = jnp.sum(grads.astype(F32).T * out, axis=0, keepdims=True)
            dq_acc[...] = jnp.zeros_like(dq_acc)

            def block(p, inner):
                total = dq_acc[...]
                for e in range(2):
                    g = jnp.minimum(2 * p + e, gq)
                    shown = 2 * p + e <= gq
                    if kind == 1:
                        shown = shown & (meta[2 * g] + meta[2 * g + 1] == clip)
                    off = jnp.where(shown, 0.0, 1e30)
                    key = keys[g, kind]
                    pt = jnp.exp(mm(key, qgt[:, :TOK_FRAME]) - (logs + off))
                    dst = (pt * (mm(key, qgt[:, TOK_FRAME:]) - drow[...])).astype(BF16)
                    acc[kind, g] += mm(dst, qs[...]) + mm(pt.astype(BF16), gs[...])
                    total = total + mm(flipped[kind, g], dst)
                dq_acc[...] = total
                return inner

            lax.fori_loop(0, lax.div(gq + 2, 2), block, 0)
            parts.append((dq_acc[:HEAD, :] * scale).T.astype(BF16))
        dq[zq] = jnp.concatenate(
            [jnp.where(first, parts[0], parts[1]), jnp.where(first, parts[1], parts[0])], axis=1
        )
        for other in range(rn):
            g = zq * rn + other
            low = meta[2 * g] == 0
            a, b = acc[0, g].astype(BF16), acc[1, g].astype(BF16)
            keys[g, 0] = jnp.where(low, a, b)
            keys[g, 1] = jnp.where(low, b, a)

    def late(units, act):
        for k in units:
            zo, ro = plan.home(k)

            @pl.when(r == ro)
            def _():
                act(k, zo, plan.grad_rank[k])

    def late_copy(rank, below, to):
        return remote(lstage.at[rank], cb.at[below, rank], t_s.at[rank], t_r.at[below, rank], to, t)

    def late_side(rank, d):
        return remote(
            late_send.at[d - 1, rank], lside.at[d - 1, rank], ls_s.at[rank, d - 1],
            ls_r.at[rank, d - 1], z * rn + lax.rem(r + d, rn), t,
        )

    def late_sides(rank, act):
        for d in range(1, rn):
            act(late_side(rank, d))

    def late_step(k, zo, rank, here_z, above, below, final):
        @pl.when(z == here_z)
        def _():
            for d in range(1, rn):
                late_side(rank, d).wait_recv()
            if above:
                late_copy(rank, 0, s).wait_recv()
            if below:
                late_copy(rank, 1, s).wait_recv()

            def body(at):
                rows = pl.ds(at, 16)
                total = late_own[rank, rows, :].astype(F32)
                for d in range(1, rn):
                    total = total + lside[d - 1, rank, rows, :].astype(F32)
                if above:
                    total = total + cb[0, rank, rows, :].astype(F32)
                if below:
                    total = total + cb[1, rank, rows, :].astype(F32)
                if final:
                    ob[k % 3, rows, :] = total
                else:
                    lstage[rank, rows, :] = total.astype(BF16)

            loop(plan.ub, 16, body)
            if not final:
                late_copy(
                    rank, 0 if here_z > zo else 1, s - rn if here_z > zo else s + rn
                ).start()

    def late_ends(k, zo, rank):
        late_step(k, zo, rank, ZN - 1, False, False, False)
        if zo > 0:
            late_step(k, zo, rank, 0, False, False, False)

    def late_inner(here):
        def act(k, zo, rank):
            if here > zo:
                late_step(k, zo, rank, here, True, False, False)

        return act

    def late_final(k, zo, rank):
        late_step(k, zo, rank, zo, True, zo > 0, True)

    def late_done(k, zo, rank):
        @pl.when(z != zo)
        def _():
            late_copy(rank, 0, s).wait_send()

    def early_units(act):
        for k in plan.early:
            zo, ro, rank = (k // 3) // rn, (k // 3) % rn, plan.rank[k]

            @pl.when(r == ro)
            def _():
                act(k, zo, rank)

    def early_final(k, zo, rank):
        @pl.when(z == zo)
        def _():
            def body(at):
                rows = pl.ds(at, 16)
                ob[k % 3, rows, :] = esum[rank, rows, :].astype(F32) + ebuf[rank, rows, :].astype(F32)

            loop(plan.ub, 16, body)

    hq = plan.uq // CUTS

    def q_rows(k, h):
        return gq.at[pl.ds(pl.multiple_of(k * plan.uq + h * hq, hq), hq)]

    def q_sides(k, act):
        tc, ro, j = k % rn, k // 3, k // rn
        for h in range(CUTS):
            @pl.when((z > 0) & (r != tc))
            def _():
                slot = lax.rem(tc - r + rn, rn) - 1
                act(
                    remote(
                        q_rows(k, h), qside.at[slot, CUTS * j + h], qo_s.at[CUTS * k + h],
                        qs_r.at[slot, CUTS * j + h], z * rn + tc, t,
                    )
                )

            @pl.when((z == 0) & (r != ro) & (r != tc))
            def _():
                slot = lax.rem(ro - r + rn, rn) - 1
                act(
                    remote(
                        q_rows(k, h), qpeer.at[slot, CUTS * (k % 3) + h], qo_s.at[CUTS * k + h],
                        qp_r.at[slot, CUTS * (k % 3) + h], ro, t,
                    )
                )

    def q_down(at, to):
        return remote(qstage.at[at], qchain.at[at], qc_s.at[at], qc_r.at[at], to, t)

    def q_chain(here, only_j):
        top = here == ZN - 1
        for j in (only_j,):
            k = r + rn * j
            for h in range(CUTS):
                at = CUTS * j + h

                @pl.when(z == here)
                def _():
                    for d in range(1, rn):
                        remote(
                            q_rows(k, h), qside.at[d - 1, at], qo_s.at[0], qs_r.at[d - 1, at], s, t
                        ).wait_recv()
                    if not top:
                        q_down(at, s).wait_recv()
                    unit = q_rows(k, h)

                    def body(row):
                        rows = pl.ds(row, 16)
                        total = unit[rows, :].astype(F32)
                        for d in range(1, rn):
                            total = total + qside[d - 1, at, rows, :].astype(F32)
                        if not top:
                            total = total + qchain[at, rows, :].astype(F32)
                        qstage[at, rows, :] = total.astype(BF16)

                    loop(hq, 16, body)
                    q_down(at, s - rn).start()

    def q_last_copy(k, h):
        tc, ro, j = k % rn, k // 3, k // rn
        slot = (ro - tc + rn) % rn - 1
        return remote(
            qstage.at[CUTS * j + h], qpeer.at[slot, CUTS * (k % 3) + h], qc_s.at[CUTS * j + h],
            qp_r.at[slot, CUTS * (k % 3) + h], ro, t,
        )

    def q_ground(act):
        for k in range(plan.nq):
            if k % rn != k // 3:
                @pl.when((z == 0) & (r == k % rn))
                def _():
                    for h in range(CUTS):
                        act(k, h)

    def q_turn(k, h):
        at = CUTS * (k // rn) + h
        q_down(at, s).wait_recv()
        unit = q_rows(k, h)

        def body(row):
            rows = pl.ds(row, 16)
            qstage[at, rows, :] = (
                unit[rows, :].astype(F32) + qchain[at, rows, :].astype(F32)
            ).astype(BF16)

        loop(hq, 16, body)
        q_last_copy(k, h).start()

    def q_final():
        for k in range(plan.nq):
            @pl.when((z == 0) & (r == k // 3))
            def _():
                straight = k % rn == k // 3
                for h in range(CUTS):
                    at = CUTS * (k // rn) + h
                    if straight:
                        q_down(at, s).wait_recv()
                    for d in range(1, rn):
                        remote(
                            q_rows(k, h), qpeer.at[d - 1, CUTS * (k % 3) + h], qo_s.at[0],
                            qp_r.at[d - 1, CUTS * (k % 3) + h], s, t,
                        ).wait_recv()
                    unit = q_rows(k, h)

                    def body(row):
                        rows = pl.ds(row, 16)
                        total = unit[rows, :].astype(F32)
                        for d in range(1, rn):
                            total = total + qpeer[d - 1, CUTS * (k % 3) + h, rows, :].astype(F32)
                        if straight:
                            total = total + qchain[at, rows, :].astype(F32)
                        oq[k % 3, pl.ds(h * hq + row, 16), :] = total

                    loop(hq, 16, body)

    start = lambda copy: copy.start()
    done = lambda copy: copy.wait_send()
    def only(rank, act):
        return lambda k, zo, own_rank: act(k, zo, own_rank) if own_rank == rank else None

    last = plan.grad_ranks - 1
    late_sides(0, start)
    for zq in range(ZN - 1, -1, -1):
        attend_back_group(zq)
        for e in range(1, rn):
            side_copy(zq, e).start()
        send_q(zq)
        if zq == ZN - 1:
            late(plan.late, only(0, late_ends))
        else:
            send_kv(zq + 1)
    for rank in range(1, plan.grad_ranks):
        late_sides(rank, start)
    send_kv(0)
    late(plan.late, only(0, late_inner(2)))
    late(plan.late, only(0, late_inner(1)))
    late(plan.late, only(1, late_ends))
    for zs in range(ZN):
        @pl.when(z != zs)
        def _():
            remote(dq.at[0], q_in.at[zs], q_s.at[0], q_r.at[zs], s, t).wait_recv()
            remote(stage.at[0], kv_in.at[zs], k_s.at[0], k_r.at[zs], s, t).wait_recv()

    for p in range(2):
        cols = slice(p * LANES, (p + 1) * LANES)
        a, b = q_in[2 * p], q_in[2 * p + 1]
        dqkv[:TOK_FRAME, cols] = jnp.concatenate([a[:, :HEAD], b[:, :HEAD]], axis=1)
        dqkv[TOK_FRAME:, cols] = jnp.concatenate([a[:, HEAD:], b[:, HEAD:]], axis=1)
        a, b = [kv_in[2 * p + i].reshape(F_DEV * TOK_FRAME, LANES) for i in range(2)]
        dqkv[:, HD + p * LANES : HD + (p + 1) * LANES] = jnp.concatenate(
            [a[:, :HEAD], b[:, :HEAD]], axis=1
        )
        dqkv[:, 2 * HD + p * LANES : 2 * HD + (p + 1) * LANES] = jnp.concatenate(
            [a[:, HEAD:], b[:, HEAD:]], axis=1
        )

    for m in range(TILES):
        gq[m * TILE : (m + 1) * TILE, :] = mm_tn(
            first_in[:, m * TILE : (m + 1) * TILE], dqkv[...]
        ).astype(BF16)
        for k in range(m * plan.nq // TILES, (m + 1) * plan.nq // TILES):
            q_sides(k, start)

    def c_copy(w):
        return remote(csend.at[w], crecv.at[w], c_s.at[w], c_r.at[w], s, sib)

    def y_copy(w):
        return remote(ysend.at[w], yrecv.at[w], y_s.at[w], y_r.at[w], s, across)

    def pass_on(w):
        c_copy(w).wait_recv()
        ysend[w] = (own[w] + crecv[w].astype(F32)).astype(BF16)
        y_copy(w).start()

    for w in range(TILES):
        weights = wq[w * TILE : (w + 1) * TILE, :]
        csend[w] = mm_nt(dqkv[pl.ds(theirs, TOK_FRAME), :], weights).astype(BF16)
        c_copy(w).start()
        own[w] = mm_nt(dqkv[pl.ds(mine, TOK_FRAME), :], weights)
        if w:
            pass_on(w - 1)
    pass_on(TILES - 1)

    for rank in range(2, plan.grad_ranks):
        late(plan.late, only(rank, late_ends))
    q_chain(ZN - 1, 0)
    q_chain(ZN - 1, 1)
    late(plan.late, only(1, late_inner(2)))
    q_chain(2, 0)
    late(plan.late, only(last, late_inner(2)))
    q_chain(2, 1)
    q_chain(1, 0)
    late(plan.late, only(1, late_inner(1)))
    q_chain(1, 1)
    late(plan.late, only(last, late_inner(1)))

    for w in range(TILES):
        y_copy(w).wait_recv()
    row = lambda part: mod[pl.ds(c * 6 + part, 1), :]
    dm[...] = jnp.zeros_like(dm)

    def input_rows(at):
        rows = pl.ds(at, 64)
        tok_rows = pl.ds(mine + at, 64)
        grads = jnp.concatenate(
            [ysend[w, rows].astype(F32) + yrecv[w, rows].astype(F32) for w in range(TILES)], axis=1
        )
        normed, inverse = normalize(tokens[tok_rows, :].astype(F32))
        add_to(dm, 0, grads)
        add_to(dm, 1, grads * normed)
        igrad[tok_rows, :] = dmid[rows, :] + norm_back(grads * (1.0 + row(1)), normed, inverse)

    loop(TOK_FRAME, 64, input_rows)

    def e_copy(base):
        ref = igrad.at[pl.ds(base, TOK_FRAME)]
        return remote(ref, ref, e_s, e_r, s, sib)

    e_copy(mine).start()

    for block in range(6 * D // LANES):
        part, at = block // (D // LANES), block % (D // LANES)
        src = dm if part < 2 else dm4
        lane = slice(at * LANES, (at + 1) * LANES)
        from_row = part if part < 2 else part - 2
        dm3[block // MCOLS, block % MCOLS : block % MCOLS + 1, :] = src[from_row : from_row + 1, lane]
    h_copy = lambda frame: remote(dm3.at[sib], dboth.at[frame], h_s, h_r, s, sib)
    h_copy(c).start()
    dboth[c] = dm3[t]
    h_copy(1 - c).wait_recv()

    def m_copy(src):
        return remote(dboth, dall.at[s], m_s.at[src - plan.first_mod], m_r.at[s], src, t)

    for src in range(plan.first_mod, n):
        @pl.when(s == src)
        def _():
            dall[s] = dboth[...]

        @pl.when(s != src)
        def _():
            m_copy(src).start()

    q_ground(q_turn)
    late(plan.late, late_final)
    early_units(early_final)
    q_final()

    @pl.when(s >= plan.first_mod)
    def _():
        for d in range(1, n):
            other = lax.rem(s + d, n)
            remote(dboth, dall.at[other], m_s.at[0], m_r.at[other], s, t).wait_recv()

    e_copy(theirs).wait_recv()
    for zs in range(ZN):
        @pl.when(z != zs)
        def _():
            q_copy(zs).wait_send()
            kv_copy(zs).wait_send()

        for e in range(1, rn):
            side_copy(zs, e).wait_send()
    for rank in range(plan.grad_ranks):
        late_sides(rank, done)
    late(plan.late, late_done)
    for k in range(plan.nq):
        q_sides(k, done)

    @pl.when(z > 0)
    def _():
        for at in range(2 * CUTS):
            q_down(at, s).wait_send()

    q_ground(lambda k, h: q_last_copy(k, h).wait_send())
    for w in range(TILES):
        c_copy(w).wait_send()
        y_copy(w).wait_send()
    e_copy(mine).wait_send()
    h_copy(c).wait_send()
    for src in range(plan.first_mod, n):
        @pl.when(s != src)
        def _():
            m_copy(src).wait_send()


def tail_part(plan, meta, q, kv, do, ot, lse, first_in, wq, tokens, dmid, mod_rows, dm4, late_own, late_send, esum, ebuf, cid):
    n, rn = plan.n, plan.r
    rows = F_DEV * TOK_FRAME
    tiles = pltpu.VMEM((TILES, TOK_FRAME, TILE), BF16)
    mods = n - plan.first_mod
    return call(
        functools.partial(tail_kernel, plan),
        (
            jax.ShapeDtypeStruct((rows, D), F32),
            jax.ShapeDtypeStruct((3, plan.uq, QKV), F32),
            jax.ShapeDtypeStruct((3, plan.ub, D), F32),
            jax.ShapeDtypeStruct((n, F_DEV, 16, LANES), F32),
        ),
        [
            pltpu.VMEM((n, 2, TOK_FRAME, LANES), BF16),
            pltpu.VMEM((2, n, LANES, TOK_FRAME), BF16),
            pltpu.VMEM((TOK_FRAME, LANES), BF16),
            pltpu.VMEM((TOK_FRAME, LANES), BF16),
            pltpu.VMEM((LANES, 2 * TOK_FRAME), BF16),
            pltpu.VMEM((1, TOK_FRAME), F32),
            pltpu.VMEM((2, n, TOK_FRAME, LANES), F32),
            pltpu.VMEM((LANES, TOK_FRAME), F32),
            pltpu.VMEM((ZN, TOK_FRAME, LANES), BF16),
            pltpu.VMEM((2, rows, LANES), BF16),
            pltpu.VMEM((rn - 1, plan.grad_ranks, plan.ub, D), BF16),
            pltpu.VMEM((ZN, 2, TOK_FRAME, LANES), BF16),
            pltpu.VMEM((rn - 1, ZN, 2, TOK_FRAME, LANES), BF16),
            pltpu.VMEM((ZN, TOK_FRAME, LANES), BF16),
            pltpu.VMEM((ZN, 2, TOK_FRAME, LANES), BF16),
            pltpu.VMEM((rows, QKV), BF16),
            pltpu.VMEM((D, QKV), BF16),
            pltpu.VMEM((TILES, TOK_FRAME, TILE), F32), tiles, tiles, tiles, tiles,
            pltpu.VMEM((8, D), F32),
            pltpu.VMEM((TP, 16, LANES), F32),
            pltpu.VMEM((F_DEV, 16, LANES), F32),
            pltpu.VMEM((plan.grad_ranks, plan.ub, D), BF16),
            pltpu.VMEM((2, plan.grad_ranks, plan.ub, D), BF16),
            pltpu.VMEM((rn - 1, 2 * CUTS, plan.uq // CUTS, QKV), BF16),
            pltpu.VMEM((rn - 1, 3 * CUTS, plan.uq // CUTS, QKV), BF16),
            pltpu.VMEM((2 * CUTS, plan.uq // CUTS, QKV), BF16),
            pltpu.VMEM((2 * CUTS, plan.uq // CUTS, QKV), BF16),
            DMA((ZN,)), DMA((ZN,)), DMA((ZN,)), DMA((ZN,)), DMA((ZN, rn - 1)), DMA((ZN, rn - 1)),
            DMA((TILES,)), DMA((TILES,)), DMA((TILES,)), DMA((TILES,)),
            DMA, DMA, DMA, DMA, DMA((mods,)), DMA((n,)),
            DMA((plan.grad_ranks,)), DMA((2, plan.grad_ranks)),
            DMA((2,)), DMA((plan.grad_ranks, rn - 1)), DMA((plan.grad_ranks, rn - 1)),
            DMA((CUTS * plan.nq,)),
            DMA((rn - 1, 2 * CUTS)), DMA((rn - 1, 3 * CUTS)), DMA((2 * CUTS,)), DMA((2 * CUTS,)),
        ],
        [SM, VM, ANY] + [VM] * 10 + [ANY, VM, VM],
        cid,
        name="tail_part",
    )(meta, q, kv, do, ot, lse, first_in, wq, tokens, dmid, mod_rows, dm4, late_own, late_send, esum, ebuf)


def adam_kernel(plan, meta, oq, ob, cond, dmod, master, one, two, average, n_master, n_one, n_two, n_average):
    s = meta[0]
    rate = RATE_FACTOR * D ** (-0.5)
    scale_one = 1.0 / (1.0 - BETA_FIRST**STEP)
    scale_two = 1.0 / (1.0 - BETA_SECOND**STEP)

    def update(rows, grad):
        first = BETA_FIRST * one[rows, :] + (1.0 - BETA_FIRST) * grad
        second = BETA_SECOND * two[rows, :] + (1.0 - BETA_SECOND) * grad * grad
        weight = master[rows, :]
        weight = weight - rate * (
            (first * scale_one) / (jnp.sqrt(second * scale_two) + ADAM_EPSILON)
            + WEIGHT_DECAY * weight
        )
        n_one[rows, :] = first
        n_two[rows, :] = second
        n_master[rows, :] = weight
        n_average[rows, :] = AVERAGE_RATE * average[rows, :] + (1.0 - AVERAGE_RATE) * weight

    if True:
        k = 3 * s + lax.div(pl.program_id(0), ADAM_CUTS)
        base = 0

        def from_matrix(kind):
            src = oq if kind == "q" else ob
            rows = (plan.uq if kind == "q" else plan.ub) // ADAM_CUTS
            cols = (QKV if kind == "q" else D) // LANES
            for j in range(cols):
                update(
                    pl.ds(base + j, rows, stride=cols), src[0, :, j * LANES : (j + 1) * LANES]
                )

        by_kind(plan, k, from_matrix)

        @pl.when(k >= plan.nb)
        def _():
            count = plan.um // ADAM_CUTS
            part = pl.multiple_of(lax.rem(pl.program_id(0), ADAM_CUTS) * count, count)
            at = cond[k - plan.nb, pl.ds(part, count), :]
            for j in range(MCOLS):
                update(
                    pl.ds(base + j, count, stride=MCOLS),
                    mm(at, dmod[pl.ds(j, plan.frames, stride=16), :].astype(BF16)),
                )


def adam(plan, meta, oq, ob, cond_rows, dmod, master, one, two, average):
    shape = jax.ShapeDtypeStruct(master.shape, F32)
    flat = pl.BlockSpec((plan.flat_rows // ADAM_CUTS, LANES), lambda i: (i, 0))
    unit = lambda rows, cols: pl.BlockSpec(
        (1, rows // ADAM_CUTS, cols), lambda i: (lax.div(i, ADAM_CUTS), lax.rem(i, ADAM_CUTS), 0)
    )
    whole = lambda x: pl.BlockSpec(x.shape, lambda i: (0,) * x.ndim)
    return pl.pallas_call(
        functools.partial(adam_kernel, plan),
        out_shape=(shape,) * 4,
        grid=(3 * ADAM_CUTS,),
        in_specs=[SM, unit(plan.uq, QKV), unit(plan.ub, D), whole(cond_rows), whole(dmod)] + [flat] * 4,
        out_specs=(flat,) * 4,
        compiler_params=pltpu.CompilerParams(vmem_limit_bytes=VMEM_LIMIT),
        name="adam",
    )(meta, oq, ob, cond_rows, dmod, master, one, two, average)


def local(
    tokens,
    grad_out,
    noise_level,
    context_mask,
    frame_clip,
    level_table,
    master,
    moment_one,
    moment_two,
    average,
):
    plan = Plan(lax.axis_size("seq"))
    s = lax.axis_index("seq")
    t = lax.axis_index("tp")
    flat = lambda x: x.reshape(-1, LANES)

    effective = noise_level * (1 - context_mask)
    condition = jax.nn.silu(
        jnp.take(level_table, effective, axis=0, mode="clip").astype(F32)
    ).astype(BF16)
    cond_units = condition.reshape(plan.frames, plan.nm, plan.um).transpose(1, 0, 2)

    meta = frame_clip.astype(jnp.int32)
    (
        wq, w_out, w_side, w_early, w_below, w_beside, wo_across, mod_rows, first_in, q_mine, kv_all,
        o_mine, o_rows, lse,
    ) = head_part(plan, meta, flat(master), cond_units, tokens, 0)
    result, late_own, late_send, early_sum, early_in, do_mine, middle_grad, mod_four = middle_part(
        plan, o_mine, wo_across, (w_out, w_side, w_beside, w_early, w_below),
        tokens, grad_out, mod_rows, 2
    )
    input_grad, own_q, own_b, mod_all = tail_part(
        plan, meta, q_mine, kv_all, do_mine, o_rows, lse, first_in, wq, tokens, middle_grad,
        mod_rows, mod_four, late_own, late_send, early_sum, early_in, 3,
    )
    updated = adam(
        plan,
        s[None].astype(jnp.int32),
        own_q,
        own_b,
        cond_units.transpose(0, 2, 1),
        flat(mod_all),
        flat(master),
        flat(moment_one),
        flat(moment_two),
        flat(average),
    )
    new_master, new_one, new_two, new_average = [x.reshape(master.shape) for x in updated]
    return (result, input_grad, new_master, new_one, new_two, new_average)


def solution(mesh):
    token_spec = P("seq", None)
    weight_spec = P("tp", "seq")
    in_specs = (token_spec, token_spec, P(), P(), P(), P()) + (weight_spec,) * 4
    out_specs = (token_spec, token_spec) + (weight_spec,) * 4
    return jax.shard_map(local, mesh=mesh, in_specs=in_specs, out_specs=out_specs, check_vma=False)
```

```python
import functools

import jax
import jax.numpy as jnp
from jax import lax
from jax.experimental import pallas as pl
from jax.experimental.pallas import tpu as pltpu
from jax.sharding import PartitionSpec as P

D = 1024
HEADS = 16
HEAD = 64
FF = 4096
TOK_FRAME = 384
STEP = 7
TP = 4
ZN = 4
HD = HEADS * HEAD // TP
QKV = 3 * HD
FT = FF // TP
MT = 6 * D // TP
F_DEV = 2
BROWS = HD + 2 * FT
LANES = 128
MCOLS = MT // LANES
PACK = TOK_FRAME // 2
TILE = 256
TILES = D // TILE
CUTS = 4
ADAM_CUTS = 2

NORM_EPSILON = 1e-06
RATE_FACTOR = 2.5
BETA_FIRST = 0.5
BETA_SECOND = 0.5
ADAM_EPSILON = 1e-08
WEIGHT_DECAY = 0.01
AVERAGE_RATE = 0.9
GELU_A = 0.7978845608028654
GELU_B = 0.044715
MESH = pl.DeviceIdType.MESH
VM = pl.BlockSpec(memory_space=pltpu.VMEM)
SM = pl.BlockSpec(memory_space=pltpu.SMEM)
ANY = pl.BlockSpec(memory_space=pl.ANY)
DMA = pltpu.SemaphoreType.DMA
F32 = jnp.float32
BF16 = jnp.bfloat16
VMEM_LIMIT = 60 * 2**20


def mm(left, right):
    return jnp.dot(left, right, preferred_element_type=F32)


def mm_tn(left, right):
    return lax.dot_general(left, right, (((0,), (0,)), ((), ())), preferred_element_type=F32)


def mm_nt(left, right):
    return lax.dot_general(left, right, (((1,), (1,)), ((), ())), preferred_element_type=F32)


def normalize(rows):
    centred = rows - jnp.mean(rows, axis=1, keepdims=True)
    inverse = lax.rsqrt(jnp.mean(centred * centred, axis=1, keepdims=True) + NORM_EPSILON)
    return (centred * inverse, inverse)


def norm_back(grads, normed, inverse):
    return inverse * (
        grads
        - jnp.mean(grads, axis=1, keepdims=True)
        - normed * jnp.mean(grads * normed, axis=1, keepdims=True)
    )


def loop(count, step, body):
    def turn(i, carry):
        body(pl.multiple_of(i * step, step))
        return carry

    lax.fori_loop(0, count // step, turn, 0)


def add_to(ref, row, values):
    ref[pl.ds(row, 1), :] += jnp.sum(values, axis=0, keepdims=True)


class Plan:
    def __init__(self, seq_count):
        self.n = seq_count
        self.r = seq_count // ZN
        self.shard = (D * QKV + BROWS * D + D * MT) // seq_count
        self.unit = self.shard // 3
        self.uq = self.unit // QKV
        self.ub = self.unit // D
        self.um = self.unit // MT
        self.nq = D // self.uq
        self.nb = self.nq + BROWS // self.ub
        self.nm = D // self.um
        self.first_mod = self.nb // 3
        self.half = (self.nq + self.nb) // 2
        self.flat_rows = self.unit // LANES
        self.frames = seq_count * F_DEV
        self.late = list(range(self.nq, self.half))
        self.early = list(range(self.half, self.nb))
        self.outs = self.late[: -(-HD // self.ub)]
        self.sided = self.late[len(self.outs) :]
        self.rank, self.ranks = self.ranked(self.early)
        self.late_rank, self.late_ranks = self.ranked(self.sided)
        self.grad_rank, self.grad_ranks = self.ranked(self.late)

    def ranked(self, units):
        seen, rank = {}, {}
        for k in units:
            column = self.home(k)[1]
            rank[k] = seen.get(column, 0)
            seen[column] = rank[k] + 1
        return rank, max(seen.values())

    def home(self, k):
        return (k // 3) // self.r, (k // 3) % self.r


def place(plan):
    s = lax.axis_index("seq")
    t = lax.axis_index("tp")
    return s, t, lax.div(s, plan.r), lax.rem(s, plan.r)


def remote(src, dst, send_sem, recv_sem, s, t):
    return pltpu.make_async_remote_copy(
        src_ref=src,
        dst_ref=dst,
        send_sem=send_sem,
        recv_sem=recv_sem,
        device_id=(s, t),
        device_id_type=MESH,
    )


def greet(peers):
    barrier = pltpu.get_barrier_semaphore()
    for s, t in peers:
        pl.semaphore_signal(barrier, inc=1, device_id=(s, t), device_id_type=MESH)
    pl.semaphore_wait(barrier, len(peers))


def by_kind(plan, k, act, low=0, high=None):
    high = plan.nb if high is None else high
    q_high, b_low = min(plan.nq, high), max(plan.nq, low)
    if low < q_high:
        @pl.when((k >= low) & (k < q_high))
        def _():
            act("q")

    if b_low < high:
        @pl.when((k >= b_low) & (k < high))
        def _():
            act("b")


def unit_of(plan, k, kind, wq, wb):
    if kind == "q":
        return wq.at[pl.ds(pl.multiple_of(k * plan.uq, plan.uq), plan.uq)]
    return wb.at[pl.ds(pl.multiple_of((k - plan.nq) * plan.ub, plan.ub), plan.ub)]


def call(kernel, outs, scratch, ins, cid=None, cost=None, name=None, out_specs=None):
    params = dict(vmem_limit_bytes=VMEM_LIMIT)
    if cid is not None:
        params.update(collective_id=cid, has_side_effects=True)
    return pl.pallas_call(
        kernel,
        out_shape=outs,
        in_specs=ins,
        out_specs=out_specs or jax.tree.map(lambda _: VM, outs),
        scratch_shapes=scratch,
        compiler_params=pltpu.CompilerParams(**params),
        cost_estimate=cost,
        name=name,
    )


def head_kernel(
    plan, meta, master, cond, tokens,
    wq, w_out, w_side, w_early, w_below, w_beside, wo_across, mods, first_in, q_out, kv_out, o, ot, lse,
    own_b, pool, flipped, qt, m_ref, l_ref, acc, tile, macc, mpart, mrecv, mod, norm, q_send, kv_send,
    qp_s, qc_s, q_r, wo_s, wo_r, ws_s, ws_r, we_s, we_r, loc_s, m_s, m_r, t_s, t_r, as_, ar, ks, kr, xs, xr,
    bl_s, bl_r, bs_s, bs_r, oa_s, oa_r,
):
    s, t, z, r = place(plan)
    n, rn = plan.n, plan.r
    greet(
        [(lax.rem(s + d, n), t) for d in range(1, n)]
        + [(s, lax.rem(t + d, TP)) for d in range(1, TP)]
    )
    start = lambda copy: copy.start()
    done = lambda copy: copy.wait_send()
    cut = plan.uq // CUTS

    def q_rows(k, h):
        return wq.at[pl.ds(pl.multiple_of(k * plan.uq + h * cut, cut), cut)]

    def q_copy(k, h, sem, to_s):
        ref = q_rows(k, h)
        return remote(ref, ref, sem, q_r.at[CUTS * k + h], to_s, t)

    def q_arrived(k, h):
        q_copy(k, h, qc_s.at[0, 0], s).wait_recv()

    def column(j):
        return r + rn * lax.rem(j + r, 2)

    def q_own(i, act):
        k = 3 * s + i

        @pl.when(k < plan.nq)
        def _():
            for h in range(CUTS):
                for d in range(1, rn):
                    act(q_copy(k, h, qp_s.at[CUTS * i + h, d - 1], lax.rem(r + d, rn)))

    def q_line(act, wait, whole=False):
        for j in range(2):
            k = column(j)
            for h in range(CUTS):
                if wait:
                    @pl.when((z > 0) | (lax.div(k, 3) != r))
                    def _():
                        q_arrived(k, h)

                @pl.when((z < ZN - 1) & ((z > 0) | (lax.div(k, 3) != r) | whole))
                def _():
                    act(q_copy(k, h, qc_s.at[CUTS * j + h, 0], s + rn))

                @pl.when(z > 0)
                def _():
                    for d in range(1, rn):
                        act(
                            q_copy(
                                k, h, qc_s.at[CUTS * j + h, d], z * rn + lax.rem(r + d, rn)
                            )
                        )

    def slot(k):
        if k in plan.outs:
            at = k - plan.nq
            return w_out.at[at], wo_s.at[at], wo_r.at[at]
        if k in plan.sided:
            at = plan.late_rank[k]
            return w_side.at[at], ws_s.at[at], ws_r.at[at]
        return w_early.at[k - plan.half], we_s.at[plan.rank[k]], we_r.at[k - plan.half]

    def along(k, src, act, up):
        dst, send_sem, recv_sem = slot(k)
        if up and k < plan.half:
            @pl.when(z < ZN - 1)
            def _():
                act(remote(src, dst, send_sem.at[0], recv_sem, s + rn, t))

        if not up:
            @pl.when(z > 0)
            def _():
                act(remote(src, dst, send_sem.at[1], recv_sem, s - rn, t))

    def beside(k, src, act):
        if k not in plan.outs:
            return
        dst, send_sem, recv_sem = slot(k)
        for d in range(1, rn):
            act(
                remote(
                    src, dst, send_sem.at[1 + d], recv_sem, z * rn + lax.rem(r + d, rn), t
                )
            )

    def arrived(k):
        dst, send_sem, recv_sem = slot(k)
        remote(own_b.at[0], dst, send_sem.at[0], recv_sem, s, t).wait_recv()

    def keep(k):
        return pltpu.make_async_copy(own_b.at[k % 3], slot(k)[0], loc_s.at[k % 3])

    def owned(units, act):
        for k in units:
            @pl.when(s == k // 3)
            def _():
                act(k, own_b.at[k % 3])

    def pass_along(units, d, act, wait):
        for k in units:
            zo, ro = plan.home(k)
            if k < plan.half and zo + d < (ZN - 1 if k in plan.sided else ZN):
                @pl.when((r == ro) & (z == zo + d))
                def _():
                    if wait:
                        arrived(k)
                    along(k, slot(k)[0], act, True)
                    beside(k, slot(k)[0], act)

            if zo - d >= (0 if k in plan.outs else 1):
                @pl.when((r == ro) & (z == zo - d))
                def _():
                    if wait:
                        arrived(k)
                    along(k, slot(k)[0], act, False)
                    beside(k, slot(k)[0], act)

    def settle(k, low):
        zo, ro = plan.home(k)

        @pl.when((r == ro) & ((z == 0) & (zo > 0) if low else (z == ZN - 1) & (zo < ZN - 1)))
        def _():
            arrived(k)

    def hop(k, act):
        zo, ro = plan.home(k)

        @pl.when(s == k // 3)
        def _():
            act(remote(own_b.at[k % 3], w_below.at[k % 3], bl_s.at[k % 3], bl_r.at[k % 3], s + rn, t))

    def hopped(k):
        zo, ro = plan.home(k)

        @pl.when((r == ro) & (z == zo + 1))
        def _():
            remote(own_b.at[0], w_below.at[k % 3], bl_s.at[0], bl_r.at[k % 3], s, t).wait_recv()

    def share(k, act, low=None):
        rank = plan.late_rank[k]
        part = True if low is None else (z <= 1) == low

        @pl.when((r == plan.home(k)[1]) & part)
        def _():
            for d in range(1, rn):
                act(
                    remote(
                        w_side.at[rank], w_beside.at[d - 1, rank], bs_s.at[rank, d - 1],
                        bs_r.at[d - 1, rank], z * rn + lax.rem(r + d, rn), t,
                    )
                )

    def shared(k):
        rank = plan.late_rank[k]

        @pl.when(r != plan.home(k)[1])
        def _():
            d = lax.rem(r - plan.home(k)[1] + rn, rn)
            remote(
                w_side.at[0], w_beside.at[d - 1, rank], bs_s.at[0, 0], bs_r.at[d - 1, rank], s, t
            ).wait_recv()

    def out_copy(w):
        count = min(plan.ub, HD - w * plan.ub)
        return remote(
            w_out.at[w].at[pl.ds(0, count)], wo_across.at[pl.ds(w * plan.ub, count)],
            oa_s.at[w], oa_r.at[w], s, lax.rem(t + 2, TP),
        )

    def sort_group(g):
        first = meta[2 * g] == 0
        a, b = kv_out[g, :TOK_FRAME, :], kv_out[g, TOK_FRAME:, :]
        pool[g, 0] = jnp.where(first, a, b)
        pool[g, 1] = jnp.where(first, b, a)
        for kind in range(2):
            flipped[kind, g] = pool[g, kind].T

    def attend_group(zq):
        gq = zq * rn + r
        first = meta[2 * gq] == 0
        clip = meta[2 * gq] + meta[2 * gq + 1]
        parts = []
        for kind in range(2):
            low = first if kind == 0 else jnp.logical_not(first)
            rows = jnp.where(low, q_out[zq][:, :HEAD], q_out[zq][:, HEAD:])
            qt[...] = (padded(rows, True) * jnp.asarray(HEAD ** (-0.5), BF16)).T
            m_ref[...] = jnp.full_like(m_ref, -1e30)
            l_ref[...] = jnp.zeros_like(l_ref)
            acc[...] = jnp.zeros_like(acc)

            def block(p, inner):
                pair = []
                m_old = m_ref[...]
                m_new = m_old
                for e in range(2):
                    g = jnp.minimum(2 * p + e, gq)
                    shown = 2 * p + e <= gq
                    if kind == 1:
                        shown = shown & (meta[2 * g] + meta[2 * g + 1] == clip)
                    off = jnp.where(shown, 0.0, 1e30)
                    st = mm(pool[g, kind], qt[...])
                    m_new = jnp.maximum(m_new, jnp.max(st, axis=0, keepdims=True) - off)
                    pair.append((g, st, off))
                alpha = jnp.exp(m_old - m_new)
                total, out = l_ref[...] * alpha, acc[...] * alpha
                for g, st, off in pair:
                    weights = jnp.exp(st - (m_new + off))
                    total = total + jnp.sum(weights, axis=0, keepdims=True)
                    out = out + mm(flipped[kind, g], weights.astype(BF16))
                m_ref[...] = m_new
                l_ref[...] = total
                acc[...] = out
                return inner

            lax.fori_loop(0, lax.div(gq + 2, 2), block, 0)
            total = l_ref[...]
            out = acc[HEAD:, :] / total
            ot[2 * zq + kind] = out
            lse[2 * zq + kind] = m_ref[...] + jnp.log(total)
            rows = out.T
            parts.append(jnp.concatenate([rows[:PACK], rows[PACK:]], axis=1).astype(BF16))
        o[zq, 0] = jnp.where(first, parts[0], parts[1])
        o[zq, 1] = jnp.where(first, parts[1], parts[0])

    units = plan.late + plan.early
    first_up = [k for k in plan.late if k % 3 == 0 and plan.home(k)[0] > 0]
    later_up = [k for k in plan.late if k not in first_up]

    def fill(i, kind):
        k = 3 * s + i
        base = i * plan.flat_rows
        rows, cols = (plan.uq, QKV // LANES) if kind == "q" else (plan.ub, D // LANES)
        at = pl.multiple_of(k * plan.uq, plan.uq)
        for j in range(cols):
            values = master[pl.ds(base + j, rows, stride=cols), :].astype(BF16)
            if kind == "q":
                wq[pl.ds(at, rows), j * LANES : (j + 1) * LANES] = values
            else:
                own_b[i, :, j * LANES : (j + 1) * LANES] = values

    for away in (True, False):
        for i in range(3):
            k = 3 * s + i

            @pl.when((k < plan.nq) & ((lax.rem(k, rn) != r) == away))
            def _():
                fill(i, "q")
                q_own(i, start)
                if not away:
                    at = lax.div(k, rn)
                    slot_j = lax.rem(at + r, 2)
                    for h in range(CUTS):
                        q_copy(k, h, qc_s.at[CUTS * slot_j + h, 0], s + rn).start()

    for i in range(3):
        @pl.when((3 * s + i >= plan.nq) & (3 * s + i < plan.nb))
        def _():
            fill(i, "b")

    @pl.when(z == 0)
    def _():
        q_line(start, True)

    owned(units, lambda k, src: along(k, src, start, False))
    owned(first_up, lambda k, src: along(k, src, start, True))
    owned(units, lambda k, src: keep(k).start())

    macc[...] = jnp.zeros_like(macc)
    for i in range(3):
        k = 3 * s + i
        base = i * plan.flat_rows

        @pl.when(k >= plan.nb)
        def _():
            for j in range(MCOLS):
                tile[:, j * LANES : (j + 1) * LANES] = master[
                    pl.ds(base + j, plan.um, stride=MCOLS), :
                ].astype(BF16)
            macc[...] += mm(cond[k - plan.nb], tile[...])

    fm = plan.first_mod

    def m_copy(d):
        to = lax.rem(s + d, n)
        return remote(mpart.at[to], mrecv.at[s - fm], m_s.at[d - 1], m_r.at[s - fm], to, t)

    @pl.when(s >= fm)
    def _():
        for f in range(plan.frames):
            for j in range(MCOLS):
                mpart[f // F_DEV, pl.ds((f % F_DEV) * MCOLS + j, 1), :] = macc[
                    pl.ds(f, 1), j * LANES : (j + 1) * LANES
                ]
        mrecv[s - fm] = mpart[s]
        for d in range(1, n):
            m_copy(d).start()

    def norm_rows(at):
        rows = pl.ds(at, 64)
        norm[rows, :] = normalize(tokens[rows, :].astype(F32))[0]

    loop(F_DEV * TOK_FRAME, 64, norm_rows)

    @pl.when(z > 0)
    def _():
        q_line(start, True)

    owned(plan.outs, lambda k, src: along(k, src, start, True))
    owned([k for k in later_up if k not in plan.outs], lambda k, src: along(k, src, start, True))
    owned(units, lambda k, src: beside(k, src, start))
    pass_along(first_up + plan.early, 1, start, True)

    for src in range(fm, n):
        @pl.when(s != src)
        def _():
            remote(mpart.at[0], mrecv.at[src - fm], m_s.at[0], m_r.at[src - fm], s, t).wait_recv()

    total = mrecv[0]
    for src in range(1, n - fm):
        total = total + mrecv[src]
    mod[t] = total

    def t_copy(d):
        return remote(mod.at[t], mod.at[t], t_s.at[d - 1], t_r.at[t], s, lax.rem(t + d, TP))

    for d in range(1, TP):
        t_copy(d).start()
    for d in range(1, TP):
        other = lax.rem(t + d, TP)
        remote(mod.at[t], mod.at[other], t_s.at[0], t_r.at[other], s, t).wait_recv()
    for f in range(F_DEV):
        for block in range(TP * MCOLS):
            part, at = block // (D // LANES), block % (D // LANES)
            mods[f * 6 + part : f * 6 + part + 1, at * LANES : (at + 1) * LANES] = mod[
                block // MCOLS, f * MCOLS + block % MCOLS : f * MCOLS + block % MCOLS + 1, :
            ]

    def affine(f):
        def body(at):
            rows = pl.ds(f * TOK_FRAME + at, 64)
            first_in[rows, :] = (
                norm[rows, :] * (1.0 + mods[f * 6 + 1 : f * 6 + 2, :]) + mods[f * 6 : f * 6 + 1, :]
            ).astype(BF16)

        loop(TOK_FRAME, 64, body)

    for f in range(F_DEV):
        affine(f)

    for k in range(plan.nq):
        for h in range(CUTS):
            if rn > 1:
                at_zero = (z == 0) & (k // 3 != r) & (k % rn != r)

                @pl.when(at_zero | (z > 0) & (k % rn != r))
                def _():
                    q_arrived(k, h)

    keys = mm(first_in[...], wq[:, HD : 2 * HD]).astype(BF16)
    values = mm(first_in[...], wq[:, 2 * HD :]).astype(BF16)
    for h in range(ZN):
        cols = slice(h * HEAD, (h + 1) * HEAD)
        kv_send[h] = jnp.concatenate([keys[:, cols], values[:, cols]], axis=1)

    def kv_copy(d):
        h = lax.rem(z + d, ZN)
        return remote(kv_send.at[h], kv_out.at[s], ks.at[d - 1], kr.at[z], h * rn + r, t)

    def a_copy(d):
        h = lax.rem(z + d, ZN)
        return remote(q_send.at[h], q_out.at[z], as_.at[d - 1], ar.at[z], h * rn + r, t)

    def side_copy(zs, e):
        at = zs * rn + r
        ref = kv_out.at[at]
        return remote(ref, ref, xs.at[zs, e - 1], xr.at[at], z * rn + lax.rem(r + e, rn), t)

    for d in range(1, ZN):
        kv_copy(d).start()
    kv_out[s] = kv_send[z]
    for e in range(1, rn):
        side_copy(z, e).start()
    queries = mm(first_in[...], wq[:, :HD]).astype(BF16)
    for h in range(ZN):
        cols = slice(h * HEAD, (h + 1) * HEAD)
        q_send[h] = jnp.concatenate([queries[:TOK_FRAME, cols], queries[TOK_FRAME:, cols]], axis=1)
    for d in range(1, ZN):
        a_copy(d).start()
    q_out[z] = q_send[z]

    rest = [k for k in plan.sided if k not in first_up]
    pass_along(plan.outs + rest, 1, start, True)
    owned(units, lambda k, src: keep(k).wait())
    for k in plan.sided:
        settle(k, True)
        share(k, start, True)

    def kv_come(zs):
        @pl.when(z != zs)
        def _():
            remote(kv_send.at[0], kv_out.at[zs * rn + r], ks.at[0], kr.at[zs], s, t).wait_recv()
            for e in range(1, rn):
                side_copy(zs, e).start()

    def ready(zq):
        for e in range(1, rn):
            at = zq * rn + lax.rem(r + e, rn)
            remote(kv_out.at[at], kv_out.at[at], xs.at[0, 0], xr.at[at], s, t).wait_recv()
        for other in range(rn):
            sort_group(zq * rn + other)

        @pl.when(z != zq)
        def _():
            remote(q_send.at[0], q_out.at[zq], as_.at[0], ar.at[zq], s, t).wait_recv()

    kv_come(0)
    kv_come(1)
    pass_along(plan.outs, 2, start, True)
    kv_come(2)
    kv_come(3)
    for k in plan.early:
        hop(k, start)
    ready(0)
    attend_group(0)
    pass_along(plan.outs, 3, start, True)
    ready(1)
    attend_group(1)
    for d in range(2, ZN):
        pass_along(plan.sided, d, start, True)
    for k in plan.sided:
        settle(k, False)
        share(k, start, False)
    ready(2)
    attend_group(2)
    for k in plan.outs:
        @pl.when(r != plan.home(k)[1])
        def _():
            arrived(k)

    for w in range(len(plan.outs)):
        out_copy(w).start()
    ready(3)
    attend_group(3)
    for k in plan.early:
        hopped(k)
        zo, ro = plan.home(k)
        if zo > 0:
            @pl.when((r == ro) & (z == 0))
            def _():
                arrived(k)

    for k in plan.sided:
        shared(k)
    for w in range(len(plan.outs)):
        out_copy(w).wait()

    for k in plan.early:
        hop(k, done)
    for k in plan.sided:
        share(k, done)
    for i in range(3):
        q_own(i, done)
    q_line(done, False, True)
    owned(units, lambda k, src: along(k, src, done, False))
    owned(plan.late, lambda k, src: along(k, src, done, True))
    owned(units, lambda k, src: beside(k, src, done))
    for d in range(1, ZN):
        pass_along(units, d, done, False)

    @pl.when(s >= fm)
    def _():
        for d in range(1, n):
            m_copy(d).wait_send()

    for d in range(1, TP):
        t_copy(d).wait_send()
    for d in range(1, ZN):
        kv_copy(d).wait_send()
        a_copy(d).wait_send()
    for zs in range(ZN):
        for e in range(1, rn):
            side_copy(zs, e).wait_send()


def head_part(plan, meta, master, cond_units, tokens, cid):
    n, rn = plan.n, plan.r
    mrows = F_DEV * MCOLS
    rows = F_DEV * TOK_FRAME
    mods = n - plan.first_mod
    return call(
        functools.partial(head_kernel, plan),
        (
            jax.ShapeDtypeStruct((D, QKV), BF16),
            jax.ShapeDtypeStruct((len(plan.outs), plan.ub, D), BF16),
            jax.ShapeDtypeStruct((plan.late_ranks, plan.ub, D), BF16),
            jax.ShapeDtypeStruct((len(plan.early), plan.ub, D), BF16),
            jax.ShapeDtypeStruct((3, plan.ub, D), BF16),
            jax.ShapeDtypeStruct((rn - 1, plan.late_ranks, plan.ub, D), BF16),
            jax.ShapeDtypeStruct((HD, D), BF16),
            jax.ShapeDtypeStruct((F_DEV * 6, D), F32),
            jax.ShapeDtypeStruct((rows, D), BF16),
            jax.ShapeDtypeStruct((ZN, TOK_FRAME, LANES), BF16),
            jax.ShapeDtypeStruct((n, rows, LANES), BF16),
            jax.ShapeDtypeStruct((ZN, F_DEV, PACK, LANES), BF16),
            jax.ShapeDtypeStruct((ZN * F_DEV, HEAD, TOK_FRAME), F32),
            jax.ShapeDtypeStruct((ZN * F_DEV, 1, TOK_FRAME), F32),
        ),
        [
            pltpu.VMEM((3, plan.ub, D), BF16),
            pltpu.VMEM((n, 2, TOK_FRAME, LANES), BF16),
            pltpu.VMEM((2, n, LANES, TOK_FRAME), BF16),
            pltpu.VMEM((LANES, TOK_FRAME), BF16),
            pltpu.VMEM((1, TOK_FRAME), F32),
            pltpu.VMEM((1, TOK_FRAME), F32),
            pltpu.VMEM((LANES, TOK_FRAME), F32),
            pltpu.VMEM((plan.um, MT), BF16),
            pltpu.VMEM((plan.frames, MT), F32),
            pltpu.VMEM((n, mrows, LANES), F32),
            pltpu.VMEM((mods, mrows, LANES), F32),
            pltpu.VMEM((TP, mrows, LANES), F32),
            pltpu.VMEM((rows, D), F32),
            pltpu.VMEM((ZN, TOK_FRAME, LANES), BF16),
            pltpu.VMEM((ZN, rows, LANES), BF16),
            DMA((3 * CUTS, rn - 1)), DMA((2 * CUTS, rn)), DMA((CUTS * plan.nq,)),
            DMA((len(plan.outs), rn + 1)), DMA((len(plan.outs),)),
            DMA((plan.late_ranks, 2)), DMA((plan.late_ranks,)),
            DMA((plan.ranks, rn + 1)), DMA((len(plan.early),)), DMA((3,)),
            DMA((n - 1,)), DMA((mods,)), DMA((TP - 1,)), DMA((TP,)),
            DMA((ZN - 1,)), DMA((ZN,)), DMA((ZN - 1,)), DMA((ZN,)), DMA((ZN, rn - 1)), DMA((n,)),
            DMA((3,)), DMA((3,)), DMA((plan.late_ranks, rn - 1)), DMA((rn - 1, plan.late_ranks)),
            DMA((len(plan.outs),)), DMA((len(plan.outs),)),
        ],
        [SM] + [VM] * 3,
        cid,
        out_specs=(VM,) + (ANY,) * 6 + (VM,) * 7,
        name="head_part",
    )(meta, master, cond_units, tokens)


def padded(rows, low):
    zero = jnp.zeros_like(rows)
    return jnp.concatenate([rows, zero] if low else [zero, rows], axis=1)


def middle_kernel(
    plan, o_mine, wo_across, w_out, w_side, w_beside, w_early, w_below, tokens, grad_out, mod,
    result, late_own, late_send, esum, ebuf, do_out, dmid, dmod,
    gb, wb, eside, eend, wo, oall, attended, attn, mid, norm, inv, sin, hidden, dmlp, slopes, dup,
    own, csend, crecv, ysend, yrecv, dattn, dsend, dwo, wsend, wrecv,
    o_s, o_r, f_s, f_r, n_s, n_r, c_s, c_r, y_s, y_r, d_s, d_r, w_s, w_r, e_s, e_r, p_s, p_r, l_s, u_s, u_r, g_s, g_r, j_s, h_s, h_r, i_s, i_r,
):
    s, t, z, r = place(plan)
    rn = plan.r
    y = lax.div(t, 2)
    c = lax.rem(t, 2)
    sib = 2 * y + 1 - c
    across = lax.rem(t + 2, TP)
    mine = pl.multiple_of(c * TOK_FRAME, TOK_FRAME)
    theirs = pl.multiple_of((1 - c) * TOK_FRAME, TOK_FRAME)
    pairs = [(d, e) for d in range(ZN) for e in range(2)][1:]

    def partner(d, e):
        return lax.rem(z + d, ZN), (c if e == 0 else 1 - c)

    greet(
        [(partner(d, e)[0] * rn + r, 2 * y + partner(d, e)[1]) for d, e in pairs]
        + [(s, across)]
        + [(z * rn + lax.rem(r + d, rn), t) for d in range(1, rn)]
    )

    def home(k):
        return (k // 3) // rn, (k // 3) % rn, k - plan.half

    def w_rows(ref, k):
        return ref.at[pl.ds((k - plan.nq) * plan.ub, plan.ub)]

    def late_loads(act):
        for k in plan.late:
            sem = l_s.at[k - plan.nq]
            if k in plan.outs:
                act(pltpu.make_async_copy(w_out.at[k - plan.nq], w_rows(wb, k), sem))
            else:
                zo, ro = plan.home(k)
                rank = plan.late_rank[k]

                @pl.when(r == ro)
                def _():
                    act(pltpu.make_async_copy(w_side.at[rank], w_rows(wb, k), sem))

                @pl.when(r != ro)
                def _():
                    d = lax.rem(r - ro + rn, rn)
                    act(pltpu.make_async_copy(w_beside.at[d - 1, rank], w_rows(wb, k), sem))

    def loads(act):
        for k in plan.early:
            zo, ro, at = home(k)

            @pl.when((z <= zo) & (r == ro))
            def _():
                act(pltpu.make_async_copy(w_early.at[at], w_rows(wb, k), l_s.at[len(plan.late) + at]))

            @pl.when((z == zo + 1) & (r == ro))
            def _():
                act(
                    pltpu.make_async_copy(
                        w_below.at[k % 3], w_rows(wb, k), l_s.at[len(plan.late) + at]
                    )
                )

    def rise(k, src, act):
        zo, ro, at = home(k)

        @pl.when((z < ZN - 1) & (z > zo))
        def _():
            act(remote(src, w_rows(wb, k), u_s.at[at, 0], u_r.at[at], s + rn, t))

        for d in range(1, rn):
            act(
                remote(
                    src, w_rows(wb, k), u_s.at[at, d], u_r.at[at],
                    z * rn + lax.rem(r + d, rn), t,
                )
            )

    def risen(k):
        remote(w_below.at[0], w_rows(wb, k), u_s.at[0, 0], u_r.at[k - plan.half], s, t).wait_recv()

    def rises(act, first, wait):
        for k in plan.early:
            zo, ro, at = home(k)
            if first:
                @pl.when((z == zo + 1) & (r == ro))
                def _():
                    rise(k, w_below.at[k % 3], act)

                @pl.when((z <= zo) & (r == ro))
                def _():
                    rise(k, w_early.at[at], act)

            else:
                @pl.when((z > zo + 1) & (r == ro))
                def _():
                    if wait:
                        risen(k)
                    rise(k, w_rows(wb, k), act)

    def o_copy(d, e):
        zd, cd = partner(d, e)
        return remote(
            o_mine.at[zd, cd], oall.at[y * 8 + c * ZN + z], o_s.at[2 * d + e],
            o_r.at[c * ZN + z], zd * rn + r, 2 * y + cd,
        )

    def f_copy(slot):
        ref = oall.at[y * 8 + slot]
        return remote(ref, ref, f_s.at[slot], f_r.at[slot], s, across)

    def p_copy(i, tp):
        ref = wo.at[pl.ds(pl.multiple_of(tp * HD, HD), HD)]
        return remote(ref, ref, p_s.at[i], p_r.at[i], s, sib)

    for d, e in pairs:
        o_copy(d, e).start()
    start = lambda copy: copy.start()
    rises(start, True, False)
    late_loads(start)
    loads(start)
    late_loads(lambda copy: copy.wait())
    wo[pl.ds(pl.multiple_of(t * HD, HD), HD), :] = wb[:HD, :]
    p_copy(0, t).start()
    wo[pl.ds(pl.multiple_of(across * HD, HD), HD), :] = wo_across[...]
    p_copy(1, across).start()
    oall[y * 8 + c * ZN + z] = o_mine[z, c]
    f_copy(c * ZN + z).start()

    def d_mlp(f):
        def body(at):
            rows = pl.ds(f * TOK_FRAME + at, 64)
            dmlp[rows, :] = (grad_out[rows, :].astype(F32) * mod[f * 6 + 5 : f * 6 + 6, :]).astype(
                BF16
            )

        loop(TOK_FRAME, 64, body)

    for f in range(F_DEV):
        d_mlp(f)

    for d, e in pairs:
        zd, cd = partner(d, e)
        slot = cd * ZN + zd
        remote(o_mine.at[0, 0], oall.at[y * 8 + slot], o_s.at[0], o_r.at[slot], s, t).wait_recv()
        f_copy(slot).start()
    for slot in range(8):
        remote(
            oall.at[0], oall.at[(1 - y) * 8 + slot], f_s.at[slot], f_r.at[slot], s, t
        ).wait_recv()
    for m in range(HEADS // 2):
        a, b = oall[2 * m], oall[2 * m + 1]
        cols = slice(m * LANES, (m + 1) * LANES)
        attended[:PACK, cols] = jnp.concatenate([a[:, :HEAD], b[:, :HEAD]], axis=1)
        attended[PACK:, cols] = jnp.concatenate([a[:, HEAD:], b[:, HEAD:]], axis=1)

    p_copy(0, sib).wait_recv()
    p_copy(1, lax.rem(sib + 2, TP)).wait_recv()

    def attn_tile(at):
        attn[:, pl.ds(at, TILE)] = mm(attended[...], wo[:, pl.ds(at, TILE)])

    loop(D, TILE, attn_tile)
    rises(start, False, True)

    row = lambda part: mod[pl.ds(c * 6 + part, 1), :]

    def norm_rows(at):
        rows = pl.ds(at, 64)
        values = tokens[pl.ds(mine + at, 64), :].astype(F32) + row(2) * attn[rows, :]
        mid[rows, :] = values
        normed, inverse = normalize(values)
        norm[rows, :] = normed
        inv[rows, :] = inverse
        sin[pl.ds(mine + at, 64), :] = (normed * (1.0 + row(4)) + row(3)).astype(BF16)

    loop(TOK_FRAME, 64, norm_rows)

    def n_copy(base):
        ref = sin.at[pl.ds(base, TOK_FRAME)]
        return remote(ref, ref, n_s.at[0], n_r.at[0], s, sib)

    n_copy(mine).start()
    loads(lambda copy: copy.wait())
    for k in plan.early:
        zo, ro, at = home(k)

        @pl.when(r != ro)
        def _():
            risen(k)

    def feed(base):
        rows = pl.ds(base, TOK_FRAME)

        def tile(at):
            cols = pl.ds(at, TILE)
            u = mm(sin[rows, :], wb[HD : HD + FT, cols])
            square = u * u
            inner = GELU_A * u * (1.0 + GELU_B * square)
            th = jnp.tanh(inner)
            half = 0.5 * (1.0 + th)
            hidden[rows, cols] = (u * half).astype(BF16)
            slopes[rows, cols] = half + 0.5 * u * (1.0 - th * th) * (
                GELU_A * (1.0 + 3.0 * GELU_B * square)
            )

        loop(FT, TILE, tile)

    feed(mine)
    n_copy(theirs).wait_recv()
    feed(theirs)

    def d_up(at):
        cols = pl.ds(at, TILE)
        dup[:, cols] = (mm_nt(dmlp[...], wb[pl.ds(HD + FT + at, TILE), :]) * slopes[:, cols]).astype(
            BF16
        )

    loop(FT, TILE, d_up)

    def c_copy(w, n):
        return remote(csend.at[w, n], crecv.at[w, n], c_s.at[w, n], c_r.at[w, n], s, sib)

    def y_copy(w, n):
        return remote(ysend.at[w, n], yrecv.at[w, n], y_s.at[w, n], y_r.at[w, n], s, across)

    def pass_on(w, n):
        c_copy(w, n).wait_recv()
        ysend[w, n] = (own[n] + crecv[w, n].astype(F32)).astype(BF16)
        y_copy(w, n).start()

    def product(w, base, n):
        rows = pl.ds(base, TOK_FRAME)
        if w == 0:
            return mm_nt(dup[rows, :], wb[HD + n * TILE : HD + (n + 1) * TILE, :])
        return mm(hidden[rows, :], wb[HD + FT :, n * TILE : (n + 1) * TILE])

    def products(w):
        for n in range(TILES):
            csend[w, n] = product(w, theirs, n).astype(BF16)
            c_copy(w, n).start()
            own[n] = product(w, mine, n)
            if n:
                pass_on(w, n - 1)
        pass_on(w, TILES - 1)

    def down_grad(at):
        gb[pl.ds(HD + FT + at, TILE), :] = mm_tn(hidden[:, pl.ds(at, TILE)], dmlp[...]).astype(BF16)

    def up_grad(at):
        gb[pl.ds(HD + at, TILE), :] = mm_tn(sin[:, pl.ds(at, TILE)], dup[...]).astype(BF16)

    def early_grad(k, d):
        zo, ro, at = home(k)
        slot = lax.rem(ro - r + rn, rn) - 1 if d is None else d - 1
        return remote(
            w_rows(gb, k), eside.at[slot, plan.rank[k]], g_s.at[at], g_r.at[slot, plan.rank[k]],
            z * rn + ro, t,
        )

    def early_grads(act):
        for k in plan.early:
            zo, ro, at = home(k)

            @pl.when(r != ro)
            def _():
                act(early_grad(k, None))

    def early_hop(rank, act):
        for here, to in ((ZN - 1, s - rn), (0, s + rn)):
            @pl.when(z == here)
            def _():
                act(remote(esum.at[rank], eend.at[rank], h_s.at[rank], h_r.at[rank], to, t))

    def early_total(rank):
        for k in plan.early:
            if plan.rank[k] == rank:
                zo, ro, at = home(k)

                @pl.when(r == ro)
                def _():
                    for d in range(1, rn):
                        early_grad(k, d).wait_recv()

                    def body(at):
                        rows = pl.ds(at, 16)
                        total = gb[pl.ds((k - plan.nq) * plan.ub + at, 16), :].astype(F32)
                        for d in range(1, rn):
                            total = total + eside[d - 1, rank, rows, :].astype(F32)
                        esum[rank, rows, :] = total.astype(BF16)

                    loop(plan.ub, 16, body)
                    early_hop(rank, start)

    def early_pass(rank, to):
        return remote(esum.at[rank], ebuf.at[rank], i_s.at[rank], i_r.at[rank], to, t)

    def early_inner(rank):
        for k in plan.early:
            if plan.rank[k] == rank:
                zo, ro, at = home(k)

                @pl.when((r == ro) & (z > 0) & (z < ZN - 1))
                def _():
                    remote(
                        esum.at[rank], eend.at[rank], h_s.at[rank], h_r.at[rank], s, t
                    ).wait_recv()

                    def body(at):
                        rows = pl.ds(at, 16)
                        esum[rank, rows, :] = (
                            esum[rank, rows, :].astype(F32) + eend[rank, rows, :].astype(F32)
                        ).astype(BF16)

                    loop(plan.ub, 16, body)

                    @pl.when(z != zo)
                    def _():
                        early_pass(rank, s + rn if zo == 2 else s - rn).start()

    def early_close(rank):
        for k in plan.early:
            if plan.rank[k] == rank:
                zo, ro, at = home(k)

                @pl.when((r == ro) & (z == zo))
                def _():
                    early_pass(rank, s).wait_recv()

                @pl.when((r == ro) & (z == 3 - zo))
                def _():
                    early_pass(rank, s).wait_send()

    def early_hops_done(rank):
        for k in plan.early:
            if plan.rank[k] == rank:
                @pl.when(r == home(k)[1])
                def _():
                    early_hop(rank, lambda copy: copy.wait_send())

    loop(FT, TILE, down_grad)
    up_grad(D - TILE)
    early_grads(start)
    products(0)
    products(1)
    loop(D - TILE, TILE, up_grad)
    early_total(0)
    early_total(1)
    early_inner(0)

    dm = dmod
    dm[...] = jnp.zeros_like(dm)
    for n in range(TILES):
        y_copy(0, n).wait_recv()

    def total(w, rows):
        return jnp.concatenate(
            [ysend[w, n, rows].astype(F32) + yrecv[w, n, rows].astype(F32) for n in range(TILES)],
            axis=1,
        )

    def back_rows(at):
        rows = pl.ds(at, 64)
        tok_rows = pl.ds(mine + at, 64)
        grads = total(0, rows)
        normed = norm[rows, :]
        add_to(dm, 1, grads)
        add_to(dm, 2, grads * normed)
        values = grad_out[tok_rows, :].astype(F32) + norm_back(
            grads * (1.0 + row(4)), normed, inv[rows, :]
        )
        dmid[rows, :] = values
        add_to(dm, 0, attn[rows, :] * values)
        dattn[rows, :] = (row(2) * values).astype(BF16)

    loop(TOK_FRAME, 64, back_rows)
    for ch in range(2):
        part = mm_nt(dattn[...], wo[pl.ds(pl.multiple_of((2 * y + ch) * HD, HD), HD), :]).astype(BF16)
        for zh in range(ZN):
            cols = slice(zh * HEAD, (zh + 1) * HEAD)
            dsend[ch * ZN + zh] = jnp.concatenate([part[:PACK, cols], part[PACK:, cols]], axis=1)

    def d_copy(d, e):
        zd, cd = partner(d, e)
        return remote(
            dsend.at[cd * ZN + zd], do_out.at[z, c], d_s.at[2 * d + e], d_r.at[2 * z + c],
            zd * rn + r, 2 * y + cd,
        )

    for d, e in pairs:
        d_copy(d, e).start()
    do_out[z, c] = dsend[c * ZN + z]
    for rank in range(2, plan.ranks):
        early_total(rank)

    def o_grad(head_core):
        cols = pl.ds(pl.multiple_of((2 * y + head_core) * HD, HD), HD)
        return mm_tn(attended[:, cols], dattn[...])

    w_copy = remote(wsend, wrecv, w_s, w_r, s, sib)
    wsend[...] = o_grad(1 - c).astype(BF16)
    w_copy.start()
    dwo[...] = o_grad(c)
    early_inner(1)

    for n in range(TILES):
        y_copy(1, n).wait_recv()

    def result_rows(at):
        rows = pl.ds(at, 64)
        tok_rows = pl.ds(mine + at, 64)
        mlp = total(1, rows)
        add_to(dm, 3, mlp * grad_out[tok_rows, :].astype(F32))
        result[tok_rows, :] = (mid[rows, :] + row(5) * mlp).astype(BF16)

    loop(TOK_FRAME, 64, result_rows)

    def e_copy(base):
        ref = result.at[pl.ds(base, TOK_FRAME)]
        return remote(ref, ref, e_s, e_r, s, sib)

    e_copy(mine).start()
    for rank in range(2, plan.ranks):
        early_inner(rank)
    w_copy.wait_recv()
    gb[:HD, :] = (dwo[...] + wrecv[...].astype(F32)).astype(BF16)

    for d, e in pairs:
        zd, cd = partner(d, e)
        remote(
            dsend.at[0], do_out.at[zd, cd], d_s.at[0], d_r.at[2 * zd + cd], s, t
        ).wait_recv()
    def late_grads(act):
        for k in plan.late:
            zo, ro = plan.home(k)
            rank, sem = plan.grad_rank[k], j_s.at[k - plan.nq]

            @pl.when(r == ro)
            def _():
                act(pltpu.make_async_copy(w_rows(gb, k), late_own.at[rank], sem))

            @pl.when(r != ro)
            def _():
                d = lax.rem(ro - r + rn, rn)
                act(pltpu.make_async_copy(w_rows(gb, k), late_send.at[d - 1, rank], sem))

    late_grads(start)
    for rank in range(plan.ranks):
        early_close(rank)
    e_copy(theirs).wait_recv()
    done = lambda copy: copy.wait_send()
    early_grads(done)
    for rank in range(plan.ranks):
        early_hops_done(rank)
    late_grads(lambda copy: copy.wait())
    rises(done, True, False)
    rises(done, False, False)
    for d, e in pairs:
        o_copy(d, e).wait_send()
        d_copy(d, e).wait_send()
    for slot in range(8):
        f_copy(slot).wait_send()
    n_copy(mine).wait_send()
    p_copy(0, t).wait_send()
    p_copy(1, across).wait_send()
    for w in range(2):
        for n in range(TILES):
            c_copy(w, n).wait_send()
            y_copy(w, n).wait_send()
    w_copy.wait_send()
    e_copy(mine).wait_send()


def middle_part(plan, o_mine, wo_across, weights, tokens, grad_out, mod_rows, cid):
    rn, count = plan.r, len(plan.early)
    rows = F_DEV * TOK_FRAME
    half = lambda dtype: pltpu.VMEM((TOK_FRAME, D), dtype)
    full = lambda dtype: pltpu.VMEM((rows, D), dtype)
    tiles = pltpu.VMEM((2, TILES, TOK_FRAME, TILE), BF16)
    return call(
        functools.partial(middle_kernel, plan),
        (
            jax.ShapeDtypeStruct((rows, D), BF16),
            jax.ShapeDtypeStruct((plan.grad_ranks, plan.ub, D), BF16),
            jax.ShapeDtypeStruct((rn - 1, plan.grad_ranks, plan.ub, D), BF16),
            jax.ShapeDtypeStruct((plan.ranks, plan.ub, D), BF16),
            jax.ShapeDtypeStruct((plan.ranks, plan.ub, D), BF16),
            jax.ShapeDtypeStruct((ZN, F_DEV, PACK, LANES), BF16),
            jax.ShapeDtypeStruct((TOK_FRAME, D), F32),
            jax.ShapeDtypeStruct((8, D), F32),
        ),
        [
            pltpu.VMEM((BROWS, D), BF16),
            pltpu.VMEM((BROWS, D), BF16),
            pltpu.VMEM((rn - 1, plan.ranks, plan.ub, D), BF16),
            pltpu.VMEM((plan.ranks, plan.ub, D), BF16),
            pltpu.VMEM((HEADS * HEAD, D), BF16),
            pltpu.VMEM((HEADS, PACK, LANES), BF16),
            half(BF16), half(F32), half(F32), half(F32), pltpu.VMEM((TOK_FRAME, 1), F32),
            full(BF16), full(BF16), full(BF16), full(F32), full(BF16),
            pltpu.VMEM((TILES, TOK_FRAME, TILE), F32), tiles, tiles, tiles, tiles,
            half(BF16), pltpu.VMEM((8, PACK, LANES), BF16),
            pltpu.VMEM((HD, D), F32), pltpu.VMEM((HD, D), BF16), pltpu.VMEM((HD, D), BF16),
            DMA((8,)), DMA((8,)), DMA((8,)), DMA((8,)), DMA((1,)), DMA((1,)),
            DMA((2, TILES)), DMA((2, TILES)), DMA((2, TILES)), DMA((2, TILES)),
            DMA((8,)), DMA((8,)), DMA, DMA, DMA, DMA, DMA((2,)), DMA((2,)),
            DMA((len(plan.late) + count,)), DMA((count, rn)), DMA((count,)), DMA((count,)), DMA((rn - 1, plan.ranks)),
            DMA((len(plan.late),)), DMA((plan.ranks,)), DMA((plan.ranks,)),
            DMA((plan.ranks,)), DMA((plan.ranks,)),
        ],
        [VM, VM, ANY, ANY, ANY, ANY, ANY, VM, VM, VM],
        cid,
        out_specs=(VM, ANY, ANY, VM, VM, VM, VM, VM),
        name="middle_part",
    )(o_mine, wo_across, *weights, tokens, grad_out, mod_rows)


def tail_kernel(
    plan, meta, q, kv, do, ot, lse, first_in, wq, tokens, dmid, mod, dm4, late_own, late_send, esum, ebuf,
    igrad, oq, ob, dall,
    keys, flipped, qs, gs, qgt, drow, acc, dq_acc, dq, kv_two, lside,
    stage, side, q_in, kv_in, dqkv, gq, own, csend, crecv, ysend, yrecv, dm, dm3, dboth,
    lstage, cb, qside, qpeer, qchain, qstage,
    q_s, q_r, k_s, k_r, x_s, x_r, c_s, c_r, y_s, y_r, e_s, e_r, h_s, h_r, m_s, m_r, t_s, t_r,
    kv_s, ls_s, ls_r, qo_s, qs_r, qp_r, qc_s, qc_r,
):
    s, t, z, r = place(plan)
    n, rn = plan.n, plan.r
    y = lax.div(t, 2)
    c = lax.rem(t, 2)
    sib = 2 * y + 1 - c
    across = lax.rem(t + 2, TP)
    mine = pl.multiple_of(c * TOK_FRAME, TOK_FRAME)
    theirs = pl.multiple_of((1 - c) * TOK_FRAME, TOK_FRAME)
    greet([(lax.rem(s + d, n), t) for d in range(1, n)] + [(s, sib), (s, across)])

    def side_copy(zs, e):
        other = lax.rem(r + e, rn)
        return remote(
            keys.at[zs * rn + other], side.at[e - 1, zs], x_s.at[zs, e - 1], x_r.at[zs, e - 1],
            z * rn + other, t,
        )

    def q_copy(zs):
        return remote(dq.at[zs], q_in.at[z], q_s.at[zs], q_r.at[z], zs * rn + r, t)

    def kv_copy(zs):
        return remote(stage.at[zs], kv_in.at[z], k_s.at[zs], k_r.at[z], zs * rn + r, t)

    def send_q(zs):
        @pl.when(z == zs)
        def _():
            q_in[zs] = dq[zs]

        @pl.when(z != zs)
        def _():
            q_copy(zs).start()

    def send_kv(zs):
        total = keys[zs * rn + r].astype(F32)
        for e in range(1, rn):
            side_copy(zs, e).wait_recv()
            total = total + side[e - 1, zs].astype(F32)
        stage[zs] = total.astype(BF16)

        @pl.when(z == zs)
        def _():
            kv_in[zs] = stage[zs]

        @pl.when(z != zs)
        def _():
            kv_copy(zs).start()

    scale = HEAD ** (-0.5)
    acc[...] = jnp.zeros_like(acc)

    def load(g, slot):
        return pltpu.make_async_copy(kv.at[g], kv_two.at[slot], kv_s.at[slot])

    load(0, 0).start()

    def sort_group(g, carry):
        slot = lax.rem(g, 2)

        @pl.when(g + 1 < n)
        def _():
            load(g + 1, 1 - slot).start()

        load(g, slot).wait()
        first = meta[2 * g] == 0
        a, b = kv_two[slot, :TOK_FRAME, :], kv_two[slot, TOK_FRAME:, :]
        keys[g, 0] = jnp.where(first, a, b)
        keys[g, 1] = jnp.where(first, b, a)
        for kind in range(2):
            flipped[kind, g] = keys[g, kind].T
        return carry

    lax.fori_loop(0, n, sort_group, 0)

    def attend_back_group(zq):
        gq = zq * rn + r
        first = meta[2 * gq] == 0
        clip = meta[2 * gq] + meta[2 * gq + 1]
        parts = []
        for kind in range(2):
            low = first if kind == 0 else jnp.logical_not(first)
            qz = padded(jnp.where(low, q[zq][:, :HEAD], q[zq][:, HEAD:]), True) * jnp.asarray(scale, BF16)
            gpack = jnp.where(low, do[zq, 0], do[zq, 1])
            grads = jnp.concatenate([gpack[:, :HEAD], gpack[:, HEAD:]], axis=0)
            out = ot[2 * zq + kind]
            logs = lse[2 * zq + kind]
            gz = padded(grads, False)
            qs[...] = qz
            gs[...] = gz
            qgt[:, :TOK_FRAME] = qz.T
            qgt[:, TOK_FRAME:] = gz.T
            drow[...] = jnp.sum(grads.astype(F32).T * out, axis=0, keepdims=True)
            dq_acc[...] = jnp.zeros_like(dq_acc)

            def block(p, inner):
                total = dq_acc[...]
                for e in range(2):
                    g = jnp.minimum(2 * p + e, gq)
                    shown = 2 * p + e <= gq
                    if kind == 1:
                        shown = shown & (meta[2 * g] + meta[2 * g + 1] == clip)
                    off = jnp.where(shown, 0.0, 1e30)
                    key = keys[g, kind]
                    pt = jnp.exp(mm(key, qgt[:, :TOK_FRAME]) - (logs + off))
                    dst = (pt * (mm(key, qgt[:, TOK_FRAME:]) - drow[...])).astype(BF16)
                    acc[kind, g] += mm(dst, qs[...]) + mm(pt.astype(BF16), gs[...])
                    total = total + mm(flipped[kind, g], dst)
                dq_acc[...] = total
                return inner

            lax.fori_loop(0, lax.div(gq + 2, 2), block, 0)
            parts.append((dq_acc[:HEAD, :] * scale).T.astype(BF16))
        dq[zq] = jnp.concatenate(
            [jnp.where(first, parts[0], parts[1]), jnp.where(first, parts[1], parts[0])], axis=1
        )
        for other in range(rn):
            g = zq * rn + other
            low = meta[2 * g] == 0
            a, b = acc[0, g].astype(BF16), acc[1, g].astype(BF16)
            keys[g, 0] = jnp.where(low, a, b)
            keys[g, 1] = jnp.where(low, b, a)

    def late(units, act):
        for k in units:
            zo, ro = plan.home(k)

            @pl.when(r == ro)
            def _():
                act(k, zo, plan.grad_rank[k])

    def late_copy(rank, below, to):
        return remote(lstage.at[rank], cb.at[below, rank], t_s.at[rank], t_r.at[below, rank], to, t)

    def late_side(rank, d):
        return remote(
            late_send.at[d - 1, rank], lside.at[d - 1, rank], ls_s.at[rank, d - 1],
            ls_r.at[rank, d - 1], z * rn + lax.rem(r + d, rn), t,
        )

    def late_sides(rank, act):
        for d in range(1, rn):
            act(late_side(rank, d))

    def late_step(k, zo, rank, here_z, above, below, final):
        @pl.when(z == here_z)
        def _():
            for d in range(1, rn):
                late_side(rank, d).wait_recv()
            if above:
                late_copy(rank, 0, s).wait_recv()
            if below:
                late_copy(rank, 1, s).wait_recv()

            def body(at):
                rows = pl.ds(at, 16)
                total = late_own[rank, rows, :].astype(F32)
                for d in range(1, rn):
                    total = total + lside[d - 1, rank, rows, :].astype(F32)
                if above:
                    total = total + cb[0, rank, rows, :].astype(F32)
                if below:
                    total = total + cb[1, rank, rows, :].astype(F32)
                if final:
                    ob[k % 3, rows, :] = total
                else:
                    lstage[rank, rows, :] = total.astype(BF16)

            loop(plan.ub, 16, body)
            if not final:
                late_copy(
                    rank, 0 if here_z > zo else 1, s - rn if here_z > zo else s + rn
                ).start()

    def late_ends(k, zo, rank):
        late_step(k, zo, rank, ZN - 1, False, False, False)
        if zo > 0:
            late_step(k, zo, rank, 0, False, False, False)

    def late_inner(here):
        def act(k, zo, rank):
            if here > zo:
                late_step(k, zo, rank, here, True, False, False)

        return act

    def late_final(k, zo, rank):
        late_step(k, zo, rank, zo, True, zo > 0, True)

    def late_done(k, zo, rank):
        @pl.when(z != zo)
        def _():
            late_copy(rank, 0, s).wait_send()

    def early_units(act):
        for k in plan.early:
            zo, ro, rank = (k // 3) // rn, (k // 3) % rn, plan.rank[k]

            @pl.when(r == ro)
            def _():
                act(k, zo, rank)

    def early_final(k, zo, rank):
        @pl.when(z == zo)
        def _():
            def body(at):
                rows = pl.ds(at, 16)
                ob[k % 3, rows, :] = esum[rank, rows, :].astype(F32) + ebuf[rank, rows, :].astype(F32)

            loop(plan.ub, 16, body)

    hq = plan.uq // CUTS

    def q_rows(k, h):
        return gq.at[pl.ds(pl.multiple_of(k * plan.uq + h * hq, hq), hq)]

    def q_sides(k, act):
        tc, ro, j = k % rn, k // 3, k // rn
        for h in range(CUTS):
            @pl.when((z > 0) & (r != tc))
            def _():
                slot = lax.rem(tc - r + rn, rn) - 1
                act(
                    remote(
                        q_rows(k, h), qside.at[slot, CUTS * j + h], qo_s.at[CUTS * k + h],
                        qs_r.at[slot, CUTS * j + h], z * rn + tc, t,
                    )
                )

            @pl.when((z == 0) & (r != ro) & (r != tc))
            def _():
                slot = lax.rem(ro - r + rn, rn) - 1
                act(
                    remote(
                        q_rows(k, h), qpeer.at[slot, CUTS * (k % 3) + h], qo_s.at[CUTS * k + h],
                        qp_r.at[slot, CUTS * (k % 3) + h], ro, t,
                    )
                )

    def q_down(at, to):
        return remote(qstage.at[at], qchain.at[at], qc_s.at[at], qc_r.at[at], to, t)

    def q_chain(here, only_j):
        top = here == ZN - 1
        for j in (only_j,):
            k = r + rn * j
            for h in range(CUTS):
                at = CUTS * j + h

                @pl.when(z == here)
                def _():
                    for d in range(1, rn):
                        remote(
                            q_rows(k, h), qside.at[d - 1, at], qo_s.at[0], qs_r.at[d - 1, at], s, t
                        ).wait_recv()
                    if not top:
                        q_down(at, s).wait_recv()
                    unit = q_rows(k, h)

                    def body(row):
                        rows = pl.ds(row, 16)
                        total = unit[rows, :].astype(F32)
                        for d in range(1, rn):
                            total = total + qside[d - 1, at, rows, :].astype(F32)
                        if not top:
                            total = total + qchain[at, rows, :].astype(F32)
                        qstage[at, rows, :] = total.astype(BF16)

                    loop(hq, 16, body)
                    q_down(at, s - rn).start()

    def q_last_copy(k, h):
        tc, ro, j = k % rn, k // 3, k // rn
        slot = (ro - tc + rn) % rn - 1
        return remote(
            qstage.at[CUTS * j + h], qpeer.at[slot, CUTS * (k % 3) + h], qc_s.at[CUTS * j + h],
            qp_r.at[slot, CUTS * (k % 3) + h], ro, t,
        )

    def q_ground(act):
        for k in range(plan.nq):
            if k % rn != k // 3:
                @pl.when((z == 0) & (r == k % rn))
                def _():
                    for h in range(CUTS):
                        act(k, h)

    def q_turn(k, h):
        at = CUTS * (k // rn) + h
        q_down(at, s).wait_recv()
        unit = q_rows(k, h)

        def body(row):
            rows = pl.ds(row, 16)
            qstage[at, rows, :] = (
                unit[rows, :].astype(F32) + qchain[at, rows, :].astype(F32)
            ).astype(BF16)

        loop(hq, 16, body)
        q_last_copy(k, h).start()

    def q_final():
        for k in range(plan.nq):
            @pl.when((z == 0) & (r == k // 3))
            def _():
                straight = k % rn == k // 3
                for h in range(CUTS):
                    at = CUTS * (k // rn) + h
                    if straight:
                        q_down(at, s).wait_recv()
                    for d in range(1, rn):
                        remote(
                            q_rows(k, h), qpeer.at[d - 1, CUTS * (k % 3) + h], qo_s.at[0],
                            qp_r.at[d - 1, CUTS * (k % 3) + h], s, t,
                        ).wait_recv()
                    unit = q_rows(k, h)

                    def body(row):
                        rows = pl.ds(row, 16)
                        total = unit[rows, :].astype(F32)
                        for d in range(1, rn):
                            total = total + qpeer[d - 1, CUTS * (k % 3) + h, rows, :].astype(F32)
                        if straight:
                            total = total + qchain[at, rows, :].astype(F32)
                        oq[k % 3, pl.ds(h * hq + row, 16), :] = total

                    loop(hq, 16, body)

    start = lambda copy: copy.start()
    done = lambda copy: copy.wait_send()
    def only(rank, act):
        return lambda k, zo, own_rank: act(k, zo, own_rank) if own_rank == rank else None

    last = plan.grad_ranks - 1
    late_sides(0, start)
    for zq in range(ZN - 1, -1, -1):
        attend_back_group(zq)
        for e in range(1, rn):
            side_copy(zq, e).start()
        send_q(zq)
        if zq == ZN - 1:
            late(plan.late, only(0, late_ends))
        else:
            send_kv(zq + 1)
    for rank in range(1, plan.grad_ranks):
        late_sides(rank, start)
    send_kv(0)
    late(plan.late, only(0, late_inner(2)))
    late(plan.late, only(0, late_inner(1)))
    late(plan.late, only(1, late_ends))
    for zs in range(ZN):
        @pl.when(z != zs)
        def _():
            remote(dq.at[0], q_in.at[zs], q_s.at[0], q_r.at[zs], s, t).wait_recv()
            remote(stage.at[0], kv_in.at[zs], k_s.at[0], k_r.at[zs], s, t).wait_recv()

    for p in range(2):
        cols = slice(p * LANES, (p + 1) * LANES)
        a, b = q_in[2 * p], q_in[2 * p + 1]
        dqkv[:TOK_FRAME, cols] = jnp.concatenate([a[:, :HEAD], b[:, :HEAD]], axis=1)
        dqkv[TOK_FRAME:, cols] = jnp.concatenate([a[:, HEAD:], b[:, HEAD:]], axis=1)
        a, b = [kv_in[2 * p + i].reshape(F_DEV * TOK_FRAME, LANES) for i in range(2)]
        dqkv[:, HD + p * LANES : HD + (p + 1) * LANES] = jnp.concatenate(
            [a[:, :HEAD], b[:, :HEAD]], axis=1
        )
        dqkv[:, 2 * HD + p * LANES : 2 * HD + (p + 1) * LANES] = jnp.concatenate(
            [a[:, HEAD:], b[:, HEAD:]], axis=1
        )

    for m in range(TILES):
        gq[m * TILE : (m + 1) * TILE, :] = mm_tn(
            first_in[:, m * TILE : (m + 1) * TILE], dqkv[...]
        ).astype(BF16)
        for k in range(m * plan.nq // TILES, (m + 1) * plan.nq // TILES):
            q_sides(k, start)

    def c_copy(w):
        return remote(csend.at[w], crecv.at[w], c_s.at[w], c_r.at[w], s, sib)

    def y_copy(w):
        return remote(ysend.at[w], yrecv.at[w], y_s.at[w], y_r.at[w], s, across)

    def pass_on(w):
        c_copy(w).wait_recv()
        ysend[w] = (own[w] + crecv[w].astype(F32)).astype(BF16)
        y_copy(w).start()

    for w in range(TILES):
        weights = wq[w * TILE : (w + 1) * TILE, :]
        csend[w] = mm_nt(dqkv[pl.ds(theirs, TOK_FRAME), :], weights).astype(BF16)
        c_copy(w).start()
        own[w] = mm_nt(dqkv[pl.ds(mine, TOK_FRAME), :], weights)
        if w:
            pass_on(w - 1)
    pass_on(TILES - 1)

    for rank in range(2, plan.grad_ranks):
        late(plan.late, only(rank, late_ends))
    q_chain(ZN - 1, 0)
    q_chain(ZN - 1, 1)
    late(plan.late, only(1, late_inner(2)))
    q_chain(2, 0)
    late(plan.late, only(last, late_inner(2)))
    q_chain(2, 1)
    q_chain(1, 0)
    late(plan.late, only(1, late_inner(1)))
    q_chain(1, 1)
    late(plan.late, only(last, late_inner(1)))

    for w in range(TILES):
        y_copy(w).wait_recv()
    row = lambda part: mod[pl.ds(c * 6 + part, 1), :]
    dm[...] = jnp.zeros_like(dm)

    def input_rows(at):
        rows = pl.ds(at, 64)
        tok_rows = pl.ds(mine + at, 64)
        grads = jnp.concatenate(
            [ysend[w, rows].astype(F32) + yrecv[w, rows].astype(F32) for w in range(TILES)], axis=1
        )
        normed, inverse = normalize(tokens[tok_rows, :].astype(F32))
        add_to(dm, 0, grads)
        add_to(dm, 1, grads * normed)
        igrad[tok_rows, :] = dmid[rows, :] + norm_back(grads * (1.0 + row(1)), normed, inverse)

    loop(TOK_FRAME, 64, input_rows)

    def e_copy(base):
        ref = igrad.at[pl.ds(base, TOK_FRAME)]
        return remote(ref, ref, e_s, e_r, s, sib)

    e_copy(mine).start()

    for block in range(6 * D // LANES):
        part, at = block // (D // LANES), block % (D // LANES)
        src = dm if part < 2 else dm4
        lane = slice(at * LANES, (at + 1) * LANES)
        from_row = part if part < 2 else part - 2
        dm3[block // MCOLS, block % MCOLS : block % MCOLS + 1, :] = src[from_row : from_row + 1, lane]
    h_copy = lambda frame: remote(dm3.at[sib], dboth.at[frame], h_s, h_r, s, sib)
    h_copy(c).start()
    dboth[c] = dm3[t]
    h_copy(1 - c).wait_recv()

    def m_copy(src):
        return remote(dboth, dall.at[s], m_s.at[src - plan.first_mod], m_r.at[s], src, t)

    for src in range(plan.first_mod, n):
        @pl.when(s == src)
        def _():
            dall[s] = dboth[...]

        @pl.when(s != src)
        def _():
            m_copy(src).start()

    q_ground(q_turn)
    late(plan.late, late_final)
    early_units(early_final)
    q_final()

    @pl.when(s >= plan.first_mod)
    def _():
        for d in range(1, n):
            other = lax.rem(s + d, n)
            remote(dboth, dall.at[other], m_s.at[0], m_r.at[other], s, t).wait_recv()

    e_copy(theirs).wait_recv()
    for zs in range(ZN):
        @pl.when(z != zs)
        def _():
            q_copy(zs).wait_send()
            kv_copy(zs).wait_send()

        for e in range(1, rn):
            side_copy(zs, e).wait_send()
    for rank in range(plan.grad_ranks):
        late_sides(rank, done)
    late(plan.late, late_done)
    for k in range(plan.nq):
        q_sides(k, done)

    @pl.when(z > 0)
    def _():
        for at in range(2 * CUTS):
            q_down(at, s).wait_send()

    q_ground(lambda k, h: q_last_copy(k, h).wait_send())
    for w in range(TILES):
        c_copy(w).wait_send()
        y_copy(w).wait_send()
    e_copy(mine).wait_send()
    h_copy(c).wait_send()
    for src in range(plan.first_mod, n):
        @pl.when(s != src)
        def _():
            m_copy(src).wait_send()


def tail_part(plan, meta, q, kv, do, ot, lse, first_in, wq, tokens, dmid, mod_rows, dm4, late_own, late_send, esum, ebuf, cid):
    n, rn = plan.n, plan.r
    rows = F_DEV * TOK_FRAME
    tiles = pltpu.VMEM((TILES, TOK_FRAME, TILE), BF16)
    mods = n - plan.first_mod
    return call(
        functools.partial(tail_kernel, plan),
        (
            jax.ShapeDtypeStruct((rows, D), F32),
            jax.ShapeDtypeStruct((3, plan.uq, QKV), F32),
            jax.ShapeDtypeStruct((3, plan.ub, D), F32),
            jax.ShapeDtypeStruct((n, F_DEV, 16, LANES), F32),
        ),
        [
            pltpu.VMEM((n, 2, TOK_FRAME, LANES), BF16),
            pltpu.VMEM((2, n, LANES, TOK_FRAME), BF16),
            pltpu.VMEM((TOK_FRAME, LANES), BF16),
            pltpu.VMEM((TOK_FRAME, LANES), BF16),
            pltpu.VMEM((LANES, 2 * TOK_FRAME), BF16),
            pltpu.VMEM((1, TOK_FRAME), F32),
            pltpu.VMEM((2, n, TOK_FRAME, LANES), F32),
            pltpu.VMEM((LANES, TOK_FRAME), F32),
            pltpu.VMEM((ZN, TOK_FRAME, LANES), BF16),
            pltpu.VMEM((2, rows, LANES), BF16),
            pltpu.VMEM((rn - 1, plan.grad_ranks, plan.ub, D), BF16),
            pltpu.VMEM((ZN, 2, TOK_FRAME, LANES), BF16),
            pltpu.VMEM((rn - 1, ZN, 2, TOK_FRAME, LANES), BF16),
            pltpu.VMEM((ZN, TOK_FRAME, LANES), BF16),
            pltpu.VMEM((ZN, 2, TOK_FRAME, LANES), BF16),
            pltpu.VMEM((rows, QKV), BF16),
            pltpu.VMEM((D, QKV), BF16),
            pltpu.VMEM((TILES, TOK_FRAME, TILE), F32), tiles, tiles, tiles, tiles,
            pltpu.VMEM((8, D), F32),
            pltpu.VMEM((TP, 16, LANES), F32),
            pltpu.VMEM((F_DEV, 16, LANES), F32),
            pltpu.VMEM((plan.grad_ranks, plan.ub, D), BF16),
            pltpu.VMEM((2, plan.grad_ranks, plan.ub, D), BF16),
            pltpu.VMEM((rn - 1, 2 * CUTS, plan.uq // CUTS, QKV), BF16),
            pltpu.VMEM((rn - 1, 3 * CUTS, plan.uq // CUTS, QKV), BF16),
            pltpu.VMEM((2 * CUTS, plan.uq // CUTS, QKV), BF16),
            pltpu.VMEM((2 * CUTS, plan.uq // CUTS, QKV), BF16),
            DMA((ZN,)), DMA((ZN,)), DMA((ZN,)), DMA((ZN,)), DMA((ZN, rn - 1)), DMA((ZN, rn - 1)),
            DMA((TILES,)), DMA((TILES,)), DMA((TILES,)), DMA((TILES,)),
            DMA, DMA, DMA, DMA, DMA((mods,)), DMA((n,)),
            DMA((plan.grad_ranks,)), DMA((2, plan.grad_ranks)),
            DMA((2,)), DMA((plan.grad_ranks, rn - 1)), DMA((plan.grad_ranks, rn - 1)),
            DMA((CUTS * plan.nq,)),
            DMA((rn - 1, 2 * CUTS)), DMA((rn - 1, 3 * CUTS)), DMA((2 * CUTS,)), DMA((2 * CUTS,)),
        ],
        [SM, VM, ANY] + [VM] * 10 + [ANY, VM, VM],
        cid,
        name="tail_part",
    )(meta, q, kv, do, ot, lse, first_in, wq, tokens, dmid, mod_rows, dm4, late_own, late_send, esum, ebuf)


def adam_kernel(plan, meta, oq, ob, cond, dmod, master, one, two, average, n_master, n_one, n_two, n_average):
    s = meta[0]
    rate = RATE_FACTOR * D ** (-0.5)
    scale_one = 1.0 / (1.0 - BETA_FIRST**STEP)
    scale_two = 1.0 / (1.0 - BETA_SECOND**STEP)

    def update(rows, grad):
        first = BETA_FIRST * one[rows, :] + (1.0 - BETA_FIRST) * grad
        second = BETA_SECOND * two[rows, :] + (1.0 - BETA_SECOND) * grad * grad
        weight = master[rows, :]
        weight = weight - rate * (
            (first * scale_one) / (jnp.sqrt(second * scale_two) + ADAM_EPSILON)
            + WEIGHT_DECAY * weight
        )
        n_one[rows, :] = first
        n_two[rows, :] = second
        n_master[rows, :] = weight
        n_average[rows, :] = AVERAGE_RATE * average[rows, :] + (1.0 - AVERAGE_RATE) * weight

    if True:
        k = 3 * s + lax.div(pl.program_id(0), ADAM_CUTS)
        base = 0

        def from_matrix(kind):
            src = oq if kind == "q" else ob
            rows = (plan.uq if kind == "q" else plan.ub) // ADAM_CUTS
            cols = (QKV if kind == "q" else D) // LANES
            for j in range(cols):
                update(
                    pl.ds(base + j, rows, stride=cols), src[0, :, j * LANES : (j + 1) * LANES]
                )

        by_kind(plan, k, from_matrix)

        @pl.when(k >= plan.nb)
        def _():
            count = plan.um // ADAM_CUTS
            part = pl.multiple_of(lax.rem(pl.program_id(0), ADAM_CUTS) * count, count)
            at = cond[k - plan.nb, pl.ds(part, count), :]
            for j in range(MCOLS):
                update(
                    pl.ds(base + j, count, stride=MCOLS),
                    mm(at, dmod[pl.ds(j, plan.frames, stride=16), :].astype(BF16)),
                )


def adam(plan, meta, oq, ob, cond_rows, dmod, master, one, two, average):
    shape = jax.ShapeDtypeStruct(master.shape, F32)
    flat = pl.BlockSpec((plan.flat_rows // ADAM_CUTS, LANES), lambda i: (i, 0))
    unit = lambda rows, cols: pl.BlockSpec(
        (1, rows // ADAM_CUTS, cols), lambda i: (lax.div(i, ADAM_CUTS), lax.rem(i, ADAM_CUTS), 0)
    )
    whole = lambda x: pl.BlockSpec(x.shape, lambda i: (0,) * x.ndim)
    return pl.pallas_call(
        functools.partial(adam_kernel, plan),
        out_shape=(shape,) * 4,
        grid=(3 * ADAM_CUTS,),
        in_specs=[SM, unit(plan.uq, QKV), unit(plan.ub, D), whole(cond_rows), whole(dmod)] + [flat] * 4,
        out_specs=(flat,) * 4,
        compiler_params=pltpu.CompilerParams(vmem_limit_bytes=VMEM_LIMIT),
        name="adam",
    )(meta, oq, ob, cond_rows, dmod, master, one, two, average)


def local(
    tokens,
    grad_out,
    noise_level,
    context_mask,
    frame_clip,
    level_table,
    master,
    moment_one,
    moment_two,
    average,
):
    plan = Plan(lax.axis_size("seq"))
    s = lax.axis_index("seq")
    t = lax.axis_index("tp")
    flat = lambda x: x.reshape(-1, LANES)

    effective = noise_level * (1 - context_mask)
    one_hot = (
        effective[:, None] == jnp.arange(level_table.shape[0], dtype=jnp.int32)[None, :]
    ).astype(BF16)
    condition = jax.nn.silu(mm(one_hot, level_table)).astype(BF16)
    cond_units = condition.reshape(plan.frames, plan.nm, plan.um).transpose(1, 0, 2)

    meta = frame_clip.astype(jnp.int32)
    (
        wq, w_out, w_side, w_early, w_below, w_beside, wo_across, mod_rows, first_in, q_mine, kv_all,
        o_mine, o_rows, lse,
    ) = head_part(plan, meta, flat(master), cond_units, tokens, 0)
    result, late_own, late_send, early_sum, early_in, do_mine, middle_grad, mod_four = middle_part(
        plan, o_mine, wo_across, (w_out, w_side, w_beside, w_early, w_below),
        tokens, grad_out, mod_rows, 2
    )
    input_grad, own_q, own_b, mod_all = tail_part(
        plan, meta, q_mine, kv_all, do_mine, o_rows, lse, first_in, wq, tokens, middle_grad,
        mod_rows, mod_four, late_own, late_send, early_sum, early_in, 3,
    )
    updated = adam(
        plan,
        s[None].astype(jnp.int32),
        own_q,
        own_b,
        cond_units.transpose(0, 2, 1),
        flat(mod_all),
        flat(master),
        flat(moment_one),
        flat(moment_two),
        flat(average),
    )
    new_master, new_one, new_two, new_average = [x.reshape(master.shape) for x in updated]
    return (result, input_grad, new_master, new_one, new_two, new_average)


def solution(mesh):
    token_spec = P("seq", None)
    weight_spec = P("tp", "seq")
    in_specs = (token_spec, token_spec, P(), P(), P(), P()) + (weight_spec,) * 4
    out_specs = (token_spec, token_spec) + (weight_spec,) * 4
    return jax.shard_map(local, mesh=mesh, in_specs=in_specs, out_specs=out_specs, check_vma=False)
```
